32 devices in a mesh: ctx: 32 (over z, y, x, core), tp: 1.
Axes of the slice: x: 2, y: 2, z: 4, core: 2. Of those that a mesh axis runs over, the one named last changes fastest.
Arguments:
- x_raw: bfloat16 [4096, 2560], P('ctx', 'tp'), may hold values from -6 to 6
- bc_raw: bfloat16 [4096, 256], P('ctx'), may hold values from -6 to 6
- gate_branch: bfloat16 [4096, 2560], P('ctx', 'tp'), may hold values from -6 to 6
- dt_raw: float32 [4096, 40], P('ctx', 'tp'), may hold values from -2 to 4
- conv_x: float32 [4, 2560], P(None, 'tp'), may hold values from -3 to 3
- conv_x_bias: float32 [2560], P('tp'), may hold values from -0.75 to -0.15
- conv_bc: float32 [4, 256], replicated, may hold values from -3 to 3
- conv_bc_bias: float32 [256], replicated, may hold values from -0.75 to -0.15
- dt_bias: float32 [40], P('tp'), may hold values from -4.2 to -3.6
- a_log: float32 [40], P('tp'), may hold values from -10 to 2
- d_skip: float32 [40], P('tp'), may hold values from 0.5 to 2
- out_weight: bfloat16 [2560, 2560], P('tp'), may hold values from -0.125 to 0.125
- grad_out: bfloat16 [4096, 2560], P('ctx'), may hold values from -6 to 6
Outputs:
- grad_x_conv: bfloat16 [4096, 2560], P('ctx', 'tp')
- grad_bc_conv: bfloat16 [4096, 256], P('ctx')
- grad_z: bfloat16 [4096, 2560], P('ctx', 'tp')
- grad_dt_raw: float32 [4096, 40], P('ctx', 'tp')
- out_weight_grad: float32 [2560, 2560], P('ctx', 'tp')
The draws below stay inside these ranges and needn't reach their ends.
All inputs are finite; a program needn't handle non-finite values.
Results may differ from the reference program's by a relative error of at most 0.003.
Values may be sent and summed in bfloat16 or wider, within the bound.
No kernel may reach another device: no remote copies, remote signals or barrier semaphores. Data moves between devices by JAX's collectives and lax.ppermute only.
A program may use at most 192 MiB of HBM per device.

```python
import jax
import jax.numpy as jnp
from jax import lax

D = 2560
SHARD_ATTENDERS = 40
P_SIZE = 64
N = 128
KERNEL = 4
TOK_DEV = 128
SEQUENCE_TOKENS = 4096
N_CTX = 32


def draw_a_log(key, part):
    pick_key, slow_key, middle_key, fast_key = jax.random.split(key, 4)
    slow_share = 0.5
    middle_share = 0.3
    chooser = jax.random.uniform(pick_key, (SHARD_ATTENDERS,), jnp.float32)
    slow_rate = jax.random.uniform(slow_key, (SHARD_ATTENDERS,), jnp.float32, 0.6, 0.9) / (SEQUENCE_TOKENS * 0.025)
    middle_rate = jax.random.uniform(middle_key, (SHARD_ATTENDERS,), jnp.float32, 0.45, 1.0) / (TOK_DEV * 0.03)
    fast_rate = jax.random.uniform(fast_key, (SHARD_ATTENDERS,), jnp.float32, 0.8, 2.5)
    picked = jnp.where(chooser < slow_share, slow_rate, jnp.where(chooser < slow_share + middle_share, middle_rate, fast_rate))
    return jnp.log(picked)


def draw_dt_raw(key, part):
    baseline_key, place_key, shift_random_key, lift_key = jax.random.split(key, 4)
    base_level = 0.5 * jax.random.truncated_normal(baseline_key, -4.0, 4.0, (SEQUENCE_TOKENS, SHARD_ATTENDERS), jnp.float32)
    span_width = SEQUENCE_TOKENS // 8
    window_positions = jax.random.permutation(place_key, 4)[:2]
    span_begin_index = window_positions * (2 * span_width) + jax.random.randint(shift_random_key, (2,), 0, span_width + 1)
    element_position = lax.broadcasted_iota(jnp.int32, (SEQUENCE_TOKENS, 1), 0)
    within_span_mask = jnp.any((element_position >= span_begin_index[None, :]) & (element_position < span_begin_index[None, :] + span_width), axis=1, keepdims=True)
    raise_offset = jax.random.uniform(lift_key, (SEQUENCE_TOKENS, SHARD_ATTENDERS), jnp.float32, 0.8, 1.6)
    return base_level + jnp.where(within_span_mask, raise_offset, 0.0)


def strengthened(values, rng, source, target, blocks, factor):
    def block_of(position):
        return (jnp.arange(values.shape[position]) // (values.shape[position] // blocks)).reshape((-1,) + (1,) * (values.ndim - 1 - position))

    first = jax.random.permutation(rng, blocks)[block_of(target)]
    far = (block_of(target) + blocks // 2) % blocks
    return jnp.where((block_of(source) == first) | (block_of(source) == far), factor * values, values)


def block_scale(stream_key, dims, shards, least, largest):
    gain = 1.0
    for position, blocks in shards:
        heights = jax.random.uniform(jax.random.fold_in(jax.random.fold_in(stream_key, 6), position), (blocks,), jnp.float32, least / len(shards), largest / len(shards))
        gain = gain * jnp.repeat(jnp.exp(heights), dims[position] // blocks).reshape((-1,) + (1,) * (len(dims) - 1 - position))
    return gain


def bell_draw(own_key, shape, width, limit, cuts=(), dtype=jnp.bfloat16):
    gain = block_scale(own_key, shape, cuts, -0.22, 0.18) if cuts else 1.0
    values = jax.random.normal(own_key, shape, jnp.float32) * width * gain
    return jnp.minimum(jnp.maximum(values, -limit), limit).astype(dtype)


def noise_with(stream_key, dims, scale, most, cuts, heavy, dtype=jnp.bfloat16):
    values = scale * jax.random.normal(stream_key, dims, jnp.float32)
    if cuts:
        values = values * block_scale(stream_key, dims, cuts, -0.22, 0.18)
    return jnp.clip(strengthened(values, jax.random.fold_in(stream_key, 3), *heavy), -most, most).astype(dtype)


def setup_inputs(seed: int = 0) -> dict:
    arg_keys = jax.random.split(jax.random.key(seed), 14)
    x_raw = bell_draw(arg_keys[0], (SEQUENCE_TOKENS, SHARD_ATTENDERS * P_SIZE), 1.0, 6.0, ((0, 32),))
    bc_raw = bell_draw(arg_keys[1], (SEQUENCE_TOKENS, 2 * N), 1.0, 6.0, ((0, 32),))
    gate_branch = bell_draw(arg_keys[2], (SEQUENCE_TOKENS, SHARD_ATTENDERS * P_SIZE), 1.0, 6.0, ((0, 32),))
    dt_raw = draw_dt_raw(jax.random.fold_in(arg_keys[13], 71), 0)
    conv_x = bell_draw(arg_keys[4], (KERNEL, SHARD_ATTENDERS * P_SIZE), KERNEL ** -0.5, 3.0, (), jnp.float32)
    conv_x_bias = jnp.clip(jax.random.uniform(arg_keys[5], (SHARD_ATTENDERS * P_SIZE,), jnp.float32, -0.75, -0.15), -0.75, -0.15)
    conv_bc = bell_draw(arg_keys[6], (KERNEL, 2 * N), KERNEL ** -0.5, 3.0, (), jnp.float32)
    conv_bc_bias = jnp.clip(jax.random.uniform(arg_keys[7], (2 * N,), jnp.float32, -0.75, -0.15), -0.75, -0.15)
    dt_bias = jnp.clip(jax.random.uniform(arg_keys[8], (SHARD_ATTENDERS,), jnp.float32, -4.2, -3.6), -4.2, -3.6)
    a_log = draw_a_log(jax.random.fold_in(arg_keys[13], 71), 0)
    d_skip = jnp.clip(jax.random.uniform(arg_keys[10], (SHARD_ATTENDERS,), jnp.float32, 0.5, 2.0), 0.5, 2.0)
    out_weight = bell_draw(arg_keys[11], (SHARD_ATTENDERS * P_SIZE, D), (SHARD_ATTENDERS * P_SIZE) ** -0.5, 0.125)
    grad_out = noise_with(arg_keys[12], (SEQUENCE_TOKENS, D), 1.0, 6.0, ((0, 32),), (0, 1, 32, 2.75))
    return {"x_raw": x_raw, "bc_raw": bc_raw, "gate_branch": gate_branch, "dt_raw": dt_raw, "conv_x": conv_x, "conv_x_bias": conv_x_bias, "conv_bc": conv_bc, "conv_bc_bias": conv_bc_bias, "dt_bias": dt_bias, "a_log": a_log, "d_skip": d_skip, "out_weight": out_weight, "grad_out": grad_out}


HIGH = lax.Precision.HIGHEST

def convolve(padded, kernel_weight, kernel_bias):
    length = padded.shape[0] - kernel_weight.shape[0] + 1
    result = jnp.broadcast_to(kernel_bias[None, :], (length, padded.shape[1]))
    for offset in range(kernel_weight.shape[0]):
        result = result + kernel_weight[offset][None, :] * padded[offset:offset + length]
    return result

def silu_slope(argument):
    gate_value = jax.nn.sigmoid(argument)
    return gate_value * (1.0 + argument * (1.0 - gate_value))

def decay_matrix(log_decay):
    length = log_decay.shape[0]
    row_index = lax.broadcasted_iota(jnp.int32, (length, length), 0)
    col_index = lax.broadcasted_iota(jnp.int32, (length, length), 1)
    causal = (row_index >= col_index)[None, :, :]
    per_head = log_decay.T
    spread = per_head[:, :, None] - per_head[:, None, :]
    return jnp.where(causal, jnp.exp(jnp.where(causal, spread, 0.0)), 0.0)

def local_state(inputs, b_rows, step_size, log_decay):
    last_decay = log_decay[-1]
    weight = jnp.exp(last_decay[None, :] - log_decay) * step_size
    scaled_in = weight[:, :, None] * inputs
    partial_state = jnp.einsum('shp,sn->hpn', scaled_in, b_rows, precision=HIGH)
    return (jnp.exp(last_decay), partial_state)

def local_grad(log_decay, grad_y, c_rows):
    scaled_grad = jnp.exp(log_decay)[:, :, None] * grad_y
    return jnp.einsum('thp,tn->hpn', scaled_grad, c_rows, precision=HIGH)

def block_forward(inputs, b_rows, c_rows, step_size, log_decay, state_in, skip_gain):
    decays = decay_matrix(log_decay)
    scores = jnp.dot(c_rows, b_rows.T, precision=HIGH)
    mixing = decays * scores[None, :, :] * step_size.T[:, None, :]
    within = jnp.einsum('hts,shp->thp', mixing, inputs, precision=HIGH)
    carried = jnp.einsum('hpn,tn->thp', state_in, c_rows, precision=HIGH)
    return within + jnp.exp(log_decay)[:, :, None] * carried + skip_gain[None, :, None] * inputs

def block_backward(inputs, b_rows, c_rows, step_size, log_decay, decay_rate, state_in, carry_in, grad_y, skip_gain):
    decays = decay_matrix(log_decay)
    scores = jnp.dot(c_rows, b_rows.T, precision=HIGH)
    products = jnp.einsum('thp,shp->hts', grad_y, inputs, precision=HIGH)
    weighted = decays * products
    direct = weighted * scores[None, :, :]
    term_grid = direct * step_size.T[:, None, :]
    mixing = decays * scores[None, :, :] * step_size.T[:, None, :]
    grad_in = skip_gain[None, :, None] * grad_y + jnp.einsum('hts,thp->shp', mixing, grad_y, precision=HIGH)
    last_decay = log_decay[-1]
    to_end = jnp.exp(last_decay[None, :] - log_decay)
    carry_b = jnp.einsum('hpn,sn->shp', carry_in, b_rows, precision=HIGH)
    grad_in = grad_in + (to_end * step_size)[:, :, None] * carry_b
    shared = jnp.einsum('hts,sh->ts', weighted, step_size, precision=HIGH)
    scaled_in = (to_end * step_size)[:, :, None] * inputs
    scaled_grad = jnp.exp(log_decay)[:, :, None] * grad_y
    grad_b = jnp.dot(shared.T, c_rows, precision=HIGH) + jnp.einsum('shp,hpn->sn', scaled_in, carry_in, precision=HIGH)
    grad_c = jnp.dot(shared, b_rows, precision=HIGH) + jnp.einsum('thp,hpn->tn', scaled_grad, state_in, precision=HIGH)
    carried = jnp.einsum('hpn,tn->thp', state_in, c_rows, precision=HIGH)
    carry_dot = lax.optimization_barrier(jnp.sum(inputs * carry_b, axis=2))
    leaving = to_end * step_size * carry_dot
    entering = jnp.exp(log_decay) * lax.optimization_barrier(jnp.sum(grad_y * carried, axis=2))
    grad_log = lax.optimization_barrier(jnp.sum(term_grid, axis=2)).T - lax.optimization_barrier(jnp.sum(term_grid, axis=1)).T + entering - leaving
    constant = lax.optimization_barrier(jnp.sum(leaving, axis=0)) + jnp.exp(last_decay) * lax.optimization_barrier(jnp.sum(carry_in * state_in, axis=(1, 2)))
    grad_rate = jnp.flip(jnp.cumsum(jnp.flip(grad_log, 0), axis=0), 0) + constant[None, :]
    grad_step = lax.optimization_barrier(jnp.sum(direct, axis=1)).T + to_end * carry_dot + decay_rate[None, :] * grad_rate
    return (grad_in, grad_b, grad_c, grad_step)

def reference(x_raw, bc_raw, gate_branch, dt_raw, conv_x, conv_x_bias, conv_bc, conv_bc_bias, dt_bias, a_log, d_skip, out_weight, grad_out):
    margin = KERNEL - 1
    pre_x = convolve(jnp.concatenate([jnp.zeros((margin, x_raw.shape[1]), jnp.float32), x_raw.astype(jnp.float32)]), conv_x, conv_x_bias)
    pre_bc = convolve(jnp.concatenate([jnp.zeros((margin, bc_raw.shape[1]), jnp.float32), bc_raw.astype(jnp.float32)]), conv_bc, conv_bc_bias)
    act_x = jax.nn.silu(pre_x)
    act_bc = jax.nn.silu(pre_bc)
    step_all = jax.nn.softplus(dt_raw + dt_bias[None, :])
    decay_rate = -jnp.exp(a_log)

    def split_blocks(array):
        return array.reshape((N_CTX, TOK_DEV) + array.shape[1:])
    inputs_b = split_blocks(act_x.reshape(SEQUENCE_TOKENS, SHARD_ATTENDERS, P_SIZE))
    b_blocks = split_blocks(act_bc[:, :N])
    c_blocks = split_blocks(act_bc[:, N:])
    step_b = split_blocks(step_all)
    log_b = jnp.cumsum(step_b * decay_rate[None, None, :], axis=1)

    def forward_step(state_in, parts):
        inputs, b_rows, step_size, log_decay = parts
        last_exp, partial_state = local_state(inputs, b_rows, step_size, log_decay)
        return (last_exp[:, None, None] * state_in + partial_state, state_in)
    zero_state = jnp.zeros((SHARD_ATTENDERS, P_SIZE, N), jnp.float32)
    _, states_in = lax.scan(forward_step, zero_state, (inputs_b, b_blocks, step_b, log_b))

    def forward_block(parts):
        inputs, b_rows, c_rows, step_size, log_decay, state_in = parts
        return block_forward(inputs, b_rows, c_rows, step_size, log_decay, state_in, d_skip)
    y_blocks = lax.map(forward_block, (inputs_b, b_blocks, c_blocks, step_b, log_b, states_in))
    y_all = y_blocks.reshape(SEQUENCE_TOKENS, SHARD_ATTENDERS * P_SIZE)
    gate_input = gate_branch.astype(jnp.float32)
    gated = (y_all * jax.nn.silu(gate_input)).astype(jnp.bfloat16)
    grad_gated = lax.dot_general(grad_out, out_weight, (((1,), (1,)), ((), ())), preferred_element_type=jnp.float32)
    grad_z = (grad_gated * y_all * silu_slope(gate_input)).astype(jnp.bfloat16)
    weight_grad = lax.dot_general(grad_out, gated, (((0,), (0,)), ((), ())), preferred_element_type=jnp.float32)
    grad_y = grad_gated * jax.nn.silu(gate_input)
    grad_y_b = split_blocks(grad_y.reshape(SEQUENCE_TOKENS, SHARD_ATTENDERS, P_SIZE))

    def reverse_step(carry, parts):
        log_decay, grad_block, c_rows = parts
        return (jnp.exp(log_decay[-1])[:, None, None] * carry + local_grad(log_decay, grad_block, c_rows), carry)
    _, carries = lax.scan(reverse_step, zero_state, (log_b, grad_y_b, c_blocks), reverse=True)

    def backward_block(parts):
        inputs, b_rows, c_rows, step_size, log_decay, state_in, carry_in, grad_block = parts
        return block_backward(inputs, b_rows, c_rows, step_size, log_decay, decay_rate, state_in, carry_in, grad_block, d_skip)
    grad_in, grad_b, grad_c, grad_step = lax.map(backward_block, (inputs_b, b_blocks, c_blocks, step_b, log_b, states_in, carries, grad_y_b))
    grad_x_conv = (grad_in.reshape(SEQUENCE_TOKENS, SHARD_ATTENDERS * P_SIZE) * silu_slope(pre_x)).astype(jnp.bfloat16)
    grad_bc = jnp.concatenate([grad_b.reshape(SEQUENCE_TOKENS, N), grad_c.reshape(SEQUENCE_TOKENS, N)], axis=1)
    grad_bc_conv = (grad_bc * silu_slope(pre_bc)).astype(jnp.bfloat16)
    grad_dt_raw = grad_step.reshape(SEQUENCE_TOKENS, SHARD_ATTENDERS) * jax.nn.sigmoid(dt_raw + dt_bias[None, :])
    return (grad_x_conv, grad_bc_conv, grad_z, grad_dt_raw, weight_grad)
```

```python
import functools

import jax
import jax.numpy as jnp
from jax import lax
from jax.experimental import pallas as pl
from jax.experimental.pallas import tpu as pltpu
from jax.sharding import PartitionSpec as P

KERNEL = 4


HIGH = lax.Precision.HIGHEST


def from_behind(value, axis, steps):
    count = lax.axis_size(axis)
    first, last = (max(0, -steps), min(count, count - steps))
    return lax.ppermute(value, axis, [(source, source + steps) for source in range(first, last)])


def fold_kernel(rows, reverse, t_ref, o_ref):
    count = t_ref.shape[0]
    padded = t_ref.shape[1] - 8
    decay = jnp.transpose(t_ref[:, padded, :])
    state = jnp.zeros((padded, t_ref.shape[2]), jnp.float32)
    for s in range(count - 1, -1, -1) if reverse else range(count):
        o_ref[s] = state[:rows]
        state = decay[:padded, s : s + 1] * state + t_ref[s, :padded]


def carried_in(last_exp, value, reverse):
    count = lax.axis_size("ctx")
    heads, head_size, state_size = value.shape
    rows = heads * head_size // count
    padded = -(-rows // 8) * 8
    flat = value.reshape(count, rows, state_size)
    decay = jnp.broadcast_to(last_exp[:, None], (heads, head_size)).reshape(count, 1, rows)
    message = jnp.concatenate(
        [
            jnp.pad(flat, ((0, 0), (0, padded - rows), (0, 0))),
            jnp.pad(decay, ((0, 0), (0, 7), (0, state_size - rows))),
        ],
        axis=1,
    )
    held = lax.all_to_all(message, "ctx", 0, 0, tiled=True)
    folded = pl.pallas_call(
        functools.partial(fold_kernel, rows, reverse),
        out_shape=jax.ShapeDtypeStruct((count, rows, state_size), jnp.float32),
        compiler_params=pltpu.CompilerParams(vmem_limit_bytes=32 * 1024 * 1024),
        cost_estimate=pl.CostEstimate(flops=4 * count * rows * 128, bytes_accessed=8 * count * rows * 128, transcendentals=0),
    )(held)
    back = lax.all_to_all(folded, "ctx", 0, 0, tiled=True)
    return back.reshape(heads, head_size, state_size)


def convolve(padded, kernel_weight, kernel_bias):
    length = padded.shape[0] - kernel_weight.shape[0] + 1
    result = jnp.broadcast_to(kernel_bias[None, :], (length, padded.shape[1]))
    for offset in range(kernel_weight.shape[0]):
        result = result + kernel_weight[offset][None, :] * padded[offset : offset + length]
    return result


def silu_slope(argument):
    gate_value = jax.nn.sigmoid(argument)
    return gate_value * (1.0 + argument * (1.0 - gate_value))


def decay_matrix(log_decay):
    length = log_decay.shape[0]
    row_index = lax.broadcasted_iota(jnp.int32, (length, length), 0)
    col_index = lax.broadcasted_iota(jnp.int32, (length, length), 1)
    causal = (row_index >= col_index)[None, :, :]
    per_head = log_decay.T
    spread = per_head[:, :, None] - per_head[:, None, :]
    return jnp.where(causal, jnp.exp(jnp.where(causal, spread, 0.0)), 0.0)


def local_state(inputs, b_rows, step_size, log_decay):
    last_decay = log_decay[-1]
    weight = jnp.exp(last_decay[None, :] - log_decay) * step_size
    scaled_in = weight[:, :, None] * inputs
    partial_state = jnp.einsum("shp,sn->hpn", scaled_in, b_rows, precision=HIGH)
    return (jnp.exp(last_decay), partial_state)


def local_grad(log_decay, grad_y, c_rows):
    scaled_grad = jnp.exp(log_decay)[:, :, None] * grad_y
    return jnp.einsum("thp,tn->hpn", scaled_grad, c_rows, precision=HIGH)


def block_forward(inputs, b_rows, c_rows, step_size, log_decay, state_in, skip_gain):
    decays = decay_matrix(log_decay)
    scores = jnp.dot(c_rows, b_rows.T, precision=HIGH)
    mixing = decays * scores[None, :, :] * step_size.T[:, None, :]
    within = jnp.einsum("hts,shp->thp", mixing, inputs, precision=HIGH)
    carried = jnp.einsum("hpn,tn->thp", state_in, c_rows, precision=HIGH)
    return within + jnp.exp(log_decay)[:, :, None] * carried + skip_gain[None, :, None] * inputs


def block_backward(
    inputs, b_rows, c_rows, step_size, log_decay, decay_rate, state_in, carry_in, grad_y, skip_gain
):
    decays = decay_matrix(log_decay)
    scores = jnp.dot(c_rows, b_rows.T, precision=HIGH)
    products = jnp.einsum("thp,shp->hts", grad_y, inputs, precision=HIGH)
    weighted = decays * products
    direct = weighted * scores[None, :, :]
    term_grid = direct * step_size.T[:, None, :]
    mixing = decays * scores[None, :, :] * step_size.T[:, None, :]
    grad_in = skip_gain[None, :, None] * grad_y + jnp.einsum(
        "hts,thp->shp", mixing, grad_y, precision=HIGH
    )
    last_decay = log_decay[-1]
    to_end = jnp.exp(last_decay[None, :] - log_decay)
    carry_b = jnp.einsum("hpn,sn->shp", carry_in, b_rows, precision=HIGH)
    grad_in = grad_in + (to_end * step_size)[:, :, None] * carry_b
    shared = jnp.einsum("hts,sh->ts", weighted, step_size, precision=HIGH)
    scaled_in = (to_end * step_size)[:, :, None] * inputs
    scaled_grad = jnp.exp(log_decay)[:, :, None] * grad_y
    grad_b = jnp.dot(shared.T, c_rows, precision=HIGH) + jnp.einsum(
        "shp,hpn->sn", scaled_in, carry_in, precision=HIGH
    )
    grad_c = jnp.dot(shared, b_rows, precision=HIGH) + jnp.einsum(
        "thp,hpn->tn", scaled_grad, state_in, precision=HIGH
    )
    carried = jnp.einsum("hpn,tn->thp", state_in, c_rows, precision=HIGH)
    carry_dot = jnp.sum(inputs * carry_b, axis=2)
    leaving = to_end * step_size * carry_dot
    entering = jnp.exp(log_decay) * jnp.sum(grad_y * carried, axis=2)
    grad_log = jnp.sum(term_grid, axis=2).T - jnp.sum(term_grid, axis=1).T + entering - leaving
    constant = jnp.sum(leaving, axis=0) + jnp.exp(last_decay) * jnp.sum(
        carry_in * state_in, axis=(1, 2)
    )
    grad_rate = jnp.flip(jnp.cumsum(jnp.flip(grad_log, 0), axis=0), 0) + constant[None, :]
    grad_step = jnp.sum(direct, axis=1).T + to_end * carry_dot + decay_rate[None, :] * grad_rate
    return (grad_in, grad_b, grad_c, grad_step)


def group_of(count):
    for size in (16, 8, 4, 2):
        if count % size == 0:
            return size
    return 1


def weight_gradient(gated, gathered, groups):
    count = lax.axis_size("ctx")
    size = len(groups[0])
    length, channels = gated.shape
    width = gathered.shape[-1]
    share = channels // size
    rows = width // count
    turned = gated.T.reshape(size, share, length)
    held = lax.all_to_all(turned, "ctx", 0, 0, axis_index_groups=groups, tiled=True)
    partial = lax.dot_general(
        gathered, held, (((0, 1), (0, 2)), ((), ())), preferred_element_type=jnp.float32
    )
    lanes = 128 if rows * share % 128 == 0 else share
    message = partial.astype(jnp.bfloat16).reshape(count, rows * share // lanes, lanes)
    parts = lax.all_to_all(message, "ctx", 0, 0, tiled=True)
    parts = parts.reshape(count // size, size, rows, share).astype(jnp.float32)
    return jnp.sum(parts, axis=0).transpose(1, 0, 2).reshape(rows, channels)


def per_device(
    x_raw,
    bc_raw,
    gate_branch,
    dt_raw,
    conv_x,
    conv_x_bias,
    conv_bc,
    conv_bc_bias,
    dt_bias,
    a_log,
    d_skip,
    out_weight,
    grad_out,
):
    length, head_count = dt_raw.shape
    margin = KERNEL - 1
    channels = x_raw.shape[1]
    count = lax.axis_size("ctx")
    size = group_of(count)
    groups = [list(range(at, at + size)) for at in range(0, count, size)]
    gathered = lax.all_gather(grad_out, "ctx", axis_index_groups=groups)
    joined = jnp.concatenate([x_raw[length - margin :], bc_raw[length - margin :]], axis=1)
    rim_rows = from_behind(joined, "ctx", 1)
    pre_x = convolve(
        jnp.concatenate([rim_rows[:, :channels], x_raw]).astype(jnp.float32), conv_x, conv_x_bias
    )
    pre_bc = convolve(
        jnp.concatenate([rim_rows[:, channels:], bc_raw]).astype(jnp.float32), conv_bc, conv_bc_bias
    )
    act_x = jax.nn.silu(pre_x)
    act_bc = jax.nn.silu(pre_bc)
    head_size = channels // head_count
    state_size = act_bc.shape[1] // 2
    inputs = act_x.reshape(length, head_count, head_size)
    b_rows = act_bc[:, :state_size]
    c_rows = act_bc[:, state_size:]
    step_size = jax.nn.softplus(dt_raw + dt_bias[None, :])
    decay_rate = -jnp.exp(a_log)
    log_decay = jnp.cumsum(step_size * decay_rate[None, :], axis=0)
    last_exp, partial_state = local_state(inputs, b_rows, step_size, log_decay)
    gate_input = gate_branch.astype(jnp.float32)
    grad_gated = lax.dot_general(
        grad_out, out_weight, (((1,), (1,)), ((), ())), preferred_element_type=jnp.float32
    )
    grad_y = (grad_gated * jax.nn.silu(gate_input)).reshape(length, head_count, head_size)
    state_in = carried_in(last_exp, partial_state, False)
    output_y = block_forward(inputs, b_rows, c_rows, step_size, log_decay, state_in, d_skip)
    state_grad = local_grad(log_decay, grad_y, c_rows)
    carry_in = carried_in(last_exp, state_grad, True)
    y_flat = output_y.reshape(length, channels)
    gated = (y_flat * jax.nn.silu(gate_input)).astype(jnp.bfloat16)
    grad_z = (grad_gated * y_flat * silu_slope(gate_input)).astype(jnp.bfloat16)
    weight_grad = weight_gradient(gated, gathered, groups)
    grad_in, grad_b, grad_c, grad_step = block_backward(
        inputs, b_rows, c_rows, step_size, log_decay, decay_rate, state_in, carry_in, grad_y, d_skip
    )
    grad_b, grad_c = lax.psum((grad_b, grad_c), "tp")
    grad_x_conv = (grad_in.reshape(length, channels) * silu_slope(pre_x)).astype(jnp.bfloat16)
    grad_bc = jnp.concatenate([grad_b, grad_c], axis=1)
    grad_bc_conv = (grad_bc * silu_slope(pre_bc)).astype(jnp.bfloat16)
    grad_dt_raw = grad_step * jax.nn.sigmoid(dt_raw + dt_bias[None, :])
    return (grad_x_conv, grad_bc_conv, grad_z, grad_dt_raw, weight_grad)


def solution(mesh):
    placed = (
        P("ctx", "tp"),
        P("ctx", None),
        P("ctx", "tp"),
        P("ctx", "tp"),
        P(None, "tp"),
        P("tp"),
        P(),
        P(),
        P("tp"),
        P("tp"),
        P("tp"),
        P("tp", None),
        P("ctx", None),
    )
    return jax.shard_map(
        per_device,
        mesh=mesh,
        in_specs=placed,
        out_specs=(P("ctx", "tp"), P("ctx", None), P("ctx", "tp"), P("ctx", "tp"), P("ctx", "tp")),
        check_vma=False,
    )
```

```python
import functools

import jax
import jax.numpy as jnp
from jax import lax
from jax.experimental import pallas as pl
from jax.experimental.pallas import tpu as pltpu
from jax.sharding import PartitionSpec as P

KERNEL = 4
LANES = 128
F32 = jnp.float32
BF16 = jnp.bfloat16
NN = ((1,), (0,))
NT = ((1,), (1,))
HIGH = lax.Precision.HIGHEST
PARAMS = pltpu.CompilerParams(vmem_limit_bytes=48 * 1024 * 1024)


def call(kernel, out_shapes, operands, flops, scratch=()):
    moved = sum(a.size * a.dtype.itemsize for a in (*operands, *out_shapes))
    return pl.pallas_call(
        kernel,
        out_shape=tuple(out_shapes),
        scratch_shapes=list(scratch),
        compiler_params=PARAMS,
        cost_estimate=pl.CostEstimate(flops=flops, bytes_accessed=moved, transcendentals=0),
    )(*operands)


def shape(dims, dtype=F32):
    return jax.ShapeDtypeStruct(dims, dtype)


def split(value):
    high = value.astype(BF16)
    return high, (value - high.astype(F32)).astype(BF16)


def dot(a, b, dims):
    return lax.dot_general(a, b, (dims, ((), ())), preferred_element_type=F32)


def dot3(a, b, dims=NN):
    return dot(a[0], b[0], dims) + (dot(a[0], b[1], dims) + dot(a[1], b[0], dims))


def sigmoid(value):
    return 1.0 / (1.0 + jnp.exp(-value))


def lane_ids(rows, cols=LANES):
    return lax.broadcasted_iota(jnp.int32, (rows, cols), 1)


def row_ids(rows, cols=LANES):
    return lax.broadcasted_iota(jnp.int32, (rows, cols), 0)


def spread(columns, block, heads, size):
    first = block * heads
    lanes = lane_ids(columns.shape[0])
    wide = jnp.broadcast_to(columns[:, first : first + 1], (columns.shape[0], LANES))
    for k in range(1, heads):
        wide = jnp.where(lanes >= k * size, columns[:, first + k : first + k + 1], wide)
    return wide


def head_of(block, heads, size):
    inner = row_ids(LANES)
    target = lane_ids(LANES)
    result = jnp.zeros((LANES, LANES), F32)
    for k in range(heads):
        here = (inner >= k * size) & (inner < (k + 1) * size) & (target == block * heads + k)
        result = jnp.where(here, 1.0, result)
    return result.astype(BF16)


def stacked(value, heads, size):
    lanes = lane_ids(value.shape[0])
    return jnp.concatenate(
        [jnp.where((lanes >= k * size) & (lanes < (k + 1) * size), value, 0.0) for k in range(heads)],
        axis=0,
    )


def up8(value):
    return -(-value // 8) * 8


def pack_blocks(source, message, last_exp, size, rows):
    count = message.shape[0]
    padded = up8(rows)
    heads = source.shape[0] // size
    shift = size.bit_length() - 1
    owner = lax.shift_right_logical(
        lax.broadcasted_iota(jnp.int32, (count, LANES), 0) * rows + lane_ids(count), shift
    )
    table = jnp.zeros((count, LANES), F32)
    for h in range(heads):
        table = jnp.where(owner == h, last_exp[:, h : h + 1], table)
    high = table.astype(BF16).astype(F32)
    low = table - high
    place = row_ids(8)
    for d in range(count):
        block = source[rows * d : rows * (d + 1), :]
        top = jnp.max(jnp.max(jnp.abs(block), axis=0, keepdims=True), axis=1, keepdims=True)
        exponent = jnp.floor(jnp.log2(jnp.maximum(jnp.broadcast_to(top, (1, LANES)), 1e-30)))
        message[d, 0:rows, :] = block * jnp.exp2(13.0 - exponent)
        if padded > rows:
            message[d, rows:padded, :] = jnp.zeros((padded - rows, LANES), F32)
        notes = jnp.where(place == 0, high[d : d + 1], jnp.where(place == 1, low[d : d + 1], exponent))
        message[d, padded : padded + 8, :] = notes


def unpack_blocks(message, target, rows):
    padded = up8(rows)
    for d in range(message.shape[0]):
        scale = jnp.exp2(message[d, padded + 2 : padded + 3, :] - 13.0)
        target[rows * d : rows * (d + 1), :] = message[d, 0:rows, :] * scale


def prepare_kernel(
    heads_in, size, rows, x_ref, rim_ref, bc_ref, rim_bc_ref, wx_ref, bx_ref, wbc_ref, bbc_ref, dt_ref,
    dtb_ref, alog_ref, act_ref, slope_ref, abc_ref, sbc_ref, step_ref, ld_ref, stept_ref, ldt_ref, msg_ref,
    xs_ref, bs_ref, st_ref,
):
    length = x_ref.shape[0]
    blocks = x_ref.shape[1] // LANES

    def convolved(raw, rim, padded, weight, bias, cols):
        padded[0:8, cols] = rim[:, cols].astype(F32)[8:16]
        padded[8 : 8 + length, cols] = raw[:, cols].astype(F32)
        pre = bias[:, cols] + weight[0:1, cols] * padded[5 : 5 + length, cols]
        for k in range(1, KERNEL):
            pre = pre + weight[k : k + 1, cols] * padded[5 + k : 5 + k + length, cols]
        gate = sigmoid(pre)
        return pre * gate, gate * (1.0 + pre * (1.0 - gate))

    for j in range(bc_ref.shape[1] // LANES):
        cols = slice(j * LANES, (j + 1) * LANES)
        value, slope = convolved(bc_ref, rim_bc_ref, bs_ref, wbc_ref, bbc_ref, cols)
        abc_ref[:, cols] = value
        sbc_ref[:, cols] = slope
    b_rows = split(abc_ref[:, 0:LANES])
    raised = dt_ref[...] + dtb_ref[...]
    step = jnp.maximum(raised, 0.0) + jnp.log1p(jnp.exp(-jnp.abs(raised)))
    lower = jnp.where(row_ids(length) >= lane_ids(length), 1.0, 0.0)
    ld = lax.dot_general(
        lower, step * -jnp.exp(alog_ref[...]), (NN, ((), ())), precision=HIGH, preferred_element_type=F32
    )
    step_ref[...] = step
    ld_ref[...] = ld
    stept_ref[...] = step.T
    ldt_ref[...] = ld.T
    last = ld[length - 1 : length]
    weight = jnp.exp(last - ld) * step
    for j in range(blocks):
        cols = slice(j * LANES, (j + 1) * LANES)
        value, slope = convolved(x_ref, rim_ref, xs_ref, wx_ref, bx_ref, cols)
        act_ref[:, cols] = value
        slope_ref[:, cols] = slope
        scaled = value * spread(weight, j, heads_in, size)
        st_ref[cols, :] = dot3(split(scaled.T), b_rows)
    pack_blocks(st_ref, msg_ref, jnp.exp(last), size, rows)


def grad_kernel(heads_in, size, rows, gg_ref, gate_ref, abc_ref, ld_ref, gy_ref, msg_ref, st_ref):
    length = gg_ref.shape[0]
    c_rows = split(abc_ref[:, LANES : 2 * LANES])
    ld = ld_ref[...]
    grown = jnp.exp(ld)
    for j in range(gg_ref.shape[1] // LANES):
        cols = slice(j * LANES, (j + 1) * LANES)
        gate = gate_ref[:, cols].astype(F32)
        grad_y = gg_ref[:, cols] * (gate * sigmoid(gate))
        gy_ref[:, cols] = grad_y
        scaled = grad_y * spread(grown, j, heads_in, size)
        st_ref[cols, :] = dot3(split(scaled.T), c_rows)
    pack_blocks(st_ref, msg_ref, grown[length - 1 : length], size, rows)


def fold_kernel(rows, reverse, t_ref, o_ref):
    count = t_ref.shape[0]
    padded = up8(rows)
    decay = jnp.transpose(t_ref[:, padded, :] + t_ref[:, padded + 1, :])[:padded]
    state = jnp.zeros((padded, LANES), F32)
    for s in range(count - 1, -1, -1) if reverse else range(count):
        top = jnp.max(jnp.max(jnp.abs(state), axis=0, keepdims=True), axis=1, keepdims=True)
        exponent = jnp.floor(jnp.log2(jnp.maximum(jnp.broadcast_to(top, (1, LANES)), 1e-30)))
        o_ref[s, 0:padded, :] = state * jnp.exp2(13.0 - exponent)
        o_ref[s, padded : padded + 8, :] = jnp.broadcast_to(exponent, (8, LANES))
        scale = jnp.exp2(t_ref[s, padded + 2 : padded + 3, :] - 13.0)
        state = decay[:, s : s + 1] * state + t_ref[s, 0:padded, :] * scale


def local_kernel(
    heads_in, size, act_ref, gy_ref, abc_ref, step_ref, ld_ref, stept_ref, ldt_ref, yw_ref, gw_ref, gbc_ref, sh_ref
):
    length = act_ref.shape[0]
    b_rows = split(abc_ref[:, 0:LANES])
    c_rows = split(abc_ref[:, LANES : 2 * LANES])
    scores = dot3(c_rows, b_rows, NT)
    turned = dot3(b_rows, c_rows, NT)
    causal = row_ids(length) >= lane_ids(length)
    causal_t = row_ids(length) <= lane_ids(length)
    sh_ref[...] = jnp.zeros_like(sh_ref)
    for j in range(act_ref.shape[1] // LANES):
        cols = slice(j * LANES, (j + 1) * LANES)
        mixes, mixes_t, steps = [], [], []
        for h in range(j * heads_in, (j + 1) * heads_in):
            column, row = ld_ref[:, h : h + 1], ldt_ref[h : h + 1, :]
            decays = jnp.exp(jnp.where(causal, column - row, -1e30))
            stepped = decays * stept_ref[h : h + 1, :]
            decays_t = jnp.exp(jnp.where(causal_t, row - column, -1e30))
            steps.append(stepped)
            mixes.append(stepped * scores)
            mixes_t.append(decays_t * turned * step_ref[:, h : h + 1])
        inputs = act_ref[:, cols]
        grad_y = gy_ref[:, cols]
        inputs_s = stacked(inputs, heads_in, size)
        grads_s = split(stacked(grad_y, heads_in, size))
        yw_ref[:, cols] = dot3(split(jnp.concatenate(mixes, axis=1)), split(inputs_s))
        gw_ref[:, cols] = dot3(split(jnp.concatenate(mixes_t, axis=1)), grads_s)
        products = dot3(grads_s, split(inputs), NT)
        total = sh_ref[...]
        for k in range(heads_in):
            total = total + steps[k] * products[k * length : (k + 1) * length]
        sh_ref[...] = total
    shared = sh_ref[...]
    gbc_ref[:, 0:LANES] = dot3(split(shared.T), c_rows)
    gbc_ref[:, LANES : 2 * LANES] = dot3(split(shared), b_rows)


def place_of(channel, share, size):
    if share > LANES:
        if channel < LANES * size:
            return channel // LANES, channel % LANES
        rest = share - LANES
        return (channel - LANES * size) // rest, LANES + (channel - LANES * size) % rest
    return channel // share, channel % share


def forward_kernel(
    heads_in, size, rows, msg_ref, act_ref, gg_ref, gy_ref, gate_ref, abc_ref, ld_ref, yw_ref, skip_ref,
    gz_ref, gt_ref, yg_ref, st_ref,
):
    share = gt_ref.shape[1]
    unpack_blocks(msg_ref, st_ref, rows)
    c_rows = split(abc_ref[:, LANES : 2 * LANES])
    grown = jnp.exp(ld_ref[...])
    sums = jnp.zeros(yg_ref.shape, F32)
    for j in range(act_ref.shape[1] // LANES):
        cols = slice(j * LANES, (j + 1) * LANES)
        carried = dot3(c_rows, split(st_ref[cols, :]), NT)
        within = yw_ref[:, cols] + spread(grown, j, heads_in, size) * carried
        output = within + skip_ref[:, cols] * act_ref[:, cols]
        gate = gate_ref[:, cols].astype(F32)
        opened = sigmoid(gate)
        gated = output * (gate * opened)
        turned = gated.T.astype(BF16)
        for k in range(0, LANES, 16):
            to, at = place_of(j * LANES + k, share, gt_ref.shape[0])
            gt_ref[to, at : at + 16, :] = turned[k : k + 16]
        gz_ref[:, cols] = (gg_ref[:, cols] * output * (opened * (1.0 + gate * (1.0 - opened)))).astype(BF16)
        high, low = split(gy_ref[:, cols] * within)
        onehot = head_of(j, heads_in, size)
        sums = sums + (dot(high, onehot, NN) + dot(low, onehot, NN))
    yg_ref[...] = sums


def backward_kernel(
    heads_in, size, rows, msg_ref, msgf_ref, act_ref, slope_ref, gy_ref, abc_ref, step_ref, ld_ref, gw_ref,
    gbcl_ref, yg_ref, skip_ref, dt_ref, dtb_ref, alog_ref, gx_ref, gbc_ref, gdt_ref, ca_ref, st_ref, cs_ref,
):
    length = act_ref.shape[0]
    unpack_blocks(msg_ref, ca_ref, rows)
    unpack_blocks(msgf_ref, st_ref, rows)
    b_rows = split(abc_ref[:, 0:LANES])
    ld = ld_ref[...]
    step = step_ref[...]
    last = ld[length - 1 : length]
    grown = jnp.exp(ld)
    weight = jnp.exp(last - ld) * step
    sums = jnp.zeros((length, LANES), F32)
    leaving = jnp.zeros((8, LANES), F32)
    grad_b = gbcl_ref[:, 0:LANES]
    grad_c = gbcl_ref[:, LANES : 2 * LANES]
    cs_ref[...] = jnp.zeros_like(cs_ref)
    for j in range(act_ref.shape[1] // LANES):
        cols = slice(j * LANES, (j + 1) * LANES)
        inputs = act_ref[:, cols]
        grad_y = gy_ref[:, cols]
        carry = ca_ref[cols, :]
        state = st_ref[cols, :]
        carry_s = split(carry)
        wide = spread(weight, j, heads_in, size)
        gone = wide * dot3(b_rows, carry_s, NT)
        grad_in = gw_ref[:, cols] + gone
        gx_ref[:, cols] = ((skip_ref[:, cols] * grad_y + grad_in) * slope_ref[:, cols]).astype(BF16)
        onehot = head_of(j, heads_in, size)
        high, low = split(inputs * grad_in)
        sums = sums + (dot(high, onehot, NN) + dot(low, onehot, NN))
        folded = jnp.sum((inputs * gone).reshape(length // 8, 8, LANES), axis=0)
        high, low = split(folded)
        leaving = leaving + (dot(high, onehot, NN) + dot(low, onehot, NN))
        product = carry * state
        for k in range(heads_in):
            h = j * heads_in + k
            cs_ref[h : h + 1, :] = jnp.sum(product[k * size : (k + 1) * size], axis=0, keepdims=True)
        grad_b = grad_b + dot3(split(wide * inputs), carry_s)
        grad_c = grad_c + dot3(split(spread(grown, j, heads_in, size) * grad_y), split(state))
    gbc_ref[:, 0:LANES] = grad_b
    gbc_ref[:, LANES : 2 * LANES] = grad_c
    both = lax.dot_general(
        jnp.ones((8, LANES), F32), cs_ref[...], (NT, ((), ())), precision=HIGH, preferred_element_type=F32
    )
    constant = jnp.sum(leaving, axis=0, keepdims=True) + jnp.exp(last) * both[0:1]
    upper = jnp.where(row_ids(length) <= lane_ids(length), 1.0, 0.0)
    grad_rate = constant + lax.dot_general(
        upper, yg_ref[...] - sums, (NN, ((), ())), precision=HIGH, preferred_element_type=F32
    )
    grad_step = sums / step - jnp.exp(alog_ref[...]) * grad_rate
    gdt_ref[...] = grad_step * sigmoid(dt_ref[...] + dtb_ref[...])


def product_kernel(rows, held_ref, go_ref, out_ref, lhs_ref):
    size, share, length = held_ref.shape

    @pl.when(pl.program_id(0) == 0)
    def _():
        for s in range(size):
            lhs_ref[:, s * length : (s + 1) * length] = held_ref[s]

    result = dot(lhs_ref[...], go_ref[...], NN).T
    for d in range(out_ref.shape[0]):
        block = result[rows * d : rows * (d + 1)]
        top = jnp.max(jnp.max(jnp.abs(block), axis=0, keepdims=True), axis=1, keepdims=True)
        exponent = jnp.floor(jnp.log2(jnp.maximum(jnp.broadcast_to(top, (1, LANES)), 1e-30)))
        scale = jnp.exp2(13.0 - exponent)
        if share > LANES:
            rest = share - LANES
            across = LANES // rest
            out_ref[d, 0:rows, :] = block[:, 0:LANES] * scale
            extra = block[:, LANES:share] * scale[:, 0:rest]
            for k in range(0, rows // 16, across):
                pieces = [extra[16 * m : 16 * m + 16] for m in range(k, min(k + across, rows // 16))]
                at = rows + 16 * (k // across)
                filled = rest * len(pieces)
                if filled < LANES:
                    pieces.append(jnp.broadcast_to(exponent[:, filled:], (16, LANES - filled)))
                out_ref[d, at : at + 16, :] = jnp.concatenate(pieces, axis=1)
        else:
            out_ref[d, 0:rows, :] = block * scale[:, 0:share]
            out_ref[d, rows : rows + 4, :] = jnp.broadcast_to(exponent[:, 0:share], (4, share))


def assemble_kernel(rows, size, share, parts_ref, out_ref):
    count = parts_ref.shape[0]
    last = parts_ref.shape[2] - 1
    scales = [jnp.exp2(parts_ref[s, parts_ref.shape[1] - 1, last] - 13.0) for s in range(count)]
    if share > LANES:
        rest = share - LANES
        across = LANES // rest
        for c in range(size):
            total = parts_ref[c, 0:rows, :] * scales[c]
            for s in range(c + size, count, size):
                total = total + parts_ref[s, 0:rows, :] * scales[s]
            out_ref[:, c * LANES : (c + 1) * LANES] = total
        for q in range(size // across):
            for k in range(rows // 16):
                at = rows + 16 * (k // across)
                lanes = slice(rest * (k % across), rest * (k % across + 1))
                pieces = []
                for c in range(q * across, (q + 1) * across):
                    total = parts_ref[c, at : at + 16, lanes] * scales[c]
                    for s in range(c + size, count, size):
                        total = total + parts_ref[s, at : at + 16, lanes] * scales[s]
                    pieces.append(total)
                first = (size + q) * LANES
                out_ref[16 * k : 16 * k + 16, first : first + LANES] = jnp.concatenate(pieces, axis=1)
    else:
        for c in range(size):
            total = parts_ref[c, 0:rows, :] * scales[c]
            for s in range(c + size, count, size):
                total = total + parts_ref[s, 0:rows, :] * scales[s]
            out_ref[:, c * share : (c + 1) * share] = total


def exchange(message):
    return lax.all_to_all(message.astype(jnp.float16), "ctx", 0, 0, tiled=True).astype(F32)


def carried_in(message, rows, reverse):
    held = exchange(message)
    (folded,) = call(
        functools.partial(fold_kernel, rows, reverse), [shape(message.shape)], [held], 8 * message.size
    )
    return exchange(folded)


def group_of(count):
    for size in (16, 8, 4, 2):
        if count % size == 0:
            return size
    return 1


def from_behind(value, axis):
    count = lax.axis_size(axis)
    return lax.ppermute(value, axis, [(source, source + 1) for source in range(count - 1)])


def per_device(
    x_raw,
    bc_raw,
    gate_branch,
    dt_raw,
    conv_x,
    conv_x_bias,
    conv_bc,
    conv_bc_bias,
    dt_bias,
    a_log,
    d_skip,
    out_weight,
    grad_out,
):
    length, head_count = dt_raw.shape
    channels = x_raw.shape[1]
    width = grad_out.shape[1]
    head_size = channels // head_count
    heads_in = LANES // head_size
    count = lax.axis_size("ctx")
    rows = channels // count
    size = group_of(count)
    share = channels // size
    groups = [list(range(at, at + size)) for at in range(0, count, size)]
    gathered = lax.all_gather(grad_out, "ctx", axis_index_groups=groups, tiled=True)

    rim = from_behind(jnp.concatenate([x_raw[length - 16 :], bc_raw[length - 16 :]], axis=1), "ctx")
    fill = ((0, 0), (0, LANES - head_count))
    dt_wide = jnp.pad(dt_raw, fill)
    dtb_wide = jnp.pad(dt_bias[None, :], fill)
    alog_wide = jnp.pad(a_log[None, :], fill)
    skip = jnp.repeat(d_skip, head_size)[None, :]
    whole = (length, channels)
    square = (length, LANES)
    packed = (count, up8(rows) + 8, LANES)
    stored = pltpu.VMEM((channels, LANES), F32)
    unit = 2 * length * channels * LANES

    act_x, slope_x, act_bc, slope_bc, step, ld, step_t, ld_t, message = call(
        functools.partial(prepare_kernel, heads_in, head_size, rows),
        [shape(whole), shape(whole), shape(bc_raw.shape), shape(bc_raw.shape)]
        + [shape(square)] * 2
        + [shape((LANES, length))] * 2
        + [shape(packed)],
        [
            x_raw,
            rim[:, :channels],
            bc_raw,
            rim[:, channels:],
            conv_x,
            conv_x_bias[None, :],
            conv_bc,
            conv_bc_bias[None, :],
            dt_wide,
            dtb_wide,
            alog_wide,
        ],
        20 * unit,
        [pltpu.VMEM((length + 8, channels), F32), pltpu.VMEM((length + 8, bc_raw.shape[1]), F32), stored],
    )
    grad_gated = lax.dot_general(
        grad_out, out_weight, (((1,), (1,)), ((), ())), preferred_element_type=F32
    )
    state_message = carried_in(message, rows, False)
    grad_y, message = call(
        functools.partial(grad_kernel, heads_in, head_size, rows),
        [shape(whole), shape(packed)],
        [grad_gated, gate_branch, act_bc, ld],
        20 * unit,
        [stored],
    )
    carry_message = carried_in(message, rows, True)
    y_within, grad_within, grad_bc_within = call(
        functools.partial(local_kernel, heads_in, head_size),
        [shape(whole), shape(whole), shape(act_bc.shape)],
        [act_x, grad_y, act_bc, step, ld, step_t, ld_t],
        40 * unit,
        [pltpu.VMEM(square, F32)],
    )
    grad_z, gated, y_sums = call(
        functools.partial(forward_kernel, heads_in, head_size, rows),
        [shape(whole, BF16), shape((size, share, length), BF16), shape(square)],
        [state_message, act_x, grad_gated, grad_y, gate_branch, act_bc, ld, y_within, skip],
        20 * unit,
        [stored],
    )
    held = lax.all_to_all(gated, "ctx", 0, 0, axis_index_groups=groups, tiled=True)
    out_rows = width // count
    part = width
    for candidate in (640, 1280):
        if width % candidate == 0 and candidate % out_rows == 0:
            part = candidate
            break
    if share > LANES:
        across = LANES // (share - LANES)
        dims = (out_rows + 16 * (-(-(out_rows // 16) // across)), LANES)
    else:
        dims = (out_rows + 4, share)
    partial = pl.pallas_call(
        functools.partial(product_kernel, out_rows),
        grid=(width // part,),
        in_specs=[
            pl.BlockSpec((size, share, length), lambda i: (0, 0, 0)),
            pl.BlockSpec((size * length, part), lambda i: (0, i)),
        ],
        out_specs=pl.BlockSpec((part // out_rows, *dims), lambda i: (i, 0, 0)),
        out_shape=shape((count, *dims)),
        scratch_shapes=[pltpu.VMEM((share, size * length), BF16)],
        compiler_params=PARAMS,
        cost_estimate=pl.CostEstimate(
            flops=2 * size * length * share * width, bytes_accessed=2 * size * length * width, transcendentals=0
        ),
    )(held, gathered)
    parts = exchange(partial)
    (weight_grad,) = call(
        functools.partial(assemble_kernel, out_rows, size, share),
        [shape((out_rows, channels))],
        [parts],
        2 * parts.size,
    )
    grad_x_conv, grad_bc, grad_dt_raw = call(
        functools.partial(backward_kernel, heads_in, head_size, rows),
        [shape(whole, BF16), shape(act_bc.shape), shape(square)],
        [
            carry_message,
            state_message,
            act_x,
            slope_x,
            grad_y,
            act_bc,
            step,
            ld,
            grad_within,
            grad_bc_within,
            y_sums,
            skip,
            dt_wide,
            dtb_wide,
            alog_wide,
        ],
        40 * unit,
        [stored, stored, pltpu.VMEM((LANES, LANES), F32)],
    )
    grad_bc_conv = (lax.psum(grad_bc, "tp") * slope_bc).astype(BF16)
    return (grad_x_conv, grad_bc_conv, grad_z, grad_dt_raw[:, :head_count], weight_grad)


def solution(mesh):
    placed = (
        P("ctx", "tp"),
        P("ctx", None),
        P("ctx", "tp"),
        P("ctx", "tp"),
        P(None, "tp"),
        P("tp"),
        P(),
        P(),
        P("tp"),
        P("tp"),
        P("tp"),
        P("tp", None),
        P("ctx", None),
    )
    return jax.shard_map(
        per_device,
        mesh=mesh,
        in_specs=placed,
        out_specs=(P("ctx", "tp"), P("ctx", None), P("ctx", "tp"), P("ctx", "tp"), P("ctx", "tp")),
        check_vma=False,
    )
```

```python
import functools

import jax
import jax.numpy as jnp
from jax import lax
from jax.experimental import pallas as pl
from jax.experimental.pallas import tpu as pltpu
from jax.sharding import PartitionSpec as P

KERNEL = 4
LANES = 128
F32 = jnp.float32
BF16 = jnp.bfloat16
NN = ((1,), (0,))
NT = ((1,), (1,))
HIGH = lax.Precision.HIGHEST
PARAMS = pltpu.CompilerParams(vmem_limit_bytes=48 * 1024 * 1024)


def call(kernel, out_shapes, operands, flops, scratch=()):
    moved = sum(a.size * a.dtype.itemsize for a in (*operands, *out_shapes))
    return pl.pallas_call(
        kernel,
        out_shape=tuple(out_shapes),
        scratch_shapes=list(scratch),
        compiler_params=PARAMS,
        cost_estimate=pl.CostEstimate(flops=flops, bytes_accessed=moved, transcendentals=0),
    )(*operands)


def shape(dims, dtype=F32):
    return jax.ShapeDtypeStruct(dims, dtype)


def split(value):
    high = value.astype(BF16)
    return high, (value - high.astype(F32)).astype(BF16)


def dot(a, b, dims):
    return lax.dot_general(a, b, (dims, ((), ())), preferred_element_type=F32)


def dot3(a, b, dims=NN):
    return dot(a[0], b[0], dims) + (dot(a[0], b[1], dims) + dot(a[1], b[0], dims))


def sigmoid(value):
    return 1.0 / (1.0 + jnp.exp(-value))


def lane_ids(rows, cols=LANES):
    return lax.broadcasted_iota(jnp.int32, (rows, cols), 1)


def row_ids(rows, cols=LANES):
    return lax.broadcasted_iota(jnp.int32, (rows, cols), 0)


def spread(columns, block, heads, size):
    first = block * heads
    lanes = lane_ids(columns.shape[0])
    wide = jnp.broadcast_to(columns[:, first : first + 1], (columns.shape[0], LANES))
    for k in range(1, heads):
        wide = jnp.where(lanes >= k * size, columns[:, first + k : first + k + 1], wide)
    return wide


def head_of(block, heads, size):
    inner = row_ids(LANES)
    target = lane_ids(LANES)
    result = jnp.zeros((LANES, LANES), F32)
    for k in range(heads):
        here = (inner >= k * size) & (inner < (k + 1) * size) & (target == block * heads + k)
        result = jnp.where(here, 1.0, result)
    return result.astype(BF16)


def stacked(value, heads, size):
    lanes = lane_ids(value.shape[0])
    return jnp.concatenate(
        [jnp.where((lanes >= k * size) & (lanes < (k + 1) * size), value, 0.0) for k in range(heads)],
        axis=0,
    )


def up8(value):
    return -(-value // 8) * 8


def notes_of(rows):
    return -(-rows // LANES)


def exponent_of(block):
    top = jnp.max(jnp.max(jnp.abs(block), axis=0, keepdims=True), axis=1, keepdims=True)
    return jnp.floor(jnp.log2(jnp.maximum(jnp.broadcast_to(top, (1, LANES)), 1e-30)))


def write_block(message, at, block, decays, exponent):
    rows = block.shape[0]
    padded = up8(rows)
    message[at, 0:rows, :] = block * jnp.exp2(13.0 - exponent)
    if padded > rows:
        message[at, rows:padded, :] = jnp.zeros((padded - rows, LANES), F32)
    highs = [d.astype(BF16).astype(F32) for d in decays]
    lows = [d - h for d, h in zip(decays, highs)]
    place = row_ids(8)
    notes = jnp.broadcast_to(exponent, (8, LANES))
    for k, line in enumerate(highs + lows):
        notes = jnp.where(place == k, line, notes)
    message[at, padded : padded + 8, :] = notes


def pack_blocks(source, message, last_exp, size, rows):
    heads = source.shape[0] // size
    shift = size.bit_length() - 1
    lines = notes_of(rows)
    for d in range(message.shape[0]):
        decays = []
        for k in range(lines):
            first = rows * d + LANES * k
            owner = lax.shift_right_logical(lane_ids(1) + first, shift)
            table = jnp.zeros((1, LANES), F32)
            for h in range(first // size, min(heads, (first + LANES - 1) // size + 1)):
                table = jnp.where(owner == h, last_exp[:, h : h + 1], table)
            decays.append(table)
        block = source[rows * d : rows * (d + 1), :]
        write_block(message, d, block, decays, exponent_of(block))


def decay_lines(message, at, rows):
    padded, lines = up8(rows), notes_of(rows)
    return [
        message[at, padded + k : padded + k + 1, :] + message[at, padded + lines + k : padded + lines + k + 1, :]
        for k in range(lines)
    ]


def decay_columns(message, rows):
    padded, lines = up8(rows), notes_of(rows)
    turned = [
        jnp.transpose(message[:, padded + k, :] + message[:, padded + lines + k, :]) for k in range(lines)
    ]
    return jnp.concatenate(turned, axis=0)[0:rows]


def read_block(message, at, rows):
    padded = up8(rows)
    return message[at, 0:rows, :] * jnp.exp2(message[at, padded + 7 : padded + 8, :] - 13.0)


def unpack_blocks(message, target, rows):
    for d in range(message.shape[0]):
        target[rows * d : rows * (d + 1), :] = read_block(message, d, rows)


def total_kernel(rows, reverse, held_ref, out_ref):
    count = held_ref.shape[0]
    columns = decay_columns(held_ref, rows)
    state = None
    for s in range(count - 1, -1, -1) if reverse else range(count):
        block = read_block(held_ref, s, rows)
        state = block if state is None else columns[:, s : s + 1] * state + block
    decays = decay_lines(held_ref, 0, rows)
    for s in range(1, count):
        decays = [a * b for a, b in zip(decays, decay_lines(held_ref, s, rows))]
    write_block(out_ref, 0, state, decays, exponent_of(state))


def fold_kernel(rows, reverse, held_ref, *refs):
    others, out_ref = refs[:-1], refs[-1]
    count = held_ref.shape[0]
    columns = decay_columns(held_ref, rows)
    state = jnp.zeros((rows, LANES), F32)
    for other in reversed(others):
        state = decay_columns(other, rows) * state + read_block(other, 0, rows)
    for s in range(count - 1, -1, -1) if reverse else range(count):
        write_block(out_ref, s, state, [], exponent_of(state))
        if s != (0 if reverse else count - 1):
            state = columns[:, s : s + 1] * state + read_block(held_ref, s, rows)


def prepare_kernel(
    heads_in, size, rows, x_ref, rim_ref, bc_ref, rim_bc_ref, wx_ref, bx_ref, wbc_ref, bbc_ref, dt_ref,
    dtb_ref, alog_ref, act_ref, slope_ref, abc_ref, sbc_ref, step_ref, ld_ref, stept_ref, ldt_ref, msg_ref,
    xs_ref, bs_ref, st_ref,
):
    length = x_ref.shape[0]
    blocks = x_ref.shape[1] // LANES

    def convolved(raw, rim, padded, weight, bias, cols):
        padded[0:8, cols] = rim[:, cols].astype(F32)[8:16]
        padded[8 : 8 + length, cols] = raw[:, cols].astype(F32)
        pre = bias[:, cols] + weight[0:1, cols] * padded[5 : 5 + length, cols]
        for k in range(1, KERNEL):
            pre = pre + weight[k : k + 1, cols] * padded[5 + k : 5 + k + length, cols]
        gate = sigmoid(pre)
        return pre * gate, gate * (1.0 + pre * (1.0 - gate))

    for j in range(bc_ref.shape[1] // LANES):
        cols = slice(j * LANES, (j + 1) * LANES)
        value, slope = convolved(bc_ref, rim_bc_ref, bs_ref, wbc_ref, bbc_ref, cols)
        abc_ref[:, cols] = value
        sbc_ref[:, cols] = slope
    b_rows = split(abc_ref[:, 0:LANES])
    raised = dt_ref[...] + dtb_ref[...]
    step = jnp.maximum(raised, 0.0) + jnp.log1p(jnp.exp(-jnp.abs(raised)))
    lower = jnp.where(row_ids(length) >= lane_ids(length), 1.0, 0.0)
    ld = lax.dot_general(
        lower, step * -jnp.exp(alog_ref[...]), (NN, ((), ())), precision=HIGH, preferred_element_type=F32
    )
    step_ref[...] = step
    ld_ref[...] = ld
    stept_ref[...] = step.T
    ldt_ref[...] = ld.T
    last = ld[length - 1 : length]
    weight = jnp.exp(last - ld) * step
    for j in range(blocks):
        cols = slice(j * LANES, (j + 1) * LANES)
        value, slope = convolved(x_ref, rim_ref, xs_ref, wx_ref, bx_ref, cols)
        act_ref[:, cols] = value
        slope_ref[:, cols] = slope
        scaled = value * spread(weight, j, heads_in, size)
        st_ref[cols, :] = dot3(split(scaled.T), b_rows)
    pack_blocks(st_ref, msg_ref, jnp.exp(last), size, rows)


def grad_kernel(heads_in, size, rows, gg_ref, gate_ref, abc_ref, ld_ref, gy_ref, msg_ref, st_ref):
    length = gg_ref.shape[0]
    c_rows = split(abc_ref[:, LANES : 2 * LANES])
    ld = ld_ref[...]
    grown = jnp.exp(ld)
    for j in range(gg_ref.shape[1] // LANES):
        cols = slice(j * LANES, (j + 1) * LANES)
        gate = gate_ref[:, cols].astype(F32)
        grad_y = gg_ref[:, cols] * (gate * sigmoid(gate))
        gy_ref[:, cols] = grad_y
        scaled = grad_y * spread(grown, j, heads_in, size)
        st_ref[cols, :] = dot3(split(scaled.T), c_rows)
    pack_blocks(st_ref, msg_ref, grown[length - 1 : length], size, rows)


def local_kernel(
    heads_in, size, act_ref, gy_ref, abc_ref, step_ref, ld_ref, stept_ref, ldt_ref, yw_ref, gw_ref, gbc_ref, sh_ref
):
    length = act_ref.shape[0]
    b_rows = split(abc_ref[:, 0:LANES])
    c_rows = split(abc_ref[:, LANES : 2 * LANES])
    scores = dot3(c_rows, b_rows, NT)
    turned = dot3(b_rows, c_rows, NT)
    causal = row_ids(length) >= lane_ids(length)
    causal_t = row_ids(length) <= lane_ids(length)
    sh_ref[...] = jnp.zeros_like(sh_ref)
    for j in range(act_ref.shape[1] // LANES):
        cols = slice(j * LANES, (j + 1) * LANES)
        mixes, mixes_t, steps = [], [], []
        for h in range(j * heads_in, (j + 1) * heads_in):
            column, row = ld_ref[:, h : h + 1], ldt_ref[h : h + 1, :]
            decays = jnp.exp(jnp.where(causal, column - row, -1e30))
            stepped = decays * stept_ref[h : h + 1, :]
            decays_t = jnp.exp(jnp.where(causal_t, row - column, -1e30))
            steps.append(stepped)
            mixes.append(stepped * scores)
            mixes_t.append(decays_t * turned * step_ref[:, h : h + 1])
        inputs = act_ref[:, cols]
        grad_y = gy_ref[:, cols]
        inputs_s = stacked(inputs, heads_in, size)
        grads_s = split(stacked(grad_y, heads_in, size))
        yw_ref[:, cols] = dot3(split(jnp.concatenate(mixes, axis=1)), split(inputs_s))
        gw_ref[:, cols] = dot3(split(jnp.concatenate(mixes_t, axis=1)), grads_s)
        products = dot3(grads_s, split(inputs), NT)
        total = sh_ref[...]
        for k in range(heads_in):
            total = total + steps[k] * products[k * length : (k + 1) * length]
        sh_ref[...] = total
    shared = sh_ref[...]
    gbc_ref[:, 0:LANES] = dot3(split(shared.T), c_rows)
    gbc_ref[:, LANES : 2 * LANES] = dot3(split(shared), b_rows)


def place_of(channel, share, size):
    if share > LANES:
        if channel < LANES * size:
            return channel // LANES, channel % LANES
        rest = share - LANES
        return (channel - LANES * size) // rest, LANES + (channel - LANES * size) % rest
    return channel // share, channel % share


def forward_kernel(
    heads_in, size, rows, msg_ref, act_ref, gg_ref, gy_ref, gate_ref, abc_ref, ld_ref, yw_ref, skip_ref,
    gz_ref, gt_ref, yg_ref, st_ref,
):
    share = gt_ref.shape[1]
    unpack_blocks(msg_ref, st_ref, rows)
    c_rows = split(abc_ref[:, LANES : 2 * LANES])
    grown = jnp.exp(ld_ref[...])
    sums = jnp.zeros(yg_ref.shape, F32)
    for j in range(act_ref.shape[1] // LANES):
        cols = slice(j * LANES, (j + 1) * LANES)
        carried = dot3(c_rows, split(st_ref[cols, :]), NT)
        within = yw_ref[:, cols] + spread(grown, j, heads_in, size) * carried
        output = within + skip_ref[:, cols] * act_ref[:, cols]
        gate = gate_ref[:, cols].astype(F32)
        opened = sigmoid(gate)
        gated = output * (gate * opened)
        turned = gated.T.astype(BF16)
        for k in range(0, LANES, 16):
            to, at = place_of(j * LANES + k, share, gt_ref.shape[0])
            gt_ref[to, at : at + 16, :] = turned[k : k + 16]
        gz_ref[:, cols] = (gg_ref[:, cols] * output * (opened * (1.0 + gate * (1.0 - opened)))).astype(BF16)
        high, low = split(gy_ref[:, cols] * within)
        onehot = head_of(j, heads_in, size)
        sums = sums + (dot(high, onehot, NN) + dot(low, onehot, NN))
    yg_ref[...] = sums


def backward_kernel(
    heads_in, size, rows, msg_ref, msgf_ref, act_ref, slope_ref, gy_ref, abc_ref, step_ref, ld_ref, gw_ref,
    gbcl_ref, yg_ref, skip_ref, dt_ref, dtb_ref, alog_ref, gx_ref, gbc_ref, gdt_ref, ca_ref, st_ref, cs_ref,
):
    length = act_ref.shape[0]
    unpack_blocks(msg_ref, ca_ref, rows)
    unpack_blocks(msgf_ref, st_ref, rows)
    b_rows = split(abc_ref[:, 0:LANES])
    ld = ld_ref[...]
    step = step_ref[...]
    last = ld[length - 1 : length]
    grown = jnp.exp(ld)
    weight = jnp.exp(last - ld) * step
    sums = jnp.zeros((length, LANES), F32)
    leaving = jnp.zeros((8, LANES), F32)
    grad_b = gbcl_ref[:, 0:LANES]
    grad_c = gbcl_ref[:, LANES : 2 * LANES]
    cs_ref[...] = jnp.zeros_like(cs_ref)
    for j in range(act_ref.shape[1] // LANES):
        cols = slice(j * LANES, (j + 1) * LANES)
        inputs = act_ref[:, cols]
        grad_y = gy_ref[:, cols]
        carry = ca_ref[cols, :]
        state = st_ref[cols, :]
        carry_s = split(carry)
        wide = spread(weight, j, heads_in, size)
        gone = wide * dot3(b_rows, carry_s, NT)
        grad_in = gw_ref[:, cols] + gone
        gx_ref[:, cols] = ((skip_ref[:, cols] * grad_y + grad_in) * slope_ref[:, cols]).astype(BF16)
        onehot = head_of(j, heads_in, size)
        high, low = split(inputs * grad_in)
        sums = sums + (dot(high, onehot, NN) + dot(low, onehot, NN))
        folded = jnp.sum((inputs * gone).reshape(length // 8, 8, LANES), axis=0)
        high, low = split(folded)
        leaving = leaving + (dot(high, onehot, NN) + dot(low, onehot, NN))
        product = carry * state
        for k in range(heads_in):
            h = j * heads_in + k
            cs_ref[h : h + 1, :] = jnp.sum(product[k * size : (k + 1) * size], axis=0, keepdims=True)
        grad_b = grad_b + dot3(split(wide * inputs), carry_s)
        grad_c = grad_c + dot3(split(spread(grown, j, heads_in, size) * grad_y), split(state))
    gbc_ref[:, 0:LANES] = grad_b
    gbc_ref[:, LANES : 2 * LANES] = grad_c
    both = lax.dot_general(
        jnp.ones((8, LANES), F32), cs_ref[...], (NT, ((), ())), precision=HIGH, preferred_element_type=F32
    )
    constant = jnp.sum(leaving, axis=0, keepdims=True) + jnp.exp(last) * both[0:1]
    upper = jnp.where(row_ids(length) <= lane_ids(length), 1.0, 0.0)
    grad_rate = constant + lax.dot_general(
        upper, yg_ref[...] - sums, (NN, ((), ())), precision=HIGH, preferred_element_type=F32
    )
    grad_step = sums / step - jnp.exp(alog_ref[...]) * grad_rate
    gdt_ref[...] = grad_step * sigmoid(dt_ref[...] + dtb_ref[...])


def product_kernel(rows, held_ref, go_ref, out_ref, lhs_ref):
    size, share, length = held_ref.shape

    @pl.when(pl.program_id(0) == 0)
    def _():
        for s in range(size):
            lhs_ref[:, s * length : (s + 1) * length] = held_ref[s]

    result = dot(lhs_ref[...], go_ref[...], NN).T
    for d in range(out_ref.shape[0]):
        block = result[rows * d : rows * (d + 1)]
        top = jnp.max(jnp.max(jnp.abs(block), axis=0, keepdims=True), axis=1, keepdims=True)
        exponent = jnp.floor(jnp.log2(jnp.maximum(jnp.broadcast_to(top, (1, LANES)), 1e-30)))
        scale = jnp.exp2(13.0 - exponent)
        if share > LANES:
            rest = share - LANES
            across = LANES // rest
            out_ref[d, 0:rows, :] = block[:, 0:LANES] * scale
            extra = block[:, LANES:share] * scale[:, 0:rest]
            for k in range(0, rows // 16, across):
                pieces = [extra[16 * m : 16 * m + 16] for m in range(k, min(k + across, rows // 16))]
                at = rows + 16 * (k // across)
                filled = rest * len(pieces)
                if filled < LANES:
                    pieces.append(jnp.broadcast_to(exponent[:, filled:], (16, LANES - filled)))
                out_ref[d, at : at + 16, :] = jnp.concatenate(pieces, axis=1)
        else:
            out_ref[d, 0:rows, :] = block * scale[:, 0:share]
            out_ref[d, rows : rows + 4, :] = jnp.broadcast_to(exponent[:, 0:share], (4, share))


def assemble_kernel(rows, size, share, parts_ref, out_ref):
    count = parts_ref.shape[0]
    last = parts_ref.shape[2] - 1
    scales = [jnp.exp2(parts_ref[s, parts_ref.shape[1] - 1, last] - 13.0) for s in range(count)]
    if share > LANES:
        rest = share - LANES
        across = LANES // rest
        for c in range(size):
            total = parts_ref[c, 0:rows, :] * scales[c]
            for s in range(c + size, count, size):
                total = total + parts_ref[s, 0:rows, :] * scales[s]
            out_ref[:, c * LANES : (c + 1) * LANES] = total
        for q in range(size // across):
            for k in range(rows // 16):
                at = rows + 16 * (k // across)
                lanes = slice(rest * (k % across), rest * (k % across + 1))
                pieces = []
                for c in range(q * across, (q + 1) * across):
                    total = parts_ref[c, at : at + 16, lanes] * scales[c]
                    for s in range(c + size, count, size):
                        total = total + parts_ref[s, at : at + 16, lanes] * scales[s]
                    pieces.append(total)
                first = (size + q) * LANES
                out_ref[16 * k : 16 * k + 16, first : first + LANES] = jnp.concatenate(pieces, axis=1)
    else:
        for c in range(size):
            total = parts_ref[c, 0:rows, :] * scales[c]
            for s in range(c + size, count, size):
                total = total + parts_ref[s, 0:rows, :] * scales[s]
            out_ref[:, c * share : (c + 1) * share] = total


def exchange(message, groups=None):
    half = message.astype(jnp.float16)
    return lax.all_to_all(half, "ctx", 0, 0, axis_index_groups=groups, tiled=True).astype(F32)


def groups_of(count, size):
    return [list(range(at, at + size)) for at in range(0, count, size)]


def entering(held, rows, reverse):
    size = held.shape[0]
    count = lax.axis_size("ctx")
    (total,) = call(
        functools.partial(total_kernel, rows, reverse), [shape((1, *held.shape[1:]))], [held], 4 * held.size
    )
    total = total.astype(jnp.float16)
    others = []
    for hops in range(size, count, size):
        pairs = [(at, at + hops) for at in range(count - hops)]
        if reverse:
            pairs = [(b, a) for a, b in pairs]
        others.append(lax.ppermute(total, "ctx", pairs).astype(F32))
    (folded,) = call(
        functools.partial(fold_kernel, rows, reverse), [shape(held.shape)], [held, *others], 8 * held.size
    )
    return folded


def group_of(count):
    for size in (16, 8, 4, 2):
        if count % size == 0:
            return size
    return 1


def from_behind(value, axis):
    count = lax.axis_size(axis)
    return lax.ppermute(value, axis, [(source, source + 1) for source in range(count - 1)])


def per_device(
    x_raw,
    bc_raw,
    gate_branch,
    dt_raw,
    conv_x,
    conv_x_bias,
    conv_bc,
    conv_bc_bias,
    dt_bias,
    a_log,
    d_skip,
    out_weight,
    grad_out,
):
    length, head_count = dt_raw.shape
    channels = x_raw.shape[1]
    width = grad_out.shape[1]
    head_size = channels // head_count
    heads_in = LANES // head_size
    count = lax.axis_size("ctx")
    plane = min(8, group_of(count))
    planes = groups_of(count, plane)
    rows = channels // plane
    size = group_of(count)
    share = channels // size
    groups = groups_of(count, size)
    gathered = lax.all_gather(grad_out, "ctx", axis_index_groups=groups, tiled=True)

    rim = from_behind(jnp.concatenate([x_raw[length - 16 :], bc_raw[length - 16 :]], axis=1), "ctx")
    fill = ((0, 0), (0, LANES - head_count))
    dt_wide = jnp.pad(dt_raw, fill)
    dtb_wide = jnp.pad(dt_bias[None, :], fill)
    alog_wide = jnp.pad(a_log[None, :], fill)
    skip = jnp.repeat(d_skip, head_size)[None, :]
    whole = (length, channels)
    square = (length, LANES)
    packed = (plane, up8(rows) + 8, LANES)
    stored = pltpu.VMEM((channels, LANES), F32)
    unit = 2 * length * channels * LANES

    act_x, slope_x, act_bc, slope_bc, step, ld, step_t, ld_t, message = call(
        functools.partial(prepare_kernel, heads_in, head_size, rows),
        [shape(whole), shape(whole), shape(bc_raw.shape), shape(bc_raw.shape)]
        + [shape(square)] * 2
        + [shape((LANES, length))] * 2
        + [shape(packed)],
        [
            x_raw,
            rim[:, :channels],
            bc_raw,
            rim[:, channels:],
            conv_x,
            conv_x_bias[None, :],
            conv_bc,
            conv_bc_bias[None, :],
            dt_wide,
            dtb_wide,
            alog_wide,
        ],
        20 * unit,
        [pltpu.VMEM((length + 8, channels), F32), pltpu.VMEM((length + 8, bc_raw.shape[1]), F32), stored],
    )
    grad_gated = lax.dot_general(
        grad_out, out_weight, (((1,), (1,)), ((), ())), preferred_element_type=F32
    )
    held_state = exchange(message, planes)
    grad_y, message = call(
        functools.partial(grad_kernel, heads_in, head_size, rows),
        [shape(whole), shape(packed)],
        [grad_gated, gate_branch, act_bc, ld],
        20 * unit,
        [stored],
    )
    message, held_state = lax.optimization_barrier((message, held_state))
    held_carry = exchange(message, planes)
    state_message = exchange(entering(held_state, rows, False), planes)
    y_within, grad_within, grad_bc_within = call(
        functools.partial(local_kernel, heads_in, head_size),
        [shape(whole), shape(whole), shape(act_bc.shape)],
        [act_x, grad_y, act_bc, step, ld, step_t, ld_t],
        40 * unit,
        [pltpu.VMEM(square, F32)],
    )
    grad_z, gated, y_sums = call(
        functools.partial(forward_kernel, heads_in, head_size, rows),
        [shape(whole, BF16), shape((size, share, length), BF16), shape(square)],
        [state_message, act_x, grad_gated, grad_y, gate_branch, act_bc, ld, y_within, skip],
        20 * unit,
        [stored],
    )
    held = lax.all_to_all(gated, "ctx", 0, 0, axis_index_groups=groups, tiled=True)
    entered, held = lax.optimization_barrier((entering(held_carry, rows, True), held))
    carry_message = exchange(entered, planes)
    out_rows = width // count
    part = width
    for candidate in (640, 1280):
        if width % candidate == 0 and candidate % out_rows == 0:
            part = candidate
            break
    if share > LANES:
        across = LANES // (share - LANES)
        dims = (out_rows + 16 * (-(-(out_rows // 16) // across)), LANES)
    else:
        dims = (out_rows + 4, share)
    partial = pl.pallas_call(
        functools.partial(product_kernel, out_rows),
        grid=(width // part,),
        in_specs=[
            pl.BlockSpec((size, share, length), lambda i: (0, 0, 0)),
            pl.BlockSpec((size * length, part), lambda i: (0, i)),
        ],
        out_specs=pl.BlockSpec((part // out_rows, *dims), lambda i: (i, 0, 0)),
        out_shape=shape((count, *dims)),
        scratch_shapes=[pltpu.VMEM((share, size * length), BF16)],
        compiler_params=PARAMS,
        cost_estimate=pl.CostEstimate(
            flops=2 * size * length * share * width, bytes_accessed=2 * size * length * width, transcendentals=0
        ),
    )(held, gathered)
    parts = exchange(partial)
    (weight_grad,) = call(
        functools.partial(assemble_kernel, out_rows, size, share),
        [shape((out_rows, channels))],
        [parts],
        2 * parts.size,
    )
    grad_x_conv, grad_bc, grad_dt_raw = call(
        functools.partial(backward_kernel, heads_in, head_size, rows),
        [shape(whole, BF16), shape(act_bc.shape), shape(square)],
        [
            carry_message,
            state_message,
            act_x,
            slope_x,
            grad_y,
            act_bc,
            step,
            ld,
            grad_within,
            grad_bc_within,
            y_sums,
            skip,
            dt_wide,
            dtb_wide,
            alog_wide,
        ],
        40 * unit,
        [stored, stored, pltpu.VMEM((LANES, LANES), F32)],
    )
    grad_bc_conv = (lax.psum(grad_bc, "tp") * slope_bc).astype(BF16)
    return (grad_x_conv, grad_bc_conv, grad_z, grad_dt_raw[:, :head_count], weight_grad)


def solution(mesh):
    placed = (
        P("ctx", "tp"),
        P("ctx", None),
        P("ctx", "tp"),
        P("ctx", "tp"),
        P(None, "tp"),
        P("tp"),
        P(),
        P(),
        P("tp"),
        P("tp"),
        P("tp"),
        P("tp", None),
        P("ctx", None),
    )
    return jax.shard_map(
        per_device,
        mesh=mesh,
        in_specs=placed,
        out_specs=(P("ctx", "tp"), P("ctx", None), P("ctx", "tp"), P("ctx", "tp"), P("ctx", "tp")),
        check_vma=False,
    )
```

```python
import functools

import jax
import jax.numpy as jnp
from jax import lax
from jax.experimental import pallas as pl
from jax.experimental.pallas import tpu as pltpu
from jax.sharding import PartitionSpec as P

KERNEL = 4
LANES = 128
F32 = jnp.float32
BF16 = jnp.bfloat16
NN = ((1,), (0,))
NT = ((1,), (1,))
HIGH = lax.Precision.HIGHEST
SMEM = pl.BlockSpec(memory_space=pltpu.SMEM)
MIB = 1024 * 1024


def call(kernel, out_shapes, operands, flops, vmem, scratch=(), specs=None):
    extra = {} if specs is None else {"in_specs": specs}
    moved = sum(a.size * a.dtype.itemsize for a in (*operands, *out_shapes))
    return pl.pallas_call(
        kernel,
        out_shape=tuple(out_shapes),
        scratch_shapes=list(scratch),
        compiler_params=pltpu.CompilerParams(vmem_limit_bytes=vmem * MIB),
        cost_estimate=pl.CostEstimate(flops=flops, bytes_accessed=moved, transcendentals=0),
        **extra,
    )(*operands)


def shape(dims, dtype=F32):
    return jax.ShapeDtypeStruct(dims, dtype)


def split(value):
    high = value.astype(BF16)
    return high, (value - high.astype(F32)).astype(BF16)


def dot(a, b, dims):
    return lax.dot_general(a, b, (dims, ((), ())), preferred_element_type=F32)


def dot3(a, b, dims=NN):
    return dot(a[0], b[0], dims) + (dot(a[0], b[1], dims) + dot(a[1], b[0], dims))


def sigmoid(value):
    return 1.0 / (1.0 + jnp.exp(-value))


def lane_ids(rows, cols=LANES):
    return lax.broadcasted_iota(jnp.int32, (rows, cols), 1)


def row_ids(rows, cols=LANES):
    return lax.broadcasted_iota(jnp.int32, (rows, cols), 0)


def spread(columns, block, heads, size):
    first = block * heads
    lanes = lane_ids(columns.shape[0])
    wide = jnp.broadcast_to(columns[:, first : first + 1], (columns.shape[0], LANES))
    for k in range(1, heads):
        wide = jnp.where(lanes >= k * size, columns[:, first + k : first + k + 1], wide)
    return wide


def head_of(block, heads, size):
    inner = row_ids(LANES)
    target = lane_ids(LANES)
    result = jnp.zeros((LANES, LANES), F32)
    for k in range(heads):
        here = (inner >= k * size) & (inner < (k + 1) * size) & (target == block * heads + k)
        result = jnp.where(here, 1.0, result)
    return result.astype(BF16)


def stacked(value, heads, size):
    lanes = lane_ids(value.shape[0])
    return jnp.concatenate(
        [jnp.where((lanes >= k * size) & (lanes < (k + 1) * size), value, 0.0) for k in range(heads)],
        axis=0,
    )


def up8(value):
    return -(-value // 8) * 8


def notes_of(rows):
    return -(-rows // LANES)


def exponent_of(block):
    top = jnp.max(jnp.max(jnp.abs(block), axis=0, keepdims=True), axis=1, keepdims=True)
    return jnp.floor(jnp.log2(jnp.maximum(jnp.broadcast_to(top, (1, LANES)), 1e-30)))


def write_block(message, at, first, block, decays, exponent):
    rows = block.shape[0]
    padded = up8(rows)
    message[at, first : first + rows, :] = block * jnp.exp2(13.0 - exponent)
    if padded > rows:
        message[at, first + rows : first + padded, :] = jnp.zeros((padded - rows, LANES), F32)
    highs = [d.astype(BF16).astype(F32) for d in decays]
    lows = [d - h for d, h in zip(decays, highs)]
    place = row_ids(8)
    notes = jnp.broadcast_to(exponent, (8, LANES))
    for k, line in enumerate(highs + lows):
        notes = jnp.where(place == k, line, notes)
    message[at, first + padded : first + padded + 8, :] = notes


def decay_tables(last_exp, heads, size, rows, count):
    shift = size.bit_length() - 1
    tables = []
    for d in range(count):
        lines = []
        for k in range(notes_of(rows)):
            first = rows * d + LANES * k
            owner = lax.shift_right_logical(lane_ids(1) + first, shift)
            table = jnp.zeros((1, LANES), F32)
            for h in range(first // size, min(heads, (first + LANES - 1) // size + 1)):
                table = jnp.where(owner == h, last_exp[:, h : h + 1], table)
            lines.append(table)
        tables.append(lines)
    return tables


def decay_lines(message, at, rows):
    padded, lines = up8(rows), notes_of(rows)
    return [
        message[at, padded + k : padded + k + 1, :] + message[at, padded + lines + k : padded + lines + k + 1, :]
        for k in range(lines)
    ]


def decay_columns(message, rows):
    padded, lines = up8(rows), notes_of(rows)
    turned = [
        jnp.transpose(message[:, padded + k, :] + message[:, padded + lines + k, :]) for k in range(lines)
    ]
    return jnp.concatenate(turned, axis=0)[0:rows]


def read_block(message, at, rows):
    padded = up8(rows)
    return message[at, 0:rows, :] * jnp.exp2(message[at, padded + 7 : padded + 8, :] - 13.0)


def unpack_blocks(message, target, rows):
    for d in range(message.shape[0]):
        target[rows * d : rows * (d + 1), :] = read_block(message, d, rows)


def total_kernel(rows, ahead_ref, behind_ref, out_ref):
    count = ahead_ref.shape[0]
    columns = decay_columns(ahead_ref, rows)
    state, grad = read_block(ahead_ref, 0, rows), read_block(behind_ref, count - 1, rows)
    for s in range(1, count):
        state = columns[:, s : s + 1] * state + read_block(ahead_ref, s, rows)
        r = count - 1 - s
        grad = columns[:, r : r + 1] * grad + read_block(behind_ref, r, rows)
    decays = decay_lines(ahead_ref, 0, rows)
    for s in range(1, count):
        decays = [a * b for a, b in zip(decays, decay_lines(ahead_ref, s, rows))]
    write_block(out_ref, 0, 0, state, decays, exponent_of(state))
    write_block(out_ref, 1, 0, grad, decays, exponent_of(grad))


def fold_kernel(rows, me_ref, ahead_ref, behind_ref, totals_ref, out_ref):
    count, others = ahead_ref.shape[0], totals_ref.shape[0]
    me = me_ref[0]
    columns = decay_columns(ahead_ref, rows)
    passing = decay_columns(totals_ref, rows)
    state = jnp.zeros((rows, LANES), F32)
    grad = jnp.zeros((rows, LANES), F32)
    for g in range(others - 1):
        there = passing[:, g : g + 1] * state + read_block(totals_ref, g, rows)
        state = jnp.where(g < me, there, state)
        g = others - 1 - g
        there = passing[:, g : g + 1] * grad + read_block(totals_ref, g, rows)
        grad = jnp.where(g > me, there, grad)
    first = up8(rows) + 8
    for s in range(count):
        write_block(out_ref, s, 0, state, [], exponent_of(state))
        r = count - 1 - s
        write_block(out_ref, r, first, grad, [], exponent_of(grad))
        if s < count - 1:
            state = columns[:, s : s + 1] * state + read_block(ahead_ref, s, rows)
            grad = columns[:, r : r + 1] * grad + read_block(behind_ref, r, rows)


def prepare_kernel(
    heads_in, size, rows, x_ref, rim_ref, bc_ref, rim_bc_ref, wx_ref, bx_ref, wbc_ref, bbc_ref, dt_ref,
    dtb_ref, alog_ref, gy_ref, act_ref, slope_ref, abc_ref, sbc_ref, step_ref, ld_ref, stept_ref, ldt_ref, msg_ref,
    xs_ref, bs_ref, st_ref, gt_ref,
):
    length = x_ref.shape[0]
    blocks = x_ref.shape[1] // LANES

    def convolved(raw, rim, padded, weight, bias, cols):
        padded[0:8, cols] = rim[:, cols].astype(F32)[8:16]
        padded[8 : 8 + length, cols] = raw[:, cols].astype(F32)
        pre = bias[:, cols] + weight[0:1, cols] * padded[5 : 5 + length, cols]
        for k in range(1, KERNEL):
            pre = pre + weight[k : k + 1, cols] * padded[5 + k : 5 + k + length, cols]
        gate = sigmoid(pre)
        return pre * gate, gate * (1.0 + pre * (1.0 - gate))

    for j in range(bc_ref.shape[1] // LANES):
        cols = slice(j * LANES, (j + 1) * LANES)
        value, slope = convolved(bc_ref, rim_bc_ref, bs_ref, wbc_ref, bbc_ref, cols)
        abc_ref[:, cols] = value
        sbc_ref[:, cols] = slope
    b_rows = split(abc_ref[:, 0:LANES])
    c_rows = split(abc_ref[:, LANES : 2 * LANES])
    raised = dt_ref[...] + dtb_ref[...]
    step = jnp.maximum(raised, 0.0) + jnp.log1p(jnp.exp(-jnp.abs(raised)))
    lower = jnp.where(row_ids(length) >= lane_ids(length), 1.0, 0.0)
    ld = lax.dot_general(
        lower, step * -jnp.exp(alog_ref[...]), (NN, ((), ())), precision=HIGH, preferred_element_type=F32
    )
    step_ref[...] = step
    ld_ref[...] = ld
    stept_ref[...] = step.T
    ldt_ref[...] = ld.T
    last = ld[length - 1 : length]
    weight = jnp.exp(last - ld) * step
    grown = jnp.exp(ld)
    for j in range(blocks):
        cols = slice(j * LANES, (j + 1) * LANES)
        value, slope = convolved(x_ref, rim_ref, xs_ref, wx_ref, bx_ref, cols)
        act_ref[:, cols] = value
        slope_ref[:, cols] = slope
        scaled = value * spread(weight, j, heads_in, size)
        st_ref[cols, :] = dot3(split(scaled.T), b_rows)
        scaled = gy_ref[:, cols] * spread(grown, j, heads_in, size)
        gt_ref[cols, :] = dot3(split(scaled.T), c_rows)
    count = msg_ref.shape[0]
    tables = decay_tables(grown[length - 1 : length], blocks * heads_in, size, rows, count)
    for d in range(count):
        for source, first in ((st_ref, 0), (gt_ref, up8(rows) + 8)):
            block = source[rows * d : rows * (d + 1), :]
            write_block(msg_ref, d, first, block, tables[d], exponent_of(block))


def gate_kernel(go_ref, w_ref, gate_ref, gg_ref, gy_ref):
    grad = dot(w_ref[...], go_ref[...], NT).T
    gate = gate_ref[...].astype(F32)
    gg_ref[...] = grad
    gy_ref[...] = grad * (gate * sigmoid(gate))


def local_kernel(
    heads_in, size, act_ref, gy_ref, abc_ref, step_ref, ld_ref, stept_ref, ldt_ref, yw_ref, gw_ref, gbc_ref, sh_ref
):
    length = act_ref.shape[0]
    b_rows = split(abc_ref[:, 0:LANES])
    c_rows = split(abc_ref[:, LANES : 2 * LANES])
    scores = dot3(c_rows, b_rows, NT)
    turned = dot3(b_rows, c_rows, NT)
    causal = row_ids(length) >= lane_ids(length)
    causal_t = row_ids(length) <= lane_ids(length)
    sh_ref[...] = jnp.zeros_like(sh_ref)
    for j in range(act_ref.shape[1] // LANES):
        cols = slice(j * LANES, (j + 1) * LANES)
        mixes, mixes_t, steps = [], [], []
        for h in range(j * heads_in, (j + 1) * heads_in):
            column, row = ld_ref[:, h : h + 1], ldt_ref[h : h + 1, :]
            decays = jnp.exp(jnp.where(causal, column - row, -1e30))
            stepped = decays * stept_ref[h : h + 1, :]
            decays_t = jnp.exp(jnp.where(causal_t, row - column, -1e30))
            steps.append(stepped)
            mixes.append(stepped * scores)
            mixes_t.append(decays_t * turned * step_ref[:, h : h + 1])
        inputs = act_ref[:, cols]
        grad_y = gy_ref[:, cols]
        inputs_s = stacked(inputs, heads_in, size)
        grads_s = split(stacked(grad_y, heads_in, size))
        yw_ref[:, cols] = dot3(split(jnp.concatenate(mixes, axis=1)), split(inputs_s))
        gw_ref[:, cols] = dot3(split(jnp.concatenate(mixes_t, axis=1)), grads_s)
        products = dot3(grads_s, split(inputs), NT)
        total = sh_ref[...]
        for k in range(heads_in):
            total = total + steps[k] * products[k * length : (k + 1) * length]
        sh_ref[...] = total
    shared = sh_ref[...]
    gbc_ref[:, 0:LANES] = dot3(split(shared.T), c_rows)
    gbc_ref[:, LANES : 2 * LANES] = dot3(split(shared), b_rows)


def place_of(channel, share, size):
    if share > LANES:
        if channel < LANES * size:
            return channel // LANES, channel % LANES
        rest = share - LANES
        return (channel - LANES * size) // rest, LANES + (channel - LANES * size) % rest
    return channel // share, channel % share


def forward_kernel(
    heads_in, size, rows, msg_ref, act_ref, gate_ref, abc_ref, ld_ref, yw_ref, skip_ref, gt_ref, ys_ref, st_ref
):
    share = gt_ref.shape[1]
    unpack_blocks(msg_ref, st_ref, rows)
    c_rows = split(abc_ref[:, LANES : 2 * LANES])
    grown = jnp.exp(ld_ref[...])
    for j in range(act_ref.shape[1] // LANES):
        cols = slice(j * LANES, (j + 1) * LANES)
        carried = dot3(c_rows, split(st_ref[cols, :]), NT)
        within = yw_ref[:, cols] + spread(grown, j, heads_in, size) * carried
        ys_ref[:, cols] = within
        output = within + skip_ref[:, cols] * act_ref[:, cols]
        gate = gate_ref[:, cols].astype(F32)
        turned = (output * (gate * sigmoid(gate))).T.astype(BF16)
        for k in range(0, LANES, 16):
            to, at = place_of(j * LANES + k, share, gt_ref.shape[0])
            gt_ref[to, at : at + 16, :] = turned[k : k + 16]


def backward_kernel(
    heads_in, size, rows, msg_ref, msgf_ref, act_ref, slope_ref, gy_ref, abc_ref, step_ref, ld_ref, gw_ref,
    gbcl_ref, ys_ref, gg_ref, gate_ref, skip_ref, dt_ref, dtb_ref, alog_ref, gx_ref, gbc_ref, gdt_ref, gz_ref,
    ca_ref, st_ref, cs_ref,
):
    length = act_ref.shape[0]
    unpack_blocks(msg_ref, ca_ref, rows)
    unpack_blocks(msgf_ref, st_ref, rows)
    b_rows = split(abc_ref[:, 0:LANES])
    ld = ld_ref[...]
    step = step_ref[...]
    last = ld[length - 1 : length]
    grown = jnp.exp(ld)
    weight = jnp.exp(last - ld) * step
    sums = jnp.zeros((length, LANES), F32)
    sums_y = jnp.zeros((length, LANES), F32)
    leaving = jnp.zeros((8, LANES), F32)
    grad_b = gbcl_ref[:, 0:LANES]
    grad_c = gbcl_ref[:, LANES : 2 * LANES]
    cs_ref[...] = jnp.zeros_like(cs_ref)
    for j in range(act_ref.shape[1] // LANES):
        cols = slice(j * LANES, (j + 1) * LANES)
        inputs = act_ref[:, cols]
        grad_y = gy_ref[:, cols]
        carry = ca_ref[cols, :]
        state = st_ref[cols, :]
        carry_s = split(carry)
        wide = spread(weight, j, heads_in, size)
        gone = wide * dot3(b_rows, carry_s, NT)
        grad_in = gw_ref[:, cols] + gone
        gx_ref[:, cols] = ((skip_ref[:, cols] * grad_y + grad_in) * slope_ref[:, cols]).astype(BF16)
        onehot = head_of(j, heads_in, size)
        within = ys_ref[:, cols]
        gate = gate_ref[:, cols].astype(F32)
        opened = sigmoid(gate)
        output = within + skip_ref[:, cols] * inputs
        gz_ref[:, cols] = (gg_ref[:, cols] * output * (opened * (1.0 + gate * (1.0 - opened)))).astype(BF16)
        high, low = split(grad_y * within)
        sums_y = sums_y + (dot(high, onehot, NN) + dot(low, onehot, NN))
        high, low = split(inputs * grad_in)
        sums = sums + (dot(high, onehot, NN) + dot(low, onehot, NN))
        folded = jnp.sum((inputs * gone).reshape(length // 8, 8, LANES), axis=0)
        high, low = split(folded)
        leaving = leaving + (dot(high, onehot, NN) + dot(low, onehot, NN))
        product = carry * state
        for k in range(heads_in):
            h = j * heads_in + k
            cs_ref[h : h + 1, :] = jnp.sum(product[k * size : (k + 1) * size], axis=0, keepdims=True)
        grad_b = grad_b + dot3(split(wide * inputs), carry_s)
        grad_c = grad_c + dot3(split(spread(grown, j, heads_in, size) * grad_y), split(state))
    gbc_ref[:, 0:LANES] = grad_b
    gbc_ref[:, LANES : 2 * LANES] = grad_c
    both = lax.dot_general(
        jnp.ones((8, LANES), F32), cs_ref[...], (NT, ((), ())), precision=HIGH, preferred_element_type=F32
    )
    constant = jnp.sum(leaving, axis=0, keepdims=True) + jnp.exp(last) * both[0:1]
    upper = jnp.where(row_ids(length) <= lane_ids(length), 1.0, 0.0)
    grad_rate = constant + lax.dot_general(
        upper, sums_y - sums, (NN, ((), ())), precision=HIGH, preferred_element_type=F32
    )
    grad_step = sums / step - jnp.exp(alog_ref[...]) * grad_rate
    gdt_ref[...] = grad_step * sigmoid(dt_ref[...] + dtb_ref[...])


def product_kernel(rows, held_ref, go_ref, out_ref):
    size, share, length = held_ref.shape
    result = dot(go_ref[0], held_ref[0], NT)
    for s in range(1, size):
        result = result + dot(go_ref[s], held_ref[s], NT)
    for d in range(out_ref.shape[0]):
        block = result[rows * d : rows * (d + 1)]
        exponent = exponent_of(block)
        scale = jnp.exp2(13.0 - exponent)
        if share > LANES:
            rest = share - LANES
            across = LANES // rest
            tall = rows // across
            out_ref[d, 0:rows, :] = block[:, 0:LANES] * scale
            extra = block[:, LANES:share] * scale[:, 0:rest]
            pieces = [extra[tall * m : tall * (m + 1)] for m in range(across)]
            out_ref[d, rows : rows + tall, :] = jnp.concatenate(pieces, axis=1)
            out_ref[d, rows + tall : rows + tall + 4, :] = jnp.broadcast_to(exponent, (4, LANES))
        else:
            out_ref[d, 0:rows, :] = block * scale[:, 0:share]
            out_ref[d, rows : rows + 4, :] = jnp.broadcast_to(exponent[:, 0:share], (4, share))


def assemble_kernel(rows, size, share, parts_ref, out_ref):
    count = parts_ref.shape[0]
    last = parts_ref.shape[2] - 1
    scales = [jnp.exp2(parts_ref[s, parts_ref.shape[1] - 1, last] - 13.0) for s in range(count)]
    if share > LANES:
        rest = share - LANES
        across = LANES // rest
        for c in range(size):
            total = parts_ref[c, 0:rows, :] * scales[c]
            for s in range(c + size, count, size):
                total = total + parts_ref[s, 0:rows, :] * scales[s]
            out_ref[:, c * LANES : (c + 1) * LANES] = total
        tall = rows // across
        for c in range(size):
            total = parts_ref[c, rows : rows + tall, :] * scales[c]
            for s in range(c + size, count, size):
                total = total + parts_ref[s, rows : rows + tall, :] * scales[s]
            for m in range(across):
                first = size * LANES + rest * c
                out_ref[tall * m : tall * (m + 1), first : first + rest] = total[:, rest * m : rest * (m + 1)]
    else:
        for c in range(size):
            total = parts_ref[c, 0:rows, :] * scales[c]
            for s in range(c + size, count, size):
                total = total + parts_ref[s, 0:rows, :] * scales[s]
            out_ref[:, c * share : (c + 1) * share] = total


def exchange(message, groups=None):
    half = message.astype(jnp.float16)
    return lax.all_to_all(half, "ctx", 0, 0, axis_index_groups=groups, tiled=True)


def groups_of(count, size):
    return [list(range(at, at + size)) for at in range(0, count, size)]


def group_of(count):
    for size in (16, 8, 4, 2):
        if count % size == 0:
            return size
    return 1


def from_behind(value, axis):
    count = lax.axis_size(axis)
    return lax.ppermute(value, axis, [(source, source + 1) for source in range(count - 1)])


def per_device(
    x_raw,
    bc_raw,
    gate_branch,
    dt_raw,
    conv_x,
    conv_x_bias,
    conv_bc,
    conv_bc_bias,
    dt_bias,
    a_log,
    d_skip,
    out_weight,
    grad_out,
):
    length, head_count = dt_raw.shape
    channels = x_raw.shape[1]
    width = grad_out.shape[1]
    head_size = channels // head_count
    heads_in = LANES // head_size
    count = lax.axis_size("ctx")
    plane = min(8, group_of(count))
    planes = groups_of(count, plane)
    rows = channels // plane
    size = group_of(count)
    share = channels // size
    groups = groups_of(count, size)
    gathered = lax.all_gather(grad_out.T, "ctx", axis_index_groups=groups)

    rim = from_behind(jnp.concatenate([x_raw[length - 16 :], bc_raw[length - 16 :]], axis=1), "ctx")
    fill = ((0, 0), (0, LANES - head_count))
    dt_wide = jnp.pad(dt_raw, fill)
    dtb_wide = jnp.pad(dt_bias[None, :], fill)
    alog_wide = jnp.pad(a_log[None, :], fill)
    skip = jnp.repeat(d_skip, head_size)[None, :]
    whole = (length, channels)
    square = (length, LANES)
    block = up8(rows) + 8
    stored = pltpu.VMEM((channels, LANES), F32)
    unit = 2 * length * channels * LANES

    part = 640 if channels % 640 == 0 else channels
    grad_gated, grad_y = pl.pallas_call(
        gate_kernel,
        grid=(channels // part,),
        in_specs=[
            pl.BlockSpec((length, width), lambda i: (0, 0)),
            pl.BlockSpec((part, width), lambda i: (i, 0)),
            pl.BlockSpec((length, part), lambda i: (0, i)),
        ],
        out_specs=(pl.BlockSpec((length, part), lambda i: (0, i)), pl.BlockSpec((length, part), lambda i: (0, i))),
        out_shape=(shape(whole), shape(whole)),
        compiler_params=pltpu.CompilerParams(vmem_limit_bytes=24 * MIB),
        cost_estimate=pl.CostEstimate(
            flops=2 * length * channels * width, bytes_accessed=2 * channels * width, transcendentals=0
        ),
    )(grad_out, out_weight, gate_branch)
    act_x, slope_x, act_bc, slope_bc, step, ld, step_t, ld_t, message = call(
        functools.partial(prepare_kernel, heads_in, head_size, rows),
        [shape(whole), shape(whole), shape(bc_raw.shape), shape(bc_raw.shape)]
        + [shape(square)] * 2
        + [shape((LANES, length))] * 2
        + [shape((plane, 2 * block, LANES))],
        [
            x_raw,
            rim[:, :channels],
            bc_raw,
            rim[:, channels:],
            conv_x,
            conv_x_bias[None, :],
            conv_bc,
            conv_bc_bias[None, :],
            dt_wide,
            dtb_wide,
            alog_wide,
            grad_y,
        ],
        20 * unit,
        20,
        [
            pltpu.VMEM((length + 8, channels), F32),
            pltpu.VMEM((length + 8, bc_raw.shape[1]), F32),
            stored,
            stored,
        ],
    )
    arrived = exchange(message, planes)
    ahead, behind = arrived[:, :block].astype(F32), arrived[:, block:].astype(F32)
    y_within, grad_within, grad_bc_within = call(
        functools.partial(local_kernel, heads_in, head_size),
        [shape(whole), shape(whole), shape(act_bc.shape)],
        [act_x, grad_y, act_bc, step, ld, step_t, ld_t],
        40 * unit,
        16,
        [pltpu.VMEM(square, F32)],
    )
    (total,) = call(
        functools.partial(total_kernel, rows), [shape((2, block, LANES))], [ahead, behind], 4 * ahead.size, 12
    )
    level = lax.axis_index("ctx") // plane
    later = (jnp.arange(count // plane) > level)[:, None, None]
    columns = [list(range(at, count, plane)) for at in range(plane)]
    totals = exchange(jnp.where(later, total[0][None], total[1][None]), columns).astype(F32)
    (folded,) = call(
        functools.partial(fold_kernel, rows),
        [shape(message.shape)],
        [level.astype(jnp.int32).reshape(1), ahead, behind, totals],
        8 * message.size,
        16,
        specs=[SMEM] + [pl.BlockSpec(memory_space=pltpu.VMEM)] * 3,
    )
    entered = exchange(folded, planes)
    state_message = entered[:, :block].astype(F32)
    gated, y_ahead = call(
        functools.partial(forward_kernel, heads_in, head_size, rows),
        [shape((size, share, length), BF16), shape(whole)],
        [state_message, act_x, gate_branch, act_bc, ld, y_within, skip],
        20 * unit,
        16,
        [stored],
    )
    held = lax.all_to_all(gated, "ctx", 0, 0, axis_index_groups=groups, tiled=True)
    out_rows = width // count
    part = width
    for candidate in (320, 640, 1280):
        if width % candidate == 0 and candidate % out_rows == 0:
            part = candidate
            break
    dims = (out_rows + 4, share)
    if share > LANES:
        dims = (out_rows + out_rows // (LANES // (share - LANES)) + 4, LANES)
    partial = pl.pallas_call(
        functools.partial(product_kernel, out_rows),
        grid=(width // part,),
        in_specs=[
            pl.BlockSpec((size, share, length), lambda i: (0, 0, 0)),
            pl.BlockSpec((size, part, length), lambda i: (0, i, 0)),
        ],
        out_specs=pl.BlockSpec((part // out_rows, *dims), lambda i: (i, 0, 0)),
        out_shape=shape((count, *dims)),
        compiler_params=pltpu.CompilerParams(vmem_limit_bytes=24 * MIB),
        cost_estimate=pl.CostEstimate(
            flops=2 * size * length * share * width, bytes_accessed=2 * size * length * width, transcendentals=0
        ),
    )(held, gathered)
    parts = exchange(partial).astype(F32)
    (weight_grad,) = call(
        functools.partial(assemble_kernel, out_rows, size, share),
        [shape((out_rows, channels))],
        [parts],
        2 * parts.size,
        12,
    )
    carry_message = entered[:, block:].astype(F32)
    grad_x_conv, grad_bc, grad_dt_raw, grad_z = call(
        functools.partial(backward_kernel, heads_in, head_size, rows),
        [shape(whole, BF16), shape(act_bc.shape), shape(square), shape(whole, BF16)],
        [
            carry_message,
            state_message,
            act_x,
            slope_x,
            grad_y,
            act_bc,
            step,
            ld,
            grad_within,
            grad_bc_within,
            y_ahead,
            grad_gated,
            gate_branch,
            skip,
            dt_wide,
            dtb_wide,
            alog_wide,
        ],
        40 * unit,
        28,
        [stored, stored, pltpu.VMEM((LANES, LANES), F32)],
    )
    grad_bc_conv = (lax.psum(grad_bc, "tp") * slope_bc).astype(BF16)
    return (grad_x_conv, grad_bc_conv, grad_z, grad_dt_raw[:, :head_count], weight_grad)


def solution(mesh):
    placed = (
        P("ctx", "tp"),
        P("ctx", None),
        P("ctx", "tp"),
        P("ctx", "tp"),
        P(None, "tp"),
        P("tp"),
        P(),
        P(),
        P("tp"),
        P("tp"),
        P("tp"),
        P("tp", None),
        P("ctx", None),
    )
    return jax.shard_map(
        per_device,
        mesh=mesh,
        in_specs=placed,
        out_specs=(P("ctx", "tp"), P("ctx", None), P("ctx", "tp"), P("ctx", "tp"), P("ctx", "tp")),
        check_vma=False,
    )
```

```python
import functools

import jax
import jax.numpy as jnp
from jax import lax
from jax.experimental import pallas as pl
from jax.experimental.pallas import tpu as pltpu
from jax.sharding import PartitionSpec as P

KERNEL = 4
LANES = 128
F32 = jnp.float32
BF16 = jnp.bfloat16
NN = ((1,), (0,))
NT = ((1,), (1,))
HIGH = lax.Precision.HIGHEST
SMEM = pl.BlockSpec(memory_space=pltpu.SMEM)
MIB = 1024 * 1024


def call(kernel, out_shapes, operands, flops, vmem, scratch=(), specs=None):
    extra = {} if specs is None else {"in_specs": specs}
    moved = sum(a.size * a.dtype.itemsize for a in (*operands, *out_shapes))
    return pl.pallas_call(
        kernel,
        out_shape=tuple(out_shapes),
        scratch_shapes=list(scratch),
        compiler_params=pltpu.CompilerParams(vmem_limit_bytes=vmem * MIB),
        cost_estimate=pl.CostEstimate(flops=flops, bytes_accessed=moved, transcendentals=0),
        **extra,
    )(*operands)


def shape(dims, dtype=F32):
    return jax.ShapeDtypeStruct(dims, dtype)


def split(value):
    high = value.astype(BF16)
    return high, (value - high.astype(F32)).astype(BF16)


def dot(a, b, dims):
    return lax.dot_general(a, b, (dims, ((), ())), preferred_element_type=F32)


def dot3(a, b, dims=NN):
    return dot(a[0], b[0], dims) + (dot(a[0], b[1], dims) + dot(a[1], b[0], dims))


def sigmoid(value):
    return 1.0 / (1.0 + jnp.exp(-value))


def lane_ids(rows, cols=LANES):
    return lax.broadcasted_iota(jnp.int32, (rows, cols), 1)


def row_ids(rows, cols=LANES):
    return lax.broadcasted_iota(jnp.int32, (rows, cols), 0)


def spread(columns, block, heads, size):
    first = block * heads
    lanes = lane_ids(columns.shape[0])
    wide = jnp.broadcast_to(columns[:, first : first + 1], (columns.shape[0], LANES))
    for k in range(1, heads):
        wide = jnp.where(lanes >= k * size, columns[:, first + k : first + k + 1], wide)
    return wide


def head_of(block, heads, size):
    inner = row_ids(LANES)
    target = lane_ids(LANES)
    result = jnp.zeros((LANES, LANES), F32)
    for k in range(heads):
        here = (inner >= k * size) & (inner < (k + 1) * size) & (target == block * heads + k)
        result = jnp.where(here, 1.0, result)
    return result.astype(BF16)


def stacked(value, heads, size):
    lanes = lane_ids(value.shape[0])
    return jnp.concatenate(
        [jnp.where((lanes >= k * size) & (lanes < (k + 1) * size), value, 0.0) for k in range(heads)],
        axis=0,
    )


def up8(value):
    return -(-value // 8) * 8


def notes_of(rows):
    return -(-rows // LANES)


def exponent_of(block):
    top = jnp.max(jnp.max(jnp.abs(block), axis=0, keepdims=True), axis=1, keepdims=True)
    return jnp.floor(jnp.log2(jnp.maximum(jnp.broadcast_to(top, (1, LANES)), 1e-30)))


def write_block(message, at, first, block, decays, exponent):
    rows = block.shape[0]
    padded = up8(rows)
    message[at, first : first + rows, :] = block * jnp.exp2(13.0 - exponent)
    if padded > rows:
        message[at, first + rows : first + padded, :] = jnp.zeros((padded - rows, LANES), F32)
    highs = [d.astype(BF16).astype(F32) for d in decays]
    lows = [d - h for d, h in zip(decays, highs)]
    place = row_ids(8)
    notes = jnp.broadcast_to(exponent, (8, LANES))
    for k, line in enumerate(highs + lows):
        notes = jnp.where(place == k, line, notes)
    message[at, first + padded : first + padded + 8, :] = notes


def decay_tables(last_exp, heads, size, rows, count):
    shift = size.bit_length() - 1
    tables = []
    for d in range(count):
        lines = []
        for k in range(notes_of(rows)):
            first = rows * d + LANES * k
            owner = lax.shift_right_logical(lane_ids(1) + first, shift)
            table = jnp.zeros((1, LANES), F32)
            for h in range(first // size, min(heads, (first + LANES - 1) // size + 1)):
                table = jnp.where(owner == h, last_exp[:, h : h + 1], table)
            lines.append(table)
        tables.append(lines)
    return tables


def decay_lines(message, at, rows):
    padded, lines = up8(rows), notes_of(rows)
    return [
        message[at, padded + k : padded + k + 1, :] + message[at, padded + lines + k : padded + lines + k + 1, :]
        for k in range(lines)
    ]


def decay_columns(message, rows):
    padded, lines = up8(rows), notes_of(rows)
    turned = [
        jnp.transpose(message[:, padded + k, :] + message[:, padded + lines + k, :]) for k in range(lines)
    ]
    return jnp.concatenate(turned, axis=0)[0:rows]


def read_block(message, at, rows):
    padded = up8(rows)
    return message[at, 0:rows, :] * jnp.exp2(message[at, padded + 7 : padded + 8, :] - 13.0)


def unpack_blocks(message, target, rows):
    for d in range(message.shape[0]):
        target[rows * d : rows * (d + 1), :] = read_block(message, d, rows)


def total_kernel(rows, ahead_ref, behind_ref, out_ref):
    count = ahead_ref.shape[0]
    columns = decay_columns(ahead_ref, rows)
    state, grad = read_block(ahead_ref, 0, rows), read_block(behind_ref, count - 1, rows)
    for s in range(1, count):
        state = columns[:, s : s + 1] * state + read_block(ahead_ref, s, rows)
        r = count - 1 - s
        grad = columns[:, r : r + 1] * grad + read_block(behind_ref, r, rows)
    decays = decay_lines(ahead_ref, 0, rows)
    for s in range(1, count):
        decays = [a * b for a, b in zip(decays, decay_lines(ahead_ref, s, rows))]
    write_block(out_ref, 0, 0, state, decays, exponent_of(state))
    write_block(out_ref, 1, 0, grad, decays, exponent_of(grad))


def fold_kernel(rows, me_ref, ahead_ref, behind_ref, totals_ref, out_ref):
    count, others = ahead_ref.shape[0], totals_ref.shape[0]
    me = me_ref[0]
    columns = decay_columns(ahead_ref, rows)
    passing = decay_columns(totals_ref, rows)
    state = jnp.zeros((rows, LANES), F32)
    grad = jnp.zeros((rows, LANES), F32)
    for g in range(others - 1):
        there = passing[:, g : g + 1] * state + read_block(totals_ref, g, rows)
        state = jnp.where(g < me, there, state)
        g = others - 1 - g
        there = passing[:, g : g + 1] * grad + read_block(totals_ref, g, rows)
        grad = jnp.where(g > me, there, grad)
    first = up8(rows) + 8
    for s in range(count):
        write_block(out_ref, s, 0, state, [], exponent_of(state))
        r = count - 1 - s
        write_block(out_ref, r, first, grad, [], exponent_of(grad))
        if s < count - 1:
            state = columns[:, s : s + 1] * state + read_block(ahead_ref, s, rows)
            grad = columns[:, r : r + 1] * grad + read_block(behind_ref, r, rows)


def prepare_kernel(
    heads_in, size, rows, x_ref, rim_ref, bc_ref, rim_bc_ref, wx_ref, bx_ref, wbc_ref, bbc_ref, dt_ref,
    per_ref, gy_ref, act_ref, slope_ref, abc_ref, sbc_ref, step_ref, ld_ref, stept_ref, ldt_ref, dtw_ref, perw_ref, msg_ref,
    xs_ref, bs_ref, st_ref, gt_ref,
):
    length = x_ref.shape[0]
    blocks = x_ref.shape[1] // LANES

    def convolved(raw, rim, padded, weight, bias, cols):
        padded[0:8, cols] = rim[:, cols].astype(F32)[8:16]
        padded[8 : 8 + length, cols] = raw[:, cols].astype(F32)
        pre = bias[:, cols] + weight[0:1, cols] * padded[5 : 5 + length, cols]
        for k in range(1, KERNEL):
            pre = pre + weight[k : k + 1, cols] * padded[5 + k : 5 + k + length, cols]
        gate = sigmoid(pre)
        return pre * gate, gate * (1.0 + pre * (1.0 - gate))

    for j in range(bc_ref.shape[1] // LANES):
        cols = slice(j * LANES, (j + 1) * LANES)
        value, slope = convolved(bc_ref, rim_bc_ref, bs_ref, wbc_ref, bbc_ref, cols)
        abc_ref[:, cols] = value
        sbc_ref[:, cols] = slope
    b_rows = split(abc_ref[:, 0:LANES])
    c_rows = split(abc_ref[:, LANES : 2 * LANES])
    heads = dt_ref.shape[1]
    dtw_ref[...] = jnp.zeros_like(dtw_ref)
    dtw_ref[:, 0:heads] = dt_ref[...]
    perw_ref[...] = jnp.zeros_like(perw_ref)
    perw_ref[0:2, 0:heads] = per_ref[...]
    raised = dtw_ref[...] + perw_ref[0:1, :]
    dtw_ref[...] = raised
    step = jnp.maximum(raised, 0.0) + jnp.log1p(jnp.exp(-jnp.abs(raised)))
    lower = jnp.where(row_ids(length) >= lane_ids(length), 1.0, 0.0)
    ld = lax.dot_general(
        lower, step * -jnp.exp(perw_ref[1:2, :]), (NN, ((), ())), precision=HIGH, preferred_element_type=F32
    )
    step_ref[...] = step
    ld_ref[...] = ld
    stept_ref[...] = step.T
    ldt_ref[...] = ld.T
    last = ld[length - 1 : length]
    weight = jnp.exp(last - ld) * step
    grown = jnp.exp(ld)
    for j in range(blocks):
        cols = slice(j * LANES, (j + 1) * LANES)
        value, slope = convolved(x_ref, rim_ref, xs_ref, wx_ref, bx_ref, cols)
        act_ref[:, cols] = value
        slope_ref[:, cols] = slope
        scaled = value * spread(weight, j, heads_in, size)
        st_ref[cols, :] = dot3(split(scaled.T), b_rows)
        scaled = gy_ref[:, cols] * spread(grown, j, heads_in, size)
        gt_ref[cols, :] = dot3(split(scaled.T), c_rows)
    count = msg_ref.shape[0]
    tables = decay_tables(grown[length - 1 : length], blocks * heads_in, size, rows, count)
    for d in range(count):
        for source, first in ((st_ref, 0), (gt_ref, up8(rows) + 8)):
            block = source[rows * d : rows * (d + 1), :]
            write_block(msg_ref, d, first, block, tables[d], exponent_of(block))


def turn_kernel(go_ref, *out_refs):
    first = 0
    for out_ref in out_refs:
        for at in range(0, out_ref.shape[0], LANES):
            block = go_ref[:, first + at : first + at + LANES].astype(F32)
            out_ref[at : at + LANES, :] = block.T.astype(BF16)
        first += out_ref.shape[0]


def gate_kernel(go_ref, w_ref, gate_ref, gg_ref, gy_ref):
    grad = dot(w_ref[...], go_ref[...], NT).T
    gate = gate_ref[...].astype(F32)
    gg_ref[...] = grad
    gy_ref[...] = grad * (gate * sigmoid(gate))


def local_kernel(
    heads_in, size, act_ref, gy_ref, abc_ref, step_ref, ld_ref, stept_ref, ldt_ref, yw_ref, gw_ref, gbc_ref, sh_ref
):
    length = act_ref.shape[0]
    b_rows = split(abc_ref[:, 0:LANES])
    c_rows = split(abc_ref[:, LANES : 2 * LANES])
    scores = dot3(c_rows, b_rows, NT)
    turned = dot3(b_rows, c_rows, NT)
    causal = row_ids(length) >= lane_ids(length)
    causal_t = row_ids(length) <= lane_ids(length)
    sh_ref[...] = jnp.zeros_like(sh_ref)
    for j in range(act_ref.shape[1] // LANES):
        cols = slice(j * LANES, (j + 1) * LANES)
        mixes, mixes_t, steps = [], [], []
        for h in range(j * heads_in, (j + 1) * heads_in):
            column, row = ld_ref[:, h : h + 1], ldt_ref[h : h + 1, :]
            decays = jnp.exp(jnp.where(causal, column - row, -1e30))
            stepped = decays * stept_ref[h : h + 1, :]
            decays_t = jnp.exp(jnp.where(causal_t, row - column, -1e30))
            steps.append(stepped)
            mixes.append(stepped * scores)
            mixes_t.append(decays_t * turned * step_ref[:, h : h + 1])
        inputs = act_ref[:, cols]
        grad_y = gy_ref[:, cols]
        inputs_s = stacked(inputs, heads_in, size)
        grads_s = split(stacked(grad_y, heads_in, size))
        yw_ref[:, cols] = dot3(split(jnp.concatenate(mixes, axis=1)), split(inputs_s))
        gw_ref[:, cols] = dot3(split(jnp.concatenate(mixes_t, axis=1)), grads_s)
        products = dot3(grads_s, split(inputs), NT)
        total = sh_ref[...]
        for k in range(heads_in):
            total = total + steps[k] * products[k * length : (k + 1) * length]
        sh_ref[...] = total
    shared = sh_ref[...]
    gbc_ref[:, 0:LANES] = dot3(split(shared.T), c_rows)
    gbc_ref[:, LANES : 2 * LANES] = dot3(split(shared), b_rows)


def place_of(channel, share, size):
    if share > LANES:
        if channel < LANES * size:
            return channel // LANES, channel % LANES
        rest = share - LANES
        return (channel - LANES * size) // rest, LANES + (channel - LANES * size) % rest
    return channel // share, channel % share


def forward_kernel(
    heads_in, size, rows, msg_ref, act_ref, gate_ref, abc_ref, ld_ref, yw_ref, skip_ref, gt_ref, ys_ref, st_ref
):
    share = gt_ref.shape[1]
    unpack_blocks(msg_ref, st_ref, rows)
    c_rows = split(abc_ref[:, LANES : 2 * LANES])
    grown = jnp.exp(ld_ref[...])
    for j in range(act_ref.shape[1] // LANES):
        cols = slice(j * LANES, (j + 1) * LANES)
        carried = dot3(c_rows, split(st_ref[cols, :]), NT)
        within = yw_ref[:, cols] + spread(grown, j, heads_in, size) * carried
        ys_ref[:, cols] = within
        output = within + skip_ref[:, cols] * act_ref[:, cols]
        gate = gate_ref[:, cols].astype(F32)
        turned = (output * (gate * sigmoid(gate))).T.astype(BF16)
        for k in range(0, LANES, 16):
            to, at = place_of(j * LANES + k, share, gt_ref.shape[0])
            gt_ref[to, at : at + 16, :] = turned[k : k + 16]


def backward_kernel(
    heads_in, size, rows, msg_ref, msgf_ref, act_ref, slope_ref, gy_ref, abc_ref, step_ref, ld_ref, gw_ref,
    gbcl_ref, ys_ref, gg_ref, gate_ref, skip_ref, dtw_ref, perw_ref, gx_ref, gbc_ref, gdt_ref, gz_ref,
    ca_ref, st_ref, cs_ref,
):
    length = act_ref.shape[0]
    unpack_blocks(msg_ref, ca_ref, rows)
    unpack_blocks(msgf_ref, st_ref, rows)
    b_rows = split(abc_ref[:, 0:LANES])
    ld = ld_ref[...]
    step = step_ref[...]
    last = ld[length - 1 : length]
    grown = jnp.exp(ld)
    weight = jnp.exp(last - ld) * step
    sums = jnp.zeros((length, LANES), F32)
    sums_y = jnp.zeros((length, LANES), F32)
    leaving = jnp.zeros((8, LANES), F32)
    grad_b = gbcl_ref[:, 0:LANES]
    grad_c = gbcl_ref[:, LANES : 2 * LANES]
    cs_ref[...] = jnp.zeros_like(cs_ref)
    for j in range(act_ref.shape[1] // LANES):
        cols = slice(j * LANES, (j + 1) * LANES)
        inputs = act_ref[:, cols]
        grad_y = gy_ref[:, cols]
        carry = ca_ref[cols, :]
        state = st_ref[cols, :]
        carry_s = split(carry)
        wide = spread(weight, j, heads_in, size)
        gone = wide * dot3(b_rows, carry_s, NT)
        grad_in = gw_ref[:, cols] + gone
        gx_ref[:, cols] = ((skip_ref[:, cols] * grad_y + grad_in) * slope_ref[:, cols]).astype(BF16)
        onehot = head_of(j, heads_in, size)
        within = ys_ref[:, cols]
        gate = gate_ref[:, cols].astype(F32)
        opened = sigmoid(gate)
        output = within + skip_ref[:, cols] * inputs
        gz_ref[:, cols] = (gg_ref[:, cols] * output * (opened * (1.0 + gate * (1.0 - opened)))).astype(BF16)
        high, low = split(grad_y * within)
        sums_y = sums_y + (dot(high, onehot, NN) + dot(low, onehot, NN))
        high, low = split(inputs * grad_in)
        sums = sums + (dot(high, onehot, NN) + dot(low, onehot, NN))
        folded = jnp.sum((inputs * gone).reshape(length // 8, 8, LANES), axis=0)
        high, low = split(folded)
        leaving = leaving + (dot(high, onehot, NN) + dot(low, onehot, NN))
        product = carry * state
        for k in range(heads_in):
            h = j * heads_in + k
            cs_ref[h : h + 1, :] = jnp.sum(product[k * size : (k + 1) * size], axis=0, keepdims=True)
        grad_b = grad_b + dot3(split(wide * inputs), carry_s)
        grad_c = grad_c + dot3(split(spread(grown, j, heads_in, size) * grad_y), split(state))
    gbc_ref[:, 0:LANES] = grad_b
    gbc_ref[:, LANES : 2 * LANES] = grad_c
    both = lax.dot_general(
        jnp.ones((8, LANES), F32), cs_ref[...], (NT, ((), ())), precision=HIGH, preferred_element_type=F32
    )
    constant = jnp.sum(leaving, axis=0, keepdims=True) + jnp.exp(last) * both[0:1]
    upper = jnp.where(row_ids(length) <= lane_ids(length), 1.0, 0.0)
    grad_rate = constant + lax.dot_general(
        upper, sums_y - sums, (NN, ((), ())), precision=HIGH, preferred_element_type=F32
    )
    grad_step = sums / step - jnp.exp(perw_ref[1:2, :]) * grad_rate
    gdt_ref[...] = (grad_step * sigmoid(dtw_ref[...]))[:, 0 : gdt_ref.shape[1]]


def product_kernel(rows, steps, held_ref, early_ref, late_ref, out_ref, rhs_ref):
    size, share, length = held_ref.shape
    at = pl.program_id(0)

    @pl.when(at == 0)
    def _():
        for s in range(size):
            rhs_ref[s * length : (s + 1) * length, :] = held_ref[s].astype(F32).T.astype(BF16)

    @pl.when(at < steps)
    def _():
        send_blocks(rows, share, early_ref, rhs_ref, out_ref)

    @pl.when(at >= steps)
    def _():
        send_blocks(rows, share, late_ref, rhs_ref, out_ref)


def send_blocks(rows, share, go_ref, rhs_ref, out_ref):
    lhs = jnp.concatenate([go_ref[s] for s in range(go_ref.shape[0])], axis=1)
    result = dot(lhs, rhs_ref[...], NN)
    for d in range(out_ref.shape[0]):
        block = result[rows * d : rows * (d + 1)]
        exponent = exponent_of(block)
        scale = jnp.exp2(13.0 - exponent)
        if share > LANES:
            rest = share - LANES
            across = LANES // rest
            tall = rows // across
            out_ref[d, 0:rows, :] = block[:, 0:LANES] * scale
            extra = block[:, LANES:share] * scale[:, 0:rest]
            pieces = [extra[tall * m : tall * (m + 1)] for m in range(across)]
            out_ref[d, rows : rows + tall, :] = jnp.concatenate(pieces, axis=1)
            out_ref[d, rows + tall : rows + tall + 4, :] = jnp.broadcast_to(exponent, (4, LANES))
        else:
            out_ref[d, 0:rows, :] = block * scale[:, 0:share]
            out_ref[d, rows : rows + 4, :] = jnp.broadcast_to(exponent[:, 0:share], (4, share))


def assemble_kernel(rows, size, share, parts_ref, out_ref):
    count = parts_ref.shape[0]
    last = parts_ref.shape[2] - 1
    scales = [jnp.exp2(parts_ref[s, parts_ref.shape[1] - 1, last] - 13.0) for s in range(count)]
    if share > LANES:
        rest = share - LANES
        across = LANES // rest
        for c in range(size):
            total = parts_ref[c, 0:rows, :] * scales[c]
            for s in range(c + size, count, size):
                total = total + parts_ref[s, 0:rows, :] * scales[s]
            out_ref[:, c * LANES : (c + 1) * LANES] = total
        tall = rows // across
        for c in range(size):
            total = parts_ref[c, rows : rows + tall, :] * scales[c]
            for s in range(c + size, count, size):
                total = total + parts_ref[s, rows : rows + tall, :] * scales[s]
            for m in range(across):
                first = size * LANES + rest * c
                out_ref[tall * m : tall * (m + 1), first : first + rest] = total[:, rest * m : rest * (m + 1)]
    else:
        for c in range(size):
            total = parts_ref[c, 0:rows, :] * scales[c]
            for s in range(c + size, count, size):
                total = total + parts_ref[s, 0:rows, :] * scales[s]
            out_ref[:, c * share : (c + 1) * share] = total


def exchange(message, groups=None):
    half = message.astype(jnp.float16)
    return lax.all_to_all(half, "ctx", 0, 0, axis_index_groups=groups, tiled=True)


def groups_of(count, size):
    return [list(range(at, at + size)) for at in range(0, count, size)]


def group_of(count):
    for size in (16, 8, 4, 2):
        if count % size == 0:
            return size
    return 1


def from_behind(value, axis):
    count = lax.axis_size(axis)
    return lax.ppermute(value, axis, [(source, source + 1) for source in range(count - 1)])


def per_device(
    x_raw,
    bc_raw,
    gate_branch,
    dt_raw,
    conv_x,
    conv_x_bias,
    conv_bc,
    conv_bc_bias,
    dt_bias,
    a_log,
    d_skip,
    out_weight,
    grad_out,
):
    length, head_count = dt_raw.shape
    channels = x_raw.shape[1]
    width = grad_out.shape[1]
    head_size = channels // head_count
    heads_in = LANES // head_size
    count = lax.axis_size("ctx")
    plane = min(8, group_of(count))
    planes = groups_of(count, plane)
    rows = channels // plane
    size = group_of(count)
    share = channels // size
    groups = groups_of(count, size)
    turned = call(
        turn_kernel, [shape((width // 2, length), BF16)] * 2, [grad_out], length * width, 8
    )
    early = lax.all_gather(turned[0], "ctx", axis_index_groups=groups)

    rim = from_behind(jnp.concatenate([x_raw[length - 16 :], bc_raw[length - 16 :]], axis=1), "ctx")
    skip = jnp.repeat(d_skip, head_size)[None, :]
    whole = (length, channels)
    square = (length, LANES)
    block = up8(rows) + 8
    stored = pltpu.VMEM((channels, LANES), F32)
    unit = 2 * length * channels * LANES

    part = 640 if channels % 640 == 0 else channels
    grad_gated, grad_y = pl.pallas_call(
        gate_kernel,
        grid=(channels // part,),
        in_specs=[
            pl.BlockSpec((length, width), lambda i: (0, 0)),
            pl.BlockSpec((part, width), lambda i: (i, 0)),
            pl.BlockSpec((length, part), lambda i: (0, i)),
        ],
        out_specs=(pl.BlockSpec((length, part), lambda i: (0, i)), pl.BlockSpec((length, part), lambda i: (0, i))),
        out_shape=(shape(whole), shape(whole)),
        compiler_params=pltpu.CompilerParams(vmem_limit_bytes=56 * MIB),
        cost_estimate=pl.CostEstimate(
            flops=2 * length * channels * width, bytes_accessed=2 * channels * width, transcendentals=0
        ),
    )(grad_out, out_weight, gate_branch)
    act_x, slope_x, act_bc, slope_bc, step, ld, step_t, ld_t, raised, per_head, message = call(
        functools.partial(prepare_kernel, heads_in, head_size, rows),
        [shape(whole), shape(whole), shape(bc_raw.shape), shape(bc_raw.shape)]
        + [shape(square)] * 2
        + [shape((LANES, length))] * 2
        + [shape(square), shape((8, LANES))]
        + [shape((plane, 2 * block, LANES))],
        [
            x_raw,
            rim[:, :channels],
            bc_raw,
            rim[:, channels:],
            conv_x,
            conv_x_bias[None, :],
            conv_bc,
            conv_bc_bias[None, :],
            dt_raw,
            jnp.stack([dt_bias, a_log]),
            grad_y,
        ],
        20 * unit,
        20,
        [
            pltpu.VMEM((length + 8, channels), F32),
            pltpu.VMEM((length + 8, bc_raw.shape[1]), F32),
            stored,
            stored,
        ],
    )
    arrived = exchange(message, planes)
    ahead, behind = arrived[:, :block].astype(F32), arrived[:, block:].astype(F32)
    y_within, grad_within, grad_bc_within = call(
        functools.partial(local_kernel, heads_in, head_size),
        [shape(whole), shape(whole), shape(act_bc.shape)],
        [act_x, grad_y, act_bc, step, ld, step_t, ld_t],
        40 * unit,
        16,
        [pltpu.VMEM(square, F32)],
    )
    (total,) = call(
        functools.partial(total_kernel, rows), [shape((2, block, LANES))], [ahead, behind], 4 * ahead.size, 12
    )
    level = lax.axis_index("ctx") // plane
    later = (jnp.arange(count // plane) > level)[:, None, None]
    columns = [list(range(at, count, plane)) for at in range(plane)]
    totals = exchange(jnp.where(later, total[0][None], total[1][None]), columns).astype(F32)
    (folded,) = call(
        functools.partial(fold_kernel, rows),
        [shape(message.shape)],
        [level.astype(jnp.int32).reshape(1), ahead, behind, totals],
        8 * message.size,
        16,
        specs=[SMEM] + [pl.BlockSpec(memory_space=pltpu.VMEM)] * 3,
    )
    entered, rest = lax.optimization_barrier((exchange(folded, planes), turned[1]))
    late = lax.all_gather(rest, "ctx", axis_index_groups=groups)
    state_message = entered[:, :block].astype(F32)
    gated, y_ahead = call(
        functools.partial(forward_kernel, heads_in, head_size, rows),
        [shape((size, share, length), BF16), shape(whole)],
        [state_message, act_x, gate_branch, act_bc, ld, y_within, skip],
        20 * unit,
        16,
        [stored],
    )
    held = lax.all_to_all(gated, "ctx", 0, 0, axis_index_groups=groups, tiled=True)
    out_rows = width // count
    part = width // 2
    for candidate in (320, 640):
        if part % candidate == 0 and candidate % out_rows == 0:
            part = candidate
            break
    steps = width // 2 // part
    dims = (out_rows + 4, share)
    if share > LANES:
        dims = (out_rows + out_rows // (LANES // (share - LANES)) + 4, LANES)
    partial = pl.pallas_call(
        functools.partial(product_kernel, out_rows, steps),
        grid=(2 * steps,),
        in_specs=[
            pl.BlockSpec((size, share, length), lambda i: (0, 0, 0)),
            pl.BlockSpec((size, part, length), lambda i: (0, jnp.minimum(i, steps - 1), 0)),
            pl.BlockSpec((size, part, length), lambda i: (0, jnp.maximum(i - steps, 0), 0)),
        ],
        out_specs=pl.BlockSpec((part // out_rows, *dims), lambda i: (i, 0, 0)),
        out_shape=shape((count, *dims)),
        scratch_shapes=[pltpu.VMEM((size * length, share), BF16)],
        compiler_params=pltpu.CompilerParams(vmem_limit_bytes=56 * MIB),
        cost_estimate=pl.CostEstimate(
            flops=2 * size * length * share * width, bytes_accessed=2 * size * length * width, transcendentals=0
        ),
    )(held, early, late)
    parts = exchange(partial).astype(F32)
    (weight_grad,) = call(
        functools.partial(assemble_kernel, out_rows, size, share),
        [shape((out_rows, channels))],
        [parts],
        2 * parts.size,
        12,
    )
    carry_message = entered[:, block:].astype(F32)
    grad_x_conv, grad_bc, grad_dt_raw, grad_z = call(
        functools.partial(backward_kernel, heads_in, head_size, rows),
        [shape(whole, BF16), shape(act_bc.shape), shape(dt_raw.shape), shape(whole, BF16)],
        [
            carry_message,
            state_message,
            act_x,
            slope_x,
            grad_y,
            act_bc,
            step,
            ld,
            grad_within,
            grad_bc_within,
            y_ahead,
            grad_gated,
            gate_branch,
            skip,
            raised,
            per_head,
        ],
        40 * unit,
        28,
        [stored, stored, pltpu.VMEM((LANES, LANES), F32)],
    )
    grad_bc_conv = (lax.psum(grad_bc, "tp") * slope_bc).astype(BF16)
    return (grad_x_conv, grad_bc_conv, grad_z, grad_dt_raw, weight_grad)


def solution(mesh):
    placed = (
        P("ctx", "tp"),
        P("ctx", None),
        P("ctx", "tp"),
        P("ctx", "tp"),
        P(None, "tp"),
        P("tp"),
        P(),
        P(),
        P("tp"),
        P("tp"),
        P("tp"),
        P("tp", None),
        P("ctx", None),
    )
    return jax.shard_map(
        per_device,
        mesh=mesh,
        in_specs=placed,
        out_specs=(P("ctx", "tp"), P("ctx", None), P("ctx", "tp"), P("ctx", "tp"), P("ctx", "tp")),
        check_vma=False,
    )
```

```python
import functools

import jax
import jax.numpy as jnp
from jax import lax
from jax.experimental import pallas as pl
from jax.experimental.pallas import tpu as pltpu
from jax.sharding import PartitionSpec as P

KERNEL = 4
LANES = 128
F32 = jnp.float32
BF16 = jnp.bfloat16
NN = ((1,), (0,))
NT = ((1,), (1,))
HIGH = lax.Precision.HIGHEST
MIB = 1024 * 1024


def call(kernel, out_shapes, operands, flops, vmem, scratch=(), specs=None):
    extra = {} if specs is None else {"in_specs": specs}
    moved = sum(a.size * a.dtype.itemsize for a in (*operands, *out_shapes))
    return pl.pallas_call(
        kernel,
        out_shape=tuple(out_shapes),
        scratch_shapes=list(scratch),
        compiler_params=pltpu.CompilerParams(vmem_limit_bytes=vmem * MIB),
        cost_estimate=pl.CostEstimate(flops=flops, bytes_accessed=moved, transcendentals=0),
        **extra,
    )(*operands)


def shape(dims, dtype=F32):
    return jax.ShapeDtypeStruct(dims, dtype)


def split(value):
    high = value.astype(BF16)
    return high, (value - high.astype(F32)).astype(BF16)


def dot(a, b, dims):
    return lax.dot_general(a, b, (dims, ((), ())), preferred_element_type=F32)


def dot3(a, b, dims=NN):
    return dot(a[0], b[0], dims) + (dot(a[0], b[1], dims) + dot(a[1], b[0], dims))


def sigmoid(value):
    return 1.0 / (1.0 + jnp.exp(-value))


def lane_ids(rows, cols=LANES):
    return lax.broadcasted_iota(jnp.int32, (rows, cols), 1)


def row_ids(rows, cols=LANES):
    return lax.broadcasted_iota(jnp.int32, (rows, cols), 0)


def spread(columns, block, heads, size):
    first = block * heads
    lanes = lane_ids(columns.shape[0])
    wide = jnp.broadcast_to(columns[:, first : first + 1], (columns.shape[0], LANES))
    for k in range(1, heads):
        wide = jnp.where(lanes >= k * size, columns[:, first + k : first + k + 1], wide)
    return wide


def head_of(block, heads, size):
    inner = row_ids(LANES)
    target = lane_ids(LANES)
    result = jnp.zeros((LANES, LANES), F32)
    for k in range(heads):
        here = (inner >= k * size) & (inner < (k + 1) * size) & (target == block * heads + k)
        result = jnp.where(here, 1.0, result)
    return result.astype(BF16)


def stacked(value, heads, size):
    lanes = lane_ids(value.shape[0])
    return jnp.concatenate(
        [jnp.where((lanes >= k * size) & (lanes < (k + 1) * size), value, 0.0) for k in range(heads)],
        axis=0,
    )


def up8(value):
    return -(-value // 8) * 8


def notes_of(rows):
    return -(-rows // LANES)


def exponent_of(block):
    top = jnp.max(jnp.max(jnp.abs(block), axis=0, keepdims=True), axis=1, keepdims=True)
    return jnp.floor(jnp.log2(jnp.maximum(jnp.broadcast_to(top, (1, LANES)), 1e-30)))


def write_block(message, at, first, block, decays, exponent):
    rows = block.shape[0]
    padded = up8(rows)
    message[at, first : first + rows, :] = block * jnp.exp2(13.0 - exponent)
    if padded > rows:
        message[at, first + rows : first + padded, :] = jnp.zeros((padded - rows, LANES), F32)
    highs = [d.astype(BF16).astype(F32) for d in decays]
    lows = [d - h for d, h in zip(decays, highs)]
    place = row_ids(8)
    notes = jnp.broadcast_to(exponent, (8, LANES))
    for k, line in enumerate(highs + lows):
        notes = jnp.where(place == k, line, notes)
    message[at, first + padded : first + padded + 8, :] = notes


def decay_tables(last_exp, heads, size, rows, count):
    shift = size.bit_length() - 1
    tables = []
    for d in range(count):
        lines = []
        for k in range(notes_of(rows)):
            first = rows * d + LANES * k
            owner = lax.shift_right_logical(lane_ids(1) + first, shift)
            table = jnp.zeros((1, LANES), F32)
            for h in range(first // size, min(heads, (first + LANES - 1) // size + 1)):
                table = jnp.where(owner == h, last_exp[:, h : h + 1], table)
            lines.append(table)
        tables.append(lines)
    return tables


def pack_blocks(source, message, last_exp, size, rows):
    count = message.shape[0]
    tables = decay_tables(last_exp, source.shape[0] // size, size, rows, count)
    for d in range(count):
        block = source[rows * d : rows * (d + 1), :]
        write_block(message, d, 0, block, tables[d], exponent_of(block))


def decay_lines(message, at, rows):
    padded, lines = up8(rows), notes_of(rows)
    return [
        message[at, padded + k : padded + k + 1, :] + message[at, padded + lines + k : padded + lines + k + 1, :]
        for k in range(lines)
    ]


def decay_columns(message, rows):
    padded, lines = up8(rows), notes_of(rows)
    turned = [
        jnp.transpose(message[:, padded + k, :] + message[:, padded + lines + k, :]) for k in range(lines)
    ]
    return jnp.concatenate(turned, axis=0)[0:rows]


def read_block(message, at, rows):
    padded = up8(rows)
    return message[at, 0:rows, :] * jnp.exp2(message[at, padded + 7 : padded + 8, :] - 13.0)


def unpack_blocks(message, target, rows):
    for d in range(message.shape[0]):
        target[rows * d : rows * (d + 1), :] = read_block(message, d, rows)


def total_kernel(rows, reverse, held_ref, out_ref):
    count = held_ref.shape[0]
    columns = decay_columns(held_ref, rows)
    state = None
    for s in range(count - 1, -1, -1) if reverse else range(count):
        block = read_block(held_ref, s, rows)
        state = block if state is None else columns[:, s : s + 1] * state + block
    decays = decay_lines(held_ref, 0, rows)
    for s in range(1, count):
        decays = [a * b for a, b in zip(decays, decay_lines(held_ref, s, rows))]
    write_block(out_ref, 0, 0, state, decays, exponent_of(state))


def fold_kernel(rows, reverse, held_ref, *refs):
    others, out_ref = refs[:-1], refs[-1]
    count = held_ref.shape[0]
    columns = decay_columns(held_ref, rows)
    state = jnp.zeros((rows, LANES), F32)
    for other in reversed(others):
        state = decay_columns(other, rows) * state + read_block(other, 0, rows)
    for s in range(count - 1, -1, -1) if reverse else range(count):
        write_block(out_ref, s, 0, state, [], exponent_of(state))
        if s != (0 if reverse else count - 1):
            state = columns[:, s : s + 1] * state + read_block(held_ref, s, rows)


def prepare_kernel(
    heads_in, size, rows, x_ref, rim_ref, bc_ref, rim_bc_ref, wx_ref, bx_ref, wbc_ref, bbc_ref, dt_ref,
    per_ref, act_ref, slope_ref, abc_ref, sbc_ref, step_ref, ld_ref, stept_ref, ldt_ref, dtw_ref, perw_ref, msg_ref,
    xs_ref, bs_ref, st_ref,
):
    length = x_ref.shape[0]
    blocks = x_ref.shape[1] // LANES

    def convolved(raw, rim, padded, weight, bias, cols):
        padded[0:8, cols] = rim[:, cols].astype(F32)[8:16]
        padded[8 : 8 + length, cols] = raw[:, cols].astype(F32)
        pre = bias[:, cols] + weight[0:1, cols] * padded[5 : 5 + length, cols]
        for k in range(1, KERNEL):
            pre = pre + weight[k : k + 1, cols] * padded[5 + k : 5 + k + length, cols]
        gate = sigmoid(pre)
        return pre * gate, gate * (1.0 + pre * (1.0 - gate))

    for j in range(bc_ref.shape[1] // LANES):
        cols = slice(j * LANES, (j + 1) * LANES)
        value, slope = convolved(bc_ref, rim_bc_ref, bs_ref, wbc_ref, bbc_ref, cols)
        abc_ref[:, cols] = value
        sbc_ref[:, cols] = slope
    b_rows = split(abc_ref[:, 0:LANES])
    heads = dt_ref.shape[1]
    dtw_ref[...] = jnp.zeros_like(dtw_ref)
    dtw_ref[:, 0:heads] = dt_ref[...]
    perw_ref[...] = jnp.zeros_like(perw_ref)
    perw_ref[0:2, 0:heads] = per_ref[...]
    raised = dtw_ref[...] + perw_ref[0:1, :]
    dtw_ref[...] = raised
    step = jnp.maximum(raised, 0.0) + jnp.log1p(jnp.exp(-jnp.abs(raised)))
    lower = jnp.where(row_ids(length) >= lane_ids(length), 1.0, 0.0)
    ld = lax.dot_general(
        lower, step * -jnp.exp(perw_ref[1:2, :]), (NN, ((), ())), precision=HIGH, preferred_element_type=F32
    )
    step_ref[...] = step
    ld_ref[...] = ld
    stept_ref[...] = step.T
    ldt_ref[...] = ld.T
    last = ld[length - 1 : length]
    weight = jnp.exp(last - ld) * step
    for j in range(blocks):
        cols = slice(j * LANES, (j + 1) * LANES)
        value, slope = convolved(x_ref, rim_ref, xs_ref, wx_ref, bx_ref, cols)
        act_ref[:, cols] = value
        slope_ref[:, cols] = slope
        scaled = value * spread(weight, j, heads_in, size)
        st_ref[cols, :] = dot3(split(scaled.T), b_rows)
    pack_blocks(st_ref, msg_ref, jnp.exp(last), size, rows)


def grad_kernel(heads_in, size, rows, gy_ref, abc_ref, ld_ref, msg_ref, st_ref):
    length = gy_ref.shape[0]
    c_rows = split(abc_ref[:, LANES : 2 * LANES])
    grown = jnp.exp(ld_ref[...])
    for j in range(gy_ref.shape[1] // LANES):
        cols = slice(j * LANES, (j + 1) * LANES)
        scaled = gy_ref[:, cols] * spread(grown, j, heads_in, size)
        st_ref[cols, :] = dot3(split(scaled.T), c_rows)
    pack_blocks(st_ref, msg_ref, grown[length - 1 : length], size, rows)


def gate_kernel(go_ref, w_ref, gate_ref, gg_ref, gy_ref):
    grad = dot(w_ref[...], go_ref[...], NT).T
    gate = gate_ref[...].astype(F32)
    gg_ref[...] = grad
    gy_ref[...] = grad * (gate * sigmoid(gate))


def local_kernel(
    heads_in, size, act_ref, gy_ref, abc_ref, step_ref, ld_ref, stept_ref, ldt_ref, yw_ref, gw_ref, gbc_ref, sh_ref
):
    length = act_ref.shape[0]
    b_rows = split(abc_ref[:, 0:LANES])
    c_rows = split(abc_ref[:, LANES : 2 * LANES])
    scores = dot3(c_rows, b_rows, NT)
    turned = dot3(b_rows, c_rows, NT)
    causal = row_ids(length) >= lane_ids(length)
    causal_t = row_ids(length) <= lane_ids(length)
    sh_ref[...] = jnp.zeros_like(sh_ref)
    for j in range(act_ref.shape[1] // LANES):
        cols = slice(j * LANES, (j + 1) * LANES)
        mixes, mixes_t, steps = [], [], []
        for h in range(j * heads_in, (j + 1) * heads_in):
            column, row = ld_ref[:, h : h + 1], ldt_ref[h : h + 1, :]
            decays = jnp.exp(jnp.where(causal, column - row, -1e30))
            stepped = decays * stept_ref[h : h + 1, :]
            decays_t = jnp.exp(jnp.where(causal_t, row - column, -1e30))
            steps.append(stepped)
            mixes.append(stepped * scores)
            mixes_t.append(decays_t * turned * step_ref[:, h : h + 1])
        inputs = act_ref[:, cols]
        grad_y = gy_ref[:, cols]
        inputs_s = stacked(inputs, heads_in, size)
        grads_s = split(stacked(grad_y, heads_in, size))
        yw_ref[:, cols] = dot3(split(jnp.concatenate(mixes, axis=1)), split(inputs_s))
        gw_ref[:, cols] = dot3(split(jnp.concatenate(mixes_t, axis=1)), grads_s)
        products = dot3(grads_s, split(inputs), NT)
        total = sh_ref[...]
        for k in range(heads_in):
            total = total + steps[k] * products[k * length : (k + 1) * length]
        sh_ref[...] = total
    shared = sh_ref[...]
    gbc_ref[:, 0:LANES] = dot3(split(shared.T), c_rows)
    gbc_ref[:, LANES : 2 * LANES] = dot3(split(shared), b_rows)


def place_of(channel, share, size):
    if share > LANES:
        if channel < LANES * size:
            return channel // LANES, channel % LANES
        rest = share - LANES
        return (channel - LANES * size) // rest, LANES + (channel - LANES * size) % rest
    return channel // share, channel % share


def forward_kernel(
    heads_in, size, rows, msg_ref, act_ref, gate_ref, abc_ref, ld_ref, yw_ref, skip_ref, gt_ref, ys_ref, st_ref
):
    share = gt_ref.shape[1]
    unpack_blocks(msg_ref, st_ref, rows)
    c_rows = split(abc_ref[:, LANES : 2 * LANES])
    grown = jnp.exp(ld_ref[...])
    for j in range(act_ref.shape[1] // LANES):
        cols = slice(j * LANES, (j + 1) * LANES)
        carried = dot3(c_rows, split(st_ref[cols, :]), NT)
        within = yw_ref[:, cols] + spread(grown, j, heads_in, size) * carried
        ys_ref[:, cols] = within
        output = within + skip_ref[:, cols] * act_ref[:, cols]
        gate = gate_ref[:, cols].astype(F32)
        turned = (output * (gate * sigmoid(gate))).T.astype(BF16)
        for k in range(0, LANES, 16):
            to, at = place_of(j * LANES + k, share, gt_ref.shape[0])
            gt_ref[to, at : at + 16, :] = turned[k : k + 16]


def backward_kernel(
    heads_in, size, rows, msg_ref, msgf_ref, act_ref, slope_ref, gy_ref, abc_ref, step_ref, ld_ref, gw_ref,
    gbcl_ref, ys_ref, gg_ref, gate_ref, skip_ref, dtw_ref, perw_ref, gx_ref, gbc_ref, gdt_ref, gz_ref,
    ca_ref, st_ref, cs_ref,
):
    length = act_ref.shape[0]
    unpack_blocks(msg_ref, ca_ref, rows)
    unpack_blocks(msgf_ref, st_ref, rows)
    b_rows = split(abc_ref[:, 0:LANES])
    ld = ld_ref[...]
    step = step_ref[...]
    last = ld[length - 1 : length]
    grown = jnp.exp(ld)
    weight = jnp.exp(last - ld) * step
    sums = jnp.zeros((length, LANES), F32)
    sums_y = jnp.zeros((length, LANES), F32)
    leaving = jnp.zeros((8, LANES), F32)
    grad_b = gbcl_ref[:, 0:LANES]
    grad_c = gbcl_ref[:, LANES : 2 * LANES]
    cs_ref[...] = jnp.zeros_like(cs_ref)
    for j in range(act_ref.shape[1] // LANES):
        cols = slice(j * LANES, (j + 1) * LANES)
        inputs = act_ref[:, cols]
        grad_y = gy_ref[:, cols]
        carry = ca_ref[cols, :]
        state = st_ref[cols, :]
        carry_s = split(carry)
        wide = spread(weight, j, heads_in, size)
        gone = wide * dot3(b_rows, carry_s, NT)
        grad_in = gw_ref[:, cols] + gone
        gx_ref[:, cols] = ((skip_ref[:, cols] * grad_y + grad_in) * slope_ref[:, cols]).astype(BF16)
        onehot = head_of(j, heads_in, size)
        within = ys_ref[:, cols]
        gate = gate_ref[:, cols].astype(F32)
        opened = sigmoid(gate)
        output = within + skip_ref[:, cols] * inputs
        gz_ref[:, cols] = (gg_ref[:, cols] * output * (opened * (1.0 + gate * (1.0 - opened)))).astype(BF16)
        high, low = split(grad_y * within)
        sums_y = sums_y + (dot(high, onehot, NN) + dot(low, onehot, NN))
        high, low = split(inputs * grad_in)
        sums = sums + (dot(high, onehot, NN) + dot(low, onehot, NN))
        folded = jnp.sum((inputs * gone).reshape(length // 8, 8, LANES), axis=0)
        high, low = split(folded)
        leaving = leaving + (dot(high, onehot, NN) + dot(low, onehot, NN))
        product = carry * state
        for k in range(heads_in):
            h = j * heads_in + k
            cs_ref[h : h + 1, :] = jnp.sum(product[k * size : (k + 1) * size], axis=0, keepdims=True)
        grad_b = grad_b + dot3(split(wide * inputs), carry_s)
        grad_c = grad_c + dot3(split(spread(grown, j, heads_in, size) * grad_y), split(state))
    gbc_ref[:, 0:LANES] = grad_b
    gbc_ref[:, LANES : 2 * LANES] = grad_c
    both = lax.dot_general(
        jnp.ones((8, LANES), F32), cs_ref[...], (NT, ((), ())), precision=HIGH, preferred_element_type=F32
    )
    constant = jnp.sum(leaving, axis=0, keepdims=True) + jnp.exp(last) * both[0:1]
    upper = jnp.where(row_ids(length) <= lane_ids(length), 1.0, 0.0)
    grad_rate = constant + lax.dot_general(
        upper, sums_y - sums, (NN, ((), ())), precision=HIGH, preferred_element_type=F32
    )
    grad_step = sums / step - jnp.exp(perw_ref[1:2, :]) * grad_rate
    gdt_ref[...] = (grad_step * sigmoid(dtw_ref[...]))[:, 0 : gdt_ref.shape[1]]


def product_kernel(rows, held_ref, go_ref, out_ref, lhs_ref):
    size, share, length = held_ref.shape

    @pl.when(pl.program_id(0) == 0)
    def _():
        for s in range(size):
            lhs_ref[:, s * length : (s + 1) * length] = held_ref[s]

    result = dot(lhs_ref[...], go_ref[...], NN).T
    for d in range(out_ref.shape[0]):
        block = result[rows * d : rows * (d + 1)]
        if share > LANES:
            rest = share - LANES
            across = LANES // rest
            out_ref[d, 0:rows, :] = block[:, 0:LANES].astype(BF16)
            for k in range(0, rows // 16, across):
                pieces = [block[16 * m : 16 * m + 16, LANES:] for m in range(k, min(k + across, rows // 16))]
                if len(pieces) < across:
                    pieces.append(jnp.zeros((16, LANES - rest * len(pieces)), F32))
                at = rows + 16 * (k // across)
                out_ref[d, at : at + 16, :] = jnp.concatenate(pieces, axis=1).astype(BF16)
        else:
            out_ref[d] = block.astype(BF16)


def assemble_kernel(rows, size, share, parts_ref, out_ref):
    count = parts_ref.shape[0]

    def total(c, first, last):
        found = parts_ref[c, first:last, :].astype(F32)
        for s in range(c + size, count, size):
            found = found + parts_ref[s, first:last, :].astype(F32)
        return found

    if share > LANES:
        rest = share - LANES
        across = LANES // rest
        for c in range(size):
            out_ref[:, c * LANES : (c + 1) * LANES] = total(c, 0, rows)
            at = size * LANES + rest * c
            for k in range(0, rows // 16, across):
                extra = total(c, rows + 16 * (k // across), rows + 16 * (k // across) + 16)
                for m in range(k, min(k + across, rows // 16)):
                    lanes = slice(rest * (m - k), rest * (m - k + 1))
                    out_ref[16 * m : 16 * m + 16, at : at + rest] = extra[:, lanes]
    else:
        for c in range(size):
            out_ref[:, c * share : (c + 1) * share] = total(c, 0, rows)


def exchange(message, groups=None):
    half = message.astype(jnp.float16)
    return lax.all_to_all(half, "ctx", 0, 0, axis_index_groups=groups, tiled=True)


def groups_of(count, size):
    return [list(range(at, at + size)) for at in range(0, count, size)]


def enter(held, rows, reverse):
    size = held.shape[0]
    count = lax.axis_size("ctx")
    (total,) = call(
        functools.partial(total_kernel, rows, reverse), [shape((1, *held.shape[1:]))], [held], 4 * held.size, 12
    )
    total = total.astype(jnp.float16)
    others = []
    for hops in range(size, count, size):
        pairs = [(at, at + hops) for at in range(count - hops)]
        if reverse:
            pairs = [(b, a) for a, b in pairs]
        others.append(lax.ppermute(total, "ctx", pairs).astype(F32))
    (folded,) = call(
        functools.partial(fold_kernel, rows, reverse), [shape(held.shape)], [held, *others], 8 * held.size, 12
    )
    return folded


def group_of(count):
    for size in (16, 8, 4, 2):
        if count % size == 0:
            return size
    return 1


def from_behind(value, axis):
    count = lax.axis_size(axis)
    return lax.ppermute(value, axis, [(source, source + 1) for source in range(count - 1)])


def per_device(
    x_raw,
    bc_raw,
    gate_branch,
    dt_raw,
    conv_x,
    conv_x_bias,
    conv_bc,
    conv_bc_bias,
    dt_bias,
    a_log,
    d_skip,
    out_weight,
    grad_out,
):
    length, head_count = dt_raw.shape
    channels = x_raw.shape[1]
    width = grad_out.shape[1]
    head_size = channels // head_count
    heads_in = LANES // head_size
    count = lax.axis_size("ctx")
    plane = min(8, group_of(count))
    planes = groups_of(count, plane)
    rows = channels // plane
    size = group_of(count)
    share = channels // size
    groups = groups_of(count, size)
    gathered = lax.all_gather(grad_out, "ctx", axis_index_groups=groups, tiled=True)

    rim = from_behind(jnp.concatenate([x_raw[length - 16 :], bc_raw[length - 16 :]], axis=1), "ctx")
    skip = jnp.repeat(d_skip, head_size)[None, :]
    whole = (length, channels)
    square = (length, LANES)
    block = up8(rows) + 8
    stored = pltpu.VMEM((channels, LANES), F32)
    unit = 2 * length * channels * LANES

    act_x, slope_x, act_bc, slope_bc, step, ld, step_t, ld_t, raised, per_head, message = call(
        functools.partial(prepare_kernel, heads_in, head_size, rows),
        [shape(whole), shape(whole), shape(bc_raw.shape), shape(bc_raw.shape)]
        + [shape(square)] * 2
        + [shape((LANES, length))] * 2
        + [shape(square), shape((8, LANES))]
        + [shape((plane, block, LANES))],
        [
            x_raw,
            rim[:, :channels],
            bc_raw,
            rim[:, channels:],
            conv_x,
            conv_x_bias[None, :],
            conv_bc,
            conv_bc_bias[None, :],
            dt_raw,
            jnp.stack([dt_bias, a_log]),
        ],
        20 * unit,
        20,
        [
            pltpu.VMEM((length + 8, channels), F32),
            pltpu.VMEM((length + 8, bc_raw.shape[1]), F32),
            stored,
        ],
    )
    message, grad_out_then = lax.optimization_barrier((message, grad_out))
    held_state = exchange(message, planes).astype(F32)
    part = 640 if channels % 640 == 0 else channels
    grad_gated, grad_y = pl.pallas_call(
        gate_kernel,
        grid=(channels // part,),
        in_specs=[
            pl.BlockSpec((length, width), lambda i: (0, 0)),
            pl.BlockSpec((part, width), lambda i: (i, 0)),
            pl.BlockSpec((length, part), lambda i: (0, i)),
        ],
        out_specs=(pl.BlockSpec((length, part), lambda i: (0, i)), pl.BlockSpec((length, part), lambda i: (0, i))),
        out_shape=(shape(whole), shape(whole)),
        compiler_params=pltpu.CompilerParams(vmem_limit_bytes=56 * MIB),
        cost_estimate=pl.CostEstimate(
            flops=2 * length * channels * width, bytes_accessed=2 * channels * width, transcendentals=0
        ),
    )(grad_out_then, out_weight, gate_branch)
    (message,) = call(
        functools.partial(grad_kernel, heads_in, head_size, rows),
        [shape((plane, block, LANES))],
        [grad_y, act_bc, ld],
        10 * unit,
        12,
        [stored],
    )
    message, held_state = lax.optimization_barrier((message, held_state))
    held_carry = exchange(message, planes)
    y_within, grad_within, grad_bc_within = call(
        functools.partial(local_kernel, heads_in, head_size),
        [shape(whole), shape(whole), shape(act_bc.shape)],
        [act_x, grad_y, act_bc, step, ld, step_t, ld_t],
        40 * unit,
        16,
        [pltpu.VMEM(square, F32)],
    )
    folded, held_carry = lax.optimization_barrier((enter(held_state, rows, False), held_carry))
    state_message = exchange(folded, planes).astype(F32)
    gated, y_ahead = call(
        functools.partial(forward_kernel, heads_in, head_size, rows),
        [shape((size, share, length), BF16), shape(whole)],
        [state_message, act_x, gate_branch, act_bc, ld, y_within, skip],
        20 * unit,
        16,
        [stored],
    )
    held = lax.all_to_all(gated, "ctx", 0, 0, axis_index_groups=groups, tiled=True)
    entered, held = lax.optimization_barrier((enter(held_carry.astype(F32), rows, True), held))
    carry_message = exchange(entered, planes).astype(F32)
    out_rows = width // count
    part = width
    for candidate in (640, 1280):
        if width % candidate == 0 and candidate % out_rows == 0:
            part = candidate
            break
    dims = (out_rows, share)
    if share > LANES:
        dims = (out_rows + 16 * (-(-(out_rows // 16) // (LANES // (share - LANES)))), LANES)
    partial = pl.pallas_call(
        functools.partial(product_kernel, out_rows),
        grid=(width // part,),
        in_specs=[
            pl.BlockSpec((size, share, length), lambda i: (0, 0, 0)),
            pl.BlockSpec((size * length, part), lambda i: (0, i)),
        ],
        out_specs=pl.BlockSpec((part // out_rows, *dims), lambda i: (i, 0, 0)),
        out_shape=shape((count, *dims), BF16),
        scratch_shapes=[pltpu.VMEM((share, size * length), BF16)],
        compiler_params=pltpu.CompilerParams(vmem_limit_bytes=48 * MIB),
        cost_estimate=pl.CostEstimate(
            flops=2 * size * length * share * width, bytes_accessed=2 * size * length * width, transcendentals=0
        ),
    )(held, gathered)
    parts = lax.all_to_all(partial, "ctx", 0, 0, tiled=True)
    (weight_grad,) = call(
        functools.partial(assemble_kernel, out_rows, size, share),
        [shape((out_rows, channels))],
        [parts],
        2 * parts.size,
        12,
    )
    grad_x_conv, grad_bc, grad_dt_raw, grad_z = call(
        functools.partial(backward_kernel, heads_in, head_size, rows),
        [shape(whole, BF16), shape(act_bc.shape), shape(dt_raw.shape), shape(whole, BF16)],
        [
            carry_message,
            state_message,
            act_x,
            slope_x,
            grad_y,
            act_bc,
            step,
            ld,
            grad_within,
            grad_bc_within,
            y_ahead,
            grad_gated,
            gate_branch,
            skip,
            raised,
            per_head,
        ],
        40 * unit,
        48,
        [stored, stored, pltpu.VMEM((LANES, LANES), F32)],
    )
    grad_bc_conv = (lax.psum(grad_bc, "tp") * slope_bc).astype(BF16)
    return (grad_x_conv, grad_bc_conv, grad_z, grad_dt_raw, weight_grad)


def solution(mesh):
    placed = (
        P("ctx", "tp"),
        P("ctx", None),
        P("ctx", "tp"),
        P("ctx", "tp"),
        P(None, "tp"),
        P("tp"),
        P(),
        P(),
        P("tp"),
        P("tp"),
        P("tp"),
        P("tp", None),
        P("ctx", None),
    )
    return jax.shard_map(
        per_device,
        mesh=mesh,
        in_specs=placed,
        out_specs=(P("ctx", "tp"), P("ctx", None), P("ctx", "tp"), P("ctx", "tp"), P("ctx", "tp")),
        check_vma=False,
    )
```

```python
import functools

import jax
import jax.numpy as jnp
from jax import lax
from jax.experimental import pallas as pl
from jax.experimental.pallas import tpu as pltpu
from jax.sharding import PartitionSpec as P

KERNEL = 4
LANES = 128
F32 = jnp.float32
BF16 = jnp.bfloat16
NN = ((1,), (0,))
NT = ((1,), (1,))
HIGH = lax.Precision.HIGHEST
MIB = 1024 * 1024
STREAMS = 4


def call(kernel, out_shapes, operands, flops, vmem, scratch=(), specs=None):
    extra = {} if specs is None else {"in_specs": specs}
    moved = sum(a.size * a.dtype.itemsize for a in (*operands, *out_shapes))
    return pl.pallas_call(
        kernel,
        out_shape=tuple(out_shapes),
        scratch_shapes=list(scratch),
        compiler_params=pltpu.CompilerParams(vmem_limit_bytes=vmem * MIB),
        cost_estimate=pl.CostEstimate(flops=flops, bytes_accessed=moved, transcendentals=0),
        **extra,
    )(*operands)


def shape(dims, dtype=F32):
    return jax.ShapeDtypeStruct(dims, dtype)


def split(value):
    high = value.astype(BF16)
    return high, (value - high.astype(F32)).astype(BF16)


def dot(a, b, dims):
    return lax.dot_general(a, b, (dims, ((), ())), preferred_element_type=F32)


def dot3(a, b, dims=NN):
    return dot(a[0], b[0], dims) + (dot(a[0], b[1], dims) + dot(a[1], b[0], dims))


def sigmoid(value):
    return 1.0 / (1.0 + jnp.exp(-value))


def lane_ids(rows, cols=LANES):
    return lax.broadcasted_iota(jnp.int32, (rows, cols), 1)


def row_ids(rows, cols=LANES):
    return lax.broadcasted_iota(jnp.int32, (rows, cols), 0)


def spread(columns, block, heads, size):
    first = block * heads
    lanes = lane_ids(columns.shape[0])
    wide = jnp.broadcast_to(columns[:, first : first + 1], (columns.shape[0], LANES))
    for k in range(1, heads):
        wide = jnp.where(lanes >= k * size, columns[:, first + k : first + k + 1], wide)
    return wide


def head_of(block, heads, size):
    inner = row_ids(LANES)
    target = lane_ids(LANES)
    result = jnp.zeros((LANES, LANES), F32)
    for k in range(heads):
        here = (inner >= k * size) & (inner < (k + 1) * size) & (target == block * heads + k)
        result = jnp.where(here, 1.0, result)
    return result.astype(BF16)


def stacked(value, heads, size):
    lanes = lane_ids(value.shape[0])
    return jnp.concatenate(
        [jnp.where((lanes >= k * size) & (lanes < (k + 1) * size), value, 0.0) for k in range(heads)],
        axis=0,
    )


def up8(value):
    return -(-value // 8) * 8


def notes_of(rows):
    return -(-rows // LANES)


def exponent_of(block):
    top = jnp.max(jnp.max(jnp.abs(block), axis=0, keepdims=True), axis=1, keepdims=True)
    return jnp.floor(jnp.log2(jnp.maximum(jnp.broadcast_to(top, (1, LANES)), 1e-30)))


def write_block(message, at, first, block, decays, exponent):
    rows = block.shape[0]
    padded = up8(rows)
    message[at, first : first + rows, :] = block * jnp.exp2(13.0 - exponent)
    if padded > rows:
        message[at, first + rows : first + padded, :] = jnp.zeros((padded - rows, LANES), F32)
    highs = [d.astype(BF16).astype(F32) for d in decays]
    lows = [d - h for d, h in zip(decays, highs)]
    place = row_ids(8)
    notes = jnp.broadcast_to(exponent, (8, LANES))
    for k, line in enumerate(highs + lows):
        notes = jnp.where(place == k, line, notes)
    message[at, first + padded : first + padded + 8, :] = notes


def decay_tables(last_exp, heads, size, rows, count):
    shift = size.bit_length() - 1
    tables = []
    for d in range(count):
        lines = []
        for k in range(notes_of(rows)):
            first = rows * d + LANES * k
            owner = lax.shift_right_logical(lane_ids(1) + first, shift)
            table = jnp.zeros((1, LANES), F32)
            for h in range(first // size, min(heads, (first + LANES - 1) // size + 1)):
                table = jnp.where(owner == h, last_exp[:, h : h + 1], table)
            lines.append(table)
        tables.append(lines)
    return tables


def pack_blocks(source, message, last_exp, size, rows):
    count = message.shape[0]
    tables = decay_tables(last_exp, source.shape[0] // size, size, rows, count)
    for d in range(count):
        block = source[rows * d : rows * (d + 1), :]
        write_block(message, d, 0, block, tables[d], exponent_of(block))


def decay_lines(message, at, rows):
    padded, lines = up8(rows), notes_of(rows)
    return [
        message[at, padded + k : padded + k + 1, :] + message[at, padded + lines + k : padded + lines + k + 1, :]
        for k in range(lines)
    ]


def decay_columns(message, rows):
    padded, lines = up8(rows), notes_of(rows)
    turned = [
        jnp.transpose(message[:, padded + k, :] + message[:, padded + lines + k, :]) for k in range(lines)
    ]
    return jnp.concatenate(turned, axis=0)[0:rows]


def read_block(message, at, rows):
    padded = up8(rows)
    return message[at, 0:rows, :] * jnp.exp2(message[at, padded + 7 : padded + 8, :] - 13.0)


def unpack_blocks(message, target, rows):
    for d in range(message.shape[0]):
        target[rows * d : rows * (d + 1), :] = read_block(message, d, rows)


def total_kernel(rows, reverse, held_ref, out_ref):
    count = held_ref.shape[0]
    columns = decay_columns(held_ref, rows)
    state = None
    for s in range(count - 1, -1, -1) if reverse else range(count):
        block = read_block(held_ref, s, rows)
        state = block if state is None else columns[:, s : s + 1] * state + block
    decays = decay_lines(held_ref, 0, rows)
    for s in range(1, count):
        decays = [a * b for a, b in zip(decays, decay_lines(held_ref, s, rows))]
    write_block(out_ref, 0, 0, state, decays, exponent_of(state))


def fold_kernel(rows, reverse, held_ref, *refs):
    others, out_ref = refs[:-1], refs[-1]
    count = held_ref.shape[0]
    columns = decay_columns(held_ref, rows)
    state = jnp.zeros((rows, LANES), F32)
    for other in reversed(others):
        state = decay_columns(other, rows) * state + read_block(other, 0, rows)
    for s in range(count - 1, -1, -1) if reverse else range(count):
        write_block(out_ref, s, 0, state, [], exponent_of(state))
        if s != (0 if reverse else count - 1):
            state = columns[:, s : s + 1] * state + read_block(held_ref, s, rows)


def prepare_kernel(
    heads_in, size, rows, x_ref, rim_ref, bc_ref, rim_bc_ref, wx_ref, bx_ref, wbc_ref, bbc_ref, dt_ref,
    per_ref, act_ref, slope_ref, abc_ref, sbc_ref, step_ref, ld_ref, stept_ref, ldt_ref, dtw_ref, perw_ref, msg_ref,
    xs_ref, bs_ref, st_ref,
):
    length = x_ref.shape[0]
    blocks = x_ref.shape[1] // LANES

    def convolved(raw, rim, padded, weight, bias, cols):
        padded[0:8, cols] = rim[:, cols].astype(F32)[8:16]
        padded[8 : 8 + length, cols] = raw[:, cols].astype(F32)
        pre = bias[:, cols] + weight[0:1, cols] * padded[5 : 5 + length, cols]
        for k in range(1, KERNEL):
            pre = pre + weight[k : k + 1, cols] * padded[5 + k : 5 + k + length, cols]
        gate = sigmoid(pre)
        return pre * gate, gate * (1.0 + pre * (1.0 - gate))

    for j in range(bc_ref.shape[1] // LANES):
        cols = slice(j * LANES, (j + 1) * LANES)
        value, slope = convolved(bc_ref, rim_bc_ref, bs_ref, wbc_ref, bbc_ref, cols)
        abc_ref[:, cols] = value
        sbc_ref[:, cols] = slope
    b_rows = split(abc_ref[:, 0:LANES])
    heads = dt_ref.shape[1]
    dtw_ref[...] = jnp.zeros_like(dtw_ref)
    dtw_ref[:, 0:heads] = dt_ref[...]
    perw_ref[...] = jnp.zeros_like(perw_ref)
    perw_ref[0:2, 0:heads] = per_ref[...]
    raised = dtw_ref[...] + perw_ref[0:1, :]
    dtw_ref[...] = raised
    step = jnp.maximum(raised, 0.0) + jnp.log1p(jnp.exp(-jnp.abs(raised)))
    lower = jnp.where(row_ids(length) >= lane_ids(length), 1.0, 0.0)
    ld = lax.dot_general(
        lower, step * -jnp.exp(perw_ref[1:2, :]), (NN, ((), ())), precision=HIGH, preferred_element_type=F32
    )
    step_ref[...] = step
    ld_ref[...] = ld
    stept_ref[...] = step.T
    ldt_ref[...] = ld.T
    last = ld[length - 1 : length]
    weight = jnp.exp(last - ld) * step
    for j in range(blocks):
        cols = slice(j * LANES, (j + 1) * LANES)
        value, slope = convolved(x_ref, rim_ref, xs_ref, wx_ref, bx_ref, cols)
        act_ref[:, cols] = value
        slope_ref[:, cols] = slope
        scaled = value * spread(weight, j, heads_in, size)
        st_ref[cols, :] = dot3(split(scaled.T), b_rows)
    pack_blocks(st_ref, msg_ref, jnp.exp(last), size, rows)


def grad_kernel(heads_in, size, rows, gy_ref, abc_ref, ld_ref, msg_ref, st_ref):
    length = gy_ref.shape[0]
    c_rows = split(abc_ref[:, LANES : 2 * LANES])
    grown = jnp.exp(ld_ref[...])
    for j in range(gy_ref.shape[1] // LANES):
        cols = slice(j * LANES, (j + 1) * LANES)
        scaled = gy_ref[:, cols] * spread(grown, j, heads_in, size)
        st_ref[cols, :] = dot3(split(scaled.T), c_rows)
    pack_blocks(st_ref, msg_ref, grown[length - 1 : length], size, rows)


def gate_kernel(go_ref, w_ref, gate_ref, gg_ref, gy_ref):
    grad = dot(w_ref[...], go_ref[...], NT).T
    gate = gate_ref[...].astype(F32)
    gg_ref[...] = grad
    gy_ref[...] = grad * (gate * sigmoid(gate))


def local_kernel(
    heads_in, size, act_ref, gy_ref, abc_ref, step_ref, ld_ref, stept_ref, ldt_ref, yw_ref, gw_ref, gbc_ref, sh_ref
):
    length = act_ref.shape[0]
    b_rows = split(abc_ref[:, 0:LANES])
    c_rows = split(abc_ref[:, LANES : 2 * LANES])
    scores = dot3(c_rows, b_rows, NT)
    turned = dot3(b_rows, c_rows, NT)
    causal = row_ids(length) >= lane_ids(length)
    causal_t = row_ids(length) <= lane_ids(length)
    sh_ref[...] = jnp.zeros_like(sh_ref)
    for j in range(act_ref.shape[1] // LANES):
        cols = slice(j * LANES, (j + 1) * LANES)
        mixes, mixes_t, steps = [], [], []
        for h in range(j * heads_in, (j + 1) * heads_in):
            column, row = ld_ref[:, h : h + 1], ldt_ref[h : h + 1, :]
            decays = jnp.exp(jnp.where(causal, column - row, -1e30))
            stepped = decays * stept_ref[h : h + 1, :]
            decays_t = jnp.exp(jnp.where(causal_t, row - column, -1e30))
            steps.append(stepped)
            mixes.append(stepped * scores)
            mixes_t.append(decays_t * turned * step_ref[:, h : h + 1])
        inputs = act_ref[:, cols]
        grad_y = gy_ref[:, cols]
        inputs_s = stacked(inputs, heads_in, size)
        grads_s = split(stacked(grad_y, heads_in, size))
        yw_ref[:, cols] = dot3(split(jnp.concatenate(mixes, axis=1)), split(inputs_s))
        gw_ref[:, cols] = dot3(split(jnp.concatenate(mixes_t, axis=1)), grads_s)
        products = dot3(grads_s, split(inputs), NT)
        total = sh_ref[...]
        for k in range(heads_in):
            total = total + steps[k] * products[k * length : (k + 1) * length]
        sh_ref[...] = total
    shared = sh_ref[...]
    gbc_ref[:, 0:LANES] = dot3(split(shared.T), c_rows)
    gbc_ref[:, LANES : 2 * LANES] = dot3(split(shared), b_rows)


def place_of(channel, share, size):
    if share > LANES:
        if channel < LANES * size:
            return channel // LANES, channel % LANES
        rest = share - LANES
        return (channel - LANES * size) // rest, LANES + (channel - LANES * size) % rest
    return channel // share, channel % share


def forward_kernel(
    heads_in, size, rows, msg_ref, act_ref, gate_ref, abc_ref, ld_ref, yw_ref, skip_ref, gt_ref, ys_ref, st_ref
):
    share = gt_ref.shape[1]
    unpack_blocks(msg_ref, st_ref, rows)
    c_rows = split(abc_ref[:, LANES : 2 * LANES])
    grown = jnp.exp(ld_ref[...])
    for j in range(act_ref.shape[1] // LANES):
        cols = slice(j * LANES, (j + 1) * LANES)
        carried = dot3(c_rows, split(st_ref[cols, :]), NT)
        within = yw_ref[:, cols] + spread(grown, j, heads_in, size) * carried
        ys_ref[:, cols] = within
        output = within + skip_ref[:, cols] * act_ref[:, cols]
        gate = gate_ref[:, cols].astype(F32)
        turned = (output * (gate * sigmoid(gate))).T.astype(BF16)
        for k in range(0, LANES, 16):
            to, at = place_of(j * LANES + k, share, gt_ref.shape[0])
            gt_ref[to, at : at + 16, :] = turned[k : k + 16]


def backward_kernel(
    heads_in, size, rows, msg_ref, msgf_ref, act_ref, slope_ref, gy_ref, abc_ref, step_ref, ld_ref, gw_ref,
    gbcl_ref, ys_ref, gg_ref, gate_ref, skip_ref, dtw_ref, perw_ref, gx_ref, gbc_ref, gdt_ref, gz_ref,
    ca_ref, st_ref, cs_ref,
):
    length = act_ref.shape[0]
    unpack_blocks(msg_ref, ca_ref, rows)
    unpack_blocks(msgf_ref, st_ref, rows)
    b_rows = split(abc_ref[:, 0:LANES])
    ld = ld_ref[...]
    step = step_ref[...]
    last = ld[length - 1 : length]
    grown = jnp.exp(ld)
    weight = jnp.exp(last - ld) * step
    sums = jnp.zeros((length, LANES), F32)
    sums_y = jnp.zeros((length, LANES), F32)
    leaving = jnp.zeros((8, LANES), F32)
    grad_b = gbcl_ref[:, 0:LANES]
    grad_c = gbcl_ref[:, LANES : 2 * LANES]
    cs_ref[...] = jnp.zeros_like(cs_ref)
    for j in range(act_ref.shape[1] // LANES):
        cols = slice(j * LANES, (j + 1) * LANES)
        inputs = act_ref[:, cols]
        grad_y = gy_ref[:, cols]
        carry = ca_ref[cols, :]
        state = st_ref[cols, :]
        carry_s = split(carry)
        wide = spread(weight, j, heads_in, size)
        gone = wide * dot3(b_rows, carry_s, NT)
        grad_in = gw_ref[:, cols] + gone
        gx_ref[:, cols] = ((skip_ref[:, cols] * grad_y + grad_in) * slope_ref[:, cols]).astype(BF16)
        onehot = head_of(j, heads_in, size)
        within = ys_ref[:, cols]
        gate = gate_ref[:, cols].astype(F32)
        opened = sigmoid(gate)
        output = within + skip_ref[:, cols] * inputs
        gz_ref[:, cols] = (gg_ref[:, cols] * output * (opened * (1.0 + gate * (1.0 - opened)))).astype(BF16)
        high, low = split(grad_y * within)
        sums_y = sums_y + (dot(high, onehot, NN) + dot(low, onehot, NN))
        high, low = split(inputs * grad_in)
        sums = sums + (dot(high, onehot, NN) + dot(low, onehot, NN))
        folded = jnp.sum((inputs * gone).reshape(length // 8, 8, LANES), axis=0)
        high, low = split(folded)
        leaving = leaving + (dot(high, onehot, NN) + dot(low, onehot, NN))
        product = carry * state
        for k in range(heads_in):
            h = j * heads_in + k
            cs_ref[h : h + 1, :] = jnp.sum(product[k * size : (k + 1) * size], axis=0, keepdims=True)
        grad_b = grad_b + dot3(split(wide * inputs), carry_s)
        grad_c = grad_c + dot3(split(spread(grown, j, heads_in, size) * grad_y), split(state))
    gbc_ref[:, 0:LANES] = grad_b
    gbc_ref[:, LANES : 2 * LANES] = grad_c
    both = lax.dot_general(
        jnp.ones((8, LANES), F32), cs_ref[...], (NT, ((), ())), precision=HIGH, preferred_element_type=F32
    )
    constant = jnp.sum(leaving, axis=0, keepdims=True) + jnp.exp(last) * both[0:1]
    upper = jnp.where(row_ids(length) <= lane_ids(length), 1.0, 0.0)
    grad_rate = constant + lax.dot_general(
        upper, sums_y - sums, (NN, ((), ())), precision=HIGH, preferred_element_type=F32
    )
    grad_step = sums / step - jnp.exp(perw_ref[1:2, :]) * grad_rate
    gdt_ref[...] = (grad_step * sigmoid(dtw_ref[...]))[:, 0 : gdt_ref.shape[1]]


def product_kernel(rows, held_ref, *refs):
    go_refs, out_ref, lhs_ref = refs[:-2], refs[-2], refs[-1]
    size, share, length = held_ref.shape

    @pl.when(pl.program_id(0) == 0)
    def _():
        for s in range(size):
            lhs_ref[:, s * length : (s + 1) * length] = held_ref[s]

    depth = go_refs[0].shape[0]
    result = dot(lhs_ref[:, 0:depth], go_refs[0][...], NN)
    for k in range(1, len(go_refs)):
        result = result + dot(lhs_ref[:, k * depth : (k + 1) * depth], go_refs[k][...], NN)
    result = result.T
    for d in range(out_ref.shape[0]):
        block = result[rows * d : rows * (d + 1)]
        if share > LANES:
            rest = share - LANES
            across = LANES // rest
            out_ref[d, 0:rows, :] = block[:, 0:LANES].astype(BF16)
            for k in range(0, rows // 16, across):
                pieces = [block[16 * m : 16 * m + 16, LANES:] for m in range(k, min(k + across, rows // 16))]
                if len(pieces) < across:
                    pieces.append(jnp.zeros((16, LANES - rest * len(pieces)), F32))
                at = rows + 16 * (k // across)
                out_ref[d, at : at + 16, :] = jnp.concatenate(pieces, axis=1).astype(BF16)
        else:
            out_ref[d] = block.astype(BF16)


def assemble_kernel(rows, size, share, parts_ref, out_ref):
    count = parts_ref.shape[0]

    def total(c, first, last):
        found = parts_ref[c, first:last, :].astype(F32)
        for s in range(c + size, count, size):
            found = found + parts_ref[s, first:last, :].astype(F32)
        return found

    if share > LANES:
        rest = share - LANES
        across = LANES // rest
        for c in range(size):
            out_ref[:, c * LANES : (c + 1) * LANES] = total(c, 0, rows)
            at = size * LANES + rest * c
            for k in range(0, rows // 16, across):
                extra = total(c, rows + 16 * (k // across), rows + 16 * (k // across) + 16)
                for m in range(k, min(k + across, rows // 16)):
                    lanes = slice(rest * (m - k), rest * (m - k + 1))
                    out_ref[16 * m : 16 * m + 16, at : at + rest] = extra[:, lanes]
    else:
        for c in range(size):
            out_ref[:, c * share : (c + 1) * share] = total(c, 0, rows)


def exchange(message, groups=None):
    half = message.astype(jnp.float16)
    return lax.all_to_all(half, "ctx", 0, 0, axis_index_groups=groups, tiled=True)


def groups_of(count, size):
    return [list(range(at, at + size)) for at in range(0, count, size)]


def group_total(held, rows, reverse):
    (total,) = call(
        functools.partial(total_kernel, rows, reverse), [shape((1, *held.shape[1:]))], [held], 4 * held.size, 12
    )
    return total.astype(jnp.float16)


def enter(held, total, rows, reverse):
    size = held.shape[0]
    count = lax.axis_size("ctx")
    others = []
    for hops in range(size, count, size):
        pairs = [(at, at + hops) for at in range(count - hops)]
        if reverse:
            pairs = [(b, a) for a, b in pairs]
        others.append(lax.ppermute(total, "ctx", pairs).astype(F32))
    (folded,) = call(
        functools.partial(fold_kernel, rows, reverse), [shape(held.shape)], [held, *others], 8 * held.size, 12
    )
    return folded


def group_of(count):
    for size in (16, 8, 4, 2):
        if count % size == 0:
            return size
    return 1


def from_behind(value, axis):
    count = lax.axis_size(axis)
    return lax.ppermute(value, axis, [(source, source + 1) for source in range(count - 1)])


def per_device(
    x_raw,
    bc_raw,
    gate_branch,
    dt_raw,
    conv_x,
    conv_x_bias,
    conv_bc,
    conv_bc_bias,
    dt_bias,
    a_log,
    d_skip,
    out_weight,
    grad_out,
):
    length, head_count = dt_raw.shape
    channels = x_raw.shape[1]
    width = grad_out.shape[1]
    head_size = channels // head_count
    heads_in = LANES // head_size
    count = lax.axis_size("ctx")
    plane = min(8, group_of(count))
    planes = groups_of(count, plane)
    rows = channels // plane
    size = group_of(count)
    share = channels // size
    groups = groups_of(count, size)
    gathered = lax.all_gather(grad_out, "ctx", axis_index_groups=groups, tiled=True)

    rim = from_behind(jnp.concatenate([x_raw[length - 16 :], bc_raw[length - 16 :]], axis=1), "ctx")
    skip = jnp.repeat(d_skip, head_size)[None, :]
    whole = (length, channels)
    square = (length, LANES)
    block = up8(rows) + 8
    stored = pltpu.VMEM((channels, LANES), F32)
    unit = 2 * length * channels * LANES

    act_x, slope_x, act_bc, slope_bc, step, ld, step_t, ld_t, raised, per_head, message = call(
        functools.partial(prepare_kernel, heads_in, head_size, rows),
        [shape(whole), shape(whole), shape(bc_raw.shape), shape(bc_raw.shape)]
        + [shape(square)] * 2
        + [shape((LANES, length))] * 2
        + [shape(square), shape((8, LANES))]
        + [shape((plane, block, LANES))],
        [
            x_raw,
            rim[:, :channels],
            bc_raw,
            rim[:, channels:],
            conv_x,
            conv_x_bias[None, :],
            conv_bc,
            conv_bc_bias[None, :],
            dt_raw,
            jnp.stack([dt_bias, a_log]),
        ],
        20 * unit,
        48,
        [
            pltpu.VMEM((length + 8, channels), F32),
            pltpu.VMEM((length + 8, bc_raw.shape[1]), F32),
            stored,
        ],
    )
    message, grad_out_then = lax.optimization_barrier((message, grad_out))
    held_state = exchange(message, planes).astype(F32)
    part = 640 if channels % 640 == 0 else channels
    grad_gated, grad_y = pl.pallas_call(
        gate_kernel,
        grid=(channels // part,),
        in_specs=[
            pl.BlockSpec((length, width), lambda i: (0, 0)),
            pl.BlockSpec((part, width), lambda i: (i, 0)),
            pl.BlockSpec((length, part), lambda i: (0, i)),
        ],
        out_specs=(pl.BlockSpec((length, part), lambda i: (0, i)), pl.BlockSpec((length, part), lambda i: (0, i))),
        out_shape=(shape(whole), shape(whole)),
        compiler_params=pltpu.CompilerParams(vmem_limit_bytes=24 * MIB),
        cost_estimate=pl.CostEstimate(
            flops=2 * length * channels * width, bytes_accessed=2 * channels * width, transcendentals=0
        ),
    )(grad_out_then, out_weight, gate_branch)
    (message,) = call(
        functools.partial(grad_kernel, heads_in, head_size, rows),
        [shape((plane, block, LANES))],
        [grad_y, act_bc, ld],
        10 * unit,
        12,
        [stored],
    )
    message, total = lax.optimization_barrier((message, group_total(held_state, rows, False)))
    held_carry = exchange(message, planes)
    y_within, grad_within, grad_bc_within = call(
        functools.partial(local_kernel, heads_in, head_size),
        [shape(whole), shape(whole), shape(act_bc.shape)],
        [act_x, grad_y, act_bc, step, ld, step_t, ld_t],
        40 * unit,
        16,
        [pltpu.VMEM(square, F32)],
    )
    folded, held_carry = lax.optimization_barrier((enter(held_state, total, rows, False), held_carry))
    held_carry = held_carry.astype(F32)
    state_message = exchange(folded, planes).astype(F32)
    gated, y_ahead = call(
        functools.partial(forward_kernel, heads_in, head_size, rows),
        [shape((size, share, length), BF16), shape(whole)],
        [state_message, act_x, gate_branch, act_bc, ld, y_within, skip],
        20 * unit,
        16,
        [stored],
    )
    entered = enter(held_carry, group_total(held_carry, rows, True), rows, True)
    gated, entered = lax.optimization_barrier((gated, entered))
    held = lax.all_to_all(gated, "ctx", 0, 0, axis_index_groups=groups, tiled=True)
    entered, held = lax.optimization_barrier((entered, held))
    carry_message = exchange(entered, planes).astype(F32)
    out_rows = width // count
    part = width
    for candidate in (640, 1280):
        if width % candidate == 0 and candidate % out_rows == 0:
            part = candidate
            break
    dims = (out_rows, share)
    if share > LANES:
        dims = (out_rows + 16 * (-(-(out_rows // 16) // (LANES // (share - LANES)))), LANES)
    partial = pl.pallas_call(
        functools.partial(product_kernel, out_rows),
        grid=(width // part,),
        in_specs=[
            pl.BlockSpec((size, share, length), lambda i: (0, 0, 0)),
        ]
        + [
            pl.BlockSpec((size * length // STREAMS, part), functools.partial(lambda k, i: (k, i), k))
            for k in range(STREAMS)
        ],
        out_specs=pl.BlockSpec((part // out_rows, *dims), lambda i: (i, 0, 0)),
        out_shape=shape((count, *dims), BF16),
        scratch_shapes=[pltpu.VMEM((share, size * length), BF16)],
        compiler_params=pltpu.CompilerParams(vmem_limit_bytes=48 * MIB),
        cost_estimate=pl.CostEstimate(
            flops=2 * size * length * share * width, bytes_accessed=2 * size * length * width, transcendentals=0
        ),
    )(held, *[gathered] * STREAMS)
    parts = lax.all_to_all(partial, "ctx", 0, 0, tiled=True)
    (weight_grad,) = call(
        functools.partial(assemble_kernel, out_rows, size, share),
        [shape((out_rows, channels))],
        [parts],
        2 * parts.size,
        12,
    )
    grad_x_conv, grad_bc, grad_dt_raw, grad_z = call(
        functools.partial(backward_kernel, heads_in, head_size, rows),
        [shape(whole, BF16), shape(act_bc.shape), shape(dt_raw.shape), shape(whole, BF16)],
        [
            carry_message,
            state_message,
            act_x,
            slope_x,
            grad_y,
            act_bc,
            step,
            ld,
            grad_within,
            grad_bc_within,
            y_ahead,
            grad_gated,
            gate_branch,
            skip,
            raised,
            per_head,
        ],
        40 * unit,
        48,
        [stored, stored, pltpu.VMEM((LANES, LANES), F32)],
    )
    grad_bc_conv = (lax.psum(grad_bc, "tp") * slope_bc).astype(BF16)
    return (grad_x_conv, grad_bc_conv, grad_z, grad_dt_raw, weight_grad)


def solution(mesh):
    placed = (
        P("ctx", "tp"),
        P("ctx", None),
        P("ctx", "tp"),
        P("ctx", "tp"),
        P(None, "tp"),
        P("tp"),
        P(),
        P(),
        P("tp"),
        P("tp"),
        P("tp"),
        P("tp", None),
        P("ctx", None),
    )
    return jax.shard_map(
        per_device,
        mesh=mesh,
        in_specs=placed,
        out_specs=(P("ctx", "tp"), P("ctx", None), P("ctx", "tp"), P("ctx", "tp"), P("ctx", "tp")),
        check_vma=False,
    )
```

```python
import functools

import jax
import jax.numpy as jnp
from jax import lax
from jax.experimental import pallas as pl
from jax.experimental.pallas import tpu as pltpu
from jax.sharding import PartitionSpec as P

KERNEL = 4
LANES = 128
F32 = jnp.float32
BF16 = jnp.bfloat16
NN = ((1,), (0,))
NT = ((1,), (1,))
HIGH = lax.Precision.HIGHEST
SMEM = pl.BlockSpec(memory_space=pltpu.SMEM)
VMEM = pl.BlockSpec(memory_space=pltpu.VMEM)
GRANT = 60 * 1024 * 1024
STREAMS = 4


def call(kernel, out_shapes, operands, flops, scratch=(), specs=None):
    extra = {} if specs is None else {"in_specs": specs}
    moved = sum(a.size * a.dtype.itemsize for a in (*operands, *out_shapes))
    return pl.pallas_call(
        kernel,
        out_shape=tuple(out_shapes),
        scratch_shapes=list(scratch),
        compiler_params=pltpu.CompilerParams(vmem_limit_bytes=GRANT),
        cost_estimate=pl.CostEstimate(flops=flops, bytes_accessed=moved, transcendentals=0),
        **extra,
    )(*operands)


def shape(dims, dtype=F32):
    return jax.ShapeDtypeStruct(dims, dtype)


def split(value):
    high = value.astype(BF16)
    return high, (value - high.astype(F32)).astype(BF16)


def dot(a, b, dims):
    return lax.dot_general(a, b, (dims, ((), ())), preferred_element_type=F32)


def dot3(a, b, dims=NN):
    return dot(a[0], b[0], dims) + (dot(a[0], b[1], dims) + dot(a[1], b[0], dims))


def sigmoid(value):
    return 1.0 / (1.0 + jnp.exp(-value))


def lane_ids(rows, cols=LANES):
    return lax.broadcasted_iota(jnp.int32, (rows, cols), 1)


def row_ids(rows, cols=LANES):
    return lax.broadcasted_iota(jnp.int32, (rows, cols), 0)


def spread(columns, block, heads, size):
    first = block * heads
    lanes = lane_ids(columns.shape[0])
    wide = jnp.broadcast_to(columns[:, first : first + 1], (columns.shape[0], LANES))
    for k in range(1, heads):
        wide = jnp.where(lanes >= k * size, columns[:, first + k : first + k + 1], wide)
    return wide


def head_of(block, heads, size):
    inner = row_ids(LANES)
    target = lane_ids(LANES)
    result = jnp.zeros((LANES, LANES), F32)
    for k in range(heads):
        here = (inner >= k * size) & (inner < (k + 1) * size) & (target == block * heads + k)
        result = jnp.where(here, 1.0, result)
    return result.astype(BF16)


def stacked(value, heads, size):
    lanes = lane_ids(value.shape[0])
    return jnp.concatenate(
        [jnp.where((lanes >= k * size) & (lanes < (k + 1) * size), value, 0.0) for k in range(heads)],
        axis=0,
    )


def up8(value):
    return -(-value // 8) * 8


def notes_of(rows):
    return -(-rows // LANES)


def exponent_of(block):
    top = jnp.max(jnp.max(jnp.abs(block), axis=0, keepdims=True), axis=1, keepdims=True)
    return jnp.floor(jnp.log2(jnp.maximum(jnp.broadcast_to(top, (1, LANES)), 1e-30)))


def write_block(message, at, first, block, decays, exponent):
    rows = block.shape[0]
    padded = up8(rows)
    message[at, first : first + rows, :] = block * jnp.exp2(13.0 - exponent)
    if padded > rows:
        message[at, first + rows : first + padded, :] = jnp.zeros((padded - rows, LANES), F32)
    highs = [d.astype(BF16).astype(F32) for d in decays]
    lows = [d - h for d, h in zip(decays, highs)]
    place = row_ids(8)
    notes = jnp.broadcast_to(exponent, (8, LANES))
    for k, line in enumerate(highs + lows):
        notes = jnp.where(place == k, line, notes)
    message[at, first + padded : first + padded + 8, :] = notes


def decay_tables(last_exp, heads, size, rows, count):
    shift = size.bit_length() - 1
    tables = []
    for d in range(count):
        lines = []
        for k in range(notes_of(rows)):
            first = rows * d + LANES * k
            owner = lax.shift_right_logical(lane_ids(1) + first, shift)
            table = jnp.zeros((1, LANES), F32)
            for h in range(first // size, min(heads, (first + LANES - 1) // size + 1)):
                table = jnp.where(owner == h, last_exp[:, h : h + 1], table)
            lines.append(table)
        tables.append(lines)
    return tables


def pack_blocks(source, message, last_exp, size, rows):
    count = message.shape[0]
    tables = decay_tables(last_exp, source.shape[0] // size, size, rows, count)
    for d in range(count):
        block = source[rows * d : rows * (d + 1), :]
        write_block(message, d, 0, block, tables[d], exponent_of(block))


def decay_lines(message, at, rows):
    padded, lines = up8(rows), notes_of(rows)
    return [
        message[at, padded + k : padded + k + 1, :] + message[at, padded + lines + k : padded + lines + k + 1, :]
        for k in range(lines)
    ]


def decay_columns(message, rows):
    padded, lines = up8(rows), notes_of(rows)
    turned = [
        jnp.transpose(message[:, padded + k, :] + message[:, padded + lines + k, :]) for k in range(lines)
    ]
    return jnp.concatenate(turned, axis=0)[0:rows]


def read_block(message, at, rows):
    padded = up8(rows)
    return message[at, 0:rows, :] * jnp.exp2(message[at, padded + 7 : padded + 8, :] - 13.0)


def unpack_blocks(message, target, rows, me=0):
    for d in range(message.shape[0]):
        target[rows * d : rows * (d + 1), :] = read_block(message, me ^ d, rows)


def total_kernel(rows, reverse, held_ref, out_ref):
    count = held_ref.shape[0]
    columns = decay_columns(held_ref, rows)
    state = None
    for s in range(count - 1, -1, -1) if reverse else range(count):
        block = read_block(held_ref, s, rows)
        state = block if state is None else columns[:, s : s + 1] * state + block
    decays = decay_lines(held_ref, 0, rows)
    for s in range(1, count):
        decays = [a * b for a, b in zip(decays, decay_lines(held_ref, s, rows))]
    write_block(out_ref, 0, 0, state, decays, exponent_of(state))


def fold_kernel(rows, reverse, me_ref, held_ref, *refs):
    others, out_ref = refs[:-1], refs[-1]
    count = held_ref.shape[0]
    columns = decay_columns(held_ref, rows)
    state = jnp.zeros((rows, LANES), F32)
    for other in reversed(others):
        state = decay_columns(other, rows) * state + read_block(other, 0, rows)
    for s in range(count - 1, -1, -1) if reverse else range(count):
        write_block(out_ref, me_ref[0] ^ s if reverse else s, 0, state, [], exponent_of(state))
        if s != (0 if reverse else count - 1):
            state = columns[:, s : s + 1] * state + read_block(held_ref, s, rows)


def prepare_kernel(
    heads_in, size, rows, x_ref, rim_ref, bc_ref, rim_bc_ref, wx_ref, bx_ref, wbc_ref, bbc_ref, dt_ref,
    per_ref, act_ref, slope_ref, abc_ref, sbc_ref, step_ref, ld_ref, stept_ref, ldt_ref, dtw_ref, perw_ref, msg_ref,
    xs_ref, bs_ref, st_ref,
):
    length = x_ref.shape[0]
    blocks = x_ref.shape[1] // LANES

    def convolved(raw, rim, padded, weight, bias, cols):
        padded[0:8, cols] = rim[:, cols].astype(F32)[8:16]
        padded[8 : 8 + length, cols] = raw[:, cols].astype(F32)
        pre = bias[:, cols] + weight[0:1, cols] * padded[5 : 5 + length, cols]
        for k in range(1, KERNEL):
            pre = pre + weight[k : k + 1, cols] * padded[5 + k : 5 + k + length, cols]
        gate = sigmoid(pre)
        return pre * gate, gate * (1.0 + pre * (1.0 - gate))

    for j in range(bc_ref.shape[1] // LANES):
        cols = slice(j * LANES, (j + 1) * LANES)
        value, slope = convolved(bc_ref, rim_bc_ref, bs_ref, wbc_ref, bbc_ref, cols)
        abc_ref[:, cols] = value
        sbc_ref[:, cols] = slope
    b_rows = split(abc_ref[:, 0:LANES])
    heads = dt_ref.shape[1]
    dtw_ref[...] = jnp.zeros_like(dtw_ref)
    dtw_ref[:, 0:heads] = dt_ref[...]
    perw_ref[...] = jnp.zeros_like(perw_ref)
    perw_ref[0:2, 0:heads] = per_ref[...]
    raised = dtw_ref[...] + perw_ref[0:1, :]
    dtw_ref[...] = raised
    step = jnp.maximum(raised, 0.0) + jnp.log1p(jnp.exp(-jnp.abs(raised)))
    lower = jnp.where(row_ids(length) >= lane_ids(length), 1.0, 0.0)
    ld = lax.dot_general(
        lower, step * -jnp.exp(perw_ref[1:2, :]), (NN, ((), ())), precision=HIGH, preferred_element_type=F32
    )
    step_ref[...] = step
    ld_ref[...] = ld
    stept_ref[...] = step.T
    ldt_ref[...] = ld.T
    last = ld[length - 1 : length]
    weight = jnp.exp(last - ld) * step
    for j in range(blocks):
        cols = slice(j * LANES, (j + 1) * LANES)
        value, slope = convolved(x_ref, rim_ref, xs_ref, wx_ref, bx_ref, cols)
        act_ref[:, cols] = value
        slope_ref[:, cols] = slope
        scaled = value * spread(weight, j, heads_in, size)
        st_ref[cols, :] = dot3(split(scaled.T), b_rows)
    pack_blocks(st_ref, msg_ref, jnp.exp(last), size, rows)


def grad_kernel(heads_in, size, rows, gy_ref, abc_ref, ld_ref, msg_ref, st_ref):
    length = gy_ref.shape[0]
    c_rows = split(abc_ref[:, LANES : 2 * LANES])
    grown = jnp.exp(ld_ref[...])
    for j in range(gy_ref.shape[1] // LANES):
        cols = slice(j * LANES, (j + 1) * LANES)
        scaled = gy_ref[:, cols] * spread(grown, j, heads_in, size)
        st_ref[cols, :] = dot3(split(scaled.T), c_rows)
    pack_blocks(st_ref, msg_ref, grown[length - 1 : length], size, rows)


def gate_kernel(go_ref, *refs):
    w_refs, (gate_ref, gg_ref, gy_ref) = refs[:-3], refs[-3:]
    depth = w_refs[0].shape[1]
    grad = dot(w_refs[0][...], go_ref[:, 0:depth], NT)
    for k in range(1, len(w_refs)):
        grad = grad + dot(w_refs[k][...], go_ref[:, k * depth : (k + 1) * depth], NT)
    grad = grad.T
    gate = gate_ref[...].astype(F32)
    gg_ref[...] = grad
    gy_ref[...] = grad * (gate * sigmoid(gate))


def local_kernel(
    heads_in, size, act_ref, gy_ref, abc_ref, step_ref, ld_ref, stept_ref, ldt_ref, yw_ref, gw_ref, gbc_ref, sh_ref
):
    length = act_ref.shape[0]
    b_rows = split(abc_ref[:, 0:LANES])
    c_rows = split(abc_ref[:, LANES : 2 * LANES])
    scores = dot3(c_rows, b_rows, NT)
    turned = dot3(b_rows, c_rows, NT)
    causal = row_ids(length) >= lane_ids(length)
    causal_t = row_ids(length) <= lane_ids(length)
    sh_ref[...] = jnp.zeros_like(sh_ref)
    for j in range(act_ref.shape[1] // LANES):
        cols = slice(j * LANES, (j + 1) * LANES)
        mixes, mixes_t, steps = [], [], []
        for h in range(j * heads_in, (j + 1) * heads_in):
            column, row = ld_ref[:, h : h + 1], ldt_ref[h : h + 1, :]
            decays = jnp.exp(jnp.where(causal, column - row, -1e30))
            stepped = decays * stept_ref[h : h + 1, :]
            decays_t = jnp.exp(jnp.where(causal_t, row - column, -1e30))
            steps.append(stepped)
            mixes.append(stepped * scores)
            mixes_t.append(decays_t * turned * step_ref[:, h : h + 1])
        inputs = act_ref[:, cols]
        grad_y = gy_ref[:, cols]
        inputs_s = stacked(inputs, heads_in, size)
        grads_s = split(stacked(grad_y, heads_in, size))
        yw_ref[:, cols] = dot3(split(jnp.concatenate(mixes, axis=1)), split(inputs_s))
        gw_ref[:, cols] = dot3(split(jnp.concatenate(mixes_t, axis=1)), grads_s)
        products = dot3(grads_s, split(inputs), NT)
        total = sh_ref[...]
        for k in range(heads_in):
            total = total + steps[k] * products[k * length : (k + 1) * length]
        sh_ref[...] = total
    shared = sh_ref[...]
    gbc_ref[:, 0:LANES] = dot3(split(shared.T), c_rows)
    gbc_ref[:, LANES : 2 * LANES] = dot3(split(shared), b_rows)


def place_of(channel, share, size):
    if share > LANES:
        if channel < LANES * size:
            return channel // LANES, channel % LANES
        rest = share - LANES
        return (channel - LANES * size) // rest, LANES + (channel - LANES * size) % rest
    return channel // share, channel % share


def forward_kernel(
    heads_in, size, rows, msg_ref, act_ref, gate_ref, abc_ref, ld_ref, yw_ref, skip_ref, gt_ref, ys_ref, st_ref
):
    share = gt_ref.shape[1]
    unpack_blocks(msg_ref, st_ref, rows)
    c_rows = split(abc_ref[:, LANES : 2 * LANES])
    grown = jnp.exp(ld_ref[...])
    for j in range(act_ref.shape[1] // LANES):
        cols = slice(j * LANES, (j + 1) * LANES)
        carried = dot3(c_rows, split(st_ref[cols, :]), NT)
        within = yw_ref[:, cols] + spread(grown, j, heads_in, size) * carried
        ys_ref[:, cols] = within
        output = within + skip_ref[:, cols] * act_ref[:, cols]
        gate = gate_ref[:, cols].astype(F32)
        turned = (output * (gate * sigmoid(gate))).T.astype(BF16)
        for k in range(0, LANES, 16):
            to, at = place_of(j * LANES + k, share, gt_ref.shape[0])
            gt_ref[to, at : at + 16, :] = turned[k : k + 16]


def backward_kernel(
    heads_in, size, rows, me_ref, msg_ref, msgf_ref, act_ref, slope_ref, gy_ref, abc_ref, step_ref, ld_ref, gw_ref,
    gbcl_ref, ys_ref, gg_ref, gate_ref, skip_ref, dtw_ref, perw_ref, gx_ref, gbc_ref, gdt_ref, gz_ref,
    ca_ref, st_ref, cs_ref,
):
    length = act_ref.shape[0]
    unpack_blocks(msg_ref, ca_ref, rows, me_ref[0])
    unpack_blocks(msgf_ref, st_ref, rows)
    b_rows = split(abc_ref[:, 0:LANES])
    ld = ld_ref[...]
    step = step_ref[...]
    last = ld[length - 1 : length]
    grown = jnp.exp(ld)
    weight = jnp.exp(last - ld) * step
    sums = jnp.zeros((length, LANES), F32)
    sums_y = jnp.zeros((length, LANES), F32)
    leaving = jnp.zeros((8, LANES), F32)
    grad_b = gbcl_ref[:, 0:LANES]
    grad_c = gbcl_ref[:, LANES : 2 * LANES]
    cs_ref[...] = jnp.zeros_like(cs_ref)
    for j in range(act_ref.shape[1] // LANES):
        cols = slice(j * LANES, (j + 1) * LANES)
        inputs = act_ref[:, cols]
        grad_y = gy_ref[:, cols]
        carry = ca_ref[cols, :]
        state = st_ref[cols, :]
        carry_s = split(carry)
        wide = spread(weight, j, heads_in, size)
        gone = wide * dot3(b_rows, carry_s, NT)
        grad_in = gw_ref[:, cols] + gone
        gx_ref[:, cols] = ((skip_ref[:, cols] * grad_y + grad_in) * slope_ref[:, cols]).astype(BF16)
        onehot = head_of(j, heads_in, size)
        within = ys_ref[:, cols]
        gate = gate_ref[:, cols].astype(F32)
        opened = sigmoid(gate)
        output = within + skip_ref[:, cols] * inputs
        gz_ref[:, cols] = (gg_ref[:, cols] * output * (opened * (1.0 + gate * (1.0 - opened)))).astype(BF16)
        high, low = split(grad_y * within)
        sums_y = sums_y + (dot(high, onehot, NN) + dot(low, onehot, NN))
        high, low = split(inputs * grad_in)
        sums = sums + (dot(high, onehot, NN) + dot(low, onehot, NN))
        folded = jnp.sum((inputs * gone).reshape(length // 8, 8, LANES), axis=0)
        high, low = split(folded)
        leaving = leaving + (dot(high, onehot, NN) + dot(low, onehot, NN))
        product = carry * state
        for k in range(heads_in):
            h = j * heads_in + k
            cs_ref[h : h + 1, :] = jnp.sum(product[k * size : (k + 1) * size], axis=0, keepdims=True)
        grad_b = grad_b + dot3(split(wide * inputs), carry_s)
        grad_c = grad_c + dot3(split(spread(grown, j, heads_in, size) * grad_y), split(state))
    gbc_ref[:, 0:LANES] = grad_b
    gbc_ref[:, LANES : 2 * LANES] = grad_c
    both = lax.dot_general(
        jnp.ones((8, LANES), F32), cs_ref[...], (NT, ((), ())), precision=HIGH, preferred_element_type=F32
    )
    constant = jnp.sum(leaving, axis=0, keepdims=True) + jnp.exp(last) * both[0:1]
    upper = jnp.where(row_ids(length) <= lane_ids(length), 1.0, 0.0)
    grad_rate = constant + lax.dot_general(
        upper, sums_y - sums, (NN, ((), ())), precision=HIGH, preferred_element_type=F32
    )
    grad_step = sums / step - jnp.exp(perw_ref[1:2, :]) * grad_rate
    gdt_ref[...] = (grad_step * sigmoid(dtw_ref[...]))[:, 0 : gdt_ref.shape[1]]


def product_kernel(rows, held_ref, *refs):
    go_refs, out_ref, lhs_ref = refs[:-2], refs[-2], refs[-1]
    size, share, length = held_ref.shape

    @pl.when(pl.program_id(0) == 0)
    def _():
        for s in range(size):
            lhs_ref[:, s * length : (s + 1) * length] = held_ref[s]

    depth = go_refs[0].shape[0]
    result = dot(lhs_ref[:, 0:depth], go_refs[0][...], NN)
    for k in range(1, len(go_refs)):
        result = result + dot(lhs_ref[:, k * depth : (k + 1) * depth], go_refs[k][...], NN)
    result = result.T
    for d in range(out_ref.shape[0]):
        block = result[rows * d : rows * (d + 1)]
        if share > LANES:
            rest = share - LANES
            across = LANES // rest
            out_ref[d, 0:rows, :] = block[:, 0:LANES].astype(BF16)
            for k in range(0, rows // 16, across):
                pieces = [block[16 * m : 16 * m + 16, LANES:] for m in range(k, min(k + across, rows // 16))]
                if len(pieces) < across:
                    pieces.append(jnp.zeros((16, LANES - rest * len(pieces)), F32))
                at = rows + 16 * (k // across)
                out_ref[d, at : at + 16, :] = jnp.concatenate(pieces, axis=1).astype(BF16)
        else:
            out_ref[d] = block.astype(BF16)


def assemble_kernel(rows, size, share, parts_ref, out_ref):
    count = parts_ref.shape[0]

    def total(c, first, last):
        found = parts_ref[c, first:last, :].astype(F32)
        for s in range(c + size, count, size):
            found = found + parts_ref[s, first:last, :].astype(F32)
        return found

    if share > LANES:
        rest = share - LANES
        across = LANES // rest
        for c in range(size):
            out_ref[:, c * LANES : (c + 1) * LANES] = total(c, 0, rows)
            at = size * LANES + rest * c
            for k in range(0, rows // 16, across):
                extra = total(c, rows + 16 * (k // across), rows + 16 * (k // across) + 16)
                for m in range(k, min(k + across, rows // 16)):
                    lanes = slice(rest * (m - k), rest * (m - k + 1))
                    out_ref[16 * m : 16 * m + 16, at : at + rest] = extra[:, lanes]
    else:
        for c in range(size):
            out_ref[:, c * share : (c + 1) * share] = total(c, 0, rows)


def exchange(message, groups=None):
    half = message.astype(jnp.float16)
    return lax.all_to_all(half, "ctx", 0, 0, axis_index_groups=groups, tiled=True)


def swapped(message):
    half = message.astype(jnp.float16)
    count = lax.axis_size("ctx")
    slots = [half[0:1]]
    for m in range(1, message.shape[0]):
        slots.append(lax.ppermute(half[m : m + 1], "ctx", [(at, at ^ m) for at in range(count)]))
    return jnp.concatenate(slots).astype(F32)


def groups_of(count, size):
    return [list(range(at, at + size)) for at in range(0, count, size)]


def group_total(held, rows, reverse):
    (total,) = call(
        functools.partial(total_kernel, rows, reverse), [shape((1, *held.shape[1:]))], [held], 4 * held.size
    )
    return total.astype(jnp.float16)


def enter(me, held, total, rows, reverse):
    size = held.shape[0]
    count = lax.axis_size("ctx")
    others = []
    for hops in range(size, count, size):
        pairs = [(at, at + hops) for at in range(count - hops)]
        if reverse:
            pairs = [(b, a) for a, b in pairs]
        others.append(lax.ppermute(total, "ctx", pairs).astype(F32))
    (folded,) = call(
        functools.partial(fold_kernel, rows, reverse),
        [shape(held.shape)],
        [me, held, *others],
        8 * held.size,
        specs=[SMEM] + [VMEM] * (1 + len(others)),
    )
    return folded


def group_of(count):
    for size in (16, 8, 4, 2):
        if count % size == 0:
            return size
    return 1


def from_behind(value, axis):
    count = lax.axis_size(axis)
    return lax.ppermute(value, axis, [(source, source + 1) for source in range(count - 1)])


def per_device(
    x_raw,
    bc_raw,
    gate_branch,
    dt_raw,
    conv_x,
    conv_x_bias,
    conv_bc,
    conv_bc_bias,
    dt_bias,
    a_log,
    d_skip,
    out_weight,
    grad_out,
):
    length, head_count = dt_raw.shape
    channels = x_raw.shape[1]
    width = grad_out.shape[1]
    head_size = channels // head_count
    heads_in = LANES // head_size
    count = lax.axis_size("ctx")
    plane = min(8, group_of(count))
    planes = groups_of(count, plane)
    rows = channels // plane
    size = group_of(count)
    share = channels // size
    groups = groups_of(count, size)
    gathered = lax.all_gather(grad_out, "ctx", axis_index_groups=groups, tiled=True)

    rim = from_behind(jnp.concatenate([x_raw[length - 16 :], bc_raw[length - 16 :]], axis=1), "ctx")
    skip = jnp.repeat(d_skip, head_size)[None, :]
    whole = (length, channels)
    square = (length, LANES)
    block = up8(rows) + 8
    stored = pltpu.VMEM((channels, LANES), F32)
    unit = 2 * length * channels * LANES
    me = (lax.axis_index("ctx") % plane).astype(jnp.int32).reshape(1)

    act_x, slope_x, act_bc, slope_bc, step, ld, step_t, ld_t, raised, per_head, message = call(
        functools.partial(prepare_kernel, heads_in, head_size, rows),
        [shape(whole), shape(whole), shape(bc_raw.shape), shape(bc_raw.shape)]
        + [shape(square)] * 2
        + [shape((LANES, length))] * 2
        + [shape(square), shape((8, LANES))]
        + [shape((plane, block, LANES))],
        [
            x_raw,
            rim[:, :channels],
            bc_raw,
            rim[:, channels:],
            conv_x,
            conv_x_bias[None, :],
            conv_bc,
            conv_bc_bias[None, :],
            dt_raw,
            jnp.stack([dt_bias, a_log]),
        ],
        20 * unit,
        [
            pltpu.VMEM((length + 8, channels), F32),
            pltpu.VMEM((length + 8, bc_raw.shape[1]), F32),
            stored,
        ],
    )
    message, grad_out_then = lax.optimization_barrier((message, grad_out))
    held_state = exchange(message, planes).astype(F32)
    part = 640 if channels % 640 == 0 else channels
    grad_gated, grad_y = pl.pallas_call(
        gate_kernel,
        grid=(channels // part,),
        in_specs=[
            pl.BlockSpec((length, width), lambda i: (0, 0)),
        ]
        + [
            pl.BlockSpec((part, width // STREAMS), functools.partial(lambda k, i: (i, k), k))
            for k in range(STREAMS)
        ]
        + [pl.BlockSpec((length, part), lambda i: (0, i))],
        out_specs=(pl.BlockSpec((length, part), lambda i: (0, i)), pl.BlockSpec((length, part), lambda i: (0, i))),
        out_shape=(shape(whole), shape(whole)),
        compiler_params=pltpu.CompilerParams(vmem_limit_bytes=GRANT),
        cost_estimate=pl.CostEstimate(
            flops=2 * length * channels * width, bytes_accessed=2 * channels * width, transcendentals=0
        ),
    )(grad_out_then, *[out_weight] * STREAMS, gate_branch)
    (message,) = call(
        functools.partial(grad_kernel, heads_in, head_size, rows),
        [shape((plane, block, LANES))],
        [grad_y, act_bc, ld],
        10 * unit,
        [stored],
    )
    y_within, grad_within, grad_bc_within = call(
        functools.partial(local_kernel, heads_in, head_size),
        [shape(whole), shape(whole), shape(act_bc.shape)],
        [act_x, grad_y, act_bc, step, ld, step_t, ld_t],
        40 * unit,
        [pltpu.VMEM(square, F32)],
    )
    message, total, y_within = lax.optimization_barrier(
        (message, group_total(held_state, rows, False), y_within)
    )
    held_carry = exchange(message, planes)
    folded, held_carry = lax.optimization_barrier((enter(me, held_state, total, rows, False), held_carry))
    held_carry = held_carry.astype(F32)
    state_message = exchange(folded, planes).astype(F32)
    gated, y_ahead = call(
        functools.partial(forward_kernel, heads_in, head_size, rows),
        [shape((size, share, length), BF16), shape(whole)],
        [state_message, act_x, gate_branch, act_bc, ld, y_within, skip],
        20 * unit,
        [stored],
    )
    entered = enter(me, held_carry, group_total(held_carry, rows, True), rows, True)
    gated, entered = lax.optimization_barrier((gated, entered))
    held = lax.all_to_all(gated, "ctx", 0, 0, axis_index_groups=groups, tiled=True)
    carry_message = swapped(entered)
    out_rows = width // count
    part = width
    for candidate in (640, 1280):
        if width % candidate == 0 and candidate % out_rows == 0:
            part = candidate
            break
    dims = (out_rows, share)
    if share > LANES:
        dims = (out_rows + 16 * (-(-(out_rows // 16) // (LANES // (share - LANES)))), LANES)
    partial = pl.pallas_call(
        functools.partial(product_kernel, out_rows),
        grid=(width // part,),
        in_specs=[
            pl.BlockSpec((size, share, length), lambda i: (0, 0, 0)),
        ]
        + [
            pl.BlockSpec((size * length // STREAMS, part), functools.partial(lambda k, i: (k, i), k))
            for k in range(STREAMS)
        ],
        out_specs=pl.BlockSpec((part // out_rows, *dims), lambda i: (i, 0, 0)),
        out_shape=shape((count, *dims), BF16),
        scratch_shapes=[pltpu.VMEM((share, size * length), BF16)],
        compiler_params=pltpu.CompilerParams(vmem_limit_bytes=GRANT),
        cost_estimate=pl.CostEstimate(
            flops=2 * size * length * share * width, bytes_accessed=2 * size * length * width, transcendentals=0
        ),
    )(held, *[gathered] * STREAMS)
    parts = lax.all_to_all(partial, "ctx", 0, 0, tiled=True)
    (weight_grad,) = call(
        functools.partial(assemble_kernel, out_rows, size, share),
        [shape((out_rows, channels))],
        [parts],
        2 * parts.size,
    )
    grad_x_conv, grad_bc, grad_dt_raw, grad_z = call(
        functools.partial(backward_kernel, heads_in, head_size, rows),
        [shape(whole, BF16), shape(act_bc.shape), shape(dt_raw.shape), shape(whole, BF16)],
        [
            me,
            carry_message,
            state_message,
            act_x,
            slope_x,
            grad_y,
            act_bc,
            step,
            ld,
            grad_within,
            grad_bc_within,
            y_ahead,
            grad_gated,
            gate_branch,
            skip,
            raised,
            per_head,
        ],
        40 * unit,
        [stored, stored, pltpu.VMEM((LANES, LANES), F32)],
        [SMEM] + [VMEM] * 16,
    )
    grad_bc_conv = (lax.psum(grad_bc, "tp") * slope_bc).astype(BF16)
    return (grad_x_conv, grad_bc_conv, grad_z, grad_dt_raw, weight_grad)


def solution(mesh):
    placed = (
        P("ctx", "tp"),
        P("ctx", None),
        P("ctx", "tp"),
        P("ctx", "tp"),
        P(None, "tp"),
        P("tp"),
        P(),
        P(),
        P("tp"),
        P("tp"),
        P("tp"),
        P("tp", None),
        P("ctx", None),
    )
    return jax.shard_map(
        per_device,
        mesh=mesh,
        in_specs=placed,
        out_specs=(P("ctx", "tp"), P("ctx", None), P("ctx", "tp"), P("ctx", "tp"), P("ctx", "tp")),
        check_vma=False,
    )
```

```python
import functools

import jax
import jax.numpy as jnp
from jax import lax
from jax.experimental import pallas as pl
from jax.experimental.pallas import tpu as pltpu
from jax.sharding import PartitionSpec as P

KERNEL = 4
LANES = 128
F32 = jnp.float32
BF16 = jnp.bfloat16
NN = ((1,), (0,))
NT = ((1,), (1,))
HIGH = lax.Precision.HIGHEST
SMEM = pl.BlockSpec(memory_space=pltpu.SMEM)
VMEM = pl.BlockSpec(memory_space=pltpu.VMEM)
MIB = 1024 * 1024
STREAMS = 4


def call(kernel, out_shapes, operands, flops, vmem, scratch=(), specs=None):
    extra = {} if specs is None else {"in_specs": specs}
    moved = sum(a.size * a.dtype.itemsize for a in (*operands, *out_shapes))
    return pl.pallas_call(
        kernel,
        out_shape=tuple(out_shapes),
        scratch_shapes=list(scratch),
        compiler_params=pltpu.CompilerParams(vmem_limit_bytes=vmem * MIB),
        cost_estimate=pl.CostEstimate(flops=flops, bytes_accessed=moved, transcendentals=0),
        **extra,
    )(*operands)


def shape(dims, dtype=F32):
    return jax.ShapeDtypeStruct(dims, dtype)


def split(value):
    high = value.astype(BF16)
    return high, (value - high.astype(F32)).astype(BF16)


def dot(a, b, dims):
    return lax.dot_general(a, b, (dims, ((), ())), preferred_element_type=F32)


def dot3(a, b, dims=NN):
    return dot(a[0], b[0], dims) + (dot(a[0], b[1], dims) + dot(a[1], b[0], dims))


def sigmoid(value):
    return 1.0 / (1.0 + jnp.exp(-value))


def lane_ids(rows, cols=LANES):
    return lax.broadcasted_iota(jnp.int32, (rows, cols), 1)


def row_ids(rows, cols=LANES):
    return lax.broadcasted_iota(jnp.int32, (rows, cols), 0)


def spread(columns, block, heads, size):
    first = block * heads
    lanes = lane_ids(columns.shape[0])
    wide = jnp.broadcast_to(columns[:, first : first + 1], (columns.shape[0], LANES))
    for k in range(1, heads):
        wide = jnp.where(lanes >= k * size, columns[:, first + k : first + k + 1], wide)
    return wide


def head_of(block, heads, size):
    inner = row_ids(LANES)
    target = lane_ids(LANES)
    result = jnp.zeros((LANES, LANES), F32)
    for k in range(heads):
        here = (inner >= k * size) & (inner < (k + 1) * size) & (target == block * heads + k)
        result = jnp.where(here, 1.0, result)
    return result.astype(BF16)


def stacked(value, heads, size):
    lanes = lane_ids(value.shape[0])
    return jnp.concatenate(
        [jnp.where((lanes >= k * size) & (lanes < (k + 1) * size), value, 0.0) for k in range(heads)],
        axis=0,
    )


def up8(value):
    return -(-value // 8) * 8


def notes_of(rows):
    return -(-rows // LANES)


def exponent_of(block):
    top = jnp.max(jnp.max(jnp.abs(block), axis=0, keepdims=True), axis=1, keepdims=True)
    return jnp.floor(jnp.log2(jnp.maximum(jnp.broadcast_to(top, (1, LANES)), 1e-30)))


def write_block(message, at, first, block, decays, exponent):
    rows = block.shape[0]
    padded = up8(rows)
    message[at, first : first + rows, :] = block * jnp.exp2(13.0 - exponent)
    if padded > rows:
        message[at, first + rows : first + padded, :] = jnp.zeros((padded - rows, LANES), F32)
    highs = [d.astype(BF16).astype(F32) for d in decays]
    lows = [d - h for d, h in zip(decays, highs)]
    place = row_ids(8)
    notes = jnp.broadcast_to(exponent, (8, LANES))
    for k, line in enumerate(highs + lows):
        notes = jnp.where(place == k, line, notes)
    message[at, first + padded : first + padded + 8, :] = notes


def decay_tables(last_exp, heads, size, rows, count):
    shift = size.bit_length() - 1
    tables = []
    for d in range(count):
        lines = []
        for k in range(notes_of(rows)):
            first = rows * d + LANES * k
            owner = lax.shift_right_logical(lane_ids(1) + first, shift)
            table = jnp.zeros((1, LANES), F32)
            for h in range(first // size, min(heads, (first + LANES - 1) // size + 1)):
                table = jnp.where(owner == h, last_exp[:, h : h + 1], table)
            lines.append(table)
        tables.append(lines)
    return tables


def pack_blocks(source, message, last_exp, size, rows):
    count = message.shape[0]
    tables = decay_tables(last_exp, source.shape[0] // size, size, rows, count)
    for d in range(count):
        block = source[rows * d : rows * (d + 1), :]
        write_block(message, d, 0, block, tables[d], exponent_of(block))


def decay_lines(message, at, rows):
    padded, lines = up8(rows), notes_of(rows)
    return [
        message[at, padded + k : padded + k + 1, :] + message[at, padded + lines + k : padded + lines + k + 1, :]
        for k in range(lines)
    ]


def decay_columns(message, rows):
    padded, lines = up8(rows), notes_of(rows)
    turned = [
        jnp.transpose(message[:, padded + k, :] + message[:, padded + lines + k, :]) for k in range(lines)
    ]
    return jnp.concatenate(turned, axis=0)[0:rows]


def read_block(message, at, rows):
    padded = up8(rows)
    return message[at, 0:rows, :] * jnp.exp2(message[at, padded + 7 : padded + 8, :] - 13.0)


def unpack_blocks(message, target, rows, me=0):
    for d in range(message.shape[0]):
        target[rows * d : rows * (d + 1), :] = read_block(message, me ^ d, rows)


def total_kernel(rows, reverse, held_ref, out_ref):
    count = held_ref.shape[0]
    columns = decay_columns(held_ref, rows)
    state = None
    for s in range(count - 1, -1, -1) if reverse else range(count):
        block = read_block(held_ref, s, rows)
        state = block if state is None else columns[:, s : s + 1] * state + block
    decays = decay_lines(held_ref, 0, rows)
    for s in range(1, count):
        decays = [a * b for a, b in zip(decays, decay_lines(held_ref, s, rows))]
    write_block(out_ref, 0, 0, state, decays, exponent_of(state))


def fold_kernel(rows, reverse, me_ref, held_ref, *refs):
    others, out_ref = refs[:-1], refs[-1]
    count = held_ref.shape[0]
    columns = decay_columns(held_ref, rows)
    state = jnp.zeros((rows, LANES), F32)
    for other in reversed(others):
        state = decay_columns(other, rows) * state + read_block(other, 0, rows)
    for s in range(count - 1, -1, -1) if reverse else range(count):
        write_block(out_ref, me_ref[0] ^ s if reverse else s, 0, state, [], exponent_of(state))
        if s != (0 if reverse else count - 1):
            state = columns[:, s : s + 1] * state + read_block(held_ref, s, rows)


def prepare_kernel(
    heads_in, size, rows, x_ref, bc_ref, wx_ref, wbc_ref, bbc_ref, rim_ref, rim_bc_ref, bx_ref, dt_ref,
    per_ref, act_ref, slope_ref, abc_ref, sbc_ref, step_ref, ld_ref, stept_ref, ldt_ref, dtw_ref, perw_ref, msg_ref,
    xs_ref, bs_ref, st_ref,
):
    length = x_ref.shape[0]
    blocks = x_ref.shape[1] // LANES

    def convolved(raw, rim, padded, weight, bias, cols):
        padded[0:8, cols] = rim[:, cols].astype(F32)[8:16]
        padded[8 : 8 + length, cols] = raw[:, cols].astype(F32)
        pre = bias[:, cols] + weight[0:1, cols] * padded[5 : 5 + length, cols]
        for k in range(1, KERNEL):
            pre = pre + weight[k : k + 1, cols] * padded[5 + k : 5 + k + length, cols]
        gate = sigmoid(pre)
        return pre * gate, gate * (1.0 + pre * (1.0 - gate))

    for j in range(bc_ref.shape[1] // LANES):
        cols = slice(j * LANES, (j + 1) * LANES)
        value, slope = convolved(bc_ref, rim_bc_ref, bs_ref, wbc_ref, bbc_ref, cols)
        abc_ref[:, cols] = value
        sbc_ref[:, cols] = slope
    b_rows = split(abc_ref[:, 0:LANES])
    heads = dt_ref.shape[1]
    dtw_ref[...] = jnp.zeros_like(dtw_ref)
    dtw_ref[:, 0:heads] = dt_ref[...]
    perw_ref[...] = jnp.zeros_like(perw_ref)
    perw_ref[0:2, 0:heads] = per_ref[...]
    raised = dtw_ref[...] + perw_ref[0:1, :]
    dtw_ref[...] = raised
    step = jnp.maximum(raised, 0.0) + jnp.log1p(jnp.exp(-jnp.abs(raised)))
    lower = jnp.where(row_ids(length) >= lane_ids(length), 1.0, 0.0)
    ld = lax.dot_general(
        lower, step * -jnp.exp(perw_ref[1:2, :]), (NN, ((), ())), precision=HIGH, preferred_element_type=F32
    )
    step_ref[...] = step
    ld_ref[...] = ld
    stept_ref[...] = step.T
    ldt_ref[...] = ld.T
    last = ld[length - 1 : length]
    weight = jnp.exp(last - ld) * step
    for j in range(blocks):
        cols = slice(j * LANES, (j + 1) * LANES)
        value, slope = convolved(x_ref, rim_ref, xs_ref, wx_ref, bx_ref, cols)
        act_ref[:, cols] = value
        slope_ref[:, cols] = slope
        scaled = value * spread(weight, j, heads_in, size)
        st_ref[cols, :] = dot3(split(scaled.T), b_rows)
    pack_blocks(st_ref, msg_ref, jnp.exp(last), size, rows)


def grad_kernel(heads_in, size, rows, gy_ref, abc_ref, ld_ref, msg_ref, st_ref):
    length = gy_ref.shape[0]
    c_rows = split(abc_ref[:, LANES : 2 * LANES])
    grown = jnp.exp(ld_ref[...])
    for j in range(gy_ref.shape[1] // LANES):
        cols = slice(j * LANES, (j + 1) * LANES)
        scaled = gy_ref[:, cols] * spread(grown, j, heads_in, size)
        st_ref[cols, :] = dot3(split(scaled.T), c_rows)
    pack_blocks(st_ref, msg_ref, grown[length - 1 : length], size, rows)


def gate_kernel(go_ref, *refs):
    w_refs, (gate_ref, gg_ref, gy_ref) = refs[:-3], refs[-3:]
    depth = w_refs[0].shape[1]
    grad = dot(w_refs[0][...], go_ref[:, 0:depth], NT)
    for k in range(1, len(w_refs)):
        grad = grad + dot(w_refs[k][...], go_ref[:, k * depth : (k + 1) * depth], NT)
    grad = grad.T
    gate = gate_ref[...].astype(F32)
    gg_ref[...] = grad
    gy_ref[...] = grad * (gate * sigmoid(gate))


def local_kernel(
    heads_in, size, act_ref, gy_ref, abc_ref, step_ref, ld_ref, stept_ref, ldt_ref, yw_ref, gw_ref, gbc_ref, sh_ref
):
    length = act_ref.shape[0]
    b_rows = split(abc_ref[:, 0:LANES])
    c_rows = split(abc_ref[:, LANES : 2 * LANES])
    scores = dot3(c_rows, b_rows, NT)
    turned = dot3(b_rows, c_rows, NT)
    causal = row_ids(length) >= lane_ids(length)
    causal_t = row_ids(length) <= lane_ids(length)
    sh_ref[...] = jnp.zeros_like(sh_ref)
    for j in range(act_ref.shape[1] // LANES):
        cols = slice(j * LANES, (j + 1) * LANES)
        mixes, mixes_t, steps = [], [], []
        for h in range(j * heads_in, (j + 1) * heads_in):
            column, row = ld_ref[:, h : h + 1], ldt_ref[h : h + 1, :]
            decays = jnp.exp(jnp.where(causal, column - row, -1e30))
            stepped = decays * stept_ref[h : h + 1, :]
            decays_t = jnp.exp(jnp.where(causal_t, row - column, -1e30))
            steps.append(stepped)
            mixes.append(stepped * scores)
            mixes_t.append(decays_t * turned * step_ref[:, h : h + 1])
        inputs = act_ref[:, cols]
        grad_y = gy_ref[:, cols]
        inputs_s = stacked(inputs, heads_in, size)
        grads_s = split(stacked(grad_y, heads_in, size))
        yw_ref[:, cols] = dot3(split(jnp.concatenate(mixes, axis=1)), split(inputs_s))
        gw_ref[:, cols] = dot3(split(jnp.concatenate(mixes_t, axis=1)), grads_s)
        products = dot3(grads_s, split(inputs), NT)
        total = sh_ref[...]
        for k in range(heads_in):
            total = total + steps[k] * products[k * length : (k + 1) * length]
        sh_ref[...] = total
    shared = sh_ref[...]
    gbc_ref[:, 0:LANES] = dot3(split(shared.T), c_rows)
    gbc_ref[:, LANES : 2 * LANES] = dot3(split(shared), b_rows)


def place_of(channel, share, size):
    if share > LANES:
        if channel < LANES * size:
            return channel // LANES, channel % LANES
        rest = share - LANES
        return (channel - LANES * size) // rest, LANES + (channel - LANES * size) % rest
    return channel // share, channel % share


def forward_kernel(
    heads_in, size, rows, msg_ref, act_ref, gate_ref, abc_ref, ld_ref, yw_ref, skip_ref, gt_ref, ys_ref, st_ref
):
    share = gt_ref.shape[1]
    unpack_blocks(msg_ref, st_ref, rows)
    c_rows = split(abc_ref[:, LANES : 2 * LANES])
    grown = jnp.exp(ld_ref[...])
    for j in range(act_ref.shape[1] // LANES):
        cols = slice(j * LANES, (j + 1) * LANES)
        carried = dot3(c_rows, split(st_ref[cols, :]), NT)
        within = yw_ref[:, cols] + spread(grown, j, heads_in, size) * carried
        ys_ref[:, cols] = within
        output = within + skip_ref[:, cols] * act_ref[:, cols]
        gate = gate_ref[:, cols].astype(F32)
        turned = (output * (gate * sigmoid(gate))).T.astype(BF16)
        for k in range(0, LANES, 16):
            to, at = place_of(j * LANES + k, share, gt_ref.shape[0])
            gt_ref[to, at : at + 16, :] = turned[k : k + 16]


def backward_kernel(
    heads_in, size, rows, me_ref, msg_ref, msgf_ref, act_ref, slope_ref, gy_ref, abc_ref, step_ref, ld_ref, gw_ref,
    gbcl_ref, ys_ref, gg_ref, gate_ref, skip_ref, dtw_ref, perw_ref, gx_ref, gbc_ref, gdt_ref, gz_ref,
    ca_ref, st_ref, cs_ref,
):
    length = act_ref.shape[0]
    unpack_blocks(msg_ref, ca_ref, rows, me_ref[0])
    unpack_blocks(msgf_ref, st_ref, rows)
    b_rows = split(abc_ref[:, 0:LANES])
    ld = ld_ref[...]
    step = step_ref[...]
    last = ld[length - 1 : length]
    grown = jnp.exp(ld)
    weight = jnp.exp(last - ld) * step
    sums = jnp.zeros((length, LANES), F32)
    sums_y = jnp.zeros((length, LANES), F32)
    leaving = jnp.zeros((8, LANES), F32)
    grad_b = gbcl_ref[:, 0:LANES]
    grad_c = gbcl_ref[:, LANES : 2 * LANES]
    cs_ref[...] = jnp.zeros_like(cs_ref)
    for j in range(act_ref.shape[1] // LANES):
        cols = slice(j * LANES, (j + 1) * LANES)
        inputs = act_ref[:, cols]
        grad_y = gy_ref[:, cols]
        carry = ca_ref[cols, :]
        state = st_ref[cols, :]
        carry_s = split(carry)
        wide = spread(weight, j, heads_in, size)
        gone = wide * dot3(b_rows, carry_s, NT)
        grad_in = gw_ref[:, cols] + gone
        gx_ref[:, cols] = ((skip_ref[:, cols] * grad_y + grad_in) * slope_ref[:, cols]).astype(BF16)
        onehot = head_of(j, heads_in, size)
        within = ys_ref[:, cols]
        gate = gate_ref[:, cols].astype(F32)
        opened = sigmoid(gate)
        output = within + skip_ref[:, cols] * inputs
        gz_ref[:, cols] = (gg_ref[:, cols] * output * (opened * (1.0 + gate * (1.0 - opened)))).astype(BF16)
        high, low = split(grad_y * within)
        sums_y = sums_y + (dot(high, onehot, NN) + dot(low, onehot, NN))
        high, low = split(inputs * grad_in)
        sums = sums + (dot(high, onehot, NN) + dot(low, onehot, NN))
        folded = jnp.sum((inputs * gone).reshape(length // 8, 8, LANES), axis=0)
        high, low = split(folded)
        leaving = leaving + (dot(high, onehot, NN) + dot(low, onehot, NN))
        product = carry * state
        for k in range(heads_in):
            h = j * heads_in + k
            cs_ref[h : h + 1, :] = jnp.sum(product[k * size : (k + 1) * size], axis=0, keepdims=True)
        grad_b = grad_b + dot3(split(wide * inputs), carry_s)
        grad_c = grad_c + dot3(split(spread(grown, j, heads_in, size) * grad_y), split(state))
    gbc_ref[:, 0:LANES] = grad_b
    gbc_ref[:, LANES : 2 * LANES] = grad_c
    both = lax.dot_general(
        jnp.ones((8, LANES), F32), cs_ref[...], (NT, ((), ())), precision=HIGH, preferred_element_type=F32
    )
    constant = jnp.sum(leaving, axis=0, keepdims=True) + jnp.exp(last) * both[0:1]
    upper = jnp.where(row_ids(length) <= lane_ids(length), 1.0, 0.0)
    grad_rate = constant + lax.dot_general(
        upper, sums_y - sums, (NN, ((), ())), precision=HIGH, preferred_element_type=F32
    )
    grad_step = sums / step - jnp.exp(perw_ref[1:2, :]) * grad_rate
    gdt_ref[...] = (grad_step * sigmoid(dtw_ref[...]))[:, 0 : gdt_ref.shape[1]]


def product_kernel(rows, held_ref, *refs):
    go_refs, out_ref, lhs_ref = refs[:-2], refs[-2], refs[-1]
    size, share, length = held_ref.shape

    @pl.when(pl.program_id(0) == 0)
    def _():
        for s in range(size):
            lhs_ref[:, s * length : (s + 1) * length] = held_ref[s]

    depth = go_refs[0].shape[0]
    result = dot(lhs_ref[:, 0:depth], go_refs[0][...], NN)
    for k in range(1, len(go_refs)):
        result = result + dot(lhs_ref[:, k * depth : (k + 1) * depth], go_refs[k][...], NN)
    result = result.T
    for d in range(out_ref.shape[0]):
        block = result[rows * d : rows * (d + 1)]
        if share > LANES:
            rest = share - LANES
            across = LANES // rest
            out_ref[d, 0:rows, :] = block[:, 0:LANES].astype(BF16)
            for k in range(0, rows // 16, across):
                pieces = [block[16 * m : 16 * m + 16, LANES:] for m in range(k, min(k + across, rows // 16))]
                if len(pieces) < across:
                    pieces.append(jnp.zeros((16, LANES - rest * len(pieces)), F32))
                at = rows + 16 * (k // across)
                out_ref[d, at : at + 16, :] = jnp.concatenate(pieces, axis=1).astype(BF16)
        else:
            out_ref[d] = block.astype(BF16)


def assemble_kernel(rows, size, share, parts_ref, out_ref):
    count = parts_ref.shape[0]

    def total(c, first, last):
        found = parts_ref[c, first:last, :].astype(F32)
        for s in range(c + size, count, size):
            found = found + parts_ref[s, first:last, :].astype(F32)
        return found

    if share > LANES:
        rest = share - LANES
        across = LANES // rest
        for c in range(size):
            out_ref[:, c * LANES : (c + 1) * LANES] = total(c, 0, rows)
            at = size * LANES + rest * c
            for k in range(0, rows // 16, across):
                extra = total(c, rows + 16 * (k // across), rows + 16 * (k // across) + 16)
                for m in range(k, min(k + across, rows // 16)):
                    lanes = slice(rest * (m - k), rest * (m - k + 1))
                    out_ref[16 * m : 16 * m + 16, at : at + rest] = extra[:, lanes]
    else:
        for c in range(size):
            out_ref[:, c * share : (c + 1) * share] = total(c, 0, rows)


def exchange(message, groups=None):
    half = message.astype(jnp.float16)
    return lax.all_to_all(half, "ctx", 0, 0, axis_index_groups=groups, tiled=True)


def swapped(message):
    half = message.astype(jnp.float16)
    count = lax.axis_size("ctx")
    slots = [half[0:1]]
    for m in range(1, message.shape[0]):
        slots.append(lax.ppermute(half[m : m + 1], "ctx", [(at, at ^ m) for at in range(count)]))
    return jnp.concatenate(slots).astype(F32)


def groups_of(count, size):
    return [list(range(at, at + size)) for at in range(0, count, size)]


def group_total(held, rows, reverse):
    (total,) = call(
        functools.partial(total_kernel, rows, reverse), [shape((1, *held.shape[1:]))], [held], 4 * held.size, 12
    )
    return total.astype(jnp.float16)


def enter(me, held, total, rows, reverse):
    size = held.shape[0]
    count = lax.axis_size("ctx")
    others = []
    for hops in range(size, count, size):
        pairs = [(at, at + hops) for at in range(count - hops)]
        if reverse:
            pairs = [(b, a) for a, b in pairs]
        others.append(lax.ppermute(total, "ctx", pairs).astype(F32))
    (folded,) = call(
        functools.partial(fold_kernel, rows, reverse),
        [shape(held.shape)],
        [me, held, *others],
        8 * held.size,
        12,
        specs=[SMEM] + [VMEM] * (1 + len(others)),
    )
    return folded


def group_of(count):
    for size in (16, 8, 4, 2):
        if count % size == 0:
            return size
    return 1


def from_behind(value, axis):
    count = lax.axis_size(axis)
    return lax.ppermute(value, axis, [(source, source + 1) for source in range(count - 1)])


def per_device(
    x_raw,
    bc_raw,
    gate_branch,
    dt_raw,
    conv_x,
    conv_x_bias,
    conv_bc,
    conv_bc_bias,
    dt_bias,
    a_log,
    d_skip,
    out_weight,
    grad_out,
):
    length, head_count = dt_raw.shape
    channels = x_raw.shape[1]
    width = grad_out.shape[1]
    head_size = channels // head_count
    heads_in = LANES // head_size
    count = lax.axis_size("ctx")
    plane = min(8, group_of(count))
    planes = groups_of(count, plane)
    rows = channels // plane
    size = group_of(count)
    share = channels // size
    groups = groups_of(count, size)
    gathered = lax.all_gather(grad_out, "ctx", axis_index_groups=groups, tiled=True)

    rim = from_behind(jnp.concatenate([x_raw[length - 16 :], bc_raw[length - 16 :]], axis=1), "ctx")
    skip = jnp.repeat(d_skip, head_size)[None, :]
    whole = (length, channels)
    square = (length, LANES)
    block = up8(rows) + 8
    stored = pltpu.VMEM((channels, LANES), F32)
    unit = 2 * length * channels * LANES
    me = (lax.axis_index("ctx") % plane).astype(jnp.int32).reshape(1)

    act_x, slope_x, act_bc, slope_bc, step, ld, step_t, ld_t, raised, per_head, message = call(
        functools.partial(prepare_kernel, heads_in, head_size, rows),
        [shape(whole), shape(whole), shape(bc_raw.shape), shape(bc_raw.shape)]
        + [shape(square)] * 2
        + [shape((LANES, length))] * 2
        + [shape(square), shape((8, LANES))]
        + [shape((plane, block, LANES))],
        [
            x_raw,
            bc_raw,
            conv_x,
            conv_bc,
            conv_bc_bias[None, :],
            rim[:, :channels],
            rim[:, channels:],
            conv_x_bias[None, :],
            dt_raw,
            jnp.stack([dt_bias, a_log]),
        ],
        20 * unit,
        20,
        [
            pltpu.VMEM((length + 8, channels), F32),
            pltpu.VMEM((length + 8, bc_raw.shape[1]), F32),
            stored,
        ],
    )
    message, grad_out_then = lax.optimization_barrier((message, grad_out))
    held_state = exchange(message, planes).astype(F32)
    part = 640 if channels % 640 == 0 else channels
    grad_gated, grad_y = pl.pallas_call(
        gate_kernel,
        grid=(channels // part,),
        in_specs=[
            pl.BlockSpec((length, width), lambda i: (0, 0)),
        ]
        + [
            pl.BlockSpec((part, width // STREAMS), functools.partial(lambda k, i: (i, k), k))
            for k in range(STREAMS)
        ]
        + [pl.BlockSpec((length, part), lambda i: (0, i))],
        out_specs=(pl.BlockSpec((length, part), lambda i: (0, i)), pl.BlockSpec((length, part), lambda i: (0, i))),
        out_shape=(shape(whole), shape(whole)),
        compiler_params=pltpu.CompilerParams(vmem_limit_bytes=24 * MIB),
        cost_estimate=pl.CostEstimate(
            flops=2 * length * channels * width, bytes_accessed=2 * channels * width, transcendentals=0
        ),
    )(grad_out_then, *[out_weight] * STREAMS, gate_branch)
    (message,) = call(
        functools.partial(grad_kernel, heads_in, head_size, rows),
        [shape((plane, block, LANES))],
        [grad_y, act_bc, ld],
        10 * unit,
        12,
        [stored],
    )
    y_within, grad_within, grad_bc_within = call(
        functools.partial(local_kernel, heads_in, head_size),
        [shape(whole), shape(whole), shape(act_bc.shape)],
        [act_x, grad_y, act_bc, step, ld, step_t, ld_t],
        40 * unit,
        16,
        [pltpu.VMEM(square, F32)],
    )
    message, total, y_within = lax.optimization_barrier(
        (message, group_total(held_state, rows, False), y_within)
    )
    held_carry = exchange(message, planes)
    folded, held_carry = lax.optimization_barrier((enter(me, held_state, total, rows, False), held_carry))
    held_carry = held_carry.astype(F32)
    state_message = exchange(folded, planes).astype(F32)
    gated, y_ahead = call(
        functools.partial(forward_kernel, heads_in, head_size, rows),
        [shape((size, share, length), BF16), shape(whole)],
        [state_message, act_x, gate_branch, act_bc, ld, y_within, skip],
        20 * unit,
        16,
        [stored],
    )
    entered = enter(me, held_carry, group_total(held_carry, rows, True), rows, True)
    gated, entered, gathered = lax.optimization_barrier((gated, entered, gathered))
    held = lax.all_to_all(gated, "ctx", 0, 0, axis_index_groups=groups, tiled=True)
    held, carry_message = lax.optimization_barrier((held, swapped(entered)))
    out_rows = width // count
    part = width
    for candidate in (640, 1280):
        if width % candidate == 0 and candidate % out_rows == 0:
            part = candidate
            break
    dims = (out_rows, share)
    if share > LANES:
        dims = (out_rows + 16 * (-(-(out_rows // 16) // (LANES // (share - LANES)))), LANES)
    partial = pl.pallas_call(
        functools.partial(product_kernel, out_rows),
        grid=(width // part,),
        in_specs=[
            pl.BlockSpec((size, share, length), lambda i: (0, 0, 0)),
        ]
        + [
            pl.BlockSpec((size * length // STREAMS, part), functools.partial(lambda k, i: (k, i), k))
            for k in range(STREAMS)
        ],
        out_specs=pl.BlockSpec((part // out_rows, *dims), lambda i: (i, 0, 0)),
        out_shape=shape((count, *dims), BF16),
        scratch_shapes=[pltpu.VMEM((share, size * length), BF16)],
        compiler_params=pltpu.CompilerParams(vmem_limit_bytes=24 * MIB),
        cost_estimate=pl.CostEstimate(
            flops=2 * size * length * share * width, bytes_accessed=2 * size * length * width, transcendentals=0
        ),
    )(held, *[gathered] * STREAMS)
    parts = lax.all_to_all(partial, "ctx", 0, 0, tiled=True)
    (weight_grad,) = call(
        functools.partial(assemble_kernel, out_rows, size, share),
        [shape((out_rows, channels))],
        [parts],
        2 * parts.size,
        12,
    )
    grad_x_conv, grad_bc, grad_dt_raw, grad_z = call(
        functools.partial(backward_kernel, heads_in, head_size, rows),
        [shape(whole, BF16), shape(act_bc.shape), shape(dt_raw.shape), shape(whole, BF16)],
        [
            me,
            carry_message,
            state_message,
            act_x,
            slope_x,
            grad_y,
            act_bc,
            step,
            ld,
            grad_within,
            grad_bc_within,
            y_ahead,
            grad_gated,
            gate_branch,
            skip,
            raised,
            per_head,
        ],
        40 * unit,
        28,
        [stored, stored, pltpu.VMEM((LANES, LANES), F32)],
        [SMEM] + [VMEM] * 16,
    )
    grad_bc_conv = (lax.psum(grad_bc, "tp") * slope_bc).astype(BF16)
    return (grad_x_conv, grad_bc_conv, grad_z, grad_dt_raw, weight_grad)


def solution(mesh):
    placed = (
        P("ctx", "tp"),
        P("ctx", None),
        P("ctx", "tp"),
        P("ctx", "tp"),
        P(None, "tp"),
        P("tp"),
        P(),
        P(),
        P("tp"),
        P("tp"),
        P("tp"),
        P("tp", None),
        P("ctx", None),
    )
    return jax.shard_map(
        per_device,
        mesh=mesh,
        in_specs=placed,
        out_specs=(P("ctx", "tp"), P("ctx", None), P("ctx", "tp"), P("ctx", "tp"), P("ctx", "tp")),
        check_vma=False,
    )
```

```python
import functools

import jax
import jax.numpy as jnp
from jax import lax
from jax.experimental import pallas as pl
from jax.experimental.pallas import tpu as pltpu
from jax.sharding import PartitionSpec as P

KERNEL = 4
LANES = 128
F32 = jnp.float32
BF16 = jnp.bfloat16
NN = ((1,), (0,))
NT = ((1,), (1,))
HIGH = lax.Precision.HIGHEST
SMEM = pl.BlockSpec(memory_space=pltpu.SMEM)
VMEM = pl.BlockSpec(memory_space=pltpu.VMEM)
MIB = 1024 * 1024
STREAMS = 4


def call(kernel, out_shapes, operands, flops, vmem, scratch=(), specs=None):
    extra = {} if specs is None else {"in_specs": specs}
    moved = sum(a.size * a.dtype.itemsize for a in (*operands, *out_shapes))
    return pl.pallas_call(
        kernel,
        out_shape=tuple(out_shapes),
        scratch_shapes=list(scratch),
        compiler_params=pltpu.CompilerParams(vmem_limit_bytes=vmem * MIB),
        cost_estimate=pl.CostEstimate(flops=flops, bytes_accessed=moved, transcendentals=0),
        **extra,
    )(*operands)


def shape(dims, dtype=F32):
    return jax.ShapeDtypeStruct(dims, dtype)


def split(value):
    high = value.astype(BF16)
    return high, (value - high.astype(F32)).astype(BF16)


def dot(a, b, dims):
    return lax.dot_general(a, b, (dims, ((), ())), preferred_element_type=F32)


def dot3(a, b, dims=NN):
    return dot(a[0], b[0], dims) + (dot(a[0], b[1], dims) + dot(a[1], b[0], dims))


def sigmoid(value):
    return 1.0 / (1.0 + jnp.exp(-value))


def lane_ids(rows, cols=LANES):
    return lax.broadcasted_iota(jnp.int32, (rows, cols), 1)


def row_ids(rows, cols=LANES):
    return lax.broadcasted_iota(jnp.int32, (rows, cols), 0)


def spread(columns, block, heads, size):
    first = block * heads
    lanes = lane_ids(columns.shape[0])
    wide = jnp.broadcast_to(columns[:, first : first + 1], (columns.shape[0], LANES))
    for k in range(1, heads):
        wide = jnp.where(lanes >= k * size, columns[:, first + k : first + k + 1], wide)
    return wide


def head_of(block, heads, size):
    inner = row_ids(LANES)
    target = lane_ids(LANES)
    result = jnp.zeros((LANES, LANES), F32)
    for k in range(heads):
        here = (inner >= k * size) & (inner < (k + 1) * size) & (target == block * heads + k)
        result = jnp.where(here, 1.0, result)
    return result.astype(BF16)


def stacked(value, heads, size):
    lanes = lane_ids(value.shape[0])
    return jnp.concatenate(
        [jnp.where((lanes >= k * size) & (lanes < (k + 1) * size), value, 0.0) for k in range(heads)],
        axis=0,
    )


def up8(value):
    return -(-value // 8) * 8


def notes_of(rows):
    return -(-rows // LANES)


def exponent_of(block):
    top = jnp.max(jnp.max(jnp.abs(block), axis=0, keepdims=True), axis=1, keepdims=True)
    return jnp.floor(jnp.log2(jnp.maximum(jnp.broadcast_to(top, (1, LANES)), 1e-30)))


def write_block(message, at, first, block, decays, exponent):
    rows = block.shape[0]
    padded = up8(rows)
    message[at, first : first + rows, :] = block * jnp.exp2(13.0 - exponent)
    if padded > rows:
        message[at, first + rows : first + padded, :] = jnp.zeros((padded - rows, LANES), F32)
    highs = [d.astype(BF16).astype(F32) for d in decays]
    lows = [d - h for d, h in zip(decays, highs)]
    place = row_ids(8)
    notes = jnp.broadcast_to(exponent, (8, LANES))
    for k, line in enumerate(highs + lows):
        notes = jnp.where(place == k, line, notes)
    message[at, first + padded : first + padded + 8, :] = notes


def decay_tables(last_exp, heads, size, rows, count):
    shift = size.bit_length() - 1
    tables = []
    for d in range(count):
        lines = []
        for k in range(notes_of(rows)):
            first = rows * d + LANES * k
            owner = lax.shift_right_logical(lane_ids(1) + first, shift)
            table = jnp.zeros((1, LANES), F32)
            for h in range(first // size, min(heads, (first + LANES - 1) // size + 1)):
                table = jnp.where(owner == h, last_exp[:, h : h + 1], table)
            lines.append(table)
        tables.append(lines)
    return tables


def pack_blocks(source, message, last_exp, size, rows, me=0):
    count = message.shape[0]
    tables = decay_tables(last_exp, source.shape[0] // size, size, rows, count)
    for d in range(count):
        block = source[rows * d : rows * (d + 1), :]
        write_block(message, me ^ d, 0, block, tables[d], exponent_of(block))


def decay_lines(message, at, rows):
    padded, lines = up8(rows), notes_of(rows)
    return [
        message[at, padded + k : padded + k + 1, :] + message[at, padded + lines + k : padded + lines + k + 1, :]
        for k in range(lines)
    ]


def decay_columns(message, rows):
    padded, lines = up8(rows), notes_of(rows)
    turned = [
        jnp.transpose(message[:, padded + k, :] + message[:, padded + lines + k, :]) for k in range(lines)
    ]
    return jnp.concatenate(turned, axis=0)[0:rows]


def read_block(message, at, rows):
    padded = up8(rows)
    return message[at, 0:rows, :] * jnp.exp2(message[at, padded + 7 : padded + 8, :] - 13.0)


def unpack_blocks(message, target, rows, me=0):
    for d in range(message.shape[0]):
        target[rows * d : rows * (d + 1), :] = read_block(message, me ^ d, rows)


def in_order(me_ref, held_ref, order_ref):
    for s in range(held_ref.shape[0]):
        order_ref[s] = held_ref[me_ref[0] ^ s]
    return order_ref


def total_kernel(rows, reverse, me_ref, held_ref, out_ref, order_ref):
    count = held_ref.shape[0]
    if reverse:
        held_ref = in_order(me_ref, held_ref, order_ref)
    columns = decay_columns(held_ref, rows)
    state = None
    for s in range(count - 1, -1, -1) if reverse else range(count):
        block = read_block(held_ref, s, rows)
        state = block if state is None else columns[:, s : s + 1] * state + block
    decays = decay_lines(held_ref, 0, rows)
    for s in range(1, count):
        decays = [a * b for a, b in zip(decays, decay_lines(held_ref, s, rows))]
    write_block(out_ref, 0, 0, state, decays, exponent_of(state))


def fold_kernel(rows, reverse, me_ref, held_ref, *refs):
    others, out_ref, order_ref = refs[:-2], refs[-2], refs[-1]
    count = held_ref.shape[0]
    if reverse:
        held_ref = in_order(me_ref, held_ref, order_ref)
    columns = decay_columns(held_ref, rows)
    state = jnp.zeros((rows, LANES), F32)
    for other in reversed(others):
        state = decay_columns(other, rows) * state + read_block(other, 0, rows)
    for s in range(count - 1, -1, -1) if reverse else range(count):
        write_block(out_ref, me_ref[0] ^ s if reverse else s, 0, state, [], exponent_of(state))
        if s != (0 if reverse else count - 1):
            state = columns[:, s : s + 1] * state + read_block(held_ref, s, rows)


def prepare_kernel(
    heads_in, size, rows, x_ref, bc_ref, wx_ref, wbc_ref, bbc_ref, rim_ref, rim_bc_ref, bx_ref, dt_ref,
    per_ref, act_ref, slope_ref, abc_ref, sbc_ref, step_ref, ld_ref, stept_ref, ldt_ref, dtw_ref, perw_ref, msg_ref,
    xs_ref, bs_ref, st_ref,
):
    length = x_ref.shape[0]
    blocks = x_ref.shape[1] // LANES

    def convolved(raw, rim, padded, weight, bias, cols):
        padded[0:8, cols] = rim[:, cols].astype(F32)[8:16]
        padded[8 : 8 + length, cols] = raw[:, cols].astype(F32)
        pre = bias[:, cols] + weight[0:1, cols] * padded[5 : 5 + length, cols]
        for k in range(1, KERNEL):
            pre = pre + weight[k : k + 1, cols] * padded[5 + k : 5 + k + length, cols]
        gate = sigmoid(pre)
        return pre * gate, gate * (1.0 + pre * (1.0 - gate))

    for j in range(bc_ref.shape[1] // LANES):
        cols = slice(j * LANES, (j + 1) * LANES)
        value, slope = convolved(bc_ref, rim_bc_ref, bs_ref, wbc_ref, bbc_ref, cols)
        abc_ref[:, cols] = value
        sbc_ref[:, cols] = slope
    b_rows = split(abc_ref[:, 0:LANES])
    heads = dt_ref.shape[1]
    dtw_ref[...] = jnp.zeros_like(dtw_ref)
    dtw_ref[:, 0:heads] = dt_ref[...]
    perw_ref[...] = jnp.zeros_like(perw_ref)
    perw_ref[0:2, 0:heads] = per_ref[...]
    raised = dtw_ref[...] + perw_ref[0:1, :]
    dtw_ref[...] = raised
    step = jnp.maximum(raised, 0.0) + jnp.log1p(jnp.exp(-jnp.abs(raised)))
    lower = jnp.where(row_ids(length) >= lane_ids(length), 1.0, 0.0)
    ld = lax.dot_general(
        lower, step * -jnp.exp(perw_ref[1:2, :]), (NN, ((), ())), precision=HIGH, preferred_element_type=F32
    )
    step_ref[...] = step
    ld_ref[...] = ld
    stept_ref[...] = step.T
    ldt_ref[...] = ld.T
    last = ld[length - 1 : length]
    weight = jnp.exp(last - ld) * step
    for j in range(blocks):
        cols = slice(j * LANES, (j + 1) * LANES)
        value, slope = convolved(x_ref, rim_ref, xs_ref, wx_ref, bx_ref, cols)
        act_ref[:, cols] = value
        slope_ref[:, cols] = slope
        scaled = value * spread(weight, j, heads_in, size)
        st_ref[cols, :] = dot3(split(scaled.T), b_rows)
    pack_blocks(st_ref, msg_ref, jnp.exp(last), size, rows)


def grad_kernel(heads_in, size, rows, me_ref, gy_ref, abc_ref, ld_ref, msg_ref, st_ref):
    length = gy_ref.shape[0]
    c_rows = split(abc_ref[:, LANES : 2 * LANES])
    grown = jnp.exp(ld_ref[...])
    for j in range(gy_ref.shape[1] // LANES):
        cols = slice(j * LANES, (j + 1) * LANES)
        scaled = gy_ref[:, cols] * spread(grown, j, heads_in, size)
        st_ref[cols, :] = dot3(split(scaled.T), c_rows)
    pack_blocks(st_ref, msg_ref, grown[length - 1 : length], size, rows, me_ref[0])


def gate_kernel(go_ref, *refs):
    w_refs, (gate_ref, gg_ref, gy_ref) = refs[:-3], refs[-3:]
    depth = w_refs[0].shape[1]
    grad = dot(w_refs[0][...], go_ref[:, 0:depth], NT)
    for k in range(1, len(w_refs)):
        grad = grad + dot(w_refs[k][...], go_ref[:, k * depth : (k + 1) * depth], NT)
    grad = grad.T
    gate = gate_ref[...].astype(F32)
    gg_ref[...] = grad
    gy_ref[...] = grad * (gate * sigmoid(gate))


def local_kernel(
    heads_in, size, act_ref, gy_ref, abc_ref, step_ref, ld_ref, stept_ref, ldt_ref, yw_ref, gw_ref, gbc_ref, sh_ref
):
    length = act_ref.shape[0]
    b_rows = split(abc_ref[:, 0:LANES])
    c_rows = split(abc_ref[:, LANES : 2 * LANES])
    scores = dot3(c_rows, b_rows, NT)
    turned = dot3(b_rows, c_rows, NT)
    causal = row_ids(length) >= lane_ids(length)
    causal_t = row_ids(length) <= lane_ids(length)
    sh_ref[...] = jnp.zeros_like(sh_ref)
    for j in range(act_ref.shape[1] // LANES):
        cols = slice(j * LANES, (j + 1) * LANES)
        mixes, mixes_t, steps = [], [], []
        for h in range(j * heads_in, (j + 1) * heads_in):
            column, row = ld_ref[:, h : h + 1], ldt_ref[h : h + 1, :]
            decays = jnp.exp(jnp.where(causal, column - row, -1e30))
            stepped = decays * stept_ref[h : h + 1, :]
            decays_t = jnp.exp(jnp.where(causal_t, row - column, -1e30))
            steps.append(stepped)
            mixes.append(stepped * scores)
            mixes_t.append(decays_t * turned * step_ref[:, h : h + 1])
        inputs = act_ref[:, cols]
        grad_y = gy_ref[:, cols]
        inputs_s = stacked(inputs, heads_in, size)
        grads_s = split(stacked(grad_y, heads_in, size))
        yw_ref[:, cols] = dot3(split(jnp.concatenate(mixes, axis=1)), split(inputs_s))
        gw_ref[:, cols] = dot3(split(jnp.concatenate(mixes_t, axis=1)), grads_s)
        products = dot3(grads_s, split(inputs), NT)
        total = sh_ref[...]
        for k in range(heads_in):
            total = total + steps[k] * products[k * length : (k + 1) * length]
        sh_ref[...] = total
    shared = sh_ref[...]
    gbc_ref[:, 0:LANES] = dot3(split(shared.T), c_rows)
    gbc_ref[:, LANES : 2 * LANES] = dot3(split(shared), b_rows)


def place_of(channel, share, size):
    if share > LANES:
        if channel < LANES * size:
            return channel // LANES, channel % LANES
        rest = share - LANES
        return (channel - LANES * size) // rest, LANES + (channel - LANES * size) % rest
    return channel // share, channel % share


def forward_kernel(
    heads_in, size, rows, msg_ref, act_ref, gate_ref, abc_ref, ld_ref, yw_ref, skip_ref, gt_ref, ys_ref, st_ref
):
    share = gt_ref.shape[1]
    unpack_blocks(msg_ref, st_ref, rows)
    c_rows = split(abc_ref[:, LANES : 2 * LANES])
    grown = jnp.exp(ld_ref[...])
    for j in range(act_ref.shape[1] // LANES):
        cols = slice(j * LANES, (j + 1) * LANES)
        carried = dot3(c_rows, split(st_ref[cols, :]), NT)
        within = yw_ref[:, cols] + spread(grown, j, heads_in, size) * carried
        ys_ref[:, cols] = within
        output = within + skip_ref[:, cols] * act_ref[:, cols]
        gate = gate_ref[:, cols].astype(F32)
        turned = (output * (gate * sigmoid(gate))).T.astype(BF16)
        for k in range(0, LANES, 16):
            to, at = place_of(j * LANES + k, share, gt_ref.shape[0])
            gt_ref[to, at : at + 16, :] = turned[k : k + 16]


def ahead_kernel(
    heads_in, size, rows, msg_ref, act_ref, gy_ref, ld_ref, gbcl_ref, ys_ref, gg_ref, gate_ref, skip_ref,
    gz_ref, yg_ref, gbc_ref, st_ref,
):
    unpack_blocks(msg_ref, st_ref, rows)
    grown = jnp.exp(ld_ref[...])
    sums = jnp.zeros(yg_ref.shape, F32)
    grad_c = gbcl_ref[:, LANES : 2 * LANES]
    for j in range(act_ref.shape[1] // LANES):
        cols = slice(j * LANES, (j + 1) * LANES)
        grad_y = gy_ref[:, cols]
        within = ys_ref[:, cols]
        gate = gate_ref[:, cols].astype(F32)
        opened = sigmoid(gate)
        output = within + skip_ref[:, cols] * act_ref[:, cols]
        gz_ref[:, cols] = (gg_ref[:, cols] * output * (opened * (1.0 + gate * (1.0 - opened)))).astype(BF16)
        onehot = head_of(j, heads_in, size)
        high, low = split(grad_y * within)
        sums = sums + (dot(high, onehot, NN) + dot(low, onehot, NN))
        grad_c = grad_c + dot3(split(spread(grown, j, heads_in, size) * grad_y), split(st_ref[cols, :]))
    yg_ref[...] = sums
    gbc_ref[:, 0:LANES] = gbcl_ref[:, 0:LANES]
    gbc_ref[:, LANES : 2 * LANES] = grad_c


def backward_kernel(
    heads_in, size, rows, me_ref, msg_ref, msgf_ref, act_ref, slope_ref, gy_ref, abc_ref, step_ref, ld_ref, gw_ref,
    gbcl_ref, yg_ref, skip_ref, dtw_ref, perw_ref, gx_ref, gbc_ref, gdt_ref,
    ca_ref, st_ref, cs_ref,
):
    length = act_ref.shape[0]
    unpack_blocks(msg_ref, ca_ref, rows, me_ref[0])
    unpack_blocks(msgf_ref, st_ref, rows)
    b_rows = split(abc_ref[:, 0:LANES])
    ld = ld_ref[...]
    step = step_ref[...]
    last = ld[length - 1 : length]
    weight = jnp.exp(last - ld) * step
    sums = jnp.zeros((length, LANES), F32)
    leaving = jnp.zeros((8, LANES), F32)
    grad_b = gbcl_ref[:, 0:LANES]
    cs_ref[...] = jnp.zeros_like(cs_ref)
    for j in range(act_ref.shape[1] // LANES):
        cols = slice(j * LANES, (j + 1) * LANES)
        inputs = act_ref[:, cols]
        grad_y = gy_ref[:, cols]
        carry = ca_ref[cols, :]
        state = st_ref[cols, :]
        carry_s = split(carry)
        wide = spread(weight, j, heads_in, size)
        gone = wide * dot3(b_rows, carry_s, NT)
        grad_in = gw_ref[:, cols] + gone
        gx_ref[:, cols] = ((skip_ref[:, cols] * grad_y + grad_in) * slope_ref[:, cols]).astype(BF16)
        onehot = head_of(j, heads_in, size)
        high, low = split(inputs * grad_in)
        sums = sums + (dot(high, onehot, NN) + dot(low, onehot, NN))
        folded = jnp.sum((inputs * gone).reshape(length // 8, 8, LANES), axis=0)
        high, low = split(folded)
        leaving = leaving + (dot(high, onehot, NN) + dot(low, onehot, NN))
        product = carry * state
        for k in range(heads_in):
            h = j * heads_in + k
            cs_ref[h : h + 1, :] = jnp.sum(product[k * size : (k + 1) * size], axis=0, keepdims=True)
        grad_b = grad_b + dot3(split(wide * inputs), carry_s)
    gbc_ref[:, 0:LANES] = grad_b
    gbc_ref[:, LANES : 2 * LANES] = gbcl_ref[:, LANES : 2 * LANES]
    both = lax.dot_general(
        jnp.ones((8, LANES), F32), cs_ref[...], (NT, ((), ())), precision=HIGH, preferred_element_type=F32
    )
    constant = jnp.sum(leaving, axis=0, keepdims=True) + jnp.exp(last) * both[0:1]
    upper = jnp.where(row_ids(length) <= lane_ids(length), 1.0, 0.0)
    grad_rate = constant + lax.dot_general(
        upper, yg_ref[...] - sums, (NN, ((), ())), precision=HIGH, preferred_element_type=F32
    )
    grad_step = sums / step - jnp.exp(perw_ref[1:2, :]) * grad_rate
    gdt_ref[...] = (grad_step * sigmoid(dtw_ref[...]))[:, 0 : gdt_ref.shape[1]]


def product_kernel(rows, held_ref, *refs):
    go_refs, out_ref, lhs_ref = refs[:-2], refs[-2], refs[-1]
    size, share, length = held_ref.shape

    @pl.when(pl.program_id(0) == 0)
    def _():
        for s in range(size):
            lhs_ref[:, s * length : (s + 1) * length] = held_ref[s]

    depth = go_refs[0].shape[0]
    result = dot(lhs_ref[:, 0:depth], go_refs[0][...], NN)
    for k in range(1, len(go_refs)):
        result = result + dot(lhs_ref[:, k * depth : (k + 1) * depth], go_refs[k][...], NN)
    result = result.T
    for d in range(out_ref.shape[0]):
        block = result[rows * d : rows * (d + 1)]
        if share > LANES:
            rest = share - LANES
            across = LANES // rest
            out_ref[d, 0:rows, :] = block[:, 0:LANES].astype(BF16)
            for k in range(0, rows // 16, across):
                pieces = [block[16 * m : 16 * m + 16, LANES:] for m in range(k, min(k + across, rows // 16))]
                if len(pieces) < across:
                    pieces.append(jnp.zeros((16, LANES - rest * len(pieces)), F32))
                at = rows + 16 * (k // across)
                out_ref[d, at : at + 16, :] = jnp.concatenate(pieces, axis=1).astype(BF16)
        else:
            out_ref[d] = block.astype(BF16)


def assemble_kernel(rows, size, share, parts_ref, out_ref):
    count = parts_ref.shape[0]

    def total(c, first, last):
        found = parts_ref[c, first:last, :].astype(F32)
        for s in range(c + size, count, size):
            found = found + parts_ref[s, first:last, :].astype(F32)
        return found

    if share > LANES:
        rest = share - LANES
        across = LANES // rest
        for c in range(size):
            out_ref[:, c * LANES : (c + 1) * LANES] = total(c, 0, rows)
            at = size * LANES + rest * c
            for k in range(0, rows // 16, across):
                extra = total(c, rows + 16 * (k // across), rows + 16 * (k // across) + 16)
                for m in range(k, min(k + across, rows // 16)):
                    lanes = slice(rest * (m - k), rest * (m - k + 1))
                    out_ref[16 * m : 16 * m + 16, at : at + rest] = extra[:, lanes]
    else:
        for c in range(size):
            out_ref[:, c * share : (c + 1) * share] = total(c, 0, rows)


def exchange(message, groups=None):
    half = message.astype(jnp.float16)
    return lax.all_to_all(half, "ctx", 0, 0, axis_index_groups=groups, tiled=True)


def swapped(message):
    half = message.astype(jnp.float16)
    count = lax.axis_size("ctx")
    slots = [half[0:1]]
    for m in range(1, message.shape[0]):
        slots.append(lax.ppermute(half[m : m + 1], "ctx", [(at, at ^ m) for at in range(count)]))
    return jnp.concatenate(slots).astype(F32)


def groups_of(count, size):
    return [list(range(at, at + size)) for at in range(0, count, size)]


def group_total(me, held, rows, reverse):
    (total,) = call(
        functools.partial(total_kernel, rows, reverse),
        [shape((1, *held.shape[1:]))],
        [me, held],
        4 * held.size,
        12,
        [pltpu.VMEM(held.shape, F32)],
        [SMEM, VMEM],
    )
    return total.astype(jnp.float16)


def enter(me, held, total, rows, reverse):
    size = held.shape[0]
    count = lax.axis_size("ctx")
    others = []
    for hops in range(size, count, size):
        pairs = [(at, at + hops) for at in range(count - hops)]
        if reverse:
            pairs = [(b, a) for a, b in pairs]
        others.append(lax.ppermute(total, "ctx", pairs).astype(F32))
    (folded,) = call(
        functools.partial(fold_kernel, rows, reverse),
        [shape(held.shape)],
        [me, held, *others],
        8 * held.size,
        12,
        [pltpu.VMEM(held.shape, F32)],
        [SMEM] + [VMEM] * (1 + len(others)),
    )
    return folded


def group_of(count):
    for size in (16, 8, 4, 2):
        if count % size == 0:
            return size
    return 1


def from_behind(value, axis):
    count = lax.axis_size(axis)
    return lax.ppermute(value, axis, [(source, source + 1) for source in range(count - 1)])


def per_device(
    x_raw,
    bc_raw,
    gate_branch,
    dt_raw,
    conv_x,
    conv_x_bias,
    conv_bc,
    conv_bc_bias,
    dt_bias,
    a_log,
    d_skip,
    out_weight,
    grad_out,
):
    length, head_count = dt_raw.shape
    channels = x_raw.shape[1]
    width = grad_out.shape[1]
    head_size = channels // head_count
    heads_in = LANES // head_size
    count = lax.axis_size("ctx")
    plane = min(8, group_of(count))
    planes = groups_of(count, plane)
    rows = channels // plane
    size = group_of(count)
    share = channels // size
    groups = groups_of(count, size)
    gathered = lax.all_gather(grad_out, "ctx", axis_index_groups=groups, tiled=True)

    rim = from_behind(jnp.concatenate([x_raw[length - 16 :], bc_raw[length - 16 :]], axis=1), "ctx")
    skip = jnp.repeat(d_skip, head_size)[None, :]
    whole = (length, channels)
    square = (length, LANES)
    block = up8(rows) + 8
    stored = pltpu.VMEM((channels, LANES), F32)
    unit = 2 * length * channels * LANES
    me = (lax.axis_index("ctx") % plane).astype(jnp.int32).reshape(1)

    act_x, slope_x, act_bc, slope_bc, step, ld, step_t, ld_t, raised, per_head, message = call(
        functools.partial(prepare_kernel, heads_in, head_size, rows),
        [shape(whole), shape(whole), shape(bc_raw.shape), shape(bc_raw.shape)]
        + [shape(square)] * 2
        + [shape((LANES, length))] * 2
        + [shape(square), shape((8, LANES))]
        + [shape((plane, block, LANES))],
        [
            x_raw,
            bc_raw,
            conv_x,
            conv_bc,
            conv_bc_bias[None, :],
            rim[:, :channels],
            rim[:, channels:],
            conv_x_bias[None, :],
            dt_raw,
            jnp.stack([dt_bias, a_log]),
        ],
        20 * unit,
        20,
        [
            pltpu.VMEM((length + 8, channels), F32),
            pltpu.VMEM((length + 8, bc_raw.shape[1]), F32),
            stored,
        ],
    )
    message, grad_out_then = lax.optimization_barrier((message, grad_out))
    held_state = exchange(message, planes).astype(F32)
    part = 640 if channels % 640 == 0 else channels
    grad_gated, grad_y = pl.pallas_call(
        gate_kernel,
        grid=(channels // part,),
        in_specs=[
            pl.BlockSpec((length, width), lambda i: (0, 0)),
        ]
        + [
            pl.BlockSpec((part, width // STREAMS), functools.partial(lambda k, i: (i, k), k))
            for k in range(STREAMS)
        ]
        + [pl.BlockSpec((length, part), lambda i: (0, i))],
        out_specs=(pl.BlockSpec((length, part), lambda i: (0, i)), pl.BlockSpec((length, part), lambda i: (0, i))),
        out_shape=(shape(whole), shape(whole)),
        compiler_params=pltpu.CompilerParams(vmem_limit_bytes=52 * MIB),
        cost_estimate=pl.CostEstimate(
            flops=2 * length * channels * width, bytes_accessed=2 * channels * width, transcendentals=0
        ),
    )(grad_out_then, *[out_weight] * STREAMS, gate_branch)
    (message,) = call(
        functools.partial(grad_kernel, heads_in, head_size, rows),
        [shape((plane, block, LANES))],
        [me, grad_y, act_bc, ld],
        10 * unit,
        12,
        [stored],
        [SMEM] + [VMEM] * 3,
    )
    y_within, grad_within, grad_bc_within = call(
        functools.partial(local_kernel, heads_in, head_size),
        [shape(whole), shape(whole), shape(act_bc.shape)],
        [act_x, grad_y, act_bc, step, ld, step_t, ld_t],
        40 * unit,
        16,
        [pltpu.VMEM(square, F32)],
    )
    total, y_within, message = lax.optimization_barrier(
        (group_total(me, held_state, rows, False), y_within, message)
    )
    folded, message = lax.optimization_barrier((enter(me, held_state, total, rows, False), message))
    held_carry = swapped(message)
    state_message = exchange(folded, planes).astype(F32)
    gated, y_ahead = call(
        functools.partial(forward_kernel, heads_in, head_size, rows),
        [shape((size, share, length), BF16), shape(whole)],
        [state_message, act_x, gate_branch, act_bc, ld, y_within, skip],
        20 * unit,
        16,
        [stored],
    )
    gated, held_carry, gathered, y_ahead = lax.optimization_barrier((gated, held_carry, gathered, y_ahead))
    held = lax.all_to_all(gated, "ctx", 0, 0, axis_index_groups=groups, tiled=True)
    entered = enter(me, held_carry, group_total(me, held_carry, rows, True), rows, True)
    grad_z, y_sums, grad_bc_ahead = call(
        functools.partial(ahead_kernel, heads_in, head_size, rows),
        [shape(whole, BF16), shape(square), shape(act_bc.shape)],
        [state_message, act_x, grad_y, ld, grad_bc_within, y_ahead, grad_gated, gate_branch, skip],
        20 * unit,
        16,
        [stored],
    )
    held, entered, y_sums = lax.optimization_barrier((held, entered, y_sums))
    out_rows = width // count
    part = width
    for candidate in (640, 1280):
        if width % candidate == 0 and candidate % out_rows == 0:
            part = candidate
            break
    dims = (out_rows, share)
    if share > LANES:
        dims = (out_rows + 16 * (-(-(out_rows // 16) // (LANES // (share - LANES)))), LANES)
    partial = pl.pallas_call(
        functools.partial(product_kernel, out_rows),
        grid=(width // part,),
        in_specs=[
            pl.BlockSpec((size, share, length), lambda i: (0, 0, 0)),
        ]
        + [
            pl.BlockSpec((size * length // STREAMS, part), functools.partial(lambda k, i: (k, i), k))
            for k in range(STREAMS)
        ],
        out_specs=pl.BlockSpec((part // out_rows, *dims), lambda i: (i, 0, 0)),
        out_shape=shape((count, *dims), BF16),
        scratch_shapes=[pltpu.VMEM((share, size * length), BF16)],
        compiler_params=pltpu.CompilerParams(vmem_limit_bytes=54 * MIB),
        cost_estimate=pl.CostEstimate(
            flops=2 * size * length * share * width, bytes_accessed=2 * size * length * width, transcendentals=0
        ),
    )(held, *[gathered] * STREAMS)
    partial, entered = lax.optimization_barrier((partial, entered))
    parts = lax.all_to_all(partial, "ctx", 0, 0, tiled=True)
    carry_message = swapped(entered)
    (weight_grad,) = call(
        functools.partial(assemble_kernel, out_rows, size, share),
        [shape((out_rows, channels))],
        [parts],
        2 * parts.size,
        12,
    )
    grad_x_conv, grad_bc, grad_dt_raw = call(
        functools.partial(backward_kernel, heads_in, head_size, rows),
        [shape(whole, BF16), shape(act_bc.shape), shape(dt_raw.shape)],
        [
            me,
            carry_message,
            state_message,
            act_x,
            slope_x,
            grad_y,
            act_bc,
            step,
            ld,
            grad_within,
            grad_bc_ahead,
            y_sums,
            skip,
            raised,
            per_head,
        ],
        40 * unit,
        28,
        [stored, stored, pltpu.VMEM((LANES, LANES), F32)],
        [SMEM] + [VMEM] * 14,
    )
    grad_bc_conv = (lax.psum(grad_bc, "tp") * slope_bc).astype(BF16)
    return (grad_x_conv, grad_bc_conv, grad_z, grad_dt_raw, weight_grad)


def solution(mesh):
    placed = (
        P("ctx", "tp"),
        P("ctx", None),
        P("ctx", "tp"),
        P("ctx", "tp"),
        P(None, "tp"),
        P("tp"),
        P(),
        P(),
        P("tp"),
        P("tp"),
        P("tp"),
        P("tp", None),
        P("ctx", None),
    )
    return jax.shard_map(
        per_device,
        mesh=mesh,
        in_specs=placed,
        out_specs=(P("ctx", "tp"), P("ctx", None), P("ctx", "tp"), P("ctx", "tp"), P("ctx", "tp")),
        check_vma=False,
    )
```

```python
import functools

import jax
import jax.numpy as jnp
from jax import lax
from jax.experimental import pallas as pl
from jax.experimental.pallas import tpu as pltpu
from jax.sharding import PartitionSpec as P

KERNEL = 4
LANES = 128
F32 = jnp.float32
BF16 = jnp.bfloat16
NN = ((1,), (0,))
NT = ((1,), (1,))
HIGH = lax.Precision.HIGHEST
SMEM = pl.BlockSpec(memory_space=pltpu.SMEM)
VMEM = pl.BlockSpec(memory_space=pltpu.VMEM)
MIB = 1024 * 1024
STREAMS = 4


def call(kernel, out_shapes, operands, flops, vmem, scratch=(), specs=None):
    extra = {} if specs is None else {"in_specs": specs}
    moved = sum(a.size * a.dtype.itemsize for a in (*operands, *out_shapes))
    return pl.pallas_call(
        kernel,
        out_shape=tuple(out_shapes),
        scratch_shapes=list(scratch),
        compiler_params=pltpu.CompilerParams(vmem_limit_bytes=vmem * MIB),
        cost_estimate=pl.CostEstimate(flops=flops, bytes_accessed=moved, transcendentals=0),
        **extra,
    )(*operands)


def shape(dims, dtype=F32):
    return jax.ShapeDtypeStruct(dims, dtype)


def split(value):
    high = value.astype(BF16)
    return high, (value - high.astype(F32)).astype(BF16)


def dot(a, b, dims):
    return lax.dot_general(a, b, (dims, ((), ())), preferred_element_type=F32)


def dot3(a, b, dims=NN):
    return dot(a[0], b[0], dims) + (dot(a[0], b[1], dims) + dot(a[1], b[0], dims))


def sigmoid(value):
    return 1.0 / (1.0 + jnp.exp(-value))


def lane_ids(rows, cols=LANES):
    return lax.broadcasted_iota(jnp.int32, (rows, cols), 1)


def row_ids(rows, cols=LANES):
    return lax.broadcasted_iota(jnp.int32, (rows, cols), 0)


def spread(columns, block, heads, size):
    first = block * heads
    lanes = lane_ids(columns.shape[0])
    wide = jnp.broadcast_to(columns[:, first : first + 1], (columns.shape[0], LANES))
    for k in range(1, heads):
        wide = jnp.where(lanes >= k * size, columns[:, first + k : first + k + 1], wide)
    return wide


def head_of(block, heads, size):
    inner = row_ids(LANES)
    target = lane_ids(LANES)
    result = jnp.zeros((LANES, LANES), F32)
    for k in range(heads):
        here = (inner >= k * size) & (inner < (k + 1) * size) & (target == block * heads + k)
        result = jnp.where(here, 1.0, result)
    return result.astype(BF16)


def stacked(value, heads, size):
    lanes = lane_ids(value.shape[0])
    return jnp.concatenate(
        [jnp.where((lanes >= k * size) & (lanes < (k + 1) * size), value, 0.0) for k in range(heads)],
        axis=0,
    )


def up8(value):
    return -(-value // 8) * 8


def notes_of(rows):
    return -(-rows // LANES)


def exponent_of(block):
    top = jnp.max(jnp.max(jnp.abs(block), axis=0, keepdims=True), axis=1, keepdims=True)
    return jnp.floor(jnp.log2(jnp.maximum(jnp.broadcast_to(top, (1, LANES)), 1e-30)))


def write_block(message, at, first, block, decays, exponent):
    rows = block.shape[0]
    padded = up8(rows)
    message[at, first : first + rows, :] = block * jnp.exp2(13.0 - exponent)
    if padded > rows:
        message[at, first + rows : first + padded, :] = jnp.zeros((padded - rows, LANES), F32)
    highs = [d.astype(BF16).astype(F32) for d in decays]
    lows = [d - h for d, h in zip(decays, highs)]
    place = row_ids(8)
    notes = jnp.broadcast_to(exponent, (8, LANES))
    for k, line in enumerate(highs + lows):
        notes = jnp.where(place == k, line, notes)
    message[at, first + padded : first + padded + 8, :] = notes


def decay_tables(last_exp, heads, size, rows, count):
    shift = size.bit_length() - 1
    tables = []
    for d in range(count):
        lines = []
        for k in range(notes_of(rows)):
            first = rows * d + LANES * k
            owner = lax.shift_right_logical(lane_ids(1) + first, shift)
            table = jnp.zeros((1, LANES), F32)
            for h in range(first // size, min(heads, (first + LANES - 1) // size + 1)):
                table = jnp.where(owner == h, last_exp[:, h : h + 1], table)
            lines.append(table)
        tables.append(lines)
    return tables


def pack_blocks(source, message, last_exp, size, rows, me=0):
    count = message.shape[0]
    tables = decay_tables(last_exp, source.shape[0] // size, size, rows, count)
    for d in range(count):
        block = source[rows * d : rows * (d + 1), :]
        write_block(message, me ^ d, 0, block, tables[d], exponent_of(block))


def decay_lines(message, at, rows):
    padded, lines = up8(rows), notes_of(rows)
    return [
        message[at, padded + k : padded + k + 1, :] + message[at, padded + lines + k : padded + lines + k + 1, :]
        for k in range(lines)
    ]


def decay_columns(message, rows):
    padded, lines = up8(rows), notes_of(rows)
    turned = [
        jnp.transpose(message[:, padded + k, :] + message[:, padded + lines + k, :]) for k in range(lines)
    ]
    return jnp.concatenate(turned, axis=0)[0:rows]


def read_block(message, at, rows):
    padded = up8(rows)
    return message[at, 0:rows, :] * jnp.exp2(message[at, padded + 7 : padded + 8, :] - 13.0)


def unpack_blocks(message, target, rows, me=0):
    for d in range(message.shape[0]):
        target[rows * d : rows * (d + 1), :] = read_block(message, me ^ d, rows)


def in_order(me_ref, held_ref, order_ref):
    for s in range(held_ref.shape[0]):
        order_ref[s] = held_ref[me_ref[0] ^ s]
    return order_ref


def total_kernel(rows, reverse, me_ref, held_ref, out_ref, order_ref):
    count = held_ref.shape[0]
    if reverse:
        held_ref = in_order(me_ref, held_ref, order_ref)
    columns = decay_columns(held_ref, rows)
    state = None
    for s in range(count - 1, -1, -1) if reverse else range(count):
        block = read_block(held_ref, s, rows)
        state = block if state is None else columns[:, s : s + 1] * state + block
    decays = decay_lines(held_ref, 0, rows)
    for s in range(1, count):
        decays = [a * b for a, b in zip(decays, decay_lines(held_ref, s, rows))]
    write_block(out_ref, 0, 0, state, decays, exponent_of(state))


def fold_kernel(rows, reverse, me_ref, held_ref, *refs):
    others, out_ref, order_ref = refs[:-2], refs[-2], refs[-1]
    count = held_ref.shape[0]
    if reverse:
        held_ref = in_order(me_ref, held_ref, order_ref)
    columns = decay_columns(held_ref, rows)
    state = jnp.zeros((rows, LANES), F32)
    for other in reversed(others):
        state = decay_columns(other, rows) * state + read_block(other, 0, rows)
    for s in range(count - 1, -1, -1) if reverse else range(count):
        write_block(out_ref, me_ref[0] ^ s if reverse else s, 0, state, [], exponent_of(state))
        if s != (0 if reverse else count - 1):
            state = columns[:, s : s + 1] * state + read_block(held_ref, s, rows)


def prepare_kernel(
    heads_in, size, rows, raw_ref, rim_ref, taps_ref, dt_ref, per_ref, act_ref, slope_ref, abc_ref, sbc_ref, step_ref, ld_ref, stept_ref, ldt_ref, dtw_ref, perw_ref, msg_ref,
    xs_ref, st_ref,
):
    length, channels = act_ref.shape
    blocks = channels // LANES

    def convolved(cols):
        xs_ref[0:8, cols] = rim_ref[:, cols].astype(F32)[8:16]
        xs_ref[8 : 8 + length, cols] = raw_ref[:, cols].astype(F32)
        pre = taps_ref[KERNEL : KERNEL + 1, cols] + taps_ref[0:1, cols] * xs_ref[5 : 5 + length, cols]
        for k in range(1, KERNEL):
            pre = pre + taps_ref[k : k + 1, cols] * xs_ref[5 + k : 5 + k + length, cols]
        gate = sigmoid(pre)
        return pre * gate, gate * (1.0 + pre * (1.0 - gate))

    for j in range(abc_ref.shape[1] // LANES):
        cols = slice(j * LANES, (j + 1) * LANES)
        value, slope = convolved(slice(channels + j * LANES, channels + (j + 1) * LANES))
        abc_ref[:, cols] = value
        sbc_ref[:, cols] = slope
    b_rows = split(abc_ref[:, 0:LANES])
    heads = dt_ref.shape[1]
    dtw_ref[...] = jnp.zeros_like(dtw_ref)
    dtw_ref[:, 0:heads] = dt_ref[...]
    perw_ref[...] = jnp.zeros_like(perw_ref)
    perw_ref[0:2, 0:heads] = per_ref[...]
    raised = dtw_ref[...] + perw_ref[0:1, :]
    dtw_ref[...] = raised
    step = jnp.maximum(raised, 0.0) + jnp.log1p(jnp.exp(-jnp.abs(raised)))
    lower = jnp.where(row_ids(length) >= lane_ids(length), 1.0, 0.0)
    ld = lax.dot_general(
        lower, step * -jnp.exp(perw_ref[1:2, :]), (NN, ((), ())), precision=HIGH, preferred_element_type=F32
    )
    step_ref[...] = step
    ld_ref[...] = ld
    stept_ref[...] = step.T
    ldt_ref[...] = ld.T
    last = ld[length - 1 : length]
    weight = jnp.exp(last - ld) * step
    for j in range(blocks):
        cols = slice(j * LANES, (j + 1) * LANES)
        value, slope = convolved(cols)
        act_ref[:, cols] = value
        slope_ref[:, cols] = slope
        scaled = value * spread(weight, j, heads_in, size)
        st_ref[cols, :] = dot3(split(scaled.T), b_rows)
    pack_blocks(st_ref, msg_ref, jnp.exp(last), size, rows)


def grad_kernel(heads_in, size, rows, me_ref, gy_ref, abc_ref, ld_ref, msg_ref, st_ref):
    length = gy_ref.shape[0]
    c_rows = split(abc_ref[:, LANES : 2 * LANES])
    grown = jnp.exp(ld_ref[...])
    for j in range(gy_ref.shape[1] // LANES):
        cols = slice(j * LANES, (j + 1) * LANES)
        scaled = gy_ref[:, cols] * spread(grown, j, heads_in, size)
        st_ref[cols, :] = dot3(split(scaled.T), c_rows)
    pack_blocks(st_ref, msg_ref, grown[length - 1 : length], size, rows, me_ref[0])


def gate_kernel(go_ref, *refs):
    w_refs, (gate_ref, gg_ref, gy_ref) = refs[:-3], refs[-3:]
    depth = w_refs[0].shape[1]
    grad = dot(w_refs[0][...], go_ref[:, 0:depth], NT)
    for k in range(1, len(w_refs)):
        grad = grad + dot(w_refs[k][...], go_ref[:, k * depth : (k + 1) * depth], NT)
    grad = grad.T
    gate = gate_ref[...].astype(F32)
    gg_ref[...] = grad
    gy_ref[...] = grad * (gate * sigmoid(gate))


def local_kernel(
    heads_in, size, act_ref, gy_ref, abc_ref, step_ref, ld_ref, stept_ref, ldt_ref, yw_ref, gw_ref, gbc_ref, sh_ref
):
    length = act_ref.shape[0]
    b_rows = split(abc_ref[:, 0:LANES])
    c_rows = split(abc_ref[:, LANES : 2 * LANES])
    scores = dot3(c_rows, b_rows, NT)
    turned = dot3(b_rows, c_rows, NT)
    causal = row_ids(length) >= lane_ids(length)
    causal_t = row_ids(length) <= lane_ids(length)
    sh_ref[...] = jnp.zeros_like(sh_ref)
    for j in range(act_ref.shape[1] // LANES):
        cols = slice(j * LANES, (j + 1) * LANES)
        mixes, mixes_t, steps = [], [], []
        for h in range(j * heads_in, (j + 1) * heads_in):
            column, row = ld_ref[:, h : h + 1], ldt_ref[h : h + 1, :]
            decays = jnp.exp(jnp.where(causal, column - row, -1e30))
            stepped = decays * stept_ref[h : h + 1, :]
            decays_t = jnp.exp(jnp.where(causal_t, row - column, -1e30))
            steps.append(stepped)
            mixes.append(stepped * scores)
            mixes_t.append(decays_t * turned * step_ref[:, h : h + 1])
        inputs = act_ref[:, cols]
        grad_y = gy_ref[:, cols]
        inputs_s = stacked(inputs, heads_in, size)
        grads_s = split(stacked(grad_y, heads_in, size))
        yw_ref[:, cols] = dot3(split(jnp.concatenate(mixes, axis=1)), split(inputs_s))
        gw_ref[:, cols] = dot3(split(jnp.concatenate(mixes_t, axis=1)), grads_s)
        products = dot3(grads_s, split(inputs), NT)
        total = sh_ref[...]
        for k in range(heads_in):
            total = total + steps[k] * products[k * length : (k + 1) * length]
        sh_ref[...] = total
    shared = sh_ref[...]
    gbc_ref[:, 0:LANES] = dot3(split(shared.T), c_rows)
    gbc_ref[:, LANES : 2 * LANES] = dot3(split(shared), b_rows)


def place_of(channel, share, size):
    if share > LANES:
        if channel < LANES * size:
            return channel // LANES, channel % LANES
        rest = share - LANES
        return (channel - LANES * size) // rest, LANES + (channel - LANES * size) % rest
    return channel // share, channel % share


def forward_kernel(
    heads_in, size, rows, msg_ref, act_ref, gate_ref, abc_ref, ld_ref, yw_ref, skip_ref, gt_ref, ys_ref, st_ref
):
    share = gt_ref.shape[1]
    unpack_blocks(msg_ref, st_ref, rows)
    c_rows = split(abc_ref[:, LANES : 2 * LANES])
    grown = jnp.exp(ld_ref[...])
    for j in range(act_ref.shape[1] // LANES):
        cols = slice(j * LANES, (j + 1) * LANES)
        carried = dot3(c_rows, split(st_ref[cols, :]), NT)
        within = yw_ref[:, cols] + spread(grown, j, heads_in, size) * carried
        ys_ref[:, cols] = within
        output = within + skip_ref[:, cols] * act_ref[:, cols]
        gate = gate_ref[:, cols].astype(F32)
        turned = (output * (gate * sigmoid(gate))).T.astype(BF16)
        for k in range(0, LANES, 16):
            to, at = place_of(j * LANES + k, share, gt_ref.shape[0])
            gt_ref[to, at : at + 16, :] = turned[k : k + 16]


def ahead_kernel(
    heads_in, size, rows, msg_ref, act_ref, gy_ref, ld_ref, gbcl_ref, ys_ref, gg_ref, gate_ref, skip_ref,
    gz_ref, yg_ref, gbc_ref, st_ref,
):
    unpack_blocks(msg_ref, st_ref, rows)
    grown = jnp.exp(ld_ref[...])
    sums = jnp.zeros(yg_ref.shape, F32)
    grad_c = gbcl_ref[:, LANES : 2 * LANES]
    for j in range(act_ref.shape[1] // LANES):
        cols = slice(j * LANES, (j + 1) * LANES)
        grad_y = gy_ref[:, cols]
        within = ys_ref[:, cols]
        gate = gate_ref[:, cols].astype(F32)
        opened = sigmoid(gate)
        output = within + skip_ref[:, cols] * act_ref[:, cols]
        gz_ref[:, cols] = (gg_ref[:, cols] * output * (opened * (1.0 + gate * (1.0 - opened)))).astype(BF16)
        onehot = head_of(j, heads_in, size)
        high, low = split(grad_y * within)
        sums = sums + (dot(high, onehot, NN) + dot(low, onehot, NN))
        grad_c = grad_c + dot3(split(spread(grown, j, heads_in, size) * grad_y), split(st_ref[cols, :]))
    yg_ref[...] = sums
    gbc_ref[:, 0:LANES] = gbcl_ref[:, 0:LANES]
    gbc_ref[:, LANES : 2 * LANES] = grad_c


def backward_kernel(
    heads_in, size, rows, me_ref, msg_ref, msgf_ref, act_ref, slope_ref, gy_ref, abc_ref, step_ref, ld_ref, gw_ref,
    gbcl_ref, yg_ref, skip_ref, dtw_ref, perw_ref, gx_ref, gbc_ref, gdt_ref,
    ca_ref, st_ref, cs_ref,
):
    length = act_ref.shape[0]
    unpack_blocks(msg_ref, ca_ref, rows, me_ref[0])
    unpack_blocks(msgf_ref, st_ref, rows)
    b_rows = split(abc_ref[:, 0:LANES])
    ld = ld_ref[...]
    step = step_ref[...]
    last = ld[length - 1 : length]
    weight = jnp.exp(last - ld) * step
    sums = jnp.zeros((length, LANES), F32)
    leaving = jnp.zeros((8, LANES), F32)
    grad_b = gbcl_ref[:, 0:LANES]
    cs_ref[...] = jnp.zeros_like(cs_ref)
    for j in range(act_ref.shape[1] // LANES):
        cols = slice(j * LANES, (j + 1) * LANES)
        inputs = act_ref[:, cols]
        grad_y = gy_ref[:, cols]
        carry = ca_ref[cols, :]
        state = st_ref[cols, :]
        carry_s = split(carry)
        wide = spread(weight, j, heads_in, size)
        gone = wide * dot3(b_rows, carry_s, NT)
        grad_in = gw_ref[:, cols] + gone
        gx_ref[:, cols] = ((skip_ref[:, cols] * grad_y + grad_in) * slope_ref[:, cols]).astype(BF16)
        onehot = head_of(j, heads_in, size)
        high, low = split(inputs * grad_in)
        sums = sums + (dot(high, onehot, NN) + dot(low, onehot, NN))
        folded = jnp.sum((inputs * gone).reshape(length // 8, 8, LANES), axis=0)
        high, low = split(folded)
        leaving = leaving + (dot(high, onehot, NN) + dot(low, onehot, NN))
        product = carry * state
        for k in range(heads_in):
            h = j * heads_in + k
            cs_ref[h : h + 1, :] = jnp.sum(product[k * size : (k + 1) * size], axis=0, keepdims=True)
        grad_b = grad_b + dot3(split(wide * inputs), carry_s)
    gbc_ref[:, 0:LANES] = grad_b
    gbc_ref[:, LANES : 2 * LANES] = gbcl_ref[:, LANES : 2 * LANES]
    both = lax.dot_general(
        jnp.ones((8, LANES), F32), cs_ref[...], (NT, ((), ())), precision=HIGH, preferred_element_type=F32
    )
    constant = jnp.sum(leaving, axis=0, keepdims=True) + jnp.exp(last) * both[0:1]
    upper = jnp.where(row_ids(length) <= lane_ids(length), 1.0, 0.0)
    grad_rate = constant + lax.dot_general(
        upper, yg_ref[...] - sums, (NN, ((), ())), precision=HIGH, preferred_element_type=F32
    )
    grad_step = sums / step - jnp.exp(perw_ref[1:2, :]) * grad_rate
    gdt_ref[...] = (grad_step * sigmoid(dtw_ref[...]))[:, 0 : gdt_ref.shape[1]]


def product_kernel(rows, held_ref, *refs):
    go_refs, out_ref, lhs_ref = refs[:-2], refs[-2], refs[-1]
    size, share, length = held_ref.shape

    @pl.when(pl.program_id(0) == 0)
    def _():
        for s in range(size):
            lhs_ref[:, s * length : (s + 1) * length] = held_ref[s]

    depth = go_refs[0].shape[0]
    result = dot(lhs_ref[:, 0:depth], go_refs[0][...], NN)
    for k in range(1, len(go_refs)):
        result = result + dot(lhs_ref[:, k * depth : (k + 1) * depth], go_refs[k][...], NN)
    result = result.T
    for d in range(out_ref.shape[0]):
        block = result[rows * d : rows * (d + 1)]
        if share > LANES:
            rest = share - LANES
            across = LANES // rest
            out_ref[d, 0:rows, :] = block[:, 0:LANES].astype(BF16)
            for k in range(0, rows // 16, across):
                pieces = [block[16 * m : 16 * m + 16, LANES:] for m in range(k, min(k + across, rows // 16))]
                if len(pieces) < across:
                    pieces.append(jnp.zeros((16, LANES - rest * len(pieces)), F32))
                at = rows + 16 * (k // across)
                out_ref[d, at : at + 16, :] = jnp.concatenate(pieces, axis=1).astype(BF16)
        else:
            out_ref[d] = block.astype(BF16)


def assemble_kernel(rows, size, share, parts_ref, out_ref):
    count = parts_ref.shape[0]

    def total(c, first, last):
        found = parts_ref[c, first:last, :].astype(F32)
        for s in range(c + size, count, size):
            found = found + parts_ref[s, first:last, :].astype(F32)
        return found

    if share > LANES:
        rest = share - LANES
        across = LANES // rest
        for c in range(size):
            out_ref[:, c * LANES : (c + 1) * LANES] = total(c, 0, rows)
            at = size * LANES + rest * c
            for k in range(0, rows // 16, across):
                extra = total(c, rows + 16 * (k // across), rows + 16 * (k // across) + 16)
                for m in range(k, min(k + across, rows // 16)):
                    lanes = slice(rest * (m - k), rest * (m - k + 1))
                    out_ref[16 * m : 16 * m + 16, at : at + rest] = extra[:, lanes]
    else:
        for c in range(size):
            out_ref[:, c * share : (c + 1) * share] = total(c, 0, rows)


def exchange(message, groups=None):
    half = message.astype(jnp.float16)
    return lax.all_to_all(half, "ctx", 0, 0, axis_index_groups=groups, tiled=True)


def swapped(message):
    half = message.astype(jnp.float16)
    count = lax.axis_size("ctx")
    slots = [half[0:1]]
    for m in range(1, message.shape[0]):
        slots.append(lax.ppermute(half[m : m + 1], "ctx", [(at, at ^ m) for at in range(count)]))
    return jnp.concatenate(slots).astype(F32)


def groups_of(count, size):
    return [list(range(at, at + size)) for at in range(0, count, size)]


def group_total(me, held, rows, reverse):
    (total,) = call(
        functools.partial(total_kernel, rows, reverse),
        [shape((1, *held.shape[1:]))],
        [me, held],
        4 * held.size,
        12,
        [pltpu.VMEM(held.shape, F32)],
        [SMEM, VMEM],
    )
    return total.astype(jnp.float16)


def enter(me, held, total, rows, reverse):
    size = held.shape[0]
    count = lax.axis_size("ctx")
    others = []
    for hops in range(size, count, size):
        pairs = [(at, at + hops) for at in range(count - hops)]
        if reverse:
            pairs = [(b, a) for a, b in pairs]
        others.append(lax.ppermute(total, "ctx", pairs).astype(F32))
    (folded,) = call(
        functools.partial(fold_kernel, rows, reverse),
        [shape(held.shape)],
        [me, held, *others],
        8 * held.size,
        12,
        [pltpu.VMEM(held.shape, F32)],
        [SMEM] + [VMEM] * (1 + len(others)),
    )
    return folded


def group_of(count):
    for size in (16, 8, 4, 2):
        if count % size == 0:
            return size
    return 1


def from_behind(value, axis):
    count = lax.axis_size(axis)
    return lax.ppermute(value, axis, [(source, source + 1) for source in range(count - 1)])


def per_device(
    x_raw,
    bc_raw,
    gate_branch,
    dt_raw,
    conv_x,
    conv_x_bias,
    conv_bc,
    conv_bc_bias,
    dt_bias,
    a_log,
    d_skip,
    out_weight,
    grad_out,
):
    length, head_count = dt_raw.shape
    channels = x_raw.shape[1]
    width = grad_out.shape[1]
    head_size = channels // head_count
    heads_in = LANES // head_size
    count = lax.axis_size("ctx")
    plane = min(8, group_of(count))
    planes = groups_of(count, plane)
    rows = channels // plane
    size = group_of(count)
    share = channels // size
    groups = groups_of(count, size)
    gathered = lax.all_gather(grad_out, "ctx", axis_index_groups=groups, tiled=True)

    raw = jnp.concatenate([x_raw, bc_raw], axis=1)
    taps = jnp.concatenate(
        [
            jnp.concatenate([conv_x, conv_bc], axis=1),
            jnp.concatenate([conv_x_bias, conv_bc_bias])[None, :],
        ]
    )
    rim = from_behind(raw[length - 16 :], "ctx")
    skip = jnp.repeat(d_skip, head_size)[None, :]
    whole = (length, channels)
    square = (length, LANES)
    block = up8(rows) + 8
    stored = pltpu.VMEM((channels, LANES), F32)
    unit = 2 * length * channels * LANES
    me = (lax.axis_index("ctx") % plane).astype(jnp.int32).reshape(1)

    act_x, slope_x, act_bc, slope_bc, step, ld, step_t, ld_t, raised, per_head, message = call(
        functools.partial(prepare_kernel, heads_in, head_size, rows),
        [shape(whole), shape(whole), shape(bc_raw.shape), shape(bc_raw.shape)]
        + [shape(square)] * 2
        + [shape((LANES, length))] * 2
        + [shape(square), shape((8, LANES))]
        + [shape((plane, block, LANES))],
        [
            raw,
            rim,
            taps,
            dt_raw,
            jnp.stack([dt_bias, a_log]),
        ],
        20 * unit,
        20,
        [
            pltpu.VMEM((length + 8, channels + bc_raw.shape[1]), F32),
            stored,
        ],
    )
    message, grad_out_then = lax.optimization_barrier((message, grad_out))
    held_state = exchange(message, planes).astype(F32)
    part = 640 if channels % 640 == 0 else channels
    grad_gated, grad_y = pl.pallas_call(
        gate_kernel,
        grid=(channels // part,),
        in_specs=[
            pl.BlockSpec((length, width), lambda i: (0, 0)),
        ]
        + [
            pl.BlockSpec((part, width // STREAMS), functools.partial(lambda k, i: (i, k), k))
            for k in range(STREAMS)
        ]
        + [pl.BlockSpec((length, part), lambda i: (0, i))],
        out_specs=(pl.BlockSpec((length, part), lambda i: (0, i)), pl.BlockSpec((length, part), lambda i: (0, i))),
        out_shape=(shape(whole), shape(whole)),
        compiler_params=pltpu.CompilerParams(vmem_limit_bytes=52 * MIB),
        cost_estimate=pl.CostEstimate(
            flops=2 * length * channels * width, bytes_accessed=2 * channels * width, transcendentals=0
        ),
    )(grad_out_then, *[out_weight] * STREAMS, gate_branch)
    (message,) = call(
        functools.partial(grad_kernel, heads_in, head_size, rows),
        [shape((plane, block, LANES))],
        [me, grad_y, act_bc, ld],
        10 * unit,
        12,
        [stored],
        [SMEM] + [VMEM] * 3,
    )
    held_carry = swapped(message)
    total, ld_t_then = lax.optimization_barrier((group_total(me, held_state, rows, False), ld_t))
    y_within, grad_within, grad_bc_within = call(
        functools.partial(local_kernel, heads_in, head_size),
        [shape(whole), shape(whole), shape(act_bc.shape)],
        [act_x, grad_y, act_bc, step, ld, step_t, ld_t_then],
        40 * unit,
        16,
        [pltpu.VMEM(square, F32)],
    )
    folded, held_carry = lax.optimization_barrier((enter(me, held_state, total, rows, False), held_carry))
    entered = enter(me, held_carry, group_total(me, held_carry, rows, True), rows, True)
    state_message = exchange(folded, planes).astype(F32)
    gated, y_ahead = call(
        functools.partial(forward_kernel, heads_in, head_size, rows),
        [shape((size, share, length), BF16), shape(whole)],
        [state_message, act_x, gate_branch, act_bc, ld, y_within, skip],
        20 * unit,
        16,
        [stored],
    )
    gated, gathered, y_ahead = lax.optimization_barrier((gated, gathered, y_ahead))
    held = lax.all_to_all(gated, "ctx", 0, 0, axis_index_groups=groups, tiled=True)
    grad_z, y_sums, grad_bc_ahead = call(
        functools.partial(ahead_kernel, heads_in, head_size, rows),
        [shape(whole, BF16), shape(square), shape(act_bc.shape)],
        [state_message, act_x, grad_y, ld, grad_bc_within, y_ahead, grad_gated, gate_branch, skip],
        20 * unit,
        16,
        [stored],
    )
    held, y_sums = lax.optimization_barrier((held, y_sums))
    out_rows = width // count
    part = width
    for candidate in (640, 1280):
        if width % candidate == 0 and candidate % out_rows == 0:
            part = candidate
            break
    dims = (out_rows, share)
    if share > LANES:
        dims = (out_rows + 16 * (-(-(out_rows // 16) // (LANES // (share - LANES)))), LANES)
    partial = pl.pallas_call(
        functools.partial(product_kernel, out_rows),
        grid=(width // part,),
        in_specs=[
            pl.BlockSpec((size, share, length), lambda i: (0, 0, 0)),
        ]
        + [
            pl.BlockSpec((size * length // STREAMS, part), functools.partial(lambda k, i: (k, i), k))
            for k in range(STREAMS)
        ],
        out_specs=pl.BlockSpec((part // out_rows, *dims), lambda i: (i, 0, 0)),
        out_shape=shape((count, *dims), BF16),
        scratch_shapes=[pltpu.VMEM((share, size * length), BF16)],
        compiler_params=pltpu.CompilerParams(vmem_limit_bytes=48 * MIB),
        cost_estimate=pl.CostEstimate(
            flops=2 * size * length * share * width, bytes_accessed=2 * size * length * width, transcendentals=0
        ),
    )(held, *[gathered] * STREAMS)
    partial, entered = lax.optimization_barrier((partial, entered))
    parts = lax.all_to_all(partial, "ctx", 0, 0, tiled=True)
    carry_message = swapped(entered)
    (weight_grad,) = call(
        functools.partial(assemble_kernel, out_rows, size, share),
        [shape((out_rows, channels))],
        [parts],
        2 * parts.size,
        12,
    )
    grad_x_conv, grad_bc, grad_dt_raw = call(
        functools.partial(backward_kernel, heads_in, head_size, rows),
        [shape(whole, BF16), shape(act_bc.shape), shape(dt_raw.shape)],
        [
            me,
            carry_message,
            state_message,
            act_x,
            slope_x,
            grad_y,
            act_bc,
            step,
            ld,
            grad_within,
            grad_bc_ahead,
            y_sums,
            skip,
            raised,
            per_head,
        ],
        40 * unit,
        28,
        [stored, stored, pltpu.VMEM((LANES, LANES), F32)],
        [SMEM] + [VMEM] * 14,
    )
    grad_bc_conv = (lax.psum(grad_bc, "tp") * slope_bc).astype(BF16)
    return (grad_x_conv, grad_bc_conv, grad_z, grad_dt_raw, weight_grad)


def solution(mesh):
    placed = (
        P("ctx", "tp"),
        P("ctx", None),
        P("ctx", "tp"),
        P("ctx", "tp"),
        P(None, "tp"),
        P("tp"),
        P(),
        P(),
        P("tp"),
        P("tp"),
        P("tp"),
        P("tp", None),
        P("ctx", None),
    )
    return jax.shard_map(
        per_device,
        mesh=mesh,
        in_specs=placed,
        out_specs=(P("ctx", "tp"), P("ctx", None), P("ctx", "tp"), P("ctx", "tp"), P("ctx", "tp")),
        check_vma=False,
    )
```

```python
import functools

import jax
import jax.numpy as jnp
from jax import lax
from jax.experimental import pallas as pl
from jax.experimental.pallas import tpu as pltpu
from jax.sharding import PartitionSpec as P

KERNEL = 4
LANES = 128
F32 = jnp.float32
BF16 = jnp.bfloat16
NN = ((1,), (0,))
NT = ((1,), (1,))
HIGH = lax.Precision.HIGHEST
SMEM = pl.BlockSpec(memory_space=pltpu.SMEM)
VMEM = pl.BlockSpec(memory_space=pltpu.VMEM)
MIB = 1024 * 1024
STREAMS = 4


def call(kernel, out_shapes, operands, flops, vmem, scratch=(), specs=None):
    extra = {} if specs is None else {"in_specs": specs}
    moved = sum(a.size * a.dtype.itemsize for a in (*operands, *out_shapes))
    return pl.pallas_call(
        kernel,
        out_shape=tuple(out_shapes),
        scratch_shapes=list(scratch),
        compiler_params=pltpu.CompilerParams(vmem_limit_bytes=vmem * MIB),
        cost_estimate=pl.CostEstimate(flops=flops, bytes_accessed=moved, transcendentals=0),
        **extra,
    )(*operands)


def shape(dims, dtype=F32):
    return jax.ShapeDtypeStruct(dims, dtype)


def split(value):
    high = value.astype(BF16)
    return high, (value - high.astype(F32)).astype(BF16)


def dot(a, b, dims):
    return lax.dot_general(a, b, (dims, ((), ())), preferred_element_type=F32)


def dot3(a, b, dims=NN):
    return dot(a[0], b[0], dims) + (dot(a[0], b[1], dims) + dot(a[1], b[0], dims))


def sigmoid(value):
    return 1.0 / (1.0 + jnp.exp(-value))


def lane_ids(rows, cols=LANES):
    return lax.broadcasted_iota(jnp.int32, (rows, cols), 1)


def row_ids(rows, cols=LANES):
    return lax.broadcasted_iota(jnp.int32, (rows, cols), 0)


def spread(columns, block, heads, size):
    first = block * heads
    lanes = lane_ids(columns.shape[0])
    wide = jnp.broadcast_to(columns[:, first : first + 1], (columns.shape[0], LANES))
    for k in range(1, heads):
        wide = jnp.where(lanes >= k * size, columns[:, first + k : first + k + 1], wide)
    return wide


def head_of(block, heads, size):
    inner = row_ids(LANES)
    target = lane_ids(LANES)
    result = jnp.zeros((LANES, LANES), F32)
    for k in range(heads):
        here = (inner >= k * size) & (inner < (k + 1) * size) & (target == block * heads + k)
        result = jnp.where(here, 1.0, result)
    return result.astype(BF16)


def stacked(value, heads, size):
    lanes = lane_ids(value.shape[0])
    return jnp.concatenate(
        [jnp.where((lanes >= k * size) & (lanes < (k + 1) * size), value, 0.0) for k in range(heads)],
        axis=0,
    )


def up8(value):
    return -(-value // 8) * 8


def notes_of(rows):
    return -(-rows // LANES)


def exponent_of(block):
    top = jnp.max(jnp.max(jnp.abs(block), axis=0, keepdims=True), axis=1, keepdims=True)
    return jnp.floor(jnp.log2(jnp.maximum(jnp.broadcast_to(top, (1, LANES)), 1e-30)))


def write_block(message, at, first, block, decays, exponent):
    rows = block.shape[0]
    padded = up8(rows)
    message[at, first : first + rows, :] = block * jnp.exp2(13.0 - exponent)
    if padded > rows:
        message[at, first + rows : first + padded, :] = jnp.zeros((padded - rows, LANES), F32)
    highs = [d.astype(BF16).astype(F32) for d in decays]
    lows = [d - h for d, h in zip(decays, highs)]
    place = row_ids(8)
    notes = jnp.broadcast_to(exponent, (8, LANES))
    for k, line in enumerate(highs + lows):
        notes = jnp.where(place == k, line, notes)
    message[at, first + padded : first + padded + 8, :] = notes


def decay_tables(last_exp, heads, size, rows, count):
    shift = size.bit_length() - 1
    tables = []
    for d in range(count):
        lines = []
        for k in range(notes_of(rows)):
            first = rows * d + LANES * k
            owner = lax.shift_right_logical(lane_ids(1) + first, shift)
            table = jnp.zeros((1, LANES), F32)
            for h in range(first // size, min(heads, (first + LANES - 1) // size + 1)):
                table = jnp.where(owner == h, last_exp[:, h : h + 1], table)
            lines.append(table)
        tables.append(lines)
    return tables


def pack_blocks(source, message, last_exp, size, rows):
    count = message.shape[0]
    tables = decay_tables(last_exp, source.shape[0] // size, size, rows, count)
    for d in range(count):
        block = source[rows * d : rows * (d + 1), :]
        write_block(message, d, 0, block, tables[d], exponent_of(block))


def decay_lines(message, at, rows):
    padded, lines = up8(rows), notes_of(rows)
    return [
        message[at, padded + k : padded + k + 1, :] + message[at, padded + lines + k : padded + lines + k + 1, :]
        for k in range(lines)
    ]


def decay_columns(message, rows):
    padded, lines = up8(rows), notes_of(rows)
    turned = [
        jnp.transpose(message[:, padded + k, :] + message[:, padded + lines + k, :]) for k in range(lines)
    ]
    return jnp.concatenate(turned, axis=0)[0:rows]


def read_block(message, at, rows):
    padded = up8(rows)
    return message[at, 0:rows, :] * jnp.exp2(message[at, padded + 7 : padded + 8, :] - 13.0)


def unpack_blocks(message, target, rows, me=0):
    for d in range(message.shape[0]):
        target[rows * d : rows * (d + 1), :] = read_block(message, me ^ d, rows)


def total_kernel(rows, reverse, held_ref, out_ref):
    count = held_ref.shape[0]
    columns = decay_columns(held_ref, rows)
    state = None
    for s in range(count - 1, -1, -1) if reverse else range(count):
        block = read_block(held_ref, s, rows)
        state = block if state is None else columns[:, s : s + 1] * state + block
    decays = decay_lines(held_ref, 0, rows)
    for s in range(1, count):
        decays = [a * b for a, b in zip(decays, decay_lines(held_ref, s, rows))]
    write_block(out_ref, 0, 0, state, decays, exponent_of(state))


def fold_kernel(rows, reverse, me_ref, held_ref, *refs):
    others, out_ref = refs[:-1], refs[-1]
    count = held_ref.shape[0]
    columns = decay_columns(held_ref, rows)
    state = jnp.zeros((rows, LANES), F32)
    for other in reversed(others):
        state = decay_columns(other, rows) * state + read_block(other, 0, rows)
    for s in range(count - 1, -1, -1) if reverse else range(count):
        write_block(out_ref, me_ref[0] ^ s if reverse else s, 0, state, [], exponent_of(state))
        if s != (0 if reverse else count - 1):
            state = columns[:, s : s + 1] * state + read_block(held_ref, s, rows)


def prepare_kernel(
    heads_in, size, rows, raw_ref, rim_ref, taps_ref, dt_ref, per_ref, act_ref, slope_ref, abc_ref, sbc_ref, step_ref, ld_ref, stept_ref, ldt_ref, dtw_ref, perw_ref, msg_ref,
    xs_ref, st_ref,
):
    length, channels = act_ref.shape
    blocks = channels // LANES

    def convolved(cols):
        xs_ref[0:8, cols] = rim_ref[:, cols].astype(F32)[8:16]
        xs_ref[8 : 8 + length, cols] = raw_ref[:, cols].astype(F32)
        pre = taps_ref[KERNEL : KERNEL + 1, cols] + taps_ref[0:1, cols] * xs_ref[5 : 5 + length, cols]
        for k in range(1, KERNEL):
            pre = pre + taps_ref[k : k + 1, cols] * xs_ref[5 + k : 5 + k + length, cols]
        gate = sigmoid(pre)
        return pre * gate, gate * (1.0 + pre * (1.0 - gate))

    for j in range(abc_ref.shape[1] // LANES):
        cols = slice(j * LANES, (j + 1) * LANES)
        value, slope = convolved(slice(channels + j * LANES, channels + (j + 1) * LANES))
        abc_ref[:, cols] = value
        sbc_ref[:, cols] = slope
    b_rows = split(abc_ref[:, 0:LANES])
    heads = dt_ref.shape[1]
    dtw_ref[...] = jnp.zeros_like(dtw_ref)
    dtw_ref[:, 0:heads] = dt_ref[...]
    perw_ref[...] = jnp.zeros_like(perw_ref)
    perw_ref[0:2, 0:heads] = per_ref[...]
    raised = dtw_ref[...] + perw_ref[0:1, :]
    dtw_ref[...] = raised
    step = jnp.maximum(raised, 0.0) + jnp.log1p(jnp.exp(-jnp.abs(raised)))
    lower = jnp.where(row_ids(length) >= lane_ids(length), 1.0, 0.0)
    ld = lax.dot_general(
        lower, step * -jnp.exp(perw_ref[1:2, :]), (NN, ((), ())), precision=HIGH, preferred_element_type=F32
    )
    step_ref[...] = step
    ld_ref[...] = ld
    stept_ref[...] = step.T
    ldt_ref[...] = ld.T
    last = ld[length - 1 : length]
    weight = jnp.exp(last - ld) * step
    for j in range(blocks):
        cols = slice(j * LANES, (j + 1) * LANES)
        value, slope = convolved(cols)
        act_ref[:, cols] = value
        slope_ref[:, cols] = slope
        scaled = value * spread(weight, j, heads_in, size)
        st_ref[cols, :] = dot3(split(scaled.T), b_rows)
    pack_blocks(st_ref, msg_ref, jnp.exp(last), size, rows)


def grad_kernel(heads_in, size, rows, gy_ref, abc_ref, ld_ref, msg_ref, st_ref):
    length = gy_ref.shape[0]
    c_rows = split(abc_ref[:, LANES : 2 * LANES])
    grown = jnp.exp(ld_ref[...])
    for j in range(gy_ref.shape[1] // LANES):
        cols = slice(j * LANES, (j + 1) * LANES)
        scaled = gy_ref[:, cols] * spread(grown, j, heads_in, size)
        st_ref[cols, :] = dot3(split(scaled.T), c_rows)
    pack_blocks(st_ref, msg_ref, grown[length - 1 : length], size, rows)


def gate_kernel(go_ref, *refs):
    w_refs, (gate_ref, gg_ref, gy_ref) = refs[:-3], refs[-3:]
    depth = w_refs[0].shape[1]
    grad = dot(w_refs[0][...], go_ref[:, 0:depth], NT)
    for k in range(1, len(w_refs)):
        grad = grad + dot(w_refs[k][...], go_ref[:, k * depth : (k + 1) * depth], NT)
    grad = grad.T
    gate = gate_ref[...].astype(F32)
    gg_ref[...] = grad
    gy_ref[...] = grad * (gate * sigmoid(gate))


def local_kernel(
    heads_in, size, act_ref, gy_ref, abc_ref, step_ref, ld_ref, stept_ref, ldt_ref, yw_ref, gw_ref, gbc_ref, sh_ref
):
    length = act_ref.shape[0]
    b_rows = split(abc_ref[:, 0:LANES])
    c_rows = split(abc_ref[:, LANES : 2 * LANES])
    scores = dot3(c_rows, b_rows, NT)
    turned = dot3(b_rows, c_rows, NT)
    causal = row_ids(length) >= lane_ids(length)
    causal_t = row_ids(length) <= lane_ids(length)
    sh_ref[...] = jnp.zeros_like(sh_ref)
    for j in range(act_ref.shape[1] // LANES):
        cols = slice(j * LANES, (j + 1) * LANES)
        mixes, mixes_t, steps = [], [], []
        for h in range(j * heads_in, (j + 1) * heads_in):
            column, row = ld_ref[:, h : h + 1], ldt_ref[h : h + 1, :]
            decays = jnp.exp(jnp.where(causal, column - row, -1e30))
            stepped = decays * stept_ref[h : h + 1, :]
            decays_t = jnp.exp(jnp.where(causal_t, row - column, -1e30))
            steps.append(stepped)
            mixes.append(stepped * scores)
            mixes_t.append(decays_t * turned * step_ref[:, h : h + 1])
        inputs = act_ref[:, cols]
        grad_y = gy_ref[:, cols]
        inputs_s = stacked(inputs, heads_in, size)
        grads_s = split(stacked(grad_y, heads_in, size))
        yw_ref[:, cols] = dot3(split(jnp.concatenate(mixes, axis=1)), split(inputs_s))
        gw_ref[:, cols] = dot3(split(jnp.concatenate(mixes_t, axis=1)), grads_s)
        products = dot3(grads_s, split(inputs), NT)
        total = sh_ref[...]
        for k in range(heads_in):
            total = total + steps[k] * products[k * length : (k + 1) * length]
        sh_ref[...] = total
    shared = sh_ref[...]
    gbc_ref[:, 0:LANES] = dot3(split(shared.T), c_rows)
    gbc_ref[:, LANES : 2 * LANES] = dot3(split(shared), b_rows)


def place_of(channel, share, size):
    if share > LANES:
        if channel < LANES * size:
            return channel // LANES, channel % LANES
        rest = share - LANES
        return (channel - LANES * size) // rest, LANES + (channel - LANES * size) % rest
    return channel // share, channel % share


def forward_kernel(
    heads_in, size, rows, msg_ref, act_ref, gate_ref, abc_ref, ld_ref, yw_ref, skip_ref, gt_ref, ys_ref, st_ref
):
    share = gt_ref.shape[1]
    unpack_blocks(msg_ref, st_ref, rows)
    c_rows = split(abc_ref[:, LANES : 2 * LANES])
    grown = jnp.exp(ld_ref[...])
    for j in range(act_ref.shape[1] // LANES):
        cols = slice(j * LANES, (j + 1) * LANES)
        carried = dot3(c_rows, split(st_ref[cols, :]), NT)
        within = yw_ref[:, cols] + spread(grown, j, heads_in, size) * carried
        ys_ref[:, cols] = within
        output = within + skip_ref[:, cols] * act_ref[:, cols]
        gate = gate_ref[:, cols].astype(F32)
        turned = (output * (gate * sigmoid(gate))).T.astype(BF16)
        for k in range(0, LANES, 16):
            to, at = place_of(j * LANES + k, share, gt_ref.shape[0])
            gt_ref[to, at : at + 16, :] = turned[k : k + 16]


def ahead_kernel(
    heads_in, size, rows, msg_ref, act_ref, gy_ref, ld_ref, gbcl_ref, ys_ref, gg_ref, gate_ref, skip_ref,
    gz_ref, yg_ref, gbc_ref, st_ref,
):
    unpack_blocks(msg_ref, st_ref, rows)
    grown = jnp.exp(ld_ref[...])
    sums = jnp.zeros(yg_ref.shape, F32)
    grad_c = gbcl_ref[:, LANES : 2 * LANES]
    for j in range(act_ref.shape[1] // LANES):
        cols = slice(j * LANES, (j + 1) * LANES)
        grad_y = gy_ref[:, cols]
        within = ys_ref[:, cols]
        gate = gate_ref[:, cols].astype(F32)
        opened = sigmoid(gate)
        output = within + skip_ref[:, cols] * act_ref[:, cols]
        gz_ref[:, cols] = (gg_ref[:, cols] * output * (opened * (1.0 + gate * (1.0 - opened)))).astype(BF16)
        onehot = head_of(j, heads_in, size)
        high, low = split(grad_y * within)
        sums = sums + (dot(high, onehot, NN) + dot(low, onehot, NN))
        grad_c = grad_c + dot3(split(spread(grown, j, heads_in, size) * grad_y), split(st_ref[cols, :]))
    yg_ref[...] = sums
    gbc_ref[:, 0:LANES] = gbcl_ref[:, 0:LANES]
    gbc_ref[:, LANES : 2 * LANES] = grad_c


def backward_kernel(
    heads_in, size, rows, me_ref, msg_ref, msgf_ref, act_ref, slope_ref, gy_ref, abc_ref, step_ref, ld_ref, gw_ref,
    gbcl_ref, yg_ref, skip_ref, dtw_ref, perw_ref, gx_ref, gbc_ref, gdt_ref,
    ca_ref, st_ref, cs_ref,
):
    length = act_ref.shape[0]
    unpack_blocks(msg_ref, ca_ref, rows, me_ref[0])
    unpack_blocks(msgf_ref, st_ref, rows)
    b_rows = split(abc_ref[:, 0:LANES])
    ld = ld_ref[...]
    step = step_ref[...]
    last = ld[length - 1 : length]
    weight = jnp.exp(last - ld) * step
    sums = jnp.zeros((length, LANES), F32)
    leaving = jnp.zeros((8, LANES), F32)
    grad_b = gbcl_ref[:, 0:LANES]
    cs_ref[...] = jnp.zeros_like(cs_ref)
    for j in range(act_ref.shape[1] // LANES):
        cols = slice(j * LANES, (j + 1) * LANES)
        inputs = act_ref[:, cols]
        grad_y = gy_ref[:, cols]
        carry = ca_ref[cols, :]
        state = st_ref[cols, :]
        carry_s = split(carry)
        wide = spread(weight, j, heads_in, size)
        gone = wide * dot3(b_rows, carry_s, NT)
        grad_in = gw_ref[:, cols] + gone
        gx_ref[:, cols] = ((skip_ref[:, cols] * grad_y + grad_in) * slope_ref[:, cols]).astype(BF16)
        onehot = head_of(j, heads_in, size)
        high, low = split(inputs * grad_in)
        sums = sums + (dot(high, onehot, NN) + dot(low, onehot, NN))
        folded = jnp.sum((inputs * gone).reshape(length // 8, 8, LANES), axis=0)
        high, low = split(folded)
        leaving = leaving + (dot(high, onehot, NN) + dot(low, onehot, NN))
        product = carry * state
        for k in range(heads_in):
            h = j * heads_in + k
            cs_ref[h : h + 1, :] = jnp.sum(product[k * size : (k + 1) * size], axis=0, keepdims=True)
        grad_b = grad_b + dot3(split(wide * inputs), carry_s)
    gbc_ref[:, 0:LANES] = grad_b
    gbc_ref[:, LANES : 2 * LANES] = gbcl_ref[:, LANES : 2 * LANES]
    both = lax.dot_general(
        jnp.ones((8, LANES), F32), cs_ref[...], (NT, ((), ())), precision=HIGH, preferred_element_type=F32
    )
    constant = jnp.sum(leaving, axis=0, keepdims=True) + jnp.exp(last) * both[0:1]
    upper = jnp.where(row_ids(length) <= lane_ids(length), 1.0, 0.0)
    grad_rate = constant + lax.dot_general(
        upper, yg_ref[...] - sums, (NN, ((), ())), precision=HIGH, preferred_element_type=F32
    )
    grad_step = sums / step - jnp.exp(perw_ref[1:2, :]) * grad_rate
    gdt_ref[...] = (grad_step * sigmoid(dtw_ref[...]))[:, 0 : gdt_ref.shape[1]]


def product_kernel(rows, held_ref, *refs):
    go_refs, out_ref, lhs_ref = refs[:-2], refs[-2], refs[-1]
    size, share, length = held_ref.shape

    @pl.when(pl.program_id(0) == 0)
    def _():
        for s in range(size):
            lhs_ref[:, s * length : (s + 1) * length] = held_ref[s]

    depth = go_refs[0].shape[0]
    result = dot(lhs_ref[:, 0:depth], go_refs[0][...], NN)
    for k in range(1, len(go_refs)):
        result = result + dot(lhs_ref[:, k * depth : (k + 1) * depth], go_refs[k][...], NN)
    result = result.T
    for d in range(out_ref.shape[0]):
        block = result[rows * d : rows * (d + 1)]
        if share > LANES:
            rest = share - LANES
            across = LANES // rest
            out_ref[d, 0:rows, :] = block[:, 0:LANES].astype(BF16)
            for k in range(0, rows // 16, across):
                pieces = [block[16 * m : 16 * m + 16, LANES:] for m in range(k, min(k + across, rows // 16))]
                if len(pieces) < across:
                    pieces.append(jnp.zeros((16, LANES - rest * len(pieces)), F32))
                at = rows + 16 * (k // across)
                out_ref[d, at : at + 16, :] = jnp.concatenate(pieces, axis=1).astype(BF16)
        else:
            out_ref[d] = block.astype(BF16)


def assemble_kernel(rows, size, share, parts_ref, out_ref):
    count = parts_ref.shape[0]

    def total(c, first, last):
        found = parts_ref[c, first:last, :].astype(F32)
        for s in range(c + size, count, size):
            found = found + parts_ref[s, first:last, :].astype(F32)
        return found

    if share > LANES:
        rest = share - LANES
        across = LANES // rest
        for c in range(size):
            out_ref[:, c * LANES : (c + 1) * LANES] = total(c, 0, rows)
            at = size * LANES + rest * c
            for k in range(0, rows // 16, across):
                extra = total(c, rows + 16 * (k // across), rows + 16 * (k // across) + 16)
                for m in range(k, min(k + across, rows // 16)):
                    lanes = slice(rest * (m - k), rest * (m - k + 1))
                    out_ref[16 * m : 16 * m + 16, at : at + rest] = extra[:, lanes]
    else:
        for c in range(size):
            out_ref[:, c * share : (c + 1) * share] = total(c, 0, rows)


def exchange(message, groups=None):
    half = message.astype(jnp.float16)
    return lax.all_to_all(half, "ctx", 0, 0, axis_index_groups=groups, tiled=True)


def swapped(message):
    half = message.astype(jnp.float16)
    count = lax.axis_size("ctx")
    slots = [half[0:1]]
    for m in range(1, message.shape[0]):
        slots.append(lax.ppermute(half[m : m + 1], "ctx", [(at, at ^ m) for at in range(count)]))
    return jnp.concatenate(slots).astype(F32)


def groups_of(count, size):
    return [list(range(at, at + size)) for at in range(0, count, size)]


def group_total(held, rows, reverse):
    (total,) = call(
        functools.partial(total_kernel, rows, reverse),
        [shape((1, *held.shape[1:]))],
        [held],
        4 * held.size,
        12,
    )
    return total.astype(jnp.float16)


def enter(me, held, total, rows, reverse):
    size = held.shape[0]
    count = lax.axis_size("ctx")
    others = []
    for hops in range(size, count, size):
        pairs = [(at, at + hops) for at in range(count - hops)]
        if reverse:
            pairs = [(b, a) for a, b in pairs]
        others.append(lax.ppermute(total, "ctx", pairs).astype(F32))
    (folded,) = call(
        functools.partial(fold_kernel, rows, reverse),
        [shape(held.shape)],
        [me, held, *others],
        8 * held.size,
        12,
        specs=[SMEM] + [VMEM] * (1 + len(others)),
    )
    return folded


def group_of(count):
    for size in (16, 8, 4, 2):
        if count % size == 0:
            return size
    return 1


def from_behind(value, axis):
    count = lax.axis_size(axis)
    return lax.ppermute(value, axis, [(source, source + 1) for source in range(count - 1)])


def per_device(
    x_raw,
    bc_raw,
    gate_branch,
    dt_raw,
    conv_x,
    conv_x_bias,
    conv_bc,
    conv_bc_bias,
    dt_bias,
    a_log,
    d_skip,
    out_weight,
    grad_out,
):
    length, head_count = dt_raw.shape
    channels = x_raw.shape[1]
    width = grad_out.shape[1]
    head_size = channels // head_count
    heads_in = LANES // head_size
    count = lax.axis_size("ctx")
    plane = min(8, group_of(count))
    planes = groups_of(count, plane)
    rows = channels // plane
    size = group_of(count)
    share = channels // size
    groups = groups_of(count, size)
    gathered = lax.all_gather(grad_out, "ctx", axis_index_groups=groups, tiled=True)

    raw = jnp.concatenate([x_raw, bc_raw], axis=1)
    taps = jnp.concatenate(
        [
            jnp.concatenate([conv_x, conv_bc], axis=1),
            jnp.concatenate([conv_x_bias, conv_bc_bias])[None, :],
        ]
    )
    rim = from_behind(raw[length - 16 :], "ctx")
    skip = jnp.repeat(d_skip, head_size)[None, :]
    whole = (length, channels)
    square = (length, LANES)
    block = up8(rows) + 8
    stored = pltpu.VMEM((channels, LANES), F32)
    unit = 2 * length * channels * LANES
    me = (lax.axis_index("ctx") % plane).astype(jnp.int32).reshape(1)

    act_x, slope_x, act_bc, slope_bc, step, ld, step_t, ld_t, raised, per_head, message = call(
        functools.partial(prepare_kernel, heads_in, head_size, rows),
        [shape(whole), shape(whole), shape(bc_raw.shape), shape(bc_raw.shape)]
        + [shape(square)] * 2
        + [shape((LANES, length))] * 2
        + [shape(square), shape((8, LANES))]
        + [shape((plane, block, LANES))],
        [
            raw,
            rim,
            taps,
            dt_raw,
            jnp.stack([dt_bias, a_log]),
        ],
        20 * unit,
        20,
        [
            pltpu.VMEM((length + 8, channels + bc_raw.shape[1]), F32),
            stored,
        ],
    )
    message, grad_out_then = lax.optimization_barrier((message, grad_out))
    held_state = exchange(message, planes).astype(F32)
    part = 640 if channels % 640 == 0 else channels
    grad_gated, grad_y = pl.pallas_call(
        gate_kernel,
        grid=(channels // part,),
        in_specs=[
            pl.BlockSpec((length, width), lambda i: (0, 0)),
        ]
        + [
            pl.BlockSpec((part, width // STREAMS), functools.partial(lambda k, i: (i, k), k))
            for k in range(STREAMS)
        ]
        + [pl.BlockSpec((length, part), lambda i: (0, i))],
        out_specs=(pl.BlockSpec((length, part), lambda i: (0, i)), pl.BlockSpec((length, part), lambda i: (0, i))),
        out_shape=(shape(whole), shape(whole)),
        compiler_params=pltpu.CompilerParams(vmem_limit_bytes=52 * MIB),
        cost_estimate=pl.CostEstimate(
            flops=2 * length * channels * width, bytes_accessed=2 * channels * width, transcendentals=0
        ),
    )(grad_out_then, *[out_weight] * STREAMS, gate_branch)
    (message,) = call(
        functools.partial(grad_kernel, heads_in, head_size, rows),
        [shape((plane, block, LANES))],
        [grad_y, act_bc, ld],
        10 * unit,
        12,
        [stored],
    )
    y_within, grad_within, grad_bc_within = call(
        functools.partial(local_kernel, heads_in, head_size),
        [shape(whole), shape(whole), shape(act_bc.shape)],
        [act_x, grad_y, act_bc, step, ld, step_t, ld_t],
        40 * unit,
        16,
        [pltpu.VMEM(square, F32)],
    )
    total, y_within, message = lax.optimization_barrier(
        (group_total(held_state, rows, False), y_within, message)
    )
    held_carry = exchange(message, planes)
    folded, held_carry = lax.optimization_barrier((enter(me, held_state, total, rows, False), held_carry))
    held_carry = held_carry.astype(F32)
    entered = enter(me, held_carry, group_total(held_carry, rows, True), rows, True)
    state_message = exchange(folded, planes).astype(F32)
    gated, y_ahead = call(
        functools.partial(forward_kernel, heads_in, head_size, rows),
        [shape((size, share, length), BF16), shape(whole)],
        [state_message, act_x, gate_branch, act_bc, ld, y_within, skip],
        20 * unit,
        16,
        [stored],
    )
    gated, entered, gathered, y_ahead = lax.optimization_barrier((gated, entered, gathered, y_ahead))
    held = lax.all_to_all(gated, "ctx", 0, 0, axis_index_groups=groups, tiled=True)
    grad_z, y_sums, grad_bc_ahead = call(
        functools.partial(ahead_kernel, heads_in, head_size, rows),
        [shape(whole, BF16), shape(square), shape(act_bc.shape)],
        [state_message, act_x, grad_y, ld, grad_bc_within, y_ahead, grad_gated, gate_branch, skip],
        20 * unit,
        16,
        [stored],
    )
    held, y_sums = lax.optimization_barrier((held, y_sums))
    out_rows = width // count
    part = width
    for candidate in (640, 1280):
        if width % candidate == 0 and candidate % out_rows == 0:
            part = candidate
            break
    dims = (out_rows, share)
    if share > LANES:
        dims = (out_rows + 16 * (-(-(out_rows // 16) // (LANES // (share - LANES)))), LANES)
    partial = pl.pallas_call(
        functools.partial(product_kernel, out_rows),
        grid=(width // part,),
        in_specs=[
            pl.BlockSpec((size, share, length), lambda i: (0, 0, 0)),
        ]
        + [
            pl.BlockSpec((size * length // STREAMS, part), functools.partial(lambda k, i: (k, i), k))
            for k in range(STREAMS)
        ],
        out_specs=pl.BlockSpec((part // out_rows, *dims), lambda i: (i, 0, 0)),
        out_shape=shape((count, *dims), BF16),
        scratch_shapes=[pltpu.VMEM((share, size * length), BF16)],
        compiler_params=pltpu.CompilerParams(vmem_limit_bytes=48 * MIB),
        cost_estimate=pl.CostEstimate(
            flops=2 * size * length * share * width, bytes_accessed=2 * size * length * width, transcendentals=0
        ),
    )(held, *[gathered] * STREAMS)
    partial, entered = lax.optimization_barrier((partial, entered))
    parts = lax.all_to_all(partial, "ctx", 0, 0, tiled=True)
    carry_message = swapped(entered)
    (weight_grad,) = call(
        functools.partial(assemble_kernel, out_rows, size, share),
        [shape((out_rows, channels))],
        [parts],
        2 * parts.size,
        12,
    )
    grad_x_conv, grad_bc, grad_dt_raw = call(
        functools.partial(backward_kernel, heads_in, head_size, rows),
        [shape(whole, BF16), shape(act_bc.shape), shape(dt_raw.shape)],
        [
            me,
            carry_message,
            state_message,
            act_x,
            slope_x,
            grad_y,
            act_bc,
            step,
            ld,
            grad_within,
            grad_bc_ahead,
            y_sums,
            skip,
            raised,
            per_head,
        ],
        40 * unit,
        28,
        [stored, stored, pltpu.VMEM((LANES, LANES), F32)],
        [SMEM] + [VMEM] * 14,
    )
    grad_bc_conv = (lax.psum(grad_bc, "tp") * slope_bc).astype(BF16)
    return (grad_x_conv, grad_bc_conv, grad_z, grad_dt_raw, weight_grad)


def solution(mesh):
    placed = (
        P("ctx", "tp"),
        P("ctx", None),
        P("ctx", "tp"),
        P("ctx", "tp"),
        P(None, "tp"),
        P("tp"),
        P(),
        P(),
        P("tp"),
        P("tp"),
        P("tp"),
        P("tp", None),
        P("ctx", None),
    )
    return jax.shard_map(
        per_device,
        mesh=mesh,
        in_specs=placed,
        out_specs=(P("ctx", "tp"), P("ctx", None), P("ctx", "tp"), P("ctx", "tp"), P("ctx", "tp")),
        check_vma=False,
    )
```

```python
import functools

import jax
import jax.numpy as jnp
from jax import lax
from jax.experimental import pallas as pl
from jax.experimental.pallas import tpu as pltpu
from jax.sharding import PartitionSpec as P

KERNEL = 4
LANES = 128
F32 = jnp.float32
BF16 = jnp.bfloat16
NN = ((1,), (0,))
NT = ((1,), (1,))
HIGH = lax.Precision.HIGHEST
SMEM = pl.BlockSpec(memory_space=pltpu.SMEM)
VMEM = pl.BlockSpec(memory_space=pltpu.VMEM)
MIB = 1024 * 1024
STREAMS = 4


def call(kernel, out_shapes, operands, flops, vmem, scratch=(), specs=None):
    extra = {} if specs is None else {"in_specs": specs}
    moved = sum(a.size * a.dtype.itemsize for a in (*operands, *out_shapes))
    return pl.pallas_call(
        kernel,
        out_shape=tuple(out_shapes),
        scratch_shapes=list(scratch),
        compiler_params=pltpu.CompilerParams(vmem_limit_bytes=vmem * MIB),
        cost_estimate=pl.CostEstimate(flops=flops, bytes_accessed=moved, transcendentals=0),
        **extra,
    )(*operands)


def shape(dims, dtype=F32):
    return jax.ShapeDtypeStruct(dims, dtype)


def split(value):
    high = value.astype(BF16)
    return high, (value - high.astype(F32)).astype(BF16)


def dot(a, b, dims):
    return lax.dot_general(a, b, (dims, ((), ())), preferred_element_type=F32)


def dot3(a, b, dims=NN):
    return dot(a[0], b[0], dims) + (dot(a[0], b[1], dims) + dot(a[1], b[0], dims))


def sigmoid(value):
    return 1.0 / (1.0 + jnp.exp(-value))


def lane_ids(rows, cols=LANES):
    return lax.broadcasted_iota(jnp.int32, (rows, cols), 1)


def row_ids(rows, cols=LANES):
    return lax.broadcasted_iota(jnp.int32, (rows, cols), 0)


def spread(columns, block, heads, size):
    first = block * heads
    lanes = lane_ids(columns.shape[0])
    wide = jnp.broadcast_to(columns[:, first : first + 1], (columns.shape[0], LANES))
    for k in range(1, heads):
        wide = jnp.where(lanes >= k * size, columns[:, first + k : first + k + 1], wide)
    return wide


def head_of(block, heads, size):
    inner = row_ids(LANES)
    target = lane_ids(LANES)
    result = jnp.zeros((LANES, LANES), F32)
    for k in range(heads):
        here = (inner >= k * size) & (inner < (k + 1) * size) & (target == block * heads + k)
        result = jnp.where(here, 1.0, result)
    return result.astype(BF16)


def stacked(value, heads, size):
    lanes = lane_ids(value.shape[0])
    return jnp.concatenate(
        [jnp.where((lanes >= k * size) & (lanes < (k + 1) * size), value, 0.0) for k in range(heads)],
        axis=0,
    )


def up8(value):
    return -(-value // 8) * 8


def notes_of(rows):
    return -(-rows // LANES)


def exponent_of(block):
    top = jnp.max(jnp.max(jnp.abs(block), axis=0, keepdims=True), axis=1, keepdims=True)
    return jnp.floor(jnp.log2(jnp.maximum(jnp.broadcast_to(top, (1, LANES)), 1e-30)))


def write_block(message, at, first, block, decays, exponent):
    rows = block.shape[0]
    padded = up8(rows)
    message[at, first : first + rows, :] = block * jnp.exp2(13.0 - exponent)
    if padded > rows:
        message[at, first + rows : first + padded, :] = jnp.zeros((padded - rows, LANES), F32)
    highs = [d.astype(BF16).astype(F32) for d in decays]
    lows = [d - h for d, h in zip(decays, highs)]
    place = row_ids(8)
    notes = jnp.broadcast_to(exponent, (8, LANES))
    for k, line in enumerate(highs + lows):
        notes = jnp.where(place == k, line, notes)
    message[at, first + padded : first + padded + 8, :] = notes


def decay_tables(last_exp, heads, size, rows, count):
    shift = size.bit_length() - 1
    tables = []
    for d in range(count):
        lines = []
        for k in range(notes_of(rows)):
            first = rows * d + LANES * k
            owner = lax.shift_right_logical(lane_ids(1) + first, shift)
            table = jnp.zeros((1, LANES), F32)
            for h in range(first // size, min(heads, (first + LANES - 1) // size + 1)):
                table = jnp.where(owner == h, last_exp[:, h : h + 1], table)
            lines.append(table)
        tables.append(lines)
    return tables


def pack_blocks(source, message, last_exp, size, rows):
    count = message.shape[0]
    tables = decay_tables(last_exp, source.shape[0] // size, size, rows, count)
    for d in range(count):
        block = source[rows * d : rows * (d + 1), :]
        write_block(message, d, 0, block, tables[d], exponent_of(block))


def decay_lines(message, at, rows):
    padded, lines = up8(rows), notes_of(rows)
    return [
        message[at, padded + k : padded + k + 1, :] + message[at, padded + lines + k : padded + lines + k + 1, :]
        for k in range(lines)
    ]


def decay_columns(message, rows):
    padded, lines = up8(rows), notes_of(rows)
    turned = [
        jnp.transpose(message[:, padded + k, :] + message[:, padded + lines + k, :]) for k in range(lines)
    ]
    return jnp.concatenate(turned, axis=0)[0:rows]


def read_block(message, at, rows):
    padded = up8(rows)
    return message[at, 0:rows, :] * jnp.exp2(message[at, padded + 7 : padded + 8, :] - 13.0)


def unpack_blocks(message, target, rows, me=0):
    for d in range(message.shape[0]):
        target[rows * d : rows * (d + 1), :] = read_block(message, me ^ d, rows)


def total_kernel(rows, reverse, held_ref, out_ref):
    count = held_ref.shape[0]
    columns = decay_columns(held_ref, rows)
    state = None
    for s in range(count - 1, -1, -1) if reverse else range(count):
        block = read_block(held_ref, s, rows)
        state = block if state is None else columns[:, s : s + 1] * state + block
    decays = decay_lines(held_ref, 0, rows)
    for s in range(1, count):
        decays = [a * b for a, b in zip(decays, decay_lines(held_ref, s, rows))]
    write_block(out_ref, 0, 0, state, decays, exponent_of(state))


def fold_kernel(rows, reverse, me_ref, held_ref, *refs):
    others, out_ref = refs[:-1], refs[-1]
    count = held_ref.shape[0]
    columns = decay_columns(held_ref, rows)
    state = jnp.zeros((rows, LANES), F32)
    for other in reversed(others):
        state = decay_columns(other, rows) * state + read_block(other, 0, rows)
    for s in range(count - 1, -1, -1) if reverse else range(count):
        write_block(out_ref, me_ref[0] ^ s if reverse else s, 0, state, [], exponent_of(state))
        if s != (0 if reverse else count - 1):
            state = columns[:, s : s + 1] * state + read_block(held_ref, s, rows)


def prepare(heads_in, size, raw_ref, rim_ref, taps_ref, dt_ref, per_ref, xs_ref, dtw_ref, perw_ref, length, channels):
    def convolved(cols):
        xs_ref[0:8, cols] = rim_ref[:, cols].astype(F32)[8:16]
        xs_ref[8 : 8 + length, cols] = raw_ref[:, cols].astype(F32)
        pre = taps_ref[KERNEL : KERNEL + 1, cols] + taps_ref[0:1, cols] * xs_ref[5 : 5 + length, cols]
        for k in range(1, KERNEL):
            pre = pre + taps_ref[k : k + 1, cols] * xs_ref[5 + k : 5 + k + length, cols]
        gate = sigmoid(pre)
        return pre * gate, gate * (1.0 + pre * (1.0 - gate))

    heads = dt_ref.shape[1]
    dtw_ref[...] = jnp.zeros_like(dtw_ref)
    dtw_ref[:, 0:heads] = dt_ref[...]
    perw_ref[...] = jnp.zeros_like(perw_ref)
    perw_ref[0:2, 0:heads] = per_ref[...]
    raised = dtw_ref[...] + perw_ref[0:1, :]
    dtw_ref[...] = raised
    step = jnp.maximum(raised, 0.0) + jnp.log1p(jnp.exp(-jnp.abs(raised)))
    lower = jnp.where(row_ids(length) >= lane_ids(length), 1.0, 0.0)
    ld = lax.dot_general(
        lower, step * -jnp.exp(perw_ref[1:2, :]), (NN, ((), ())), precision=HIGH, preferred_element_type=F32
    )
    return convolved, step, ld


def prepare_kernel(
    heads_in, size, rows, raw_ref, rim_ref, taps_ref, dt_ref, per_ref, abc_ref, ld_ref, msg_ref,
    xs_ref, st_ref, dtw_ref, perw_ref,
):
    length = raw_ref.shape[0]
    channels = st_ref.shape[0]
    convolved, step, ld = prepare(
        heads_in, size, raw_ref, rim_ref, taps_ref, dt_ref, per_ref, xs_ref, dtw_ref, perw_ref, length, channels
    )
    ld_ref[...] = ld
    for j in range(abc_ref.shape[1] // LANES):
        value, _ = convolved(slice(channels + j * LANES, channels + (j + 1) * LANES))
        abc_ref[:, j * LANES : (j + 1) * LANES] = value
    b_rows = split(abc_ref[:, 0:LANES])
    last = ld[length - 1 : length]
    weight = jnp.exp(last - ld) * step
    for j in range(channels // LANES):
        cols = slice(j * LANES, (j + 1) * LANES)
        value, _ = convolved(cols)
        scaled = value * spread(weight, j, heads_in, size)
        st_ref[cols, :] = dot3(split(scaled.T), b_rows)
    pack_blocks(st_ref, msg_ref, jnp.exp(last), size, rows)


def keep_kernel(
    heads_in, size, raw_ref, rim_ref, taps_ref, dt_ref, per_ref, act_ref, slope_ref, sbc_ref, step_ref,
    stept_ref, ldt_ref, dtw_ref, perw_ref, xs_ref,
):
    length, channels = act_ref.shape
    convolved, step, ld = prepare(
        heads_in, size, raw_ref, rim_ref, taps_ref, dt_ref, per_ref, xs_ref, dtw_ref, perw_ref, length, channels
    )
    step_ref[...] = step
    stept_ref[...] = step.T
    ldt_ref[...] = ld.T
    for j in range(sbc_ref.shape[1] // LANES):
        _, slope = convolved(slice(channels + j * LANES, channels + (j + 1) * LANES))
        sbc_ref[:, j * LANES : (j + 1) * LANES] = slope
    for j in range(channels // LANES):
        cols = slice(j * LANES, (j + 1) * LANES)
        act_ref[:, cols], slope_ref[:, cols] = convolved(cols)


def grad_kernel(heads_in, size, rows, gy_ref, abc_ref, ld_ref, msg_ref, st_ref):
    length = gy_ref.shape[0]
    c_rows = split(abc_ref[:, LANES : 2 * LANES])
    grown = jnp.exp(ld_ref[...])
    for j in range(gy_ref.shape[1] // LANES):
        cols = slice(j * LANES, (j + 1) * LANES)
        scaled = gy_ref[:, cols] * spread(grown, j, heads_in, size)
        st_ref[cols, :] = dot3(split(scaled.T), c_rows)
    pack_blocks(st_ref, msg_ref, grown[length - 1 : length], size, rows)


def gate_kernel(go_ref, *refs):
    w_refs, (gate_ref, gg_ref, gy_ref) = refs[:-3], refs[-3:]
    depth = w_refs[0].shape[1]
    grad = dot(w_refs[0][...], go_ref[:, 0:depth], NT)
    for k in range(1, len(w_refs)):
        grad = grad + dot(w_refs[k][...], go_ref[:, k * depth : (k + 1) * depth], NT)
    grad = grad.T
    gate = gate_ref[...].astype(F32)
    gg_ref[...] = grad
    gy_ref[...] = grad * (gate * sigmoid(gate))


def local_kernel(
    heads_in, size, act_ref, gy_ref, abc_ref, step_ref, ld_ref, stept_ref, ldt_ref, yw_ref, gw_ref, gbc_ref, sh_ref
):
    length = act_ref.shape[0]
    b_rows = split(abc_ref[:, 0:LANES])
    c_rows = split(abc_ref[:, LANES : 2 * LANES])
    scores = dot3(c_rows, b_rows, NT)
    turned = dot3(b_rows, c_rows, NT)
    causal = row_ids(length) >= lane_ids(length)
    causal_t = row_ids(length) <= lane_ids(length)
    sh_ref[...] = jnp.zeros_like(sh_ref)
    for j in range(act_ref.shape[1] // LANES):
        cols = slice(j * LANES, (j + 1) * LANES)
        mixes, mixes_t, steps = [], [], []
        for h in range(j * heads_in, (j + 1) * heads_in):
            column, row = ld_ref[:, h : h + 1], ldt_ref[h : h + 1, :]
            decays = jnp.exp(jnp.where(causal, column - row, -1e30))
            stepped = decays * stept_ref[h : h + 1, :]
            decays_t = jnp.exp(jnp.where(causal_t, row - column, -1e30))
            steps.append(stepped)
            mixes.append(stepped * scores)
            mixes_t.append(decays_t * turned * step_ref[:, h : h + 1])
        inputs = act_ref[:, cols]
        grad_y = gy_ref[:, cols]
        inputs_s = stacked(inputs, heads_in, size)
        grads_s = split(stacked(grad_y, heads_in, size))
        yw_ref[:, cols] = dot3(split(jnp.concatenate(mixes, axis=1)), split(inputs_s))
        gw_ref[:, cols] = dot3(split(jnp.concatenate(mixes_t, axis=1)), grads_s)
        products = dot3(grads_s, split(inputs), NT)
        total = sh_ref[...]
        for k in range(heads_in):
            total = total + steps[k] * products[k * length : (k + 1) * length]
        sh_ref[...] = total
    shared = sh_ref[...]
    gbc_ref[:, 0:LANES] = dot3(split(shared.T), c_rows)
    gbc_ref[:, LANES : 2 * LANES] = dot3(split(shared), b_rows)


def place_of(channel, share, size):
    if share > LANES:
        if channel < LANES * size:
            return channel // LANES, channel % LANES
        rest = share - LANES
        return (channel - LANES * size) // rest, LANES + (channel - LANES * size) % rest
    return channel // share, channel % share


def forward_kernel(
    heads_in, size, rows, msg_ref, act_ref, gate_ref, abc_ref, ld_ref, yw_ref, skip_ref, gt_ref, ys_ref, st_ref
):
    share = gt_ref.shape[1]
    unpack_blocks(msg_ref, st_ref, rows)
    c_rows = split(abc_ref[:, LANES : 2 * LANES])
    grown = jnp.exp(ld_ref[...])
    for j in range(act_ref.shape[1] // LANES):
        cols = slice(j * LANES, (j + 1) * LANES)
        carried = dot3(c_rows, split(st_ref[cols, :]), NT)
        within = yw_ref[:, cols] + spread(grown, j, heads_in, size) * carried
        ys_ref[:, cols] = within
        output = within + skip_ref[:, cols] * act_ref[:, cols]
        gate = gate_ref[:, cols].astype(F32)
        turned = (output * (gate * sigmoid(gate))).T.astype(BF16)
        for k in range(0, LANES, 16):
            to, at = place_of(j * LANES + k, share, gt_ref.shape[0])
            gt_ref[to, at : at + 16, :] = turned[k : k + 16]


def ahead_kernel(
    heads_in, size, rows, msg_ref, act_ref, gy_ref, ld_ref, gbcl_ref, ys_ref, gg_ref, gate_ref, skip_ref,
    gz_ref, yg_ref, gbc_ref, st_ref,
):
    unpack_blocks(msg_ref, st_ref, rows)
    grown = jnp.exp(ld_ref[...])
    sums = jnp.zeros(yg_ref.shape, F32)
    grad_c = gbcl_ref[:, LANES : 2 * LANES]
    for j in range(act_ref.shape[1] // LANES):
        cols = slice(j * LANES, (j + 1) * LANES)
        grad_y = gy_ref[:, cols]
        within = ys_ref[:, cols]
        gate = gate_ref[:, cols].astype(F32)
        opened = sigmoid(gate)
        output = within + skip_ref[:, cols] * act_ref[:, cols]
        gz_ref[:, cols] = (gg_ref[:, cols] * output * (opened * (1.0 + gate * (1.0 - opened)))).astype(BF16)
        onehot = head_of(j, heads_in, size)
        high, low = split(grad_y * within)
        sums = sums + (dot(high, onehot, NN) + dot(low, onehot, NN))
        grad_c = grad_c + dot3(split(spread(grown, j, heads_in, size) * grad_y), split(st_ref[cols, :]))
    yg_ref[...] = sums
    gbc_ref[:, 0:LANES] = gbcl_ref[:, 0:LANES]
    gbc_ref[:, LANES : 2 * LANES] = grad_c


def backward_kernel(
    heads_in, size, rows, me_ref, msg_ref, msgf_ref, act_ref, slope_ref, gy_ref, abc_ref, step_ref, ld_ref, gw_ref,
    gbcl_ref, yg_ref, skip_ref, dtw_ref, perw_ref, gx_ref, gbc_ref, gdt_ref,
    ca_ref, st_ref, cs_ref,
):
    length = act_ref.shape[0]
    unpack_blocks(msg_ref, ca_ref, rows, me_ref[0])
    unpack_blocks(msgf_ref, st_ref, rows)
    b_rows = split(abc_ref[:, 0:LANES])
    ld = ld_ref[...]
    step = step_ref[...]
    last = ld[length - 1 : length]
    weight = jnp.exp(last - ld) * step
    sums = jnp.zeros((length, LANES), F32)
    leaving = jnp.zeros((8, LANES), F32)
    grad_b = gbcl_ref[:, 0:LANES]
    cs_ref[...] = jnp.zeros_like(cs_ref)
    for j in range(act_ref.shape[1] // LANES):
        cols = slice(j * LANES, (j + 1) * LANES)
        inputs = act_ref[:, cols]
        grad_y = gy_ref[:, cols]
        carry = ca_ref[cols, :]
        state = st_ref[cols, :]
        carry_s = split(carry)
        wide = spread(weight, j, heads_in, size)
        gone = wide * dot3(b_rows, carry_s, NT)
        grad_in = gw_ref[:, cols] + gone
        gx_ref[:, cols] = ((skip_ref[:, cols] * grad_y + grad_in) * slope_ref[:, cols]).astype(BF16)
        onehot = head_of(j, heads_in, size)
        high, low = split(inputs * grad_in)
        sums = sums + (dot(high, onehot, NN) + dot(low, onehot, NN))
        folded = jnp.sum((inputs * gone).reshape(length // 8, 8, LANES), axis=0)
        high, low = split(folded)
        leaving = leaving + (dot(high, onehot, NN) + dot(low, onehot, NN))
        product = carry * state
        for k in range(heads_in):
            h = j * heads_in + k
            cs_ref[h : h + 1, :] = jnp.sum(product[k * size : (k + 1) * size], axis=0, keepdims=True)
        grad_b = grad_b + dot3(split(wide * inputs), carry_s)
    gbc_ref[:, 0:LANES] = grad_b
    gbc_ref[:, LANES : 2 * LANES] = gbcl_ref[:, LANES : 2 * LANES]
    both = lax.dot_general(
        jnp.ones((8, LANES), F32), cs_ref[...], (NT, ((), ())), precision=HIGH, preferred_element_type=F32
    )
    constant = jnp.sum(leaving, axis=0, keepdims=True) + jnp.exp(last) * both[0:1]
    upper = jnp.where(row_ids(length) <= lane_ids(length), 1.0, 0.0)
    grad_rate = constant + lax.dot_general(
        upper, yg_ref[...] - sums, (NN, ((), ())), precision=HIGH, preferred_element_type=F32
    )
    grad_step = sums / step - jnp.exp(perw_ref[1:2, :]) * grad_rate
    gdt_ref[...] = (grad_step * sigmoid(dtw_ref[...]))[:, 0 : gdt_ref.shape[1]]


def product_kernel(rows, held_ref, *refs):
    go_refs, out_ref, lhs_ref = refs[:-2], refs[-2], refs[-1]
    size, share, length = held_ref.shape

    @pl.when(pl.program_id(0) == 0)
    def _():
        for s in range(size):
            lhs_ref[:, s * length : (s + 1) * length] = held_ref[s]

    depth = go_refs[0].shape[0]
    result = dot(lhs_ref[:, 0:depth], go_refs[0][...], NN)
    for k in range(1, len(go_refs)):
        result = result + dot(lhs_ref[:, k * depth : (k + 1) * depth], go_refs[k][...], NN)
    result = result.T
    for d in range(out_ref.shape[0]):
        block = result[rows * d : rows * (d + 1)]
        if share > LANES:
            rest = share - LANES
            across = LANES // rest
            out_ref[d, 0:rows, :] = block[:, 0:LANES].astype(BF16)
            for k in range(0, rows // 16, across):
                pieces = [block[16 * m : 16 * m + 16, LANES:] for m in range(k, min(k + across, rows // 16))]
                if len(pieces) < across:
                    pieces.append(jnp.zeros((16, LANES - rest * len(pieces)), F32))
                at = rows + 16 * (k // across)
                out_ref[d, at : at + 16, :] = jnp.concatenate(pieces, axis=1).astype(BF16)
        else:
            out_ref[d] = block.astype(BF16)


def assemble_kernel(rows, size, share, parts_ref, out_ref):
    count = parts_ref.shape[0]

    def total(c, first, last):
        found = parts_ref[c, first:last, :].astype(F32)
        for s in range(c + size, count, size):
            found = found + parts_ref[s, first:last, :].astype(F32)
        return found

    if share > LANES:
        rest = share - LANES
        across = LANES // rest
        for c in range(size):
            out_ref[:, c * LANES : (c + 1) * LANES] = total(c, 0, rows)
            at = size * LANES + rest * c
            for k in range(0, rows // 16, across):
                extra = total(c, rows + 16 * (k // across), rows + 16 * (k // across) + 16)
                for m in range(k, min(k + across, rows // 16)):
                    lanes = slice(rest * (m - k), rest * (m - k + 1))
                    out_ref[16 * m : 16 * m + 16, at : at + rest] = extra[:, lanes]
    else:
        for c in range(size):
            out_ref[:, c * share : (c + 1) * share] = total(c, 0, rows)


def exchange(message, groups=None):
    half = message.astype(jnp.float16)
    return lax.all_to_all(half, "ctx", 0, 0, axis_index_groups=groups, tiled=True)


def swapped(message):
    half = message.astype(jnp.float16)
    count = lax.axis_size("ctx")
    slots = [half[0:1]]
    for m in range(1, message.shape[0]):
        slots.append(lax.ppermute(half[m : m + 1], "ctx", [(at, at ^ m) for at in range(count)]))
    return jnp.concatenate(slots).astype(F32)


def groups_of(count, size):
    return [list(range(at, at + size)) for at in range(0, count, size)]


def group_total(held, rows, reverse):
    (total,) = call(
        functools.partial(total_kernel, rows, reverse),
        [shape((1, *held.shape[1:]))],
        [held],
        4 * held.size,
        12,
    )
    return total.astype(jnp.float16)


def enter(me, held, total, rows, reverse):
    size = held.shape[0]
    count = lax.axis_size("ctx")
    others = []
    for hops in range(size, count, size):
        pairs = [(at, at + hops) for at in range(count - hops)]
        if reverse:
            pairs = [(b, a) for a, b in pairs]
        others.append(lax.ppermute(total, "ctx", pairs).astype(F32))
    (folded,) = call(
        functools.partial(fold_kernel, rows, reverse),
        [shape(held.shape)],
        [me, held, *others],
        8 * held.size,
        12,
        specs=[SMEM] + [VMEM] * (1 + len(others)),
    )
    return folded


def group_of(count):
    for size in (16, 8, 4, 2):
        if count % size == 0:
            return size
    return 1


def from_behind(value, axis):
    count = lax.axis_size(axis)
    return lax.ppermute(value, axis, [(source, source + 1) for source in range(count - 1)])


def per_device(
    x_raw,
    bc_raw,
    gate_branch,
    dt_raw,
    conv_x,
    conv_x_bias,
    conv_bc,
    conv_bc_bias,
    dt_bias,
    a_log,
    d_skip,
    out_weight,
    grad_out,
):
    length, head_count = dt_raw.shape
    channels = x_raw.shape[1]
    width = grad_out.shape[1]
    head_size = channels // head_count
    heads_in = LANES // head_size
    count = lax.axis_size("ctx")
    plane = min(8, group_of(count))
    planes = groups_of(count, plane)
    rows = channels // plane
    size = group_of(count)
    share = channels // size
    groups = groups_of(count, size)
    gathered = lax.all_gather(grad_out, "ctx", axis_index_groups=groups, tiled=True)

    raw = jnp.concatenate([x_raw, bc_raw], axis=1)
    taps = jnp.concatenate(
        [
            jnp.concatenate([conv_x, conv_bc], axis=1),
            jnp.concatenate([conv_x_bias, conv_bc_bias])[None, :],
        ]
    )
    rim = from_behind(raw[length - 16 :], "ctx")
    skip = jnp.repeat(d_skip, head_size)[None, :]
    whole = (length, channels)
    square = (length, LANES)
    block = up8(rows) + 8
    stored = pltpu.VMEM((channels, LANES), F32)
    unit = 2 * length * channels * LANES
    me = (lax.axis_index("ctx") % plane).astype(jnp.int32).reshape(1)

    padded = pltpu.VMEM((length + 8, channels + bc_raw.shape[1]), F32)
    per_raw = jnp.stack([dt_bias, a_log])
    act_bc, ld, message = call(
        functools.partial(prepare_kernel, heads_in, head_size, rows),
        [shape(bc_raw.shape), shape(square), shape((plane, block, LANES))],
        [raw, rim, taps, dt_raw, per_raw],
        20 * unit,
        20,
        [padded, stored, pltpu.VMEM(square, F32), pltpu.VMEM((8, LANES), F32)],
    )
    message, grad_out_then, raw_then = lax.optimization_barrier((message, grad_out, raw))
    held_state = exchange(message, planes).astype(F32)
    part = 640 if channels % 640 == 0 else channels
    grad_gated, grad_y = pl.pallas_call(
        gate_kernel,
        grid=(channels // part,),
        in_specs=[
            pl.BlockSpec((length, width), lambda i: (0, 0)),
        ]
        + [
            pl.BlockSpec((part, width // STREAMS), functools.partial(lambda k, i: (i, k), k))
            for k in range(STREAMS)
        ]
        + [pl.BlockSpec((length, part), lambda i: (0, i))],
        out_specs=(pl.BlockSpec((length, part), lambda i: (0, i)), pl.BlockSpec((length, part), lambda i: (0, i))),
        out_shape=(shape(whole), shape(whole)),
        compiler_params=pltpu.CompilerParams(vmem_limit_bytes=52 * MIB),
        cost_estimate=pl.CostEstimate(
            flops=2 * length * channels * width, bytes_accessed=2 * channels * width, transcendentals=0
        ),
    )(grad_out_then, *[out_weight] * STREAMS, gate_branch)
    (message,) = call(
        functools.partial(grad_kernel, heads_in, head_size, rows),
        [shape((plane, block, LANES))],
        [grad_y, act_bc, ld],
        10 * unit,
        12,
        [stored],
    )
    act_x, slope_x, slope_bc, step, step_t, ld_t, raised, per_head = call(
        functools.partial(keep_kernel, heads_in, head_size),
        [shape(whole), shape(whole), shape(bc_raw.shape), shape(square)]
        + [shape((LANES, length))] * 2
        + [shape(square), shape((8, LANES))],
        [raw_then, rim, taps, dt_raw, per_raw],
        10 * unit,
        20,
        [padded],
    )
    y_within, grad_within, grad_bc_within = call(
        functools.partial(local_kernel, heads_in, head_size),
        [shape(whole), shape(whole), shape(act_bc.shape)],
        [act_x, grad_y, act_bc, step, ld, step_t, ld_t],
        40 * unit,
        16,
        [pltpu.VMEM(square, F32)],
    )
    total, y_within, message = lax.optimization_barrier(
        (group_total(held_state, rows, False), y_within, message)
    )
    held_carry = exchange(message, planes)
    folded, held_carry = lax.optimization_barrier((enter(me, held_state, total, rows, False), held_carry))
    held_carry = held_carry.astype(F32)
    state_message = exchange(folded, planes).astype(F32)
    total, state_message = lax.optimization_barrier((group_total(held_carry, rows, True), state_message))
    entered = enter(me, held_carry, total, rows, True)
    gated, y_ahead = call(
        functools.partial(forward_kernel, heads_in, head_size, rows),
        [shape((size, share, length), BF16), shape(whole)],
        [state_message, act_x, gate_branch, act_bc, ld, y_within, skip],
        20 * unit,
        16,
        [stored],
    )
    gated, gathered, y_ahead = lax.optimization_barrier((gated, gathered, y_ahead))
    held = lax.all_to_all(gated, "ctx", 0, 0, axis_index_groups=groups, tiled=True)
    grad_z, y_sums, grad_bc_ahead = call(
        functools.partial(ahead_kernel, heads_in, head_size, rows),
        [shape(whole, BF16), shape(square), shape(act_bc.shape)],
        [state_message, act_x, grad_y, ld, grad_bc_within, y_ahead, grad_gated, gate_branch, skip],
        20 * unit,
        16,
        [stored],
    )
    held, y_sums = lax.optimization_barrier((held, y_sums))
    out_rows = width // count
    part = width
    for candidate in (640, 1280):
        if width % candidate == 0 and candidate % out_rows == 0:
            part = candidate
            break
    dims = (out_rows, share)
    if share > LANES:
        dims = (out_rows + 16 * (-(-(out_rows // 16) // (LANES // (share - LANES)))), LANES)
    partial = pl.pallas_call(
        functools.partial(product_kernel, out_rows),
        grid=(width // part,),
        in_specs=[
            pl.BlockSpec((size, share, length), lambda i: (0, 0, 0)),
        ]
        + [
            pl.BlockSpec((size * length // STREAMS, part), functools.partial(lambda k, i: (k, i), k))
            for k in range(STREAMS)
        ],
        out_specs=pl.BlockSpec((part // out_rows, *dims), lambda i: (i, 0, 0)),
        out_shape=shape((count, *dims), BF16),
        scratch_shapes=[pltpu.VMEM((share, size * length), BF16)],
        compiler_params=pltpu.CompilerParams(vmem_limit_bytes=48 * MIB),
        cost_estimate=pl.CostEstimate(
            flops=2 * size * length * share * width, bytes_accessed=2 * size * length * width, transcendentals=0
        ),
    )(held, *[gathered] * STREAMS)
    partial, entered = lax.optimization_barrier((partial, entered))
    parts = lax.all_to_all(partial, "ctx", 0, 0, tiled=True)
    carry_message = swapped(entered)
    (weight_grad,) = call(
        functools.partial(assemble_kernel, out_rows, size, share),
        [shape((out_rows, channels))],
        [parts],
        2 * parts.size,
        12,
    )
    grad_x_conv, grad_bc, grad_dt_raw = call(
        functools.partial(backward_kernel, heads_in, head_size, rows),
        [shape(whole, BF16), shape(act_bc.shape), shape(dt_raw.shape)],
        [
            me,
            carry_message,
            state_message,
            act_x,
            slope_x,
            grad_y,
            act_bc,
            step,
            ld,
            grad_within,
            grad_bc_ahead,
            y_sums,
            skip,
            raised,
            per_head,
        ],
        40 * unit,
        28,
        [stored, stored, pltpu.VMEM((LANES, LANES), F32)],
        [SMEM] + [VMEM] * 14,
    )
    grad_bc_conv = (lax.psum(grad_bc, "tp") * slope_bc).astype(BF16)
    return (grad_x_conv, grad_bc_conv, grad_z, grad_dt_raw, weight_grad)


def solution(mesh):
    placed = (
        P("ctx", "tp"),
        P("ctx", None),
        P("ctx", "tp"),
        P("ctx", "tp"),
        P(None, "tp"),
        P("tp"),
        P(),
        P(),
        P("tp"),
        P("tp"),
        P("tp"),
        P("tp", None),
        P("ctx", None),
    )
    return jax.shard_map(
        per_device,
        mesh=mesh,
        in_specs=placed,
        out_specs=(P("ctx", "tp"), P("ctx", None), P("ctx", "tp"), P("ctx", "tp"), P("ctx", "tp")),
        check_vma=False,
    )
```

```python
import functools

import jax
import jax.numpy as jnp
from jax import lax
from jax.experimental import pallas as pl
from jax.experimental.pallas import tpu as pltpu
from jax.sharding import PartitionSpec as P

KERNEL = 4
LANES = 128
F32 = jnp.float32
BF16 = jnp.bfloat16
NN = ((1,), (0,))
NT = ((1,), (1,))
HIGH = lax.Precision.HIGHEST
SMEM = pl.BlockSpec(memory_space=pltpu.SMEM)
VMEM = pl.BlockSpec(memory_space=pltpu.VMEM)
MIB = 1024 * 1024
STREAMS = 4


def call(kernel, out_shapes, operands, flops, vmem, scratch=(), specs=None):
    extra = {} if specs is None else {"in_specs": specs}
    moved = sum(a.size * a.dtype.itemsize for a in (*operands, *out_shapes))
    return pl.pallas_call(
        kernel,
        out_shape=tuple(out_shapes),
        scratch_shapes=list(scratch),
        compiler_params=pltpu.CompilerParams(vmem_limit_bytes=vmem * MIB),
        cost_estimate=pl.CostEstimate(flops=flops, bytes_accessed=moved, transcendentals=0),
        **extra,
    )(*operands)


def shape(dims, dtype=F32):
    return jax.ShapeDtypeStruct(dims, dtype)


def split(value):
    high = value.astype(BF16)
    return high, (value - high.astype(F32)).astype(BF16)


def dot(a, b, dims):
    return lax.dot_general(a, b, (dims, ((), ())), preferred_element_type=F32)


def dot3(a, b, dims=NN):
    return dot(a[0], b[0], dims) + (dot(a[0], b[1], dims) + dot(a[1], b[0], dims))


def sigmoid(value):
    return 1.0 / (1.0 + jnp.exp(-value))


def lane_ids(rows, cols=LANES):
    return lax.broadcasted_iota(jnp.int32, (rows, cols), 1)


def row_ids(rows, cols=LANES):
    return lax.broadcasted_iota(jnp.int32, (rows, cols), 0)


def spread(columns, block, heads, size):
    first = block * heads
    lanes = lane_ids(columns.shape[0])
    wide = jnp.broadcast_to(columns[:, first : first + 1], (columns.shape[0], LANES))
    for k in range(1, heads):
        wide = jnp.where(lanes >= k * size, columns[:, first + k : first + k + 1], wide)
    return wide


def head_of(block, heads, size):
    inner = row_ids(LANES)
    target = lane_ids(LANES)
    result = jnp.zeros((LANES, LANES), F32)
    for k in range(heads):
        here = (inner >= k * size) & (inner < (k + 1) * size) & (target == block * heads + k)
        result = jnp.where(here, 1.0, result)
    return result.astype(BF16)


def stacked(value, heads, size):
    lanes = lane_ids(value.shape[0])
    return jnp.concatenate(
        [jnp.where((lanes >= k * size) & (lanes < (k + 1) * size), value, 0.0) for k in range(heads)],
        axis=0,
    )


def up8(value):
    return -(-value // 8) * 8


def notes_of(rows):
    return -(-rows // LANES)


def exponent_of(block):
    top = jnp.max(jnp.max(jnp.abs(block), axis=0, keepdims=True), axis=1, keepdims=True)
    return jnp.floor(jnp.log2(jnp.maximum(jnp.broadcast_to(top, (1, LANES)), 1e-30)))


def write_block(message, at, first, block, decays, exponent):
    rows = block.shape[0]
    padded = up8(rows)
    message[at, first : first + rows, :] = block * jnp.exp2(13.0 - exponent)
    if padded > rows:
        message[at, first + rows : first + padded, :] = jnp.zeros((padded - rows, LANES), F32)
    highs = [d.astype(BF16).astype(F32) for d in decays]
    lows = [d - h for d, h in zip(decays, highs)]
    place = row_ids(8)
    notes = jnp.broadcast_to(exponent, (8, LANES))
    for k, line in enumerate(highs + lows):
        notes = jnp.where(place == k, line, notes)
    message[at, first + padded : first + padded + 8, :] = notes


def decay_tables(last_exp, heads, size, rows, count):
    shift = size.bit_length() - 1
    tables = []
    for d in range(count):
        lines = []
        for k in range(notes_of(rows)):
            first = rows * d + LANES * k
            owner = lax.shift_right_logical(lane_ids(1) + first, shift)
            table = jnp.zeros((1, LANES), F32)
            for h in range(first // size, min(heads, (first + LANES - 1) // size + 1)):
                table = jnp.where(owner == h, last_exp[:, h : h + 1], table)
            lines.append(table)
        tables.append(lines)
    return tables


def pack_blocks(source, message, last_exp, size, rows):
    count = message.shape[0]
    tables = decay_tables(last_exp, source.shape[0] // size, size, rows, count)
    for d in range(count):
        block = source[rows * d : rows * (d + 1), :]
        write_block(message, d, 0, block, tables[d], exponent_of(block))


def decay_lines(message, at, rows):
    padded, lines = up8(rows), notes_of(rows)
    return [
        message[at, padded + k : padded + k + 1, :] + message[at, padded + lines + k : padded + lines + k + 1, :]
        for k in range(lines)
    ]


def decay_columns(message, rows):
    padded, lines = up8(rows), notes_of(rows)
    turned = [
        jnp.transpose(message[:, padded + k, :] + message[:, padded + lines + k, :]) for k in range(lines)
    ]
    return jnp.concatenate(turned, axis=0)[0:rows]


def read_block(message, at, rows):
    padded = up8(rows)
    return message[at, 0:rows, :] * jnp.exp2(message[at, padded + 7 : padded + 8, :] - 13.0)


def unpack_blocks(message, target, rows, me=0):
    for d in range(message.shape[0]):
        target[rows * d : rows * (d + 1), :] = read_block(message, me ^ d, rows)


def total_kernel(rows, reverse, held_ref, out_ref):
    count = held_ref.shape[0]
    columns = decay_columns(held_ref, rows)
    state = None
    for s in range(count - 1, -1, -1) if reverse else range(count):
        block = read_block(held_ref, s, rows)
        state = block if state is None else columns[:, s : s + 1] * state + block
    decays = decay_lines(held_ref, 0, rows)
    for s in range(1, count):
        decays = [a * b for a, b in zip(decays, decay_lines(held_ref, s, rows))]
    write_block(out_ref, 0, 0, state, decays, exponent_of(state))


def fold_kernel(rows, reverse, me_ref, held_ref, *refs):
    others, out_ref = refs[:-1], refs[-1]
    count = held_ref.shape[0]
    columns = decay_columns(held_ref, rows)
    state = jnp.zeros((rows, LANES), F32)
    for other in reversed(others):
        state = decay_columns(other, rows) * state + read_block(other, 0, rows)
    for s in range(count - 1, -1, -1) if reverse else range(count):
        write_block(out_ref, me_ref[0] ^ s if reverse else s, 0, state, [], exponent_of(state))
        if s != (0 if reverse else count - 1):
            state = columns[:, s : s + 1] * state + read_block(held_ref, s, rows)


def prepare(heads_in, size, raw_ref, rim_ref, taps_ref, dt_ref, per_ref, xs_ref, dtw_ref, perw_ref, length, channels):
    def convolved(cols):
        xs_ref[0:8, cols] = rim_ref[:, cols].astype(F32)[8:16]
        xs_ref[8 : 8 + length, cols] = raw_ref[:, cols].astype(F32)
        pre = taps_ref[KERNEL : KERNEL + 1, cols] + taps_ref[0:1, cols] * xs_ref[5 : 5 + length, cols]
        for k in range(1, KERNEL):
            pre = pre + taps_ref[k : k + 1, cols] * xs_ref[5 + k : 5 + k + length, cols]
        gate = sigmoid(pre)
        return pre * gate, gate * (1.0 + pre * (1.0 - gate))

    heads = dt_ref.shape[1]
    dtw_ref[...] = jnp.zeros_like(dtw_ref)
    dtw_ref[:, 0:heads] = dt_ref[...]
    perw_ref[...] = jnp.zeros_like(perw_ref)
    perw_ref[0:2, 0:heads] = per_ref[...]
    raised = dtw_ref[...] + perw_ref[0:1, :]
    dtw_ref[...] = raised
    step = jnp.maximum(raised, 0.0) + jnp.log1p(jnp.exp(-jnp.abs(raised)))
    lower = jnp.where(row_ids(length) >= lane_ids(length), 1.0, 0.0)
    ld = lax.dot_general(
        lower, step * -jnp.exp(perw_ref[1:2, :]), (NN, ((), ())), precision=HIGH, preferred_element_type=F32
    )
    return convolved, step, ld


def prepare_kernel(
    heads_in, size, rows, raw_ref, rim_ref, taps_ref, dt_ref, per_ref, abc_ref, ld_ref, msg_ref,
    xs_ref, st_ref, dtw_ref, perw_ref,
):
    length = raw_ref.shape[0]
    channels = st_ref.shape[0]
    convolved, step, ld = prepare(
        heads_in, size, raw_ref, rim_ref, taps_ref, dt_ref, per_ref, xs_ref, dtw_ref, perw_ref, length, channels
    )
    ld_ref[...] = ld
    for j in range(abc_ref.shape[1] // LANES):
        value, _ = convolved(slice(channels + j * LANES, channels + (j + 1) * LANES))
        abc_ref[:, j * LANES : (j + 1) * LANES] = value
    b_rows = split(abc_ref[:, 0:LANES])
    last = ld[length - 1 : length]
    weight = jnp.exp(last - ld) * step
    for j in range(channels // LANES):
        cols = slice(j * LANES, (j + 1) * LANES)
        value, _ = convolved(cols)
        scaled = value * spread(weight, j, heads_in, size)
        st_ref[cols, :] = dot3(split(scaled.T), b_rows)
    pack_blocks(st_ref, msg_ref, jnp.exp(last), size, rows)


def keep_kernel(
    heads_in, size, raw_ref, rim_ref, taps_ref, dt_ref, per_ref, act_ref, slope_ref, sbc_ref, step_ref,
    stept_ref, ldt_ref, dtw_ref, perw_ref, xs_ref,
):
    length, channels = act_ref.shape
    convolved, step, ld = prepare(
        heads_in, size, raw_ref, rim_ref, taps_ref, dt_ref, per_ref, xs_ref, dtw_ref, perw_ref, length, channels
    )
    step_ref[...] = step
    stept_ref[...] = step.T
    ldt_ref[...] = ld.T
    for j in range(sbc_ref.shape[1] // LANES):
        _, slope = convolved(slice(channels + j * LANES, channels + (j + 1) * LANES))
        sbc_ref[:, j * LANES : (j + 1) * LANES] = slope
    for j in range(channels // LANES):
        cols = slice(j * LANES, (j + 1) * LANES)
        act_ref[:, cols], slope_ref[:, cols] = convolved(cols)


def grad_kernel(heads_in, size, rows, gy_ref, abc_ref, ld_ref, msg_ref, st_ref):
    length = gy_ref.shape[0]
    c_rows = split(abc_ref[:, LANES : 2 * LANES])
    grown = jnp.exp(ld_ref[...])
    for j in range(gy_ref.shape[1] // LANES):
        cols = slice(j * LANES, (j + 1) * LANES)
        scaled = gy_ref[:, cols] * spread(grown, j, heads_in, size)
        st_ref[cols, :] = dot3(split(scaled.T), c_rows)
    pack_blocks(st_ref, msg_ref, grown[length - 1 : length], size, rows)


def gate_kernel(go_ref, *refs):
    w_refs, (gate_ref, gg_ref, gy_ref) = refs[:-3], refs[-3:]
    depth = w_refs[0].shape[1]
    grad = dot(w_refs[0][...], go_ref[:, 0:depth], NT)
    for k in range(1, len(w_refs)):
        grad = grad + dot(w_refs[k][...], go_ref[:, k * depth : (k + 1) * depth], NT)
    grad = grad.T
    gate = gate_ref[...].astype(F32)
    gg_ref[...] = grad
    gy_ref[...] = grad * (gate * sigmoid(gate))


def local_kernel(
    heads_in, size, act_ref, gy_ref, abc_ref, step_ref, ld_ref, stept_ref, ldt_ref, yw_ref, gw_ref, gbc_ref, sh_ref
):
    length = act_ref.shape[0]
    b_rows = split(abc_ref[:, 0:LANES])
    c_rows = split(abc_ref[:, LANES : 2 * LANES])
    scores = dot3(c_rows, b_rows, NT)
    turned = dot3(b_rows, c_rows, NT)
    causal = row_ids(length) >= lane_ids(length)
    causal_t = row_ids(length) <= lane_ids(length)
    sh_ref[...] = jnp.zeros_like(sh_ref)
    for j in range(act_ref.shape[1] // LANES):
        cols = slice(j * LANES, (j + 1) * LANES)
        mixes, mixes_t, steps = [], [], []
        for h in range(j * heads_in, (j + 1) * heads_in):
            column, row = ld_ref[:, h : h + 1], ldt_ref[h : h + 1, :]
            decays = jnp.exp(jnp.where(causal, column - row, -1e30))
            stepped = decays * stept_ref[h : h + 1, :]
            decays_t = jnp.exp(jnp.where(causal_t, row - column, -1e30))
            steps.append(stepped)
            mixes.append(stepped * scores)
            mixes_t.append(decays_t * turned * step_ref[:, h : h + 1])
        inputs = act_ref[:, cols]
        grad_y = gy_ref[:, cols]
        inputs_s = stacked(inputs, heads_in, size)
        grads_s = split(stacked(grad_y, heads_in, size))
        yw_ref[:, cols] = dot3(split(jnp.concatenate(mixes, axis=1)), split(inputs_s))
        gw_ref[:, cols] = dot3(split(jnp.concatenate(mixes_t, axis=1)), grads_s)
        products = dot3(grads_s, split(inputs), NT)
        total = sh_ref[...]
        for k in range(heads_in):
            total = total + steps[k] * products[k * length : (k + 1) * length]
        sh_ref[...] = total
    shared = sh_ref[...]
    gbc_ref[:, 0:LANES] = dot3(split(shared.T), c_rows)
    gbc_ref[:, LANES : 2 * LANES] = dot3(split(shared), b_rows)


def place_of(channel, share, size):
    if share > LANES:
        if channel < LANES * size:
            return channel // LANES, channel % LANES
        rest = share - LANES
        return (channel - LANES * size) // rest, LANES + (channel - LANES * size) % rest
    return channel // share, channel % share


def forward_kernel(
    heads_in, size, rows, msg_ref, act_ref, gate_ref, abc_ref, ld_ref, yw_ref, skip_ref, gt_ref, ys_ref, st_ref
):
    share = gt_ref.shape[1]
    unpack_blocks(msg_ref, st_ref, rows)
    c_rows = split(abc_ref[:, LANES : 2 * LANES])
    grown = jnp.exp(ld_ref[...])
    for j in range(act_ref.shape[1] // LANES):
        cols = slice(j * LANES, (j + 1) * LANES)
        carried = dot3(c_rows, split(st_ref[cols, :]), NT)
        within = yw_ref[:, cols] + spread(grown, j, heads_in, size) * carried
        ys_ref[:, cols] = within
        output = within + skip_ref[:, cols] * act_ref[:, cols]
        gate = gate_ref[:, cols].astype(F32)
        turned = (output * (gate * sigmoid(gate))).T.astype(BF16)
        for k in range(0, LANES, 16):
            to, at = place_of(j * LANES + k, share, gt_ref.shape[0])
            gt_ref[to, at : at + 16, :] = turned[k : k + 16]


def ahead_kernel(
    heads_in, size, rows, msg_ref, act_ref, gy_ref, ld_ref, gbcl_ref, ys_ref, gg_ref, gate_ref, skip_ref,
    gz_ref, yg_ref, gbc_ref, st_ref,
):
    unpack_blocks(msg_ref, st_ref, rows)
    grown = jnp.exp(ld_ref[...])
    sums = jnp.zeros(yg_ref.shape, F32)
    grad_c = gbcl_ref[:, LANES : 2 * LANES]
    for j in range(act_ref.shape[1] // LANES):
        cols = slice(j * LANES, (j + 1) * LANES)
        grad_y = gy_ref[:, cols]
        within = ys_ref[:, cols]
        gate = gate_ref[:, cols].astype(F32)
        opened = sigmoid(gate)
        output = within + skip_ref[:, cols] * act_ref[:, cols]
        gz_ref[:, cols] = (gg_ref[:, cols] * output * (opened * (1.0 + gate * (1.0 - opened)))).astype(BF16)
        onehot = head_of(j, heads_in, size)
        high, low = split(grad_y * within)
        sums = sums + (dot(high, onehot, NN) + dot(low, onehot, NN))
        grad_c = grad_c + dot3(split(spread(grown, j, heads_in, size) * grad_y), split(st_ref[cols, :]))
    yg_ref[...] = sums
    gbc_ref[:, 0:LANES] = gbcl_ref[:, 0:LANES]
    gbc_ref[:, LANES : 2 * LANES] = grad_c


def backward_kernel(
    heads_in, size, rows, me_ref, msg_ref, msgf_ref, act_ref, slope_ref, gy_ref, abc_ref, step_ref, ld_ref, gw_ref,
    gbcl_ref, yg_ref, skip_ref, dtw_ref, perw_ref, gx_ref, gbc_ref, gdt_ref,
    ca_ref, st_ref, cs_ref,
):
    length = act_ref.shape[0]
    unpack_blocks(msg_ref, ca_ref, rows, me_ref[0])
    unpack_blocks(msgf_ref, st_ref, rows)
    b_rows = split(abc_ref[:, 0:LANES])
    ld = ld_ref[...]
    step = step_ref[...]
    last = ld[length - 1 : length]
    weight = jnp.exp(last - ld) * step
    sums = jnp.zeros((length, LANES), F32)
    leaving = jnp.zeros((8, LANES), F32)
    grad_b = gbcl_ref[:, 0:LANES]
    cs_ref[...] = jnp.zeros_like(cs_ref)
    for j in range(act_ref.shape[1] // LANES):
        cols = slice(j * LANES, (j + 1) * LANES)
        inputs = act_ref[:, cols]
        grad_y = gy_ref[:, cols]
        carry = ca_ref[cols, :]
        state = st_ref[cols, :]
        carry_s = split(carry)
        wide = spread(weight, j, heads_in, size)
        gone = wide * dot3(b_rows, carry_s, NT)
        grad_in = gw_ref[:, cols] + gone
        gx_ref[:, cols] = ((skip_ref[:, cols] * grad_y + grad_in) * slope_ref[:, cols]).astype(BF16)
        onehot = head_of(j, heads_in, size)
        high, low = split(inputs * grad_in)
        sums = sums + (dot(high, onehot, NN) + dot(low, onehot, NN))
        folded = jnp.sum((inputs * gone).reshape(length // 8, 8, LANES), axis=0)
        high, low = split(folded)
        leaving = leaving + (dot(high, onehot, NN) + dot(low, onehot, NN))
        product = carry * state
        for k in range(heads_in):
            h = j * heads_in + k
            cs_ref[h : h + 1, :] = jnp.sum(product[k * size : (k + 1) * size], axis=0, keepdims=True)
        grad_b = grad_b + dot3(split(wide * inputs), carry_s)
    gbc_ref[:, 0:LANES] = grad_b
    gbc_ref[:, LANES : 2 * LANES] = gbcl_ref[:, LANES : 2 * LANES]
    both = lax.dot_general(
        jnp.ones((8, LANES), F32), cs_ref[...], (NT, ((), ())), precision=HIGH, preferred_element_type=F32
    )
    constant = jnp.sum(leaving, axis=0, keepdims=True) + jnp.exp(last) * both[0:1]
    upper = jnp.where(row_ids(length) <= lane_ids(length), 1.0, 0.0)
    grad_rate = constant + lax.dot_general(
        upper, yg_ref[...] - sums, (NN, ((), ())), precision=HIGH, preferred_element_type=F32
    )
    grad_step = sums / step - jnp.exp(perw_ref[1:2, :]) * grad_rate
    gdt_ref[...] = (grad_step * sigmoid(dtw_ref[...]))[:, 0 : gdt_ref.shape[1]]


def product_kernel(rows, held_ref, *refs):
    go_refs, out_ref, lhs_ref = refs[:-2], refs[-2], refs[-1]
    size, share, length = held_ref.shape

    @pl.when(pl.program_id(0) == 0)
    def _():
        for s in range(size):
            lhs_ref[:, s * length : (s + 1) * length] = held_ref[s]

    depth = go_refs[0].shape[0]
    result = dot(lhs_ref[:, 0:depth], go_refs[0][...], NN)
    for k in range(1, len(go_refs)):
        result = result + dot(lhs_ref[:, k * depth : (k + 1) * depth], go_refs[k][...], NN)
    result = result.T
    for d in range(out_ref.shape[0]):
        block = result[rows * d : rows * (d + 1)]
        if share > LANES:
            rest = share - LANES
            across = LANES // rest
            out_ref[d, 0:rows, :] = block[:, 0:LANES].astype(BF16)
            for k in range(0, rows // 16, across):
                pieces = [block[16 * m : 16 * m + 16, LANES:] for m in range(k, min(k + across, rows // 16))]
                if len(pieces) < across:
                    pieces.append(jnp.zeros((16, LANES - rest * len(pieces)), F32))
                at = rows + 16 * (k // across)
                out_ref[d, at : at + 16, :] = jnp.concatenate(pieces, axis=1).astype(BF16)
        else:
            out_ref[d] = block.astype(BF16)


def assemble_kernel(rows, size, share, parts_ref, out_ref):
    count = parts_ref.shape[0]

    def total(c, first, last):
        found = parts_ref[c, first:last, :].astype(F32)
        for s in range(c + size, count, size):
            found = found + parts_ref[s, first:last, :].astype(F32)
        return found

    if share > LANES:
        rest = share - LANES
        across = LANES // rest
        for c in range(size):
            out_ref[:, c * LANES : (c + 1) * LANES] = total(c, 0, rows)
            at = size * LANES + rest * c
            for k in range(0, rows // 16, across):
                extra = total(c, rows + 16 * (k // across), rows + 16 * (k // across) + 16)
                for m in range(k, min(k + across, rows // 16)):
                    lanes = slice(rest * (m - k), rest * (m - k + 1))
                    out_ref[16 * m : 16 * m + 16, at : at + rest] = extra[:, lanes]
    else:
        for c in range(size):
            out_ref[:, c * share : (c + 1) * share] = total(c, 0, rows)


def exchange(message, groups=None):
    half = message.astype(jnp.float16)
    return lax.all_to_all(half, "ctx", 0, 0, axis_index_groups=groups, tiled=True)


def swapped(message):
    half = message.astype(jnp.float16)
    count = lax.axis_size("ctx")
    slots = [half[0:1]]
    for m in range(1, message.shape[0]):
        slots.append(lax.ppermute(half[m : m + 1], "ctx", [(at, at ^ m) for at in range(count)]))
    return jnp.concatenate(slots).astype(F32)


def groups_of(count, size):
    return [list(range(at, at + size)) for at in range(0, count, size)]


def group_total(held, rows, reverse):
    (total,) = call(
        functools.partial(total_kernel, rows, reverse),
        [shape((1, *held.shape[1:]))],
        [held],
        4 * held.size,
        12,
    )
    return total.astype(jnp.float16)


def enter(me, held, total, rows, reverse):
    size = held.shape[0]
    count = lax.axis_size("ctx")
    others = []
    for hops in range(size, count, size):
        pairs = [(at, at + hops) for at in range(count - hops)]
        if reverse:
            pairs = [(b, a) for a, b in pairs]
        others.append(lax.ppermute(total, "ctx", pairs).astype(F32))
    (folded,) = call(
        functools.partial(fold_kernel, rows, reverse),
        [shape(held.shape)],
        [me, held, *others],
        8 * held.size,
        12,
        specs=[SMEM] + [VMEM] * (1 + len(others)),
    )
    return folded


def group_of(count):
    for size in (16, 8, 4, 2):
        if count % size == 0:
            return size
    return 1


def from_behind(value, axis):
    count = lax.axis_size(axis)
    return lax.ppermute(value, axis, [(source, source + 1) for source in range(count - 1)])


def per_device(
    x_raw,
    bc_raw,
    gate_branch,
    dt_raw,
    conv_x,
    conv_x_bias,
    conv_bc,
    conv_bc_bias,
    dt_bias,
    a_log,
    d_skip,
    out_weight,
    grad_out,
):
    length, head_count = dt_raw.shape
    channels = x_raw.shape[1]
    width = grad_out.shape[1]
    head_size = channels // head_count
    heads_in = LANES // head_size
    count = lax.axis_size("ctx")
    plane = min(8, group_of(count))
    planes = groups_of(count, plane)
    rows = channels // plane
    size = group_of(count)
    share = channels // size
    groups = groups_of(count, size)
    gathered = lax.all_gather(grad_out, "ctx", axis_index_groups=groups, tiled=True)

    raw = jnp.concatenate([x_raw, bc_raw], axis=1)
    taps = jnp.concatenate(
        [
            jnp.concatenate([conv_x, conv_bc], axis=1),
            jnp.concatenate([conv_x_bias, conv_bc_bias])[None, :],
        ]
    )
    rim = from_behind(raw[length - 16 :], "ctx")
    skip = jnp.repeat(d_skip, head_size)[None, :]
    whole = (length, channels)
    square = (length, LANES)
    block = up8(rows) + 8
    stored = pltpu.VMEM((channels, LANES), F32)
    unit = 2 * length * channels * LANES
    me = (lax.axis_index("ctx") % plane).astype(jnp.int32).reshape(1)

    padded = pltpu.VMEM((length + 8, channels + bc_raw.shape[1]), F32)
    per_raw = jnp.stack([dt_bias, a_log])
    act_bc, ld, message = call(
        functools.partial(prepare_kernel, heads_in, head_size, rows),
        [shape(bc_raw.shape), shape(square), shape((plane, block, LANES))],
        [raw, rim, taps, dt_raw, per_raw],
        20 * unit,
        20,
        [padded, stored, pltpu.VMEM(square, F32), pltpu.VMEM((8, LANES), F32)],
    )
    message, grad_out_then, raw_then = lax.optimization_barrier((message, grad_out, raw))
    held_state = exchange(message, planes).astype(F32)
    part = 640 if channels % 640 == 0 else channels
    grad_gated, grad_y = pl.pallas_call(
        gate_kernel,
        grid=(channels // part,),
        in_specs=[
            pl.BlockSpec((length, width), lambda i: (0, 0)),
        ]
        + [
            pl.BlockSpec((part, width // STREAMS), functools.partial(lambda k, i: (i, k), k))
            for k in range(STREAMS)
        ]
        + [pl.BlockSpec((length, part), lambda i: (0, i))],
        out_specs=(pl.BlockSpec((length, part), lambda i: (0, i)), pl.BlockSpec((length, part), lambda i: (0, i))),
        out_shape=(shape(whole), shape(whole)),
        compiler_params=pltpu.CompilerParams(vmem_limit_bytes=52 * MIB),
        cost_estimate=pl.CostEstimate(
            flops=2 * length * channels * width, bytes_accessed=2 * channels * width, transcendentals=0
        ),
    )(grad_out_then, *[out_weight] * STREAMS, gate_branch)
    (message,) = call(
        functools.partial(grad_kernel, heads_in, head_size, rows),
        [shape((plane, block, LANES))],
        [grad_y, act_bc, ld],
        10 * unit,
        12,
        [stored],
    )
    act_x, slope_x, slope_bc, step, step_t, ld_t, raised, per_head = call(
        functools.partial(keep_kernel, heads_in, head_size),
        [shape(whole), shape(whole), shape(bc_raw.shape), shape(square)]
        + [shape((LANES, length))] * 2
        + [shape(square), shape((8, LANES))],
        [raw_then, rim, taps, dt_raw, per_raw],
        10 * unit,
        20,
        [padded],
    )
    total, ld_t_then, message = lax.optimization_barrier((group_total(held_state, rows, False), ld_t, message))
    held_carry = exchange(message, planes)
    y_within, grad_within, grad_bc_within = call(
        functools.partial(local_kernel, heads_in, head_size),
        [shape(whole), shape(whole), shape(act_bc.shape)],
        [act_x, grad_y, act_bc, step, ld, step_t, ld_t_then],
        40 * unit,
        16,
        [pltpu.VMEM(square, F32)],
    )
    folded, held_carry, y_within = lax.optimization_barrier(
        (enter(me, held_state, total, rows, False), held_carry, y_within)
    )
    held_carry = held_carry.astype(F32)
    entered = enter(me, held_carry, group_total(held_carry, rows, True), rows, True)
    state_message = exchange(folded, planes).astype(F32)
    gated, y_ahead = call(
        functools.partial(forward_kernel, heads_in, head_size, rows),
        [shape((size, share, length), BF16), shape(whole)],
        [state_message, act_x, gate_branch, act_bc, ld, y_within, skip],
        20 * unit,
        16,
        [stored],
    )
    gated, entered, gathered, y_ahead = lax.optimization_barrier((gated, entered, gathered, y_ahead))
    held = lax.all_to_all(gated, "ctx", 0, 0, axis_index_groups=groups, tiled=True)
    grad_z, y_sums, grad_bc_ahead = call(
        functools.partial(ahead_kernel, heads_in, head_size, rows),
        [shape(whole, BF16), shape(square), shape(act_bc.shape)],
        [state_message, act_x, grad_y, ld, grad_bc_within, y_ahead, grad_gated, gate_branch, skip],
        20 * unit,
        16,
        [stored],
    )
    held, y_sums = lax.optimization_barrier((held, y_sums))
    out_rows = width // count
    part = width
    for candidate in (640, 1280):
        if width % candidate == 0 and candidate % out_rows == 0:
            part = candidate
            break
    dims = (out_rows, share)
    if share > LANES:
        dims = (out_rows + 16 * (-(-(out_rows // 16) // (LANES // (share - LANES)))), LANES)
    partial = pl.pallas_call(
        functools.partial(product_kernel, out_rows),
        grid=(width // part,),
        in_specs=[
            pl.BlockSpec((size, share, length), lambda i: (0, 0, 0)),
        ]
        + [
            pl.BlockSpec((size * length // STREAMS, part), functools.partial(lambda k, i: (k, i), k))
            for k in range(STREAMS)
        ],
        out_specs=pl.BlockSpec((part // out_rows, *dims), lambda i: (i, 0, 0)),
        out_shape=shape((count, *dims), BF16),
        scratch_shapes=[pltpu.VMEM((share, size * length), BF16)],
        compiler_params=pltpu.CompilerParams(vmem_limit_bytes=48 * MIB),
        cost_estimate=pl.CostEstimate(
            flops=2 * size * length * share * width, bytes_accessed=2 * size * length * width, transcendentals=0
        ),
    )(held, *[gathered] * STREAMS)
    partial, entered = lax.optimization_barrier((partial, entered))
    parts = lax.all_to_all(partial, "ctx", 0, 0, tiled=True)
    carry_message = swapped(entered)
    (weight_grad,) = call(
        functools.partial(assemble_kernel, out_rows, size, share),
        [shape((out_rows, channels))],
        [parts],
        2 * parts.size,
        12,
    )
    grad_x_conv, grad_bc, grad_dt_raw = call(
        functools.partial(backward_kernel, heads_in, head_size, rows),
        [shape(whole, BF16), shape(act_bc.shape), shape(dt_raw.shape)],
        [
            me,
            carry_message,
            state_message,
            act_x,
            slope_x,
            grad_y,
            act_bc,
            step,
            ld,
            grad_within,
            grad_bc_ahead,
            y_sums,
            skip,
            raised,
            per_head,
        ],
        40 * unit,
        28,
        [stored, stored, pltpu.VMEM((LANES, LANES), F32)],
        [SMEM] + [VMEM] * 14,
    )
    grad_bc_conv = (lax.psum(grad_bc, "tp") * slope_bc).astype(BF16)
    return (grad_x_conv, grad_bc_conv, grad_z, grad_dt_raw, weight_grad)


def solution(mesh):
    placed = (
        P("ctx", "tp"),
        P("ctx", None),
        P("ctx", "tp"),
        P("ctx", "tp"),
        P(None, "tp"),
        P("tp"),
        P(),
        P(),
        P("tp"),
        P("tp"),
        P("tp"),
        P("tp", None),
        P("ctx", None),
    )
    return jax.shard_map(
        per_device,
        mesh=mesh,
        in_specs=placed,
        out_specs=(P("ctx", "tp"), P("ctx", None), P("ctx", "tp"), P("ctx", "tp"), P("ctx", "tp")),
        check_vma=False,
    )
```

```python
import functools

import jax
import jax.numpy as jnp
from jax import lax
from jax.experimental import pallas as pl
from jax.experimental.pallas import tpu as pltpu
from jax.sharding import PartitionSpec as P

KERNEL = 4
LANES = 128
F32 = jnp.float32
BF16 = jnp.bfloat16
NN = ((1,), (0,))
NT = ((1,), (1,))
HIGH = lax.Precision.HIGHEST
SMEM = pl.BlockSpec(memory_space=pltpu.SMEM)
VMEM = pl.BlockSpec(memory_space=pltpu.VMEM)
MIB = 1024 * 1024
STREAMS = 4


def call(kernel, out_shapes, operands, flops, vmem, scratch=(), specs=None):
    extra = {} if specs is None else {"in_specs": specs}
    moved = sum(a.size * a.dtype.itemsize for a in (*operands, *out_shapes))
    return pl.pallas_call(
        kernel,
        out_shape=tuple(out_shapes),
        scratch_shapes=list(scratch),
        compiler_params=pltpu.CompilerParams(vmem_limit_bytes=vmem * MIB),
        cost_estimate=pl.CostEstimate(flops=flops, bytes_accessed=moved, transcendentals=0),
        **extra,
    )(*operands)


def shape(dims, dtype=F32):
    return jax.ShapeDtypeStruct(dims, dtype)


def split(value):
    high = value.astype(BF16)
    return high, (value - high.astype(F32)).astype(BF16)


def dot(a, b, dims):
    return lax.dot_general(a, b, (dims, ((), ())), preferred_element_type=F32)


def dot3(a, b, dims=NN):
    return dot(a[0], b[0], dims) + (dot(a[0], b[1], dims) + dot(a[1], b[0], dims))


def sigmoid(value):
    return 1.0 / (1.0 + jnp.exp(-value))


def lane_ids(rows, cols=LANES):
    return lax.broadcasted_iota(jnp.int32, (rows, cols), 1)


def row_ids(rows, cols=LANES):
    return lax.broadcasted_iota(jnp.int32, (rows, cols), 0)


def spread(columns, block, heads, size):
    first = block * heads
    lanes = lane_ids(columns.shape[0])
    wide = jnp.broadcast_to(columns[:, first : first + 1], (columns.shape[0], LANES))
    for k in range(1, heads):
        wide = jnp.where(lanes >= k * size, columns[:, first + k : first + k + 1], wide)
    return wide


def head_of(block, heads, size):
    inner = row_ids(LANES)
    target = lane_ids(LANES)
    result = jnp.zeros((LANES, LANES), F32)
    for k in range(heads):
        here = (inner >= k * size) & (inner < (k + 1) * size) & (target == block * heads + k)
        result = jnp.where(here, 1.0, result)
    return result.astype(BF16)


def stacked(value, heads, size):
    lanes = lane_ids(value.shape[0])
    return jnp.concatenate(
        [jnp.where((lanes >= k * size) & (lanes < (k + 1) * size), value, 0.0) for k in range(heads)],
        axis=0,
    )


def up8(value):
    return -(-value // 8) * 8


def notes_of(rows):
    return -(-rows // LANES)


def exponent_of(block):
    top = jnp.max(jnp.max(jnp.abs(block), axis=0, keepdims=True), axis=1, keepdims=True)
    return jnp.floor(jnp.log2(jnp.maximum(jnp.broadcast_to(top, (1, LANES)), 1e-30)))


def write_block(message, at, first, block, decays, exponent):
    rows = block.shape[0]
    padded = up8(rows)
    message[at, first : first + rows, :] = block * jnp.exp2(13.0 - exponent)
    if padded > rows:
        message[at, first + rows : first + padded, :] = jnp.zeros((padded - rows, LANES), F32)
    highs = [d.astype(BF16).astype(F32) for d in decays]
    lows = [d - h for d, h in zip(decays, highs)]
    place = row_ids(8)
    notes = jnp.broadcast_to(exponent, (8, LANES))
    for k, line in enumerate(highs + lows):
        notes = jnp.where(place == k, line, notes)
    message[at, first + padded : first + padded + 8, :] = notes


def decay_tables(last_exp, heads, size, rows, count):
    shift = size.bit_length() - 1
    tables = []
    for d in range(count):
        lines = []
        for k in range(notes_of(rows)):
            first = rows * d + LANES * k
            owner = lax.shift_right_logical(lane_ids(1) + first, shift)
            table = jnp.zeros((1, LANES), F32)
            for h in range(first // size, min(heads, (first + LANES - 1) // size + 1)):
                table = jnp.where(owner == h, last_exp[:, h : h + 1], table)
            lines.append(table)
        tables.append(lines)
    return tables


def pack_blocks(source, message, last_exp, size, rows):
    count = message.shape[0]
    tables = decay_tables(last_exp, source.shape[0] // size, size, rows, count)
    for d in range(count):
        block = source[rows * d : rows * (d + 1), :]
        write_block(message, d, 0, block, tables[d], exponent_of(block))


def decay_lines(message, at, rows):
    padded, lines = up8(rows), notes_of(rows)
    return [
        message[at, padded + k : padded + k + 1, :] + message[at, padded + lines + k : padded + lines + k + 1, :]
        for k in range(lines)
    ]


def decay_columns(message, rows):
    padded, lines = up8(rows), notes_of(rows)
    turned = [
        jnp.transpose(message[:, padded + k, :] + message[:, padded + lines + k, :]) for k in range(lines)
    ]
    return jnp.concatenate(turned, axis=0)[0:rows]


def read_block(message, at, rows):
    padded = up8(rows)
    return message[at, 0:rows, :] * jnp.exp2(message[at, padded + 7 : padded + 8, :] - 13.0)


def unpack_blocks(message, target, rows, me=0):
    for d in range(message.shape[0]):
        target[rows * d : rows * (d + 1), :] = read_block(message, me ^ d, rows)


def total_kernel(rows, reverse, held_ref, out_ref):
    count = held_ref.shape[0]
    columns = decay_columns(held_ref, rows)
    state = None
    for s in range(count - 1, -1, -1) if reverse else range(count):
        block = read_block(held_ref, s, rows)
        state = block if state is None else columns[:, s : s + 1] * state + block
    decays = decay_lines(held_ref, 0, rows)
    for s in range(1, count):
        decays = [a * b for a, b in zip(decays, decay_lines(held_ref, s, rows))]
    write_block(out_ref, 0, 0, state, decays, exponent_of(state))


def fold_kernel(rows, reverse, me_ref, held_ref, *refs):
    others, out_ref = refs[:-1], refs[-1]
    count = held_ref.shape[0]
    columns = decay_columns(held_ref, rows)
    state = jnp.zeros((rows, LANES), F32)
    for other in reversed(others):
        state = decay_columns(other, rows) * state + read_block(other, 0, rows)
    for s in range(count - 1, -1, -1) if reverse else range(count):
        write_block(out_ref, me_ref[0] ^ s if reverse else s, 0, state, [], exponent_of(state))
        if s != (0 if reverse else count - 1):
            state = columns[:, s : s + 1] * state + read_block(held_ref, s, rows)


def prepare(heads_in, size, raw_ref, rim_ref, taps_ref, dt_ref, per_ref, xs_ref, dtw_ref, perw_ref, length, channels):
    def convolved(cols):
        xs_ref[0:8, cols] = rim_ref[:, cols].astype(F32)[8:16]
        xs_ref[8 : 8 + length, cols] = raw_ref[:, cols].astype(F32)
        pre = taps_ref[KERNEL : KERNEL + 1, cols] + taps_ref[0:1, cols] * xs_ref[5 : 5 + length, cols]
        for k in range(1, KERNEL):
            pre = pre + taps_ref[k : k + 1, cols] * xs_ref[5 + k : 5 + k + length, cols]
        gate = sigmoid(pre)
        return pre * gate, gate * (1.0 + pre * (1.0 - gate))

    heads = dt_ref.shape[1]
    dtw_ref[...] = jnp.zeros_like(dtw_ref)
    dtw_ref[:, 0:heads] = dt_ref[...]
    perw_ref[...] = jnp.zeros_like(perw_ref)
    perw_ref[0:2, 0:heads] = per_ref[...]
    raised = dtw_ref[...] + perw_ref[0:1, :]
    dtw_ref[...] = raised
    step = jnp.maximum(raised, 0.0) + jnp.log1p(jnp.exp(-jnp.abs(raised)))
    lower = jnp.where(row_ids(length) >= lane_ids(length), 1.0, 0.0)
    ld = lax.dot_general(
        lower, step * -jnp.exp(perw_ref[1:2, :]), (NN, ((), ())), precision=HIGH, preferred_element_type=F32
    )
    return convolved, step, ld


def prepare_kernel(
    heads_in, size, rows, raw_ref, rim_ref, taps_ref, dt_ref, per_ref, abc_ref, ld_ref, msg_ref,
    xs_ref, st_ref, dtw_ref, perw_ref,
):
    length = raw_ref.shape[0]
    channels = st_ref.shape[0]
    convolved, step, ld = prepare(
        heads_in, size, raw_ref, rim_ref, taps_ref, dt_ref, per_ref, xs_ref, dtw_ref, perw_ref, length, channels
    )
    ld_ref[...] = ld
    for j in range(abc_ref.shape[1] // LANES):
        value, _ = convolved(slice(channels + j * LANES, channels + (j + 1) * LANES))
        abc_ref[:, j * LANES : (j + 1) * LANES] = value
    b_rows = split(abc_ref[:, 0:LANES])
    last = ld[length - 1 : length]
    weight = jnp.exp(last - ld) * step
    for j in range(channels // LANES):
        cols = slice(j * LANES, (j + 1) * LANES)
        value, _ = convolved(cols)
        scaled = value * spread(weight, j, heads_in, size)
        st_ref[cols, :] = dot3(split(scaled.T), b_rows)
    pack_blocks(st_ref, msg_ref, jnp.exp(last), size, rows)


def keep_kernel(
    heads_in, size, raw_ref, rim_ref, taps_ref, dt_ref, per_ref, act_ref, slope_ref, sbc_ref, step_ref,
    stept_ref, ldt_ref, dtw_ref, perw_ref, xs_ref,
):
    length, channels = act_ref.shape
    convolved, step, ld = prepare(
        heads_in, size, raw_ref, rim_ref, taps_ref, dt_ref, per_ref, xs_ref, dtw_ref, perw_ref, length, channels
    )
    step_ref[...] = step
    stept_ref[...] = step.T
    ldt_ref[...] = ld.T
    for j in range(sbc_ref.shape[1] // LANES):
        _, slope = convolved(slice(channels + j * LANES, channels + (j + 1) * LANES))
        sbc_ref[:, j * LANES : (j + 1) * LANES] = slope
    for j in range(channels // LANES):
        cols = slice(j * LANES, (j + 1) * LANES)
        act_ref[:, cols], slope_ref[:, cols] = convolved(cols)


def grad_kernel(heads_in, size, rows, gy_ref, abc_ref, ld_ref, msg_ref, st_ref):
    length = gy_ref.shape[0]
    c_rows = split(abc_ref[:, LANES : 2 * LANES])
    grown = jnp.exp(ld_ref[...])
    for j in range(gy_ref.shape[1] // LANES):
        cols = slice(j * LANES, (j + 1) * LANES)
        scaled = gy_ref[:, cols] * spread(grown, j, heads_in, size)
        st_ref[cols, :] = dot3(split(scaled.T), c_rows)
    pack_blocks(st_ref, msg_ref, grown[length - 1 : length], size, rows)


def gate_kernel(go_ref, *refs):
    w_refs, (gate_ref, gg_ref, gy_ref) = refs[:-3], refs[-3:]
    depth = w_refs[0].shape[1]
    grad = dot(w_refs[0][...], go_ref[:, 0:depth], NT)
    for k in range(1, len(w_refs)):
        grad = grad + dot(w_refs[k][...], go_ref[:, k * depth : (k + 1) * depth], NT)
    grad = grad.T
    gate = gate_ref[...].astype(F32)
    gg_ref[...] = grad
    gy_ref[...] = grad * (gate * sigmoid(gate))


def local_kernel(
    heads_in, size, act_ref, gy_ref, abc_ref, step_ref, ld_ref, stept_ref, ldt_ref, yw_ref, gw_ref, gbc_ref, sh_ref
):
    length = act_ref.shape[0]
    b_rows = split(abc_ref[:, 0:LANES])
    c_rows = split(abc_ref[:, LANES : 2 * LANES])
    scores = dot3(c_rows, b_rows, NT)
    turned = dot3(b_rows, c_rows, NT)
    causal = row_ids(length) >= lane_ids(length)
    causal_t = row_ids(length) <= lane_ids(length)
    sh_ref[...] = jnp.zeros_like(sh_ref)
    for j in range(act_ref.shape[1] // LANES):
        cols = slice(j * LANES, (j + 1) * LANES)
        mixes, mixes_t, steps = [], [], []
        for h in range(j * heads_in, (j + 1) * heads_in):
            column, row = ld_ref[:, h : h + 1], ldt_ref[h : h + 1, :]
            decays = jnp.exp(jnp.where(causal, column - row, -1e30))
            stepped = decays * stept_ref[h : h + 1, :]
            decays_t = jnp.exp(jnp.where(causal_t, row - column, -1e30))
            steps.append(stepped)
            mixes.append(stepped * scores)
            mixes_t.append(decays_t * turned * step_ref[:, h : h + 1])
        inputs = act_ref[:, cols]
        grad_y = gy_ref[:, cols]
        inputs_s = stacked(inputs, heads_in, size)
        grads_s = split(stacked(grad_y, heads_in, size))
        yw_ref[:, cols] = dot3(split(jnp.concatenate(mixes, axis=1)), split(inputs_s))
        gw_ref[:, cols] = dot3(split(jnp.concatenate(mixes_t, axis=1)), grads_s)
        products = dot3(grads_s, split(inputs), NT)
        total = sh_ref[...]
        for k in range(heads_in):
            total = total + steps[k] * products[k * length : (k + 1) * length]
        sh_ref[...] = total
    shared = sh_ref[...]
    gbc_ref[:, 0:LANES] = dot3(split(shared.T), c_rows)
    gbc_ref[:, LANES : 2 * LANES] = dot3(split(shared), b_rows)


def place_of(channel, share, size):
    if share > LANES:
        if channel < LANES * size:
            return channel // LANES, channel % LANES
        rest = share - LANES
        return (channel - LANES * size) // rest, LANES + (channel - LANES * size) % rest
    return channel // share, channel % share


def forward_kernel(
    heads_in, size, rows, msg_ref, act_ref, gate_ref, abc_ref, ld_ref, yw_ref, skip_ref, gt_ref, ys_ref, st_ref
):
    share = gt_ref.shape[1]
    unpack_blocks(msg_ref, st_ref, rows)
    c_rows = split(abc_ref[:, LANES : 2 * LANES])
    grown = jnp.exp(ld_ref[...])
    for j in range(act_ref.shape[1] // LANES):
        cols = slice(j * LANES, (j + 1) * LANES)
        carried = dot3(c_rows, split(st_ref[cols, :]), NT)
        within = yw_ref[:, cols] + spread(grown, j, heads_in, size) * carried
        ys_ref[:, cols] = within
        output = within + skip_ref[:, cols] * act_ref[:, cols]
        gate = gate_ref[:, cols].astype(F32)
        turned = (output * (gate * sigmoid(gate))).T.astype(BF16)
        for k in range(0, LANES, 16):
            to, at = place_of(j * LANES + k, share, gt_ref.shape[0])
            gt_ref[to, at : at + 16, :] = turned[k : k + 16]


def ahead_kernel(
    heads_in, size, rows, msg_ref, act_ref, gy_ref, ld_ref, gbcl_ref, ys_ref, gg_ref, gate_ref, skip_ref,
    gz_ref, yg_ref, gbc_ref, st_ref,
):
    unpack_blocks(msg_ref, st_ref, rows)
    grown = jnp.exp(ld_ref[...])
    sums = jnp.zeros(yg_ref.shape, F32)
    grad_c = gbcl_ref[:, LANES : 2 * LANES]
    for j in range(act_ref.shape[1] // LANES):
        cols = slice(j * LANES, (j + 1) * LANES)
        grad_y = gy_ref[:, cols]
        within = ys_ref[:, cols]
        gate = gate_ref[:, cols].astype(F32)
        opened = sigmoid(gate)
        output = within + skip_ref[:, cols] * act_ref[:, cols]
        gz_ref[:, cols] = (gg_ref[:, cols] * output * (opened * (1.0 + gate * (1.0 - opened)))).astype(BF16)
        onehot = head_of(j, heads_in, size)
        high, low = split(grad_y * within)
        sums = sums + (dot(high, onehot, NN) + dot(low, onehot, NN))
        grad_c = grad_c + dot3(split(spread(grown, j, heads_in, size) * grad_y), split(st_ref[cols, :]))
    yg_ref[...] = sums
    gbc_ref[:, 0:LANES] = gbcl_ref[:, 0:LANES]
    gbc_ref[:, LANES : 2 * LANES] = grad_c


def backward_kernel(
    heads_in, size, rows, me_ref, msg_ref, msgf_ref, act_ref, slope_ref, gy_ref, abc_ref, step_ref, ld_ref, gw_ref,
    gbcl_ref, yg_ref, skip_ref, dtw_ref, perw_ref, gx_ref, gbc_ref, gdt_ref,
    ca_ref, st_ref, cs_ref,
):
    length = act_ref.shape[0]
    unpack_blocks(msg_ref, ca_ref, rows, me_ref[0])
    unpack_blocks(msgf_ref, st_ref, rows)
    b_rows = split(abc_ref[:, 0:LANES])
    ld = ld_ref[...]
    step = step_ref[...]
    last = ld[length - 1 : length]
    weight = jnp.exp(last - ld) * step
    sums = jnp.zeros((length, LANES), F32)
    leaving = jnp.zeros((8, LANES), F32)
    grad_b = gbcl_ref[:, 0:LANES]
    cs_ref[...] = jnp.zeros_like(cs_ref)
    for j in range(act_ref.shape[1] // LANES):
        cols = slice(j * LANES, (j + 1) * LANES)
        inputs = act_ref[:, cols]
        grad_y = gy_ref[:, cols]
        carry = ca_ref[cols, :]
        state = st_ref[cols, :]
        carry_s = split(carry)
        wide = spread(weight, j, heads_in, size)
        gone = wide * dot3(b_rows, carry_s, NT)
        grad_in = gw_ref[:, cols] + gone
        gx_ref[:, cols] = ((skip_ref[:, cols] * grad_y + grad_in) * slope_ref[:, cols]).astype(BF16)
        onehot = head_of(j, heads_in, size)
        high, low = split(inputs * grad_in)
        sums = sums + (dot(high, onehot, NN) + dot(low, onehot, NN))
        folded = jnp.sum((inputs * gone).reshape(length // 8, 8, LANES), axis=0)
        high, low = split(folded)
        leaving = leaving + (dot(high, onehot, NN) + dot(low, onehot, NN))
        product = carry * state
        for k in range(heads_in):
            h = j * heads_in + k
            cs_ref[h : h + 1, :] = jnp.sum(product[k * size : (k + 1) * size], axis=0, keepdims=True)
        grad_b = grad_b + dot3(split(wide * inputs), carry_s)
    gbc_ref[:, 0:LANES] = grad_b
    gbc_ref[:, LANES : 2 * LANES] = gbcl_ref[:, LANES : 2 * LANES]
    both = lax.dot_general(
        jnp.ones((8, LANES), F32), cs_ref[...], (NT, ((), ())), precision=HIGH, preferred_element_type=F32
    )
    constant = jnp.sum(leaving, axis=0, keepdims=True) + jnp.exp(last) * both[0:1]
    upper = jnp.where(row_ids(length) <= lane_ids(length), 1.0, 0.0)
    grad_rate = constant + lax.dot_general(
        upper, yg_ref[...] - sums, (NN, ((), ())), precision=HIGH, preferred_element_type=F32
    )
    grad_step = sums / step - jnp.exp(perw_ref[1:2, :]) * grad_rate
    gdt_ref[...] = (grad_step * sigmoid(dtw_ref[...]))[:, 0 : gdt_ref.shape[1]]


def product_kernel(rows, held_ref, *refs):
    go_refs, out_ref, lhs_ref = refs[:-2], refs[-2], refs[-1]
    size, share, length = held_ref.shape

    @pl.when(pl.program_id(0) == 0)
    def _():
        for s in range(size):
            lhs_ref[:, s * length : (s + 1) * length] = held_ref[s]

    depth = go_refs[0].shape[0]
    result = dot(lhs_ref[:, 0:depth], go_refs[0][...], NN)
    for k in range(1, len(go_refs)):
        result = result + dot(lhs_ref[:, k * depth : (k + 1) * depth], go_refs[k][...], NN)
    result = result.T
    for d in range(out_ref.shape[0]):
        block = result[rows * d : rows * (d + 1)]
        if share > LANES:
            rest = share - LANES
            across = LANES // rest
            out_ref[d, 0:rows, :] = block[:, 0:LANES].astype(BF16)
            for k in range(0, rows // 16, across):
                pieces = [block[16 * m : 16 * m + 16, LANES:] for m in range(k, min(k + across, rows // 16))]
                if len(pieces) < across:
                    pieces.append(jnp.zeros((16, LANES - rest * len(pieces)), F32))
                at = rows + 16 * (k // across)
                out_ref[d, at : at + 16, :] = jnp.concatenate(pieces, axis=1).astype(BF16)
        else:
            out_ref[d] = block.astype(BF16)


def assemble_kernel(rows, size, share, parts_ref, out_ref):
    count = parts_ref.shape[0]

    def total(c, first, last):
        found = parts_ref[c, first:last, :].astype(F32)
        for s in range(c + size, count, size):
            found = found + parts_ref[s, first:last, :].astype(F32)
        return found

    if share > LANES:
        rest = share - LANES
        across = LANES // rest
        for c in range(size):
            out_ref[:, c * LANES : (c + 1) * LANES] = total(c, 0, rows)
            at = size * LANES + rest * c
            for k in range(0, rows // 16, across):
                extra = total(c, rows + 16 * (k // across), rows + 16 * (k // across) + 16)
                for m in range(k, min(k + across, rows // 16)):
                    lanes = slice(rest * (m - k), rest * (m - k + 1))
                    out_ref[16 * m : 16 * m + 16, at : at + rest] = extra[:, lanes]
    else:
        for c in range(size):
            out_ref[:, c * share : (c + 1) * share] = total(c, 0, rows)


def exchange(message, groups=None):
    half = message.astype(jnp.float16)
    return lax.all_to_all(half, "ctx", 0, 0, axis_index_groups=groups, tiled=True)


def swapped(message):
    half = message.astype(jnp.float16)
    count = lax.axis_size("ctx")
    slots = [half[0:1]]
    for m in range(1, message.shape[0]):
        slots.append(lax.ppermute(half[m : m + 1], "ctx", [(at, at ^ m) for at in range(count)]))
    return jnp.concatenate(slots).astype(F32)


def groups_of(count, size):
    return [list(range(at, at + size)) for at in range(0, count, size)]


def group_total(held, rows, reverse):
    (total,) = call(
        functools.partial(total_kernel, rows, reverse),
        [shape((1, *held.shape[1:]))],
        [held],
        4 * held.size,
        12,
    )
    return total.astype(jnp.float16)


def enter(me, held, total, rows, reverse):
    size = held.shape[0]
    count = lax.axis_size("ctx")
    others = []
    for hops in range(size, count, size):
        pairs = [(at, at + hops) for at in range(count - hops)]
        if reverse:
            pairs = [(b, a) for a, b in pairs]
        others.append(lax.ppermute(total, "ctx", pairs).astype(F32))
    (folded,) = call(
        functools.partial(fold_kernel, rows, reverse),
        [shape(held.shape)],
        [me, held, *others],
        8 * held.size,
        12,
        specs=[SMEM] + [VMEM] * (1 + len(others)),
    )
    return folded


def group_of(count):
    for size in (16, 8, 4, 2):
        if count % size == 0:
            return size
    return 1


def from_behind(value, axis):
    count = lax.axis_size(axis)
    return lax.ppermute(value, axis, [(source, source + 1) for source in range(count - 1)])


def per_device(
    x_raw,
    bc_raw,
    gate_branch,
    dt_raw,
    conv_x,
    conv_x_bias,
    conv_bc,
    conv_bc_bias,
    dt_bias,
    a_log,
    d_skip,
    out_weight,
    grad_out,
):
    length, head_count = dt_raw.shape
    channels = x_raw.shape[1]
    width = grad_out.shape[1]
    head_size = channels // head_count
    heads_in = LANES // head_size
    count = lax.axis_size("ctx")
    plane = min(8, group_of(count))
    planes = groups_of(count, plane)
    rows = channels // plane
    size = group_of(count)
    share = channels // size
    groups = groups_of(count, size)
    gathered = lax.all_gather(grad_out, "ctx", axis_index_groups=groups, tiled=True)

    raw = jnp.concatenate([x_raw, bc_raw], axis=1)
    taps = jnp.concatenate(
        [
            jnp.concatenate([conv_x, conv_bc], axis=1),
            jnp.concatenate([conv_x_bias, conv_bc_bias])[None, :],
        ]
    )
    rim = from_behind(raw[length - 16 :], "ctx")
    skip = jnp.repeat(d_skip, head_size)[None, :]
    whole = (length, channels)
    square = (length, LANES)
    block = up8(rows) + 8
    stored = pltpu.VMEM((channels, LANES), F32)
    unit = 2 * length * channels * LANES
    me = (lax.axis_index("ctx") % plane).astype(jnp.int32).reshape(1)

    padded = pltpu.VMEM((length + 8, channels + bc_raw.shape[1]), F32)
    per_raw = jnp.stack([dt_bias, a_log])
    act_bc, ld, message = call(
        functools.partial(prepare_kernel, heads_in, head_size, rows),
        [shape(bc_raw.shape), shape(square), shape((plane, block, LANES))],
        [raw, rim, taps, dt_raw, per_raw],
        20 * unit,
        20,
        [padded, stored, pltpu.VMEM(square, F32), pltpu.VMEM((8, LANES), F32)],
    )
    message, grad_out_then, raw_then = lax.optimization_barrier((message, grad_out, raw))
    held_state = exchange(message, planes).astype(F32)
    part = 640 if channels % 640 == 0 else channels
    grad_gated, grad_y = pl.pallas_call(
        gate_kernel,
        grid=(channels // part,),
        in_specs=[
            pl.BlockSpec((length, width), lambda i: (0, 0)),
        ]
        + [
            pl.BlockSpec((part, width // STREAMS), functools.partial(lambda k, i: (i, k), k))
            for k in range(STREAMS)
        ]
        + [pl.BlockSpec((length, part), lambda i: (0, i))],
        out_specs=(pl.BlockSpec((length, part), lambda i: (0, i)), pl.BlockSpec((length, part), lambda i: (0, i))),
        out_shape=(shape(whole), shape(whole)),
        compiler_params=pltpu.CompilerParams(vmem_limit_bytes=52 * MIB),
        cost_estimate=pl.CostEstimate(
            flops=2 * length * channels * width, bytes_accessed=2 * channels * width, transcendentals=0
        ),
    )(grad_out_then, *[out_weight] * STREAMS, gate_branch)
    (message,) = call(
        functools.partial(grad_kernel, heads_in, head_size, rows),
        [shape((plane, block, LANES))],
        [grad_y, act_bc, ld],
        10 * unit,
        12,
        [stored],
    )
    act_x, slope_x, slope_bc, step, step_t, ld_t, raised, per_head = call(
        functools.partial(keep_kernel, heads_in, head_size),
        [shape(whole), shape(whole), shape(bc_raw.shape), shape(square)]
        + [shape((LANES, length))] * 2
        + [shape(square), shape((8, LANES))],
        [raw_then, rim, taps, dt_raw, per_raw],
        10 * unit,
        60,
        [padded],
    )
    total, ld_t_then, message = lax.optimization_barrier((group_total(held_state, rows, False), ld_t, message))
    held_carry = exchange(message, planes)
    y_within, grad_within, grad_bc_within = call(
        functools.partial(local_kernel, heads_in, head_size),
        [shape(whole), shape(whole), shape(act_bc.shape)],
        [act_x, grad_y, act_bc, step, ld, step_t, ld_t_then],
        40 * unit,
        60,
        [pltpu.VMEM(square, F32)],
    )
    folded, held_carry, y_within = lax.optimization_barrier(
        (enter(me, held_state, total, rows, False), held_carry, y_within)
    )
    held_carry = held_carry.astype(F32)
    entered = enter(me, held_carry, group_total(held_carry, rows, True), rows, True)
    state_message = exchange(folded, planes).astype(F32)
    gated, y_ahead = call(
        functools.partial(forward_kernel, heads_in, head_size, rows),
        [shape((size, share, length), BF16), shape(whole)],
        [state_message, act_x, gate_branch, act_bc, ld, y_within, skip],
        20 * unit,
        16,
        [stored],
    )
    gated, entered, gathered, y_ahead = lax.optimization_barrier((gated, entered, gathered, y_ahead))
    held = lax.all_to_all(gated, "ctx", 0, 0, axis_index_groups=groups, tiled=True)
    grad_z, y_sums, grad_bc_ahead = call(
        functools.partial(ahead_kernel, heads_in, head_size, rows),
        [shape(whole, BF16), shape(square), shape(act_bc.shape)],
        [state_message, act_x, grad_y, ld, grad_bc_within, y_ahead, grad_gated, gate_branch, skip],
        20 * unit,
        16,
        [stored],
    )
    held, y_sums = lax.optimization_barrier((held, y_sums))
    out_rows = width // count
    part = width
    for candidate in (640, 1280):
        if width % candidate == 0 and candidate % out_rows == 0:
            part = candidate
            break
    dims = (out_rows, share)
    if share > LANES:
        dims = (out_rows + 16 * (-(-(out_rows // 16) // (LANES // (share - LANES)))), LANES)
    partial = pl.pallas_call(
        functools.partial(product_kernel, out_rows),
        grid=(width // part,),
        in_specs=[
            pl.BlockSpec((size, share, length), lambda i: (0, 0, 0)),
        ]
        + [
            pl.BlockSpec((size * length // STREAMS, part), functools.partial(lambda k, i: (k, i), k))
            for k in range(STREAMS)
        ],
        out_specs=pl.BlockSpec((part // out_rows, *dims), lambda i: (i, 0, 0)),
        out_shape=shape((count, *dims), BF16),
        scratch_shapes=[pltpu.VMEM((share, size * length), BF16)],
        compiler_params=pltpu.CompilerParams(vmem_limit_bytes=48 * MIB),
        cost_estimate=pl.CostEstimate(
            flops=2 * size * length * share * width, bytes_accessed=2 * size * length * width, transcendentals=0
        ),
    )(held, *[gathered] * STREAMS)
    partial, entered = lax.optimization_barrier((partial, entered))
    parts = lax.all_to_all(partial, "ctx", 0, 0, tiled=True)
    carry_message = swapped(entered)
    (weight_grad,) = call(
        functools.partial(assemble_kernel, out_rows, size, share),
        [shape((out_rows, channels))],
        [parts],
        2 * parts.size,
        12,
    )
    grad_x_conv, grad_bc, grad_dt_raw = call(
        functools.partial(backward_kernel, heads_in, head_size, rows),
        [shape(whole, BF16), shape(act_bc.shape), shape(dt_raw.shape)],
        [
            me,
            carry_message,
            state_message,
            act_x,
            slope_x,
            grad_y,
            act_bc,
            step,
            ld,
            grad_within,
            grad_bc_ahead,
            y_sums,
            skip,
            raised,
            per_head,
        ],
        40 * unit,
        28,
        [stored, stored, pltpu.VMEM((LANES, LANES), F32)],
        [SMEM] + [VMEM] * 14,
    )
    grad_bc_conv = (lax.psum(grad_bc, "tp") * slope_bc).astype(BF16)
    return (grad_x_conv, grad_bc_conv, grad_z, grad_dt_raw, weight_grad)


def solution(mesh):
    placed = (
        P("ctx", "tp"),
        P("ctx", None),
        P("ctx", "tp"),
        P("ctx", "tp"),
        P(None, "tp"),
        P("tp"),
        P(),
        P(),
        P("tp"),
        P("tp"),
        P("tp"),
        P("tp", None),
        P("ctx", None),
    )
    return jax.shard_map(
        per_device,
        mesh=mesh,
        in_specs=placed,
        out_specs=(P("ctx", "tp"), P("ctx", None), P("ctx", "tp"), P("ctx", "tp"), P("ctx", "tp")),
        check_vma=False,
    )
```

```python
import functools

import jax
import jax.numpy as jnp
from jax import lax
from jax.experimental import pallas as pl
from jax.experimental.pallas import tpu as pltpu
from jax.sharding import PartitionSpec as P

KERNEL = 4
LANES = 128
F32 = jnp.float32
BF16 = jnp.bfloat16
NN = ((1,), (0,))
NT = ((1,), (1,))
HIGH = lax.Precision.HIGHEST
SMEM = pl.BlockSpec(memory_space=pltpu.SMEM)
VMEM = pl.BlockSpec(memory_space=pltpu.VMEM)
MIB = 1024 * 1024
STREAMS = 4


def call(kernel, out_shapes, operands, flops, vmem, scratch=(), specs=None):
    extra = {} if specs is None else {"in_specs": specs}
    moved = sum(a.size * a.dtype.itemsize for a in (*operands, *out_shapes))
    return pl.pallas_call(
        kernel,
        out_shape=tuple(out_shapes),
        scratch_shapes=list(scratch),
        compiler_params=pltpu.CompilerParams(vmem_limit_bytes=vmem * MIB),
        cost_estimate=pl.CostEstimate(flops=flops, bytes_accessed=moved, transcendentals=0),
        **extra,
    )(*operands)


def shape(dims, dtype=F32):
    return jax.ShapeDtypeStruct(dims, dtype)


def split(value):
    high = value.astype(BF16)
    return high, (value - high.astype(F32)).astype(BF16)


def dot(a, b, dims):
    return lax.dot_general(a, b, (dims, ((), ())), preferred_element_type=F32)


def dot3(a, b, dims=NN):
    return dot(a[0], b[0], dims) + (dot(a[0], b[1], dims) + dot(a[1], b[0], dims))


def sigmoid(value):
    return 1.0 / (1.0 + jnp.exp(-value))


def lane_ids(rows, cols=LANES):
    return lax.broadcasted_iota(jnp.int32, (rows, cols), 1)


def row_ids(rows, cols=LANES):
    return lax.broadcasted_iota(jnp.int32, (rows, cols), 0)


def spread(columns, block, heads, size):
    first = block * heads
    lanes = lane_ids(columns.shape[0])
    wide = jnp.broadcast_to(columns[:, first : first + 1], (columns.shape[0], LANES))
    for k in range(1, heads):
        wide = jnp.where(lanes >= k * size, columns[:, first + k : first + k + 1], wide)
    return wide


def head_of(block, heads, size):
    inner = row_ids(LANES)
    target = lane_ids(LANES)
    result = jnp.zeros((LANES, LANES), F32)
    for k in range(heads):
        here = (inner >= k * size) & (inner < (k + 1) * size) & (target == block * heads + k)
        result = jnp.where(here, 1.0, result)
    return result.astype(BF16)


def stacked(value, heads, size):
    lanes = lane_ids(value.shape[0])
    return jnp.concatenate(
        [jnp.where((lanes >= k * size) & (lanes < (k + 1) * size), value, 0.0) for k in range(heads)],
        axis=0,
    )


def up8(value):
    return -(-value // 8) * 8


def notes_of(rows):
    return -(-rows // LANES)


def exponent_of(block):
    top = jnp.max(jnp.max(jnp.abs(block), axis=0, keepdims=True), axis=1, keepdims=True)
    return jnp.floor(jnp.log2(jnp.maximum(jnp.broadcast_to(top, (1, LANES)), 1e-30)))


def write_block(message, at, first, block, decays, exponent):
    rows = block.shape[0]
    padded = up8(rows)
    message[at, first : first + rows, :] = block * jnp.exp2(13.0 - exponent)
    if padded > rows:
        message[at, first + rows : first + padded, :] = jnp.zeros((padded - rows, LANES), F32)
    highs = [d.astype(BF16).astype(F32) for d in decays]
    lows = [d - h for d, h in zip(decays, highs)]
    place = row_ids(8)
    notes = jnp.broadcast_to(exponent, (8, LANES))
    for k, line in enumerate(highs + lows):
        notes = jnp.where(place == k, line, notes)
    message[at, first + padded : first + padded + 8, :] = notes


def decay_tables(last_exp, heads, size, rows, count):
    shift = size.bit_length() - 1
    tables = []
    for d in range(count):
        lines = []
        for k in range(notes_of(rows)):
            first = rows * d + LANES * k
            owner = lax.shift_right_logical(lane_ids(1) + first, shift)
            table = jnp.zeros((1, LANES), F32)
            for h in range(first // size, min(heads, (first + LANES - 1) // size + 1)):
                table = jnp.where(owner == h, last_exp[:, h : h + 1], table)
            lines.append(table)
        tables.append(lines)
    return tables


def pack_blocks(source, message, last_exp, size, rows):
    count = message.shape[0]
    tables = decay_tables(last_exp, source.shape[0] // size, size, rows, count)
    for d in range(count):
        block = source[rows * d : rows * (d + 1), :]
        write_block(message, d, 0, block, tables[d], exponent_of(block))


def decay_lines(message, at, rows):
    padded, lines = up8(rows), notes_of(rows)
    return [
        message[at, padded + k : padded + k + 1, :] + message[at, padded + lines + k : padded + lines + k + 1, :]
        for k in range(lines)
    ]


def decay_columns(message, rows):
    padded, lines = up8(rows), notes_of(rows)
    turned = [
        jnp.transpose(message[:, padded + k, :] + message[:, padded + lines + k, :]) for k in range(lines)
    ]
    return jnp.concatenate(turned, axis=0)[0:rows]


def read_block(message, at, rows):
    padded = up8(rows)
    return message[at, 0:rows, :] * jnp.exp2(message[at, padded + 7 : padded + 8, :] - 13.0)


def unpack_blocks(message, target, rows, me=0):
    for d in range(message.shape[0]):
        target[rows * d : rows * (d + 1), :] = read_block(message, me ^ d, rows)


def total_kernel(rows, reverse, held_ref, out_ref):
    count = held_ref.shape[0]
    columns = decay_columns(held_ref, rows)
    state = None
    for s in range(count - 1, -1, -1) if reverse else range(count):
        block = read_block(held_ref, s, rows)
        state = block if state is None else columns[:, s : s + 1] * state + block
    decays = decay_lines(held_ref, 0, rows)
    for s in range(1, count):
        decays = [a * b for a, b in zip(decays, decay_lines(held_ref, s, rows))]
    write_block(out_ref, 0, 0, state, decays, exponent_of(state))


def fold_kernel(rows, reverse, me_ref, held_ref, *refs):
    others, out_ref = refs[:-1], refs[-1]
    count = held_ref.shape[0]
    columns = decay_columns(held_ref, rows)
    state = jnp.zeros((rows, LANES), F32)
    for other in reversed(others):
        state = decay_columns(other, rows) * state + read_block(other, 0, rows)
    for s in range(count - 1, -1, -1) if reverse else range(count):
        write_block(out_ref, me_ref[0] ^ s if reverse else s, 0, state, [], exponent_of(state))
        if s != (0 if reverse else count - 1):
            state = columns[:, s : s + 1] * state + read_block(held_ref, s, rows)


def prepare(heads_in, size, raw_ref, rim_ref, taps_ref, dt_ref, per_ref, xs_ref, dtw_ref, perw_ref, length, channels):
    def convolved(cols):
        xs_ref[0:8, cols] = rim_ref[:, cols].astype(F32)[8:16]
        xs_ref[8 : 8 + length, cols] = raw_ref[:, cols].astype(F32)
        pre = taps_ref[KERNEL : KERNEL + 1, cols] + taps_ref[0:1, cols] * xs_ref[5 : 5 + length, cols]
        for k in range(1, KERNEL):
            pre = pre + taps_ref[k : k + 1, cols] * xs_ref[5 + k : 5 + k + length, cols]
        gate = sigmoid(pre)
        return pre * gate, gate * (1.0 + pre * (1.0 - gate))

    heads = dt_ref.shape[1]
    dtw_ref[...] = jnp.zeros_like(dtw_ref)
    dtw_ref[:, 0:heads] = dt_ref[...]
    perw_ref[...] = jnp.zeros_like(perw_ref)
    perw_ref[0:2, 0:heads] = per_ref[...]
    raised = dtw_ref[...] + perw_ref[0:1, :]
    dtw_ref[...] = raised
    step = jnp.maximum(raised, 0.0) + jnp.log1p(jnp.exp(-jnp.abs(raised)))
    lower = jnp.where(row_ids(length) >= lane_ids(length), 1.0, 0.0)
    ld = lax.dot_general(
        lower, step * -jnp.exp(perw_ref[1:2, :]), (NN, ((), ())), precision=HIGH, preferred_element_type=F32
    )
    return convolved, step, ld


def prepare_kernel(
    heads_in, size, rows, raw_ref, rim_ref, taps_ref, dt_ref, per_ref, abc_ref, ld_ref, msg_ref,
    xs_ref, st_ref, dtw_ref, perw_ref,
):
    length = raw_ref.shape[0]
    channels = st_ref.shape[0]
    convolved, step, ld = prepare(
        heads_in, size, raw_ref, rim_ref, taps_ref, dt_ref, per_ref, xs_ref, dtw_ref, perw_ref, length, channels
    )
    ld_ref[...] = ld
    for j in range(abc_ref.shape[1] // LANES):
        value, _ = convolved(slice(channels + j * LANES, channels + (j + 1) * LANES))
        abc_ref[:, j * LANES : (j + 1) * LANES] = value
    b_rows = split(abc_ref[:, 0:LANES])
    last = ld[length - 1 : length]
    weight = jnp.exp(last - ld) * step
    for j in range(channels // LANES):
        cols = slice(j * LANES, (j + 1) * LANES)
        value, _ = convolved(cols)
        scaled = value * spread(weight, j, heads_in, size)
        st_ref[cols, :] = dot3(split(scaled.T), b_rows)
    pack_blocks(st_ref, msg_ref, jnp.exp(last), size, rows)


def keep_kernel(
    heads_in, size, raw_ref, rim_ref, taps_ref, dt_ref, per_ref, act_ref, slope_ref, sbc_ref, step_ref,
    stept_ref, ldt_ref, dtw_ref, perw_ref, xs_ref,
):
    length, channels = act_ref.shape
    convolved, step, ld = prepare(
        heads_in, size, raw_ref, rim_ref, taps_ref, dt_ref, per_ref, xs_ref, dtw_ref, perw_ref, length, channels
    )
    step_ref[...] = step
    stept_ref[...] = step.T
    ldt_ref[...] = ld.T
    for j in range(sbc_ref.shape[1] // LANES):
        _, slope = convolved(slice(channels + j * LANES, channels + (j + 1) * LANES))
        sbc_ref[:, j * LANES : (j + 1) * LANES] = slope
    for j in range(channels // LANES):
        cols = slice(j * LANES, (j + 1) * LANES)
        act_ref[:, cols], slope_ref[:, cols] = convolved(cols)


def grad_kernel(heads_in, size, rows, gy_ref, abc_ref, ld_ref, msg_ref, st_ref):
    length = gy_ref.shape[0]
    c_rows = split(abc_ref[:, LANES : 2 * LANES])
    grown = jnp.exp(ld_ref[...])
    for j in range(gy_ref.shape[1] // LANES):
        cols = slice(j * LANES, (j + 1) * LANES)
        scaled = gy_ref[:, cols] * spread(grown, j, heads_in, size)
        st_ref[cols, :] = dot3(split(scaled.T), c_rows)
    pack_blocks(st_ref, msg_ref, grown[length - 1 : length], size, rows)


def gate_kernel(go_ref, *refs):
    w_refs, (gate_ref, gg_ref, gy_ref) = refs[:-3], refs[-3:]
    depth = w_refs[0].shape[1]
    grad = dot(w_refs[0][...], go_ref[:, 0:depth], NT)
    for k in range(1, len(w_refs)):
        grad = grad + dot(w_refs[k][...], go_ref[:, k * depth : (k + 1) * depth], NT)
    grad = grad.T
    gate = gate_ref[...].astype(F32)
    gg_ref[...] = grad
    gy_ref[...] = grad * (gate * sigmoid(gate))


def local_kernel(
    heads_in, size, act_ref, gy_ref, abc_ref, step_ref, ld_ref, stept_ref, ldt_ref, yw_ref, gw_ref, gbc_ref, sh_ref
):
    length = act_ref.shape[0]
    b_rows = split(abc_ref[:, 0:LANES])
    c_rows = split(abc_ref[:, LANES : 2 * LANES])
    scores = dot3(c_rows, b_rows, NT)
    turned = dot3(b_rows, c_rows, NT)
    causal = row_ids(length) >= lane_ids(length)
    causal_t = row_ids(length) <= lane_ids(length)
    sh_ref[...] = jnp.zeros_like(sh_ref)
    for j in range(act_ref.shape[1] // LANES):
        cols = slice(j * LANES, (j + 1) * LANES)
        mixes, mixes_t, steps = [], [], []
        for h in range(j * heads_in, (j + 1) * heads_in):
            column, row = ld_ref[:, h : h + 1], ldt_ref[h : h + 1, :]
            decays = jnp.exp(jnp.where(causal, column - row, -1e30))
            stepped = decays * stept_ref[h : h + 1, :]
            decays_t = jnp.exp(jnp.where(causal_t, row - column, -1e30))
            steps.append(stepped)
            mixes.append(stepped * scores)
            mixes_t.append(decays_t * turned * step_ref[:, h : h + 1])
        inputs = act_ref[:, cols]
        grad_y = gy_ref[:, cols]
        inputs_s = stacked(inputs, heads_in, size)
        grads_s = split(stacked(grad_y, heads_in, size))
        yw_ref[:, cols] = dot3(split(jnp.concatenate(mixes, axis=1)), split(inputs_s))
        gw_ref[:, cols] = dot3(split(jnp.concatenate(mixes_t, axis=1)), grads_s)
        products = dot3(grads_s, split(inputs), NT)
        total = sh_ref[...]
        for k in range(heads_in):
            total = total + steps[k] * products[k * length : (k + 1) * length]
        sh_ref[...] = total
    shared = sh_ref[...]
    gbc_ref[:, 0:LANES] = dot3(split(shared.T), c_rows)
    gbc_ref[:, LANES : 2 * LANES] = dot3(split(shared), b_rows)


def place_of(channel, share, size):
    if share > LANES:
        if channel < LANES * size:
            return channel // LANES, channel % LANES
        rest = share - LANES
        return (channel - LANES * size) // rest, LANES + (channel - LANES * size) % rest
    return channel // share, channel % share


def forward_kernel(
    heads_in, size, rows, msg_ref, act_ref, gate_ref, abc_ref, ld_ref, yw_ref, skip_ref, gt_ref, ys_ref, st_ref
):
    share = gt_ref.shape[1]
    unpack_blocks(msg_ref, st_ref, rows)
    c_rows = split(abc_ref[:, LANES : 2 * LANES])
    grown = jnp.exp(ld_ref[...])
    for j in range(act_ref.shape[1] // LANES):
        cols = slice(j * LANES, (j + 1) * LANES)
        carried = dot3(c_rows, split(st_ref[cols, :]), NT)
        within = yw_ref[:, cols] + spread(grown, j, heads_in, size) * carried
        ys_ref[:, cols] = within
        output = within + skip_ref[:, cols] * act_ref[:, cols]
        gate = gate_ref[:, cols].astype(F32)
        turned = (output * (gate * sigmoid(gate))).T.astype(BF16)
        for k in range(0, LANES, 16):
            to, at = place_of(j * LANES + k, share, gt_ref.shape[0])
            gt_ref[to, at : at + 16, :] = turned[k : k + 16]


def ahead_kernel(
    heads_in, size, rows, msg_ref, act_ref, gy_ref, ld_ref, gbcl_ref, ys_ref, gg_ref, gate_ref, skip_ref,
    gz_ref, yg_ref, gbc_ref, st_ref,
):
    unpack_blocks(msg_ref, st_ref, rows)
    grown = jnp.exp(ld_ref[...])
    sums = jnp.zeros(yg_ref.shape, F32)
    grad_c = gbcl_ref[:, LANES : 2 * LANES]
    for j in range(act_ref.shape[1] // LANES):
        cols = slice(j * LANES, (j + 1) * LANES)
        grad_y = gy_ref[:, cols]
        within = ys_ref[:, cols]
        gate = gate_ref[:, cols].astype(F32)
        opened = sigmoid(gate)
        output = within + skip_ref[:, cols] * act_ref[:, cols]
        gz_ref[:, cols] = (gg_ref[:, cols] * output * (opened * (1.0 + gate * (1.0 - opened)))).astype(BF16)
        onehot = head_of(j, heads_in, size)
        high, low = split(grad_y * within)
        sums = sums + (dot(high, onehot, NN) + dot(low, onehot, NN))
        grad_c = grad_c + dot3(split(spread(grown, j, heads_in, size) * grad_y), split(st_ref[cols, :]))
    yg_ref[...] = sums
    gbc_ref[:, 0:LANES] = gbcl_ref[:, 0:LANES]
    gbc_ref[:, LANES : 2 * LANES] = grad_c


def backward_kernel(
    heads_in, size, rows, me_ref, msg_ref, msgf_ref, act_ref, slope_ref, gy_ref, abc_ref, step_ref, ld_ref, gw_ref,
    gbcl_ref, yg_ref, skip_ref, dtw_ref, perw_ref, gx_ref, gbc_ref, gdt_ref,
    ca_ref, st_ref, cs_ref,
):
    length = act_ref.shape[0]
    unpack_blocks(msg_ref, ca_ref, rows, me_ref[0])
    unpack_blocks(msgf_ref, st_ref, rows)
    b_rows = split(abc_ref[:, 0:LANES])
    ld = ld_ref[...]
    step = step_ref[...]
    last = ld[length - 1 : length]
    weight = jnp.exp(last - ld) * step
    sums = jnp.zeros((length, LANES), F32)
    leaving = jnp.zeros((8, LANES), F32)
    grad_b = gbcl_ref[:, 0:LANES]
    cs_ref[...] = jnp.zeros_like(cs_ref)
    for j in range(act_ref.shape[1] // LANES):
        cols = slice(j * LANES, (j + 1) * LANES)
        inputs = act_ref[:, cols]
        grad_y = gy_ref[:, cols]
        carry = ca_ref[cols, :]
        state = st_ref[cols, :]
        carry_s = split(carry)
        wide = spread(weight, j, heads_in, size)
        gone = wide * dot3(b_rows, carry_s, NT)
        grad_in = gw_ref[:, cols] + gone
        gx_ref[:, cols] = ((skip_ref[:, cols] * grad_y + grad_in) * slope_ref[:, cols]).astype(BF16)
        onehot = head_of(j, heads_in, size)
        high, low = split(inputs * grad_in)
        sums = sums + (dot(high, onehot, NN) + dot(low, onehot, NN))
        folded = jnp.sum((inputs * gone).reshape(length // 8, 8, LANES), axis=0)
        high, low = split(folded)
        leaving = leaving + (dot(high, onehot, NN) + dot(low, onehot, NN))
        product = carry * state
        for k in range(heads_in):
            h = j * heads_in + k
            cs_ref[h : h + 1, :] = jnp.sum(product[k * size : (k + 1) * size], axis=0, keepdims=True)
        grad_b = grad_b + dot3(split(wide * inputs), carry_s)
    gbc_ref[:, 0:LANES] = grad_b
    gbc_ref[:, LANES : 2 * LANES] = gbcl_ref[:, LANES : 2 * LANES]
    both = lax.dot_general(
        jnp.ones((8, LANES), F32), cs_ref[...], (NT, ((), ())), precision=HIGH, preferred_element_type=F32
    )
    constant = jnp.sum(leaving, axis=0, keepdims=True) + jnp.exp(last) * both[0:1]
    upper = jnp.where(row_ids(length) <= lane_ids(length), 1.0, 0.0)
    grad_rate = constant + lax.dot_general(
        upper, yg_ref[...] - sums, (NN, ((), ())), precision=HIGH, preferred_element_type=F32
    )
    grad_step = sums / step - jnp.exp(perw_ref[1:2, :]) * grad_rate
    gdt_ref[...] = (grad_step * sigmoid(dtw_ref[...]))[:, 0 : gdt_ref.shape[1]]


def product_kernel(rows, held_ref, *refs):
    go_refs, out_ref, lhs_ref = refs[:-2], refs[-2], refs[-1]
    size, share, length = held_ref.shape

    @pl.when(pl.program_id(0) == 0)
    def _():
        for s in range(size):
            lhs_ref[:, s * length : (s + 1) * length] = held_ref[s]

    depth = go_refs[0].shape[0]
    result = dot(lhs_ref[:, 0:depth], go_refs[0][...], NN)
    for k in range(1, len(go_refs)):
        result = result + dot(lhs_ref[:, k * depth : (k + 1) * depth], go_refs[k][...], NN)
    result = result.T
    for d in range(out_ref.shape[0]):
        block = result[rows * d : rows * (d + 1)]
        if share > LANES:
            rest = share - LANES
            across = LANES // rest
            out_ref[d, 0:rows, :] = block[:, 0:LANES].astype(BF16)
            for k in range(0, rows // 16, across):
                pieces = [block[16 * m : 16 * m + 16, LANES:] for m in range(k, min(k + across, rows // 16))]
                if len(pieces) < across:
                    pieces.append(jnp.zeros((16, LANES - rest * len(pieces)), F32))
                at = rows + 16 * (k // across)
                out_ref[d, at : at + 16, :] = jnp.concatenate(pieces, axis=1).astype(BF16)
        else:
            out_ref[d] = block.astype(BF16)


def assemble_kernel(rows, size, share, parts_ref, out_ref):
    count = parts_ref.shape[0]

    def total(c, first, last):
        found = parts_ref[c, first:last, :].astype(F32)
        for s in range(c + size, count, size):
            found = found + parts_ref[s, first:last, :].astype(F32)
        return found

    if share > LANES:
        rest = share - LANES
        across = LANES // rest
        for c in range(size):
            out_ref[:, c * LANES : (c + 1) * LANES] = total(c, 0, rows)
            at = size * LANES + rest * c
            for k in range(0, rows // 16, across):
                extra = total(c, rows + 16 * (k // across), rows + 16 * (k // across) + 16)
                for m in range(k, min(k + across, rows // 16)):
                    lanes = slice(rest * (m - k), rest * (m - k + 1))
                    out_ref[16 * m : 16 * m + 16, at : at + rest] = extra[:, lanes]
    else:
        for c in range(size):
            out_ref[:, c * share : (c + 1) * share] = total(c, 0, rows)


def exchange(message, groups=None):
    half = message.astype(jnp.float16)
    return lax.all_to_all(half, "ctx", 0, 0, axis_index_groups=groups, tiled=True)


def swapped(message):
    half = message.astype(jnp.float16)
    count = lax.axis_size("ctx")
    slots = [half[0:1]]
    for m in range(1, message.shape[0]):
        slots.append(lax.ppermute(half[m : m + 1], "ctx", [(at, at ^ m) for at in range(count)]))
    return jnp.concatenate(slots).astype(F32)


def groups_of(count, size):
    return [list(range(at, at + size)) for at in range(0, count, size)]


def group_total(held, rows, reverse):
    (total,) = call(
        functools.partial(total_kernel, rows, reverse),
        [shape((1, *held.shape[1:]))],
        [held],
        4 * held.size,
        12,
    )
    return total.astype(jnp.float16)


def enter(me, held, total, rows, reverse):
    size = held.shape[0]
    count = lax.axis_size("ctx")
    others = []
    for hops in reversed(range(size, count, size)):
        pairs = [(at, at + hops) for at in range(count - hops)]
        if reverse:
            pairs = [(b, a) for a, b in pairs]
        others.insert(0, lax.ppermute(total, "ctx", pairs).astype(F32))
    (folded,) = call(
        functools.partial(fold_kernel, rows, reverse),
        [shape(held.shape)],
        [me, held, *others],
        8 * held.size,
        12,
        specs=[SMEM] + [VMEM] * (1 + len(others)),
    )
    return folded


def group_of(count):
    for size in (16, 8, 4, 2):
        if count % size == 0:
            return size
    return 1


def from_behind(value, axis):
    count = lax.axis_size(axis)
    return lax.ppermute(value, axis, [(source, source + 1) for source in range(count - 1)])


def per_device(
    x_raw,
    bc_raw,
    gate_branch,
    dt_raw,
    conv_x,
    conv_x_bias,
    conv_bc,
    conv_bc_bias,
    dt_bias,
    a_log,
    d_skip,
    out_weight,
    grad_out,
):
    length, head_count = dt_raw.shape
    channels = x_raw.shape[1]
    width = grad_out.shape[1]
    head_size = channels // head_count
    heads_in = LANES // head_size
    count = lax.axis_size("ctx")
    plane = min(8, group_of(count))
    planes = groups_of(count, plane)
    rows = channels // plane
    size = group_of(count)
    share = channels // size
    groups = groups_of(count, size)
    gathered = lax.all_gather(grad_out, "ctx", axis_index_groups=groups, tiled=True)

    raw = jnp.concatenate([x_raw, bc_raw], axis=1)
    taps = jnp.concatenate(
        [
            jnp.concatenate([conv_x, conv_bc], axis=1),
            jnp.concatenate([conv_x_bias, conv_bc_bias])[None, :],
        ]
    )
    rim = from_behind(raw[length - 16 :], "ctx")
    skip = jnp.repeat(d_skip, head_size)[None, :]
    whole = (length, channels)
    square = (length, LANES)
    block = up8(rows) + 8
    stored = pltpu.VMEM((channels, LANES), F32)
    unit = 2 * length * channels * LANES
    me = (lax.axis_index("ctx") % plane).astype(jnp.int32).reshape(1)

    padded = pltpu.VMEM((length + 8, channels + bc_raw.shape[1]), F32)
    per_raw = jnp.stack([dt_bias, a_log])
    act_bc, ld, message = call(
        functools.partial(prepare_kernel, heads_in, head_size, rows),
        [shape(bc_raw.shape), shape(square), shape((plane, block, LANES))],
        [raw, rim, taps, dt_raw, per_raw],
        20 * unit,
        20,
        [padded, stored, pltpu.VMEM(square, F32), pltpu.VMEM((8, LANES), F32)],
    )
    message, grad_out_then, raw_then = lax.optimization_barrier((message, grad_out, raw))
    held_state = exchange(message, planes).astype(F32)
    part = 640 if channels % 640 == 0 else channels
    grad_gated, grad_y = pl.pallas_call(
        gate_kernel,
        grid=(channels // part,),
        in_specs=[
            pl.BlockSpec((length, width), lambda i: (0, 0)),
        ]
        + [
            pl.BlockSpec((part, width // STREAMS), functools.partial(lambda k, i: (i, k), k))
            for k in range(STREAMS)
        ]
        + [pl.BlockSpec((length, part), lambda i: (0, i))],
        out_specs=(pl.BlockSpec((length, part), lambda i: (0, i)), pl.BlockSpec((length, part), lambda i: (0, i))),
        out_shape=(shape(whole), shape(whole)),
        compiler_params=pltpu.CompilerParams(vmem_limit_bytes=52 * MIB),
        cost_estimate=pl.CostEstimate(
            flops=2 * length * channels * width, bytes_accessed=2 * channels * width, transcendentals=0
        ),
    )(grad_out_then, *[out_weight] * STREAMS, gate_branch)
    (message,) = call(
        functools.partial(grad_kernel, heads_in, head_size, rows),
        [shape((plane, block, LANES))],
        [grad_y, act_bc, ld],
        10 * unit,
        12,
        [stored],
    )
    act_x, slope_x, slope_bc, step, step_t, ld_t, raised, per_head = call(
        functools.partial(keep_kernel, heads_in, head_size),
        [shape(whole), shape(whole), shape(bc_raw.shape), shape(square)]
        + [shape((LANES, length))] * 2
        + [shape(square), shape((8, LANES))],
        [raw_then, rim, taps, dt_raw, per_raw],
        10 * unit,
        60,
        [padded],
    )
    total, ld_t_then, message = lax.optimization_barrier((group_total(held_state, rows, False), ld_t, message))
    held_carry = exchange(message, planes)
    y_within, grad_within, grad_bc_within = call(
        functools.partial(local_kernel, heads_in, head_size),
        [shape(whole), shape(whole), shape(act_bc.shape)],
        [act_x, grad_y, act_bc, step, ld, step_t, ld_t_then],
        40 * unit,
        60,
        [pltpu.VMEM(square, F32)],
    )
    folded, held_carry, y_within = lax.optimization_barrier(
        (enter(me, held_state, total, rows, False), held_carry, y_within)
    )
    held_carry = held_carry.astype(F32)
    entered = enter(me, held_carry, group_total(held_carry, rows, True), rows, True)
    state_message = exchange(folded, planes).astype(F32)
    gated, y_ahead = call(
        functools.partial(forward_kernel, heads_in, head_size, rows),
        [shape((size, share, length), BF16), shape(whole)],
        [state_message, act_x, gate_branch, act_bc, ld, y_within, skip],
        20 * unit,
        16,
        [stored],
    )
    gated, entered, gathered, y_ahead = lax.optimization_barrier((gated, entered, gathered, y_ahead))
    held = lax.all_to_all(gated, "ctx", 0, 0, axis_index_groups=groups, tiled=True)
    grad_z, y_sums, grad_bc_ahead = call(
        functools.partial(ahead_kernel, heads_in, head_size, rows),
        [shape(whole, BF16), shape(square), shape(act_bc.shape)],
        [state_message, act_x, grad_y, ld, grad_bc_within, y_ahead, grad_gated, gate_branch, skip],
        20 * unit,
        16,
        [stored],
    )
    held, y_sums = lax.optimization_barrier((held, y_sums))
    out_rows = width // count
    part = width
    for candidate in (640, 1280):
        if width % candidate == 0 and candidate % out_rows == 0:
            part = candidate
            break
    dims = (out_rows, share)
    if share > LANES:
        dims = (out_rows + 16 * (-(-(out_rows // 16) // (LANES // (share - LANES)))), LANES)
    partial = pl.pallas_call(
        functools.partial(product_kernel, out_rows),
        grid=(width // part,),
        in_specs=[
            pl.BlockSpec((size, share, length), lambda i: (0, 0, 0)),
        ]
        + [
            pl.BlockSpec((size * length // STREAMS, part), functools.partial(lambda k, i: (k, i), k))
            for k in range(STREAMS)
        ],
        out_specs=pl.BlockSpec((part // out_rows, *dims), lambda i: (i, 0, 0)),
        out_shape=shape((count, *dims), BF16),
        scratch_shapes=[pltpu.VMEM((share, size * length), BF16)],
        compiler_params=pltpu.CompilerParams(vmem_limit_bytes=48 * MIB),
        cost_estimate=pl.CostEstimate(
            flops=2 * size * length * share * width, bytes_accessed=2 * size * length * width, transcendentals=0
        ),
    )(held, *[gathered] * STREAMS)
    partial, entered = lax.optimization_barrier((partial, entered))
    parts = lax.all_to_all(partial, "ctx", 0, 0, tiled=True)
    carry_message = swapped(entered)
    (weight_grad,) = call(
        functools.partial(assemble_kernel, out_rows, size, share),
        [shape((out_rows, channels))],
        [parts],
        2 * parts.size,
        12,
    )
    grad_x_conv, grad_bc, grad_dt_raw = call(
        functools.partial(backward_kernel, heads_in, head_size, rows),
        [shape(whole, BF16), shape(act_bc.shape), shape(dt_raw.shape)],
        [
            me,
            carry_message,
            state_message,
            act_x,
            slope_x,
            grad_y,
            act_bc,
            step,
            ld,
            grad_within,
            grad_bc_ahead,
            y_sums,
            skip,
            raised,
            per_head,
        ],
        40 * unit,
        28,
        [stored, stored, pltpu.VMEM((LANES, LANES), F32)],
        [SMEM] + [VMEM] * 14,
    )
    grad_bc_conv = (lax.psum(grad_bc, "tp") * slope_bc).astype(BF16)
    return (grad_x_conv, grad_bc_conv, grad_z, grad_dt_raw, weight_grad)


def solution(mesh):
    placed = (
        P("ctx", "tp"),
        P("ctx", None),
        P("ctx", "tp"),
        P("ctx", "tp"),
        P(None, "tp"),
        P("tp"),
        P(),
        P(),
        P("tp"),
        P("tp"),
        P("tp"),
        P("tp", None),
        P("ctx", None),
    )
    return jax.shard_map(
        per_device,
        mesh=mesh,
        in_specs=placed,
        out_specs=(P("ctx", "tp"), P("ctx", None), P("ctx", "tp"), P("ctx", "tp"), P("ctx", "tp")),
        check_vma=False,
    )
```
